512 devices in a mesh: wide: 64 (over z, x), narrow: 8 (over y, core).
Axes of the slice: x: 4, y: 4, z: 16, core: 2. Of those that a mesh axis runs over, the one named last changes fastest.
Arguments:
- phase: int32 [1024, 128, 256], P('wide', 'narrow'), may hold values 0 or 1
- distance: float32 [1024, 128, 256], P('wide', 'narrow'), may hold values from 0.05 to 3
- velocity: float32 [3, 1024, 128, 256], P(None, 'wide', 'narrow'), may hold values from -3 to 3
Outputs:
- moved: float32 [1024, 128, 256], P('wide', 'narrow')
- pressure: float32 [1024, 128, 256], P('wide', 'narrow')
The draws below stay inside these ranges and needn't reach their ends.
All inputs are finite; a program needn't handle non-finite values. No bound on the sum of `phase` on one device may be relied on, other than what follows from the above.
Results may differ from the reference program's by a relative error of at most 0.0001.
Values sent between devices are 32-bit elements; how exact they have to be, the bound alone decides.
No kernel may reach another device: no remote copies, remote signals or barrier semaphores. Data moves between devices by JAX's collectives and lax.ppermute only.
A program may use at most 128 MiB of HBM per device.

```python
import math
import jax
import jax.numpy as jnp
from jax import lax

NZ = 256
LEVELS = 4
PRE = 2
POST = 2
COARSE = 4
CYCLES = 2
NX = 1024
NY = 128


def place_ends(entries, own_key, smallest, top_value):
    extent = entries.shape
    place = [jax.random.randint(jax.random.fold_in(own_key, axis), (), 0, extent[axis]) for axis in range(len(extent))]
    entries = entries.at[tuple(place)].set(smallest)
    longest = extent.index(max(extent))
    place[longest] = (place[longest] + 1) % extent[longest]
    return entries.at[tuple(place)].set(top_value)


def block_levels(rng, extent, pieces, low, top_value):
    gain = 1.0
    for dim, parts in pieces:
        draws = jax.random.uniform(jax.random.fold_in(jax.random.fold_in(rng, 6), dim), (parts,), jnp.float32, low / len(pieces), top_value / len(pieces))
        gain = gain * jnp.repeat(jnp.exp(draws), extent[dim] // parts).reshape((-1,) + (1,) * (len(extent) - 1 - dim))
    return gain


def gaussian(stream_key, shape, deviation, limit, shards=(), held_as=jnp.bfloat16):
    entries = deviation * jax.random.normal(stream_key, shape, jnp.float32)
    if shards:
        entries = entries * block_levels(stream_key, shape, shards, -0.22, 0.18)
    return jnp.clip(entries, -limit, limit).astype(held_as)


def setup_inputs(seed: int = 0) -> dict:
    key_of = jax.random.split(jax.random.key(seed), 4)
    return {
        "phase": place_ends((jax.random.randint(key_of[0], (NX, NY, NZ), 0, 3) < 1).astype(jnp.int32), jax.random.fold_in(key_of[0], 1), 0, 1),
        "distance": jnp.clip(jnp.exp(math.log(3.0) - 4.0943445 * jax.random.uniform(key_of[1], (NX, NY, NZ), jnp.float32) ** block_levels(key_of[1], (NX, NY, NZ), ((0, 64), (1, 8)), -0.2, 0.2)), 0.05, 3.0),
        "velocity": gaussian(key_of[2], (3, NX, NY, NZ), 0.5, 3.0, ((1, 64), (2, 8)), jnp.float32),
    }


TIME_STEP = 0.25
TENSION = 4.0
DELTA_SQ = 0.0025
WENO_EPS = 0.01
RELAX_WEIGHT = 0.8

def reconstruct(far_up, upwind, centre, downwind, far_down):
    smooth_zero = 13.0 / 12.0 * (far_up - 2.0 * upwind + centre) ** 2 + 0.25 * (far_up - 4.0 * upwind + 3.0 * centre) ** 2
    smooth_one = 13.0 / 12.0 * (upwind - 2.0 * centre + downwind) ** 2 + 0.25 * (upwind - downwind) ** 2
    smooth_two = 13.0 / 12.0 * (centre - 2.0 * downwind + far_down) ** 2 + 0.25 * (3.0 * centre - 4.0 * downwind + far_down) ** 2
    weight_zero = 0.1 / (WENO_EPS + smooth_zero) ** 2
    weight_one = 0.6 / (WENO_EPS + smooth_one) ** 2
    weight_two = 0.3 / (WENO_EPS + smooth_two) ** 2
    guess_zero = (2.0 * far_up - 7.0 * upwind + 11.0 * centre) / 6.0
    guess_one = (-upwind + 5.0 * centre + 2.0 * downwind) / 6.0
    guess_two = (2.0 * centre + 5.0 * downwind - far_down) / 6.0
    return (weight_zero * guess_zero + weight_one * guess_one + weight_two * guess_two) / (weight_zero + weight_one + weight_two)

def weno_divergence(values, speeds, dimension, length):
    layers = [lax.slice_in_dim(values, offset, offset + length + 1, axis=dimension) for offset in range(6)]
    face_speed = 0.5 * (lax.slice_in_dim(speeds, 0, length + 1, axis=dimension) + lax.slice_in_dim(speeds, 1, length + 2, axis=dimension))
    left_value = reconstruct(layers[0], layers[1], layers[2], layers[3], layers[4])
    right_value = reconstruct(layers[5], layers[4], layers[3], layers[2], layers[1])
    flux = jnp.maximum(face_speed, 0.0) * left_value + jnp.minimum(face_speed, 0.0) * right_value
    return lax.slice_in_dim(flux, 1, length + 1, axis=dimension) - lax.slice_in_dim(flux, 0, length, axis=dimension)

def advect(psi_pad, vel_pad):
    count_x = psi_pad.shape[0] - 6
    count_y = psi_pad.shape[1] - 6
    count_z = psi_pad.shape[2] - 6
    centre = psi_pad[3:-3, 3:-3, 3:-3]
    change = weno_divergence(psi_pad[:, 3:-3, 3:-3], vel_pad[0][:, 1:-1, 1:-1], 0, count_x)
    change = change + weno_divergence(psi_pad[3:-3, :, 3:-3], vel_pad[1][1:-1, :, 1:-1], 1, count_y)
    change = change + weno_divergence(psi_pad[3:-3, 3:-3, :], vel_pad[2][1:-1, 1:-1, :], 2, count_z)
    return centre - TIME_STEP * change

def gradient(padded):
    grad_x = 0.5 * (padded[2:, 1:-1, 1:-1] - padded[:-2, 1:-1, 1:-1])
    grad_y = 0.5 * (padded[1:-1, 2:, 1:-1] - padded[1:-1, :-2, 1:-1])
    grad_z = 0.5 * (padded[1:-1, 1:-1, 2:] - padded[1:-1, 1:-1, :-2])
    return (grad_x, grad_y, grad_z)

def curvature(padded):
    grad_x, grad_y, grad_z = gradient(padded)
    inverse = 1.0 / jnp.sqrt(grad_x * grad_x + grad_y * grad_y + grad_z * grad_z + DELTA_SQ)
    normal = jnp.stack((grad_x * inverse, grad_y * inverse, grad_z * inverse))
    bending = -(0.5 * (normal[0][2:, 1:-1, 1:-1] - normal[0][:-2, 1:-1, 1:-1]) + 0.5 * (normal[1][1:-1, 2:, 1:-1] - normal[1][1:-1, :-2, 1:-1]) + 0.5 * (normal[2][1:-1, 1:-1, 2:] - normal[2][1:-1, 1:-1, :-2]))
    inner_grad = jnp.stack((grad_x[1:-1, 1:-1, 1:-1], grad_y[1:-1, 1:-1, 1:-1], grad_z[1:-1, 1:-1, 1:-1]))
    return (bending, inner_grad)

def source_term(star_pad):
    return -(0.5 * (star_pad[0][2:, 1:-1, 1:-1] - star_pad[0][:-2, 1:-1, 1:-1]) + 0.5 * (star_pad[1][1:-1, 2:, 1:-1] - star_pad[1][1:-1, :-2, 1:-1]) + 0.5 * (star_pad[2][1:-1, 1:-1, 2:] - star_pad[2][1:-1, 1:-1, :-2]))

def apply_padded(padded, spacing_sq):
    centre = padded[1:-1, 1:-1, 1:-1]
    beside = padded[2:, 1:-1, 1:-1] + padded[:-2, 1:-1, 1:-1] + padded[1:-1, 2:, 1:-1] + padded[1:-1, :-2, 1:-1] + padded[1:-1, 1:-1, 2:] + padded[1:-1, 1:-1, :-2]
    return (6.0 * centre - beside) / spacing_sq

def smooth_step(estimate, source, spacing_sq):
    return estimate + RELAX_WEIGHT * spacing_sq / 6.0 * (source - apply_padded(jnp.pad(estimate, 1), spacing_sq))

def coarsen(values):
    size_x, size_y, size_z = values.shape
    return values.reshape(size_x // 2, 2, size_y // 2, 2, size_z // 2, 2).mean(axis=(1, 3, 5))

def refine(values):
    return jnp.repeat(jnp.repeat(jnp.repeat(values, 2, axis=0), 2, axis=1), 2, axis=2)

def v_cycle(estimate, source):
    sources = [source]
    stored = []
    for level_index in range(LEVELS - 1):
        spacing_sq = 4.0 ** level_index
        for sweep_index in range(PRE):
            estimate = smooth_step(estimate, sources[level_index], spacing_sq)
        stored.append(estimate)
        leftover = sources[level_index] - apply_padded(jnp.pad(estimate, 1), spacing_sq)
        sources.append(coarsen(leftover))
        estimate = jnp.zeros_like(sources[level_index + 1])
    for sweep_index in range(COARSE):
        estimate = smooth_step(estimate, sources[LEVELS - 1], 4.0 ** (LEVELS - 1))
    for level_index in reversed(range(LEVELS - 1)):
        spacing_sq = 4.0 ** level_index
        estimate = stored[level_index] + refine(estimate)
        for sweep_index in range(POST):
            estimate = smooth_step(estimate, sources[level_index], spacing_sq)
    return estimate

def reference(phase, distance, velocity):
    orient = 2.0 * phase.astype(jnp.float32) - 1.0
    level_set = 1.0 / (1.0 + jnp.exp(-orient * distance))
    moved = advect(jnp.pad(level_set, 3), jnp.pad(velocity, ((0, 0), (1, 1), (1, 1), (1, 1))))
    bending, inner_grad = curvature(jnp.pad(moved, 2))
    provisional = velocity + TIME_STEP * TENSION * bending[None] * inner_grad
    source = source_term(jnp.pad(provisional, ((0, 0), (1, 1), (1, 1), (1, 1))))
    pressure = jnp.zeros_like(source)
    for cycle_index in range(CYCLES):
        pressure = v_cycle(pressure, source)
    return (moved, pressure)
```

```python
import functools

import jax
import jax.numpy as jnp
from jax import lax
from jax.experimental import pallas as pl
from jax.experimental.pallas import tpu as pltpu
from jax.sharding import PartitionSpec as P

DELTA_SQ = 0.0025
WENO_EPS = 0.01
SIDE = 0.8 / 6.0
F32 = jnp.float32
HIGHEST = lax.Precision.HIGHEST
VMEM_LIMIT = 56 * 1024 * 1024

HALO = 10
ROWS = 12
GROUP = 4


def iota(shape, dim):
    return lax.broadcasted_iota(jnp.int32, shape, dim)


def roll(v, shift, axis):
    return pltpu.roll(v, shift % v.shape[axis], axis)


def z_shifted(v):
    lane = iota(v.shape, 1)
    last = v.shape[1] - 1
    lower = jnp.where(lane == 0, 0.0, roll(v, 1, 1))
    upper = jnp.where(lane == last, 0.0, roll(v, -1, 1))
    return lower, upper


def z_pair(v):
    lower, upper = z_shifted(v)
    return lower + upper


def y_pair(v):
    return roll(v, 1, 0) + roll(v, -1, 0)


def beside(ref, i):
    c = ref[i]
    return c, (ref[i - 1] + ref[i + 1]) + y_pair(c) + z_pair(c)


def inside(first, count):
    return jnp.logical_and(first >= 0, first < count)


def row_mask(shape, first, count):
    rows = iota(shape, 0) + first
    return jnp.where(inside(rows, count), 1.0, 0.0).astype(F32)


def plane_factor(index, count):
    return jnp.where(inside(index, count), 1.0, 0.0).astype(F32)


def dot(a, b):
    return lax.dot_general(
        a, b, (((1,), (0,)), ((), ())), precision=HIGHEST, preferred_element_type=F32
    )


def pair_matrix(rows, cols, value):
    return jnp.where((iota((rows, cols), 0) >> 1) == iota((rows, cols), 1), value, 0.0).astype(F32)


def copy_matrix(rows, cols):
    return jnp.where(iota((rows, cols), 0) == (iota((rows, cols), 1) >> 1), 1.0, 0.0).astype(F32)


def call(body, outs, scratch, args, flops):
    vmem = pl.BlockSpec(memory_space=pltpu.VMEM)
    smem = pl.BlockSpec(memory_space=pltpu.SMEM)
    return pl.pallas_call(
        body,
        out_shape=[jax.ShapeDtypeStruct(s, F32) for s in outs],
        in_specs=[smem if a.dtype == jnp.int32 and a.ndim == 1 else vmem for a in args],
        out_specs=[vmem] * len(outs),
        scratch_shapes=[pltpu.VMEM(s, F32) for s in scratch],
        compiler_params=pltpu.CompilerParams(vmem_limit_bytes=VMEM_LIMIT),
        cost_estimate=pl.CostEstimate(flops=flops, bytes_accessed=4000000, transcendentals=0),
    )(*args)


def prepare_body(phase, distance, velocity, psi, x_low, x_high, y_low, y_high):
    def plane(i, carry):
        orient = 2.0 * phase[i].astype(F32) - 1.0
        psi[i] = 1.0 / (1.0 + jnp.exp(-orient * distance[i]))
        y_low[i, 0:3, :] = psi[i, 0:3, :]
        y_low[i, 3:4, :] = velocity[1, i, 0:1, :]
        y_high[i, 0:3, :] = psi[i, 13:16, :]
        y_high[i, 3:4, :] = velocity[1, i, 15:16, :]
        return carry

    lax.fori_loop(0, 16, plane, 0)
    for k in range(3):
        x_low[k] = psi[k]
        x_high[k] = psi[13 + k]
    x_low[3] = velocity[0, 0]
    x_high[3] = velocity[0, 15]


def prepare(phase, distance, velocity):
    outs = [(16, 16, 256), (4, 16, 256), (4, 16, 256), (16, 4, 256), (16, 4, 256)]
    return call(prepare_body, outs, [], [phase, distance, velocity], 1000000)


def indicators(a, b, c):
    d = a - c
    curve = (a + c) - 2.0 * b
    twice = 2.0 * curve
    base = (13.0 / 12.0) * (curve * curve) + WENO_EPS
    up, down = twice - d, twice + d
    p = base + 0.25 * (up * up)
    q = base + 0.25 * (d * d)
    r = base + 0.25 * (down * down)
    return p * p, q * q, r * r


def upwind_flux(s, l, p_left, q_left, r_left, p_right, q_right, r_right):
    ahead = s > 0.0
    pick = lambda x, y: jnp.where(ahead, x, y)
    a, b, c, e, f = pick(l[0], l[5]), pick(l[1], l[4]), pick(l[2], l[3]), pick(l[3], l[2]), pick(l[4], l[1])
    p, q, r = pick(p_left, r_right), pick(q_left, q_right), pick(r_left, p_right)
    w0, w1, w2 = 0.1 * (q * r), 0.6 * (p * r), 0.3 * (p * q)
    g0 = 2.0 * a - 7.0 * b + 11.0 * c
    g1 = 5.0 * c + 2.0 * e - b
    g2 = 2.0 * c + 5.0 * e - f
    top = w0 * g0 + w1 * g1 + w2 * g2
    return (s * top) / (6.0 * (w0 + w1 + w2))


def transport_body(psi, velocity, xl, xh, yl, yh, moved, ext, p_x, q_x, r_x, rows, speed):
    for k in range(3):
        ext[k] = xl[k]
        ext[19 + k] = xh[k]

    def fill(i, carry):
        ext[3 + i] = psi[i]
        return carry

    lax.fori_loop(0, 16, fill, 0)

    def marks(i, carry):
        p, q, r = indicators(ext[i], ext[i + 1], ext[i + 2])
        p_x[i], q_x[i], r_x[i] = p, q, r
        return carry

    lax.fori_loop(0, 20, marks, 0, unroll=2)

    def x_flux(j, v_low, v_high):
        s = 0.5 * (v_low + v_high)
        l = [ext[j + k] for k in range(6)]
        return upwind_flux(
            s, l, p_x[j], q_x[j + 1], r_x[j + 2], p_x[j + 1], q_x[j + 2], r_x[j + 3]
        )

    def plane(i, below):
        here = velocity[0, i]
        following = jnp.where(i == 15, xh[3], velocity[0, jnp.minimum(i + 1, 15)])
        above = x_flux(i + 1, here, following)
        change = above - below
        rows[1:4, :] = yl[i, 0:3, :]
        rows[4:20, :] = psi[i]
        rows[20:23, :] = yh[i, 0:3, :]
        speed[3:4, :] = yl[i, 3:4, :]
        speed[4:20, :] = velocity[1, i]
        speed[20:21, :] = yh[i, 3:4, :]
        v = rows[...]
        u = speed[...]
        s = 0.5 * (u + roll(u, -1, 0))
        l = [roll(v, 2 - k, 0) for k in range(6)]
        p, q, r = indicators(l[1], l[2], l[3])
        q_next, r_next = roll(q, -1, 0), roll(r, -1, 0)
        flux = upwind_flux(s, l, roll(p, 1, 0), q, r_next, p, q_next, roll(r, -2, 0))
        rows_change = flux - roll(flux, 1, 0)
        change = change + rows_change[4:20, :]
        v = psi[i]
        w = velocity[2, i]
        lane = iota(v.shape, 1)

        def ahead(x, k):
            return jnp.where(lane > 255 - k, 0.0, roll(x, -k, 1))

        def behind(x, k):
            return jnp.where(lane < k, 0.0, roll(x, k, 1))

        l = [behind(v, 2), behind(v, 1), v, ahead(v, 1), ahead(v, 2), ahead(v, 3)]
        s = 0.5 * (w + ahead(w, 1))
        p, q, r = indicators(l[1], l[2], l[3])
        p1, q1, r1 = indicators(l[2], l[3], l[4])
        _, _, r2 = indicators(l[3], l[4], l[5])
        p0, _, _ = indicators(l[0], l[1], l[2])
        flux = upwind_flux(s, l, p0, q, r1, p, q1, r2)
        low = v[:, 0:128]
        none = jnp.zeros_like(low)
        l = [none, none, none, low, roll(low, -1, 1), roll(low, -2, 1)]
        p, q, r = indicators(l[1], l[2], l[3])
        p1, q1, r1 = indicators(l[2], l[3], l[4])
        _, _, r2 = indicators(l[3], l[4], l[5])
        p0, _, _ = indicators(none, none, none)
        wall = upwind_flux(0.5 * w[:, 0:128], l, p0, q, r1, p, q1, r2)
        wall = jnp.concatenate([wall, wall], axis=1)
        change = change + (flux - jnp.where(lane == 0, wall, roll(flux, 1, 1)))
        moved[i] = v - 0.25 * change
        return above

    rows[...] = jnp.zeros_like(rows)
    speed[...] = jnp.zeros_like(speed)
    lax.fori_loop(0, 16, plane, x_flux(0, xl[3], velocity[0, 0]))


def transport(psi, velocity, xl, xh, yl, yh):
    planes = (20, 16, 256)
    scratch = [(22, 16, 256), planes, planes, planes, (24, 256), (24, 256)]
    return call(
        transport_body, [(16, 16, 256)], scratch, [psi, velocity, xl, xh, yl, yh], 10000000
    )[0]


def force_body(nx, ny, at, mid, yl, yh, velocity, xl, xh, vyl, vyh, source, m, n_x, n_y, n_z, s_x, part, pad):
    x0, y0 = at[0] * 16, at[1] * 16
    shape = (32, 256)
    lane = iota(shape, 1)

    def fill(i, carry):
        m[i] = jnp.zeros(shape, F32)
        m[i, 5:8, :] = yl[i]
        m[i, 8:24, :] = mid[i]
        m[i, 24:27, :] = yh[i]
        return carry

    lax.fori_loop(0, 22, fill, 0)

    def gradient(i):
        c = m[i]
        lower, upper = z_shifted(c)
        gx = 0.5 * (m[i + 1] - m[i - 1])
        gy = 0.5 * (roll(c, -1, 0) - roll(c, 1, 0))
        return gx, gy, 0.5 * (upper - lower)

    def normals(i, carry):
        gx, gy, gz = gradient(i + 1)
        inverse = lax.rsqrt(gx * gx + gy * gy + gz * gz + DELTA_SQ)
        n_x[i], n_y[i], n_z[i] = gx * inverse, gy * inverse, gz * inverse
        return carry

    lax.fori_loop(0, 20, normals, 0)
    mask_y = row_mask(shape, y0 - 8, ny)

    def stars(i, carry):
        gx, gy, gz = gradient(i + 2)
        c = m[i + 2]
        edge = 0.5 * c
        edge = edge * lax.rsqrt(edge * edge + DELTA_SQ)
        nz = n_z[i + 1]
        upper = jnp.where(lane == 255, -edge, roll(nz, -1, 1))
        lower = jnp.where(lane == 0, edge, roll(nz, 1, 1))
        nn = n_y[i + 1]
        bending = -0.5 * (
            (n_x[i + 2] - n_x[i]) + (roll(nn, -1, 0) - roll(nn, 1, 0)) + (upper - lower)
        )
        keep = mask_y * plane_factor(x0 + i - 1, nx)
        bending = bending * keep
        fx, fy, fz = bending * gx, bending * gy, bending * gz
        k = jnp.clip(i - 1, 0, 15)
        vx = jnp.where(i == 0, xl[0], jnp.where(i == 17, xh[0], velocity[0, k]))
        s_x[i] = fx[8:24, :] + vx
        pad[7:8, :] = vyl[k]
        pad[8:24, :] = velocity[1, k]
        pad[24:25, :] = vyh[k]
        sy = fy + pad[...]
        dy = roll(sy, -1, 0) - roll(sy, 1, 0)
        sz = fz[8:24, :] + velocity[2, k]
        below, above = z_shifted(sz)
        part[i] = dy[8:24, :] + (above - below)
        return carry

    pad[...] = jnp.zeros_like(pad)
    lax.fori_loop(0, 18, stars, 0)

    def finish(i, carry):
        source[i] = -0.5 * (part[i + 1] + (s_x[i + 2] - s_x[i]))
        return carry

    lax.fori_loop(0, 16, finish, 0)


def force(nx, ny, at, mid, yl, yh, velocity, xl, xh, vyl, vyh):
    n = (20, 32, 256)
    scratch = [(22, 32, 256), n, n, n, (18, 16, 256), (18, 16, 256), (32, 256)]
    args = [at, mid, yl, yh, velocity, xl, xh, vyl, vyh]
    return call(functools.partial(force_body, nx, ny), [(16, 16, 256)], scratch, args, 10000000)[0]


def assemble(ext, mid, yl, yh, planes):
    def fill(i, carry):
        ext[i, 0:12, :] = yl[i]
        ext[i, 12:28, :] = mid[i]
        ext[i, 28:40, :] = yh[i]
        return carry

    lax.fori_loop(0, planes, fill, 0)


def descend(nx, ny, at, b, v, v_out, b1_out, u_out, b2_out, wide_rows, t, s1, t1):
    x1, y1 = at[0] * 8, at[1] * 8

    def keep_v(i, carry):
        v_out[i] = v[i + 7]
        return carry

    lax.fori_loop(0, 20, keep_v, 0)

    def residual(i):
        c, around = beside(v, i)
        return b[i + 1] - (6.0 * c - around)

    def pairs(i, carry):
        total = residual(2 * i + 1) + residual(2 * i + 2)
        for half in range(2):
            wide_rows[half] = total[:, 128 * half : 128 * half + 128]
            even = wide_rows[half, pl.ds(0, 20, stride=2), :]
            odd = wide_rows[half, pl.ds(1, 20, stride=2), :]
            t[i, 0:20, 128 * half : 128 * half + 128] = even + odd
        return carry

    lax.fori_loop(0, 16, pairs, 0)
    full = dot(t[...].reshape(16 * 24, 256), pair_matrix(256, 128, 0.125)).reshape(16, 24, 128)
    rows = iota((24, 128), 0)
    good = jnp.logical_and(inside(rows + (y1 - 6), ny // 2), rows < 20)
    for i in range(16):
        ok = jnp.logical_and(good, inside(x1 + i - 4, nx // 2))
        b1_out[i] = jnp.where(ok, full[i], 0.0)
    mask = jnp.where(good, 1.0, 0.0).astype(F32)
    weight = 4.0 * SIDE

    def smooth(i, carry):
        c, around = beside(b1_out, i + 1)
        u_out[i] = (weight * plane_factor(x1 + i - 3, nx // 2)) * mask * (1.2 * c + SIDE * around)
        return carry

    lax.fori_loop(0, 14, smooth, 0)
    t1[...] = jnp.zeros_like(t1)
    for k in range(4):
        total = 0.0
        for j in (2 * k, 2 * k + 1):
            c, around = beside(u_out, j + 3)
            total = total + (b1_out[j + 4] - 0.25 * (6.0 * c - around))
        s1[k] = total
        t1[k, 0:4, :] = s1[k, pl.ds(6, 4, stride=2), :] + s1[k, pl.ds(7, 4, stride=2), :]
    small = dot(t1[...].reshape(32, 128), pair_matrix(128, 128, 0.125)).reshape(4, 8, 128)
    for k in range(4):
        b2_out[k] = small[k, 0:4, 0:64]


DOWN_OUTS = [(20, 40, 256), (16, 24, 128), (14, 24, 128), (4, 4, 64)]
DOWN_SCRATCH = [(34, 40, 256), (2, 40, 128), (16, 24, 256), (4, 24, 128), (4, 8, 128)]


def first_down_body(nx, ny, at, mid, yl, yh, b, v_out, b1_out, u_out, b2_out, v, *scratch):
    assemble(b, mid, yl, yh, 36)
    mask = row_mask((40, 256), at[1] * 16 - ROWS, ny)

    def smooth(i, carry):
        c, around = beside(b, i + 1)
        keep = mask * plane_factor(at[0] * 16 + i - 9, nx)
        v[i] = SIDE * keep * (1.2 * c + SIDE * around)
        return carry

    lax.fori_loop(0, 34, smooth, 0)
    descend(nx, ny, at, b, v, v_out, b1_out, u_out, b2_out, *scratch)


def first_down(nx, ny, at, mid, yl, yh):
    return call(
        functools.partial(first_down_body, nx, ny),
        [(36, 40, 256)] + DOWN_OUTS,
        DOWN_SCRATCH,
        [at, mid, yl, yh],
        20000000,
    )


def next_down_body(nx, ny, at, mid, yl, yh, b, v_out, b1_out, u_out, b2_out, v, wide_rows, t, s1, t1, start, once):
    assemble(start, mid, yl, yh, 38)
    mask = row_mask((40, 256), at[1] * 16 - ROWS, ny)

    def sweep(src, dst, first, shift):
        def plane(i, carry):
            c, around = beside(src, i + 1)
            keep = mask * plane_factor(at[0] * 16 + i + first, nx)
            dst[i] = keep * (0.2 * c + SIDE * (around + b[i + shift]))
            return carry

        return plane

    lax.fori_loop(0, 36, sweep(start, once, -10, 0), 0)
    lax.fori_loop(0, 34, sweep(once, v, -9, 1), 0)
    descend(nx, ny, at, b, v, v_out, b1_out, u_out, b2_out, wide_rows, t, s1, t1)


def next_down(nx, ny, at, mid, yl, yh, b):
    return call(
        functools.partial(next_down_body, nx, ny),
        DOWN_OUTS,
        DOWN_SCRATCH + [(38, 40, 256), (36, 40, 256)],
        [at, mid, yl, yh, b],
        30000000,
    )


def up_body(nx, ny, at, b2_all, b1, u, b, v_down, out, s2, v2, w2, t3, b3, c3, d3, dup, row2, m1, n1, m0, n0):
    wide, narrow = at[0], at[1]
    spot = wide % GROUP
    rows2 = s2.shape[1]
    rows3 = rows2 // 2
    count = rows2 // 4
    s2[...] = jnp.zeros_like(s2)

    def gather(j, carry):
        block = spot + 1 + j
        layer, place = block // GROUP, block % GROUP
        for n in range(count):
            for k in range(4):
                s2[4 * j + k, 4 * n : 4 * n + 4, 0:64] = b2_all[place * count + n, layer, k]
        return carry

    lax.fori_loop(0, 7, gather, 0)

    def walled(c, rows, lanes):
        row, lane = iota(c.shape, 0), iota(c.shape, 1)
        lower = jnp.where(row == 0, 0.0, roll(c, 1, 0))
        upper = jnp.where(row == rows - 1, 0.0, roll(c, -1, 0))
        return (lower + upper) + (roll(c, 1, 1) + roll(c, -1, 1))

    def around(ref, i, rows, lanes):
        c = ref[i]
        return c, (ref[i - 1] + ref[i + 1]) + walled(c, rows, lanes)

    def lanes_below(rows, lanes):
        return jnp.where(iota((rows, 128), 1) < lanes, 1.0, 0.0).astype(F32)

    x2 = wide * 4
    mask2 = lanes_below(rows2, 64)
    weight2 = 16.0 * SIDE

    def smooth2(i, carry):
        c, near = around(s2, i, rows2, 64)
        v2[i] = (weight2 * plane_factor(x2 + i - 12, nx // 4)) * mask2 * (1.2 * c + SIDE * near)
        return carry

    lax.fori_loop(1, 27, smooth2, 0)

    def residual2(i):
        c, near = around(v2, i, rows2, 64)
        return s2[i] - (1.0 / 16.0) * (6.0 * c - near)

    def pairs2(i, carry):
        row2[...] = residual2(2 * i + 2) + residual2(2 * i + 3)
        t3[i] = row2[pl.ds(0, rows3, stride=2), :] + row2[pl.ds(1, rows3, stride=2), :]
        return carry

    lax.fori_loop(0, 12, pairs2, 0)
    full = dot(t3[...].reshape(12 * rows3, 128), pair_matrix(128, 128, 0.125)).reshape(12, rows3, 128)
    x3 = wide * 2
    mask3 = lanes_below(rows3, 32)
    weight3 = 64.0 * SIDE
    for i in range(12):
        value = full[i] * mask3 * (weight3 * plane_factor(x3 + i - 5, nx // 8))
        b3[i] = value
        c3[i] = value

    def sweep3(src, dst):
        def plane(i, carry):
            c, near = around(src, i, rows3, 32)
            dst[i] = mask3 * plane_factor(x3 + i - 5, nx // 8) * (0.2 * c + SIDE * near) + b3[i]
            return carry

        return plane

    lax.fori_loop(1, 11, sweep3(c3, d3), 0)
    lax.fori_loop(2, 10, sweep3(d3, c3), 0)
    lax.fori_loop(3, 9, sweep3(c3, d3), 0)
    spread = dot(d3[3:9].reshape(6 * rows3, 128), copy_matrix(128, 128)).reshape(6, rows3, 128)
    for i in range(6):
        dup[pl.ds(0, rows3, stride=2), :] = spread[i]
        dup[pl.ds(1, rows3, stride=2), :] = spread[i]
        for k in (8 + 2 * i, 9 + 2 * i):
            v2[k] = v2[k] + dup[0:rows2, :] * mask2 * plane_factor(x2 + k - 12, nx // 4)

    def sweep2(src, dst):
        def plane(i, carry):
            c, near = around(src, i, rows2, 64)
            keep = mask2 * plane_factor(x2 + i - 12, nx // 4)
            dst[i] = keep * (0.2 * c + SIDE * (near + 16.0 * s2[i]))
            return carry

        return plane

    lax.fori_loop(9, 19, sweep2(v2, w2), 0)
    lax.fori_loop(10, 18, sweep2(w2, v2), 0)
    turn = lax.rem(rows2 + 3 - 4 * narrow + rows2, rows2)
    picked = [pltpu.roll(v2[10 + i], turn, 0)[0:16, :] for i in range(8)]
    spread = dot(jnp.concatenate(picked, axis=0), copy_matrix(128, 128)).reshape(8, 16, 128)
    x1, y1 = wide * 8, narrow * 8
    mask1 = row_mask((24, 128), y1 - 6, ny // 2)
    for i in range(8):
        dup[pl.ds(0, 12, stride=2), :] = spread[i, 0:12, :]
        dup[pl.ds(1, 12, stride=2), :] = spread[i, 0:12, :]
        for k in (2 * i - 1, 2 * i):
            if 0 <= k < 14:
                m1[k] = (u[k] + dup[0:24, :]) * mask1 * plane_factor(x1 + k - 3, nx // 2)

    def sweep1(src, dst):
        def plane(i, carry):
            c, near = beside(src, i)
            keep = mask1 * plane_factor(x1 + i - 3, nx // 2)
            dst[i] = keep * (0.2 * c + SIDE * (near + 4.0 * b1[i + 1]))
            return carry

        return plane

    lax.fori_loop(1, 13, sweep1(m1, n1), 0)
    lax.fori_loop(2, 12, sweep1(n1, m1), 0)
    spread = dot(m1[2:12].reshape(10 * 24, 128), copy_matrix(128, 256)).reshape(10, 24, 256)
    x0, y0 = wide * 16, narrow * 16
    mask0 = row_mask((40, 256), y0 - ROWS, ny)
    for i in range(10):
        for half in range(2):
            value = spread[i, 0:20, 128 * half : 128 * half + 128]
            dup[pl.ds(0, 20, stride=2), :] = value
            dup[pl.ds(1, 20, stride=2), :] = value
            for k in (2 * i, 2 * i + 1):
                n0[k, :, 128 * half : 128 * half + 128] = dup[0:40, :]

    def add0(i, carry):
        m0[i] = (v_down[i] + n0[i]) * mask0 * plane_factor(x0 + i - 2, nx)
        return carry

    lax.fori_loop(0, 20, add0, 0)

    def sweep0(i, carry):
        c, near = beside(m0, i)
        keep = mask0 * plane_factor(x0 + i - 2, nx)
        n0[i] = keep * (0.2 * c + SIDE * (near + b[i + 8]))
        return carry

    lax.fori_loop(1, 19, sweep0, 0)

    def last0(i, carry):
        c, near = beside(n0, i + 2)
        value = 0.2 * c + SIDE * (near + b[i + 10])
        out[i] = value[12:28, :]
        return carry

    lax.fori_loop(0, 16, last0, 0)


def up(nx, ny, at, b2_all, b1, u, b, v_down):
    rows2 = ny // 4
    rows3 = rows2 // 2
    wide_part = (28, rows2, 128)
    small = (12, rows3, 128)
    scratch = [
        wide_part, wide_part, wide_part, small, small, small, small,
        (48, 128), (rows2, 128), (14, 24, 128), (14, 24, 128), (20, 40, 256), (20, 40, 256),
    ]
    return call(
        functools.partial(up_body, nx, ny),
        [(16, 16, 256)],
        scratch,
        [at, b2_all, b1, u, b, v_down],
        20000000,
    )[0]


def shifted(array, axis, step):
    count = lax.axis_size(axis)
    return lax.ppermute(
        array, axis, [(i, i + step) for i in range(count) if 0 <= i + step < count]
    )


def surround(array, planes, rows):
    low = shifted(array[16 - planes :], "wide", 1)
    high = shifted(array[:planes], "wide", -1)
    mid = jnp.concatenate([low, array, high], axis=0)
    y_low = shifted(mid[:, 16 - rows :, :], "narrow", 1)
    y_high = shifted(mid[:, :rows, :], "narrow", -1)
    return mid, y_low, y_high


def spread_coarse(b2):
    wide, narrow = lax.axis_size("wide"), lax.axis_size("narrow")
    before = shifted(b2, "wide", GROUP)
    after = shifted(b2, "wide", -GROUP)
    three = jnp.stack([before, b2, after])
    size = GROUP * narrow
    pieces = jnp.broadcast_to(three[None], (size,) + three.shape)
    groups = [[g * size + k for k in range(size)] for g in range(wide // GROUP)]
    return lax.all_to_all(pieces, ("wide", "narrow"), 0, 0, axis_index_groups=groups)


def on_device(phase, distance, velocity):
    nx, ny = 16 * lax.axis_size("wide"), 16 * lax.axis_size("narrow")
    at = jnp.stack([lax.axis_index("wide"), lax.axis_index("narrow")]).astype(jnp.int32)
    psi, x_low, x_high, y_low, y_high = prepare(phase, distance, velocity)
    xl = shifted(x_high, "wide", 1)
    xh = shifted(x_low, "wide", -1)
    yl = shifted(y_high, "narrow", 1)
    yh = shifted(y_low, "narrow", -1)
    moved = transport(psi, velocity, xl, xh, yl, yh)
    mid, m_low, m_high = surround(moved, 3, 3)
    source = force(
        nx, ny, at, mid, m_low, m_high, velocity, xl[3:], xh[3:], yl[:, 3:, :], yh[:, 3:, :]
    )
    b, v, b1, u, b2 = first_down(nx, ny, at, *surround(source, HALO, ROWS))
    pressure = up(nx, ny, at, spread_coarse(b2), b1, u, b, v)
    v, b1, u, b2 = next_down(nx, ny, at, *surround(pressure, HALO + 1, ROWS), b)
    pressure = up(nx, ny, at, spread_coarse(b2), b1, u, b, v)
    return (moved, pressure)


def solution(mesh):
    blocks = P("wide", "narrow", None)
    return jax.shard_map(
        on_device,
        mesh=mesh,
        in_specs=(blocks, blocks, P(None, "wide", "narrow", None)),
        out_specs=(blocks, blocks),
        check_vma=False,
    )
```

```python
import functools

import jax
import jax.numpy as jnp
from jax import lax
from jax.experimental import pallas as pl
from jax.experimental.pallas import tpu as pltpu
from jax.sharding import PartitionSpec as P

DELTA_SQ = 0.0025
WENO_EPS = 0.01
SIDE = 0.8 / 6.0
F32 = jnp.float32
HIGHEST = lax.Precision.HIGHEST
VMEM_LIMIT = 56 * 1024 * 1024

HALO = 10
ROWS = 12
GROUP = 4


def iota(shape, dim):
    return lax.broadcasted_iota(jnp.int32, shape, dim)


def roll(v, shift, axis):
    return pltpu.roll(v, shift % v.shape[axis], axis)


def z_shifted(v):
    lane = iota(v.shape, 1)
    last = v.shape[1] - 1
    lower = jnp.where(lane == 0, 0.0, roll(v, 1, 1))
    upper = jnp.where(lane == last, 0.0, roll(v, -1, 1))
    return lower, upper


def z_pair(v):
    lower, upper = z_shifted(v)
    return lower + upper


def y_pair(v):
    return roll(v, 1, 0) + roll(v, -1, 0)


def beside(ref, i):
    c = ref[i]
    return c, (ref[i - 1] + ref[i + 1]) + y_pair(c) + z_pair(c)


def inside(first, count):
    return jnp.logical_and(first >= 0, first < count)


def row_mask(shape, first, count):
    rows = iota(shape, 0) + first
    return jnp.where(inside(rows, count), 1.0, 0.0).astype(F32)


def plane_factor(index, count):
    return jnp.where(inside(index, count), 1.0, 0.0).astype(F32)


def dot(a, b):
    return lax.dot_general(
        a, b, (((1,), (0,)), ((), ())), precision=HIGHEST, preferred_element_type=F32
    )


def pair_matrix(rows, cols, value):
    return jnp.where((iota((rows, cols), 0) >> 1) == iota((rows, cols), 1), value, 0.0).astype(F32)


def copy_matrix(rows, cols):
    return jnp.where(iota((rows, cols), 0) == (iota((rows, cols), 1) >> 1), 1.0, 0.0).astype(F32)


def call(body, outs, scratch, args, flops):
    vmem = pl.BlockSpec(memory_space=pltpu.VMEM)
    smem = pl.BlockSpec(memory_space=pltpu.SMEM)
    return pl.pallas_call(
        body,
        out_shape=[jax.ShapeDtypeStruct(s, F32) for s in outs],
        in_specs=[smem if a.dtype == jnp.int32 and a.ndim == 1 else vmem for a in args],
        out_specs=[vmem] * len(outs),
        scratch_shapes=[pltpu.VMEM(s, F32) for s in scratch],
        compiler_params=pltpu.CompilerParams(vmem_limit_bytes=VMEM_LIMIT),
        cost_estimate=pl.CostEstimate(flops=flops, bytes_accessed=4000000, transcendentals=0),
    )(*args)


def send_shapes(planes):
    return [(16 + 2 * planes, 16, 256), (planes, 16, 256), (planes, 16, 256)]


def send(block, wider, low, high, planes):
    for i in range(16):
        wider[planes + i] = block[i]
    for i in range(planes):
        low[i] = block[i]
        high[i] = block[16 - planes + i]


def prepare_body(phase, distance, velocity, psi, x_low, x_high, y_low, y_high):
    def plane(i, carry):
        orient = 2.0 * phase[i].astype(F32) - 1.0
        psi[i] = 1.0 / (1.0 + jnp.exp(-orient * distance[i]))
        y_low[i, 0:3, :] = psi[i, 0:3, :]
        y_low[i, 3:4, :] = velocity[1, i, 0:1, :]
        y_high[i, 0:3, :] = psi[i, 13:16, :]
        y_high[i, 3:4, :] = velocity[1, i, 15:16, :]
        return carry

    lax.fori_loop(0, 16, plane, 0, unroll=True)
    for k in range(3):
        x_low[k] = psi[k]
        x_high[k] = psi[13 + k]
    x_low[3] = velocity[0, 0]
    x_high[3] = velocity[0, 15]


def prepare(phase, distance, velocity):
    outs = [(16, 16, 256), (4, 16, 256), (4, 16, 256), (16, 4, 256), (16, 4, 256)]
    return call(prepare_body, outs, [], [phase, distance, velocity], 1000000)


def indicators(a, b, c):
    d = a - c
    curve = (a + c) - 2.0 * b
    twice = 2.0 * curve
    base = (13.0 / 12.0) * (curve * curve) + WENO_EPS
    up, down = twice - d, twice + d
    p = base + 0.25 * (up * up)
    q = base + 0.25 * (d * d)
    r = base + 0.25 * (down * down)
    return p * p, q * q, r * r


def upwind_flux(s, l, p_left, q_left, r_left, p_right, q_right, r_right):
    ahead = s > 0.0
    pick = lambda x, y: jnp.where(ahead, x, y)
    a, b, c, e, f = pick(l[0], l[5]), pick(l[1], l[4]), pick(l[2], l[3]), pick(l[3], l[2]), pick(l[4], l[1])
    p, q, r = pick(p_left, r_right), pick(q_left, q_right), pick(r_left, p_right)
    w0, w1, w2 = 0.1 * (q * r), 0.6 * (p * r), 0.3 * (p * q)
    g0 = 2.0 * a - 7.0 * b + 11.0 * c
    g1 = 5.0 * c + 2.0 * e - b
    g2 = 2.0 * c + 5.0 * e - f
    top = w0 * g0 + w1 * g1 + w2 * g2
    return (s * top) / (6.0 * (w0 + w1 + w2))


def transport_body(psi, velocity, xl, xh, yl, yh, moved, wider, low, high, ext, p_x, q_x, r_x, rows, speed):
    for k in range(3):
        ext[k] = xl[k]
        ext[19 + k] = xh[k]

    def fill(i, carry):
        ext[3 + i] = psi[i]
        return carry

    lax.fori_loop(0, 16, fill, 0, unroll=True)

    def marks(i, carry):
        p, q, r = indicators(ext[i], ext[i + 1], ext[i + 2])
        p_x[i], q_x[i], r_x[i] = p, q, r
        return carry

    lax.fori_loop(0, 20, marks, 0, unroll=True)

    def x_flux(j, v_low, v_high):
        s = 0.5 * (v_low + v_high)
        l = [ext[j + k] for k in range(6)]
        return upwind_flux(
            s, l, p_x[j], q_x[j + 1], r_x[j + 2], p_x[j + 1], q_x[j + 2], r_x[j + 3]
        )

    def plane(i, below):
        here = velocity[0, i]
        following = jnp.where(i == 15, xh[3], velocity[0, jnp.minimum(i + 1, 15)])
        above = x_flux(i + 1, here, following)
        change = above - below
        rows[1:4, :] = yl[i, 0:3, :]
        rows[4:20, :] = psi[i]
        rows[20:23, :] = yh[i, 0:3, :]
        speed[3:4, :] = yl[i, 3:4, :]
        speed[4:20, :] = velocity[1, i]
        speed[20:21, :] = yh[i, 3:4, :]
        v = rows[...]
        u = speed[...]
        s = 0.5 * (u + roll(u, -1, 0))
        l = [roll(v, 2 - k, 0) for k in range(6)]
        p, q, r = indicators(l[1], l[2], l[3])
        q_next, r_next = roll(q, -1, 0), roll(r, -1, 0)
        flux = upwind_flux(s, l, roll(p, 1, 0), q, r_next, p, q_next, roll(r, -2, 0))
        rows_change = flux - roll(flux, 1, 0)
        change = change + rows_change[4:20, :]
        v = psi[i]
        w = velocity[2, i]
        lane = iota(v.shape, 1)

        def ahead(x, k):
            return jnp.where(lane > 255 - k, 0.0, roll(x, -k, 1))

        def behind(x, k):
            return jnp.where(lane < k, 0.0, roll(x, k, 1))

        l = [behind(v, 2), behind(v, 1), v, ahead(v, 1), ahead(v, 2), ahead(v, 3)]
        s = 0.5 * (w + ahead(w, 1))
        p, q, r = indicators(l[1], l[2], l[3])
        p1, q1, r1 = indicators(l[2], l[3], l[4])
        _, _, r2 = indicators(l[3], l[4], l[5])
        p0, _, _ = indicators(l[0], l[1], l[2])
        flux = upwind_flux(s, l, p0, q, r1, p, q1, r2)
        low = v[:, 0:128]
        none = jnp.zeros_like(low)
        l = [none, none, none, low, roll(low, -1, 1), roll(low, -2, 1)]
        p, q, r = indicators(l[1], l[2], l[3])
        p1, q1, r1 = indicators(l[2], l[3], l[4])
        _, _, r2 = indicators(l[3], l[4], l[5])
        p0, _, _ = indicators(none, none, none)
        wall = upwind_flux(0.5 * w[:, 0:128], l, p0, q, r1, p, q1, r2)
        wall = jnp.concatenate([wall, wall], axis=1)
        change = change + (flux - jnp.where(lane == 0, wall, roll(flux, 1, 1)))
        moved[i] = v - 0.25 * change
        return above

    rows[...] = jnp.zeros_like(rows)
    speed[...] = jnp.zeros_like(speed)
    lax.fori_loop(0, 16, plane, x_flux(0, xl[3], velocity[0, 0]), unroll=True)
    send(moved, wider, low, high, 3)


def transport(psi, velocity, xl, xh, yl, yh):
    planes = (20, 16, 256)
    scratch = [(22, 16, 256), planes, planes, planes, (24, 256), (24, 256)]
    outs = [(16, 16, 256)] + send_shapes(3)
    return call(transport_body, outs, scratch, [psi, velocity, xl, xh, yl, yh], 10000000)


def force_body(nx, ny, at, mid, yl, yh, velocity, xl, xh, vyl, vyh, wider, low, high, m, n_x, n_y, n_z, s_x, part, pad, source):
    x0, y0 = at[0] * 16, at[1] * 16
    shape = (32, 256)
    lane = iota(shape, 1)

    def fill(i, carry):
        m[i] = jnp.zeros(shape, F32)
        m[i, 5:8, :] = yl[i]
        m[i, 8:24, :] = mid[i]
        m[i, 24:27, :] = yh[i]
        return carry

    lax.fori_loop(0, 22, fill, 0, unroll=True)

    def gradient(i):
        c = m[i]
        lower, upper = z_shifted(c)
        gx = 0.5 * (m[i + 1] - m[i - 1])
        gy = 0.5 * (roll(c, -1, 0) - roll(c, 1, 0))
        return gx, gy, 0.5 * (upper - lower)

    def normals(i, carry):
        gx, gy, gz = gradient(i + 1)
        inverse = lax.rsqrt(gx * gx + gy * gy + gz * gz + DELTA_SQ)
        n_x[i], n_y[i], n_z[i] = gx * inverse, gy * inverse, gz * inverse
        return carry

    lax.fori_loop(0, 20, normals, 0, unroll=True)
    mask_y = row_mask(shape, y0 - 8, ny)

    def stars(i, carry):
        gx, gy, gz = gradient(i + 2)
        c = m[i + 2]
        edge = 0.5 * c
        edge = edge * lax.rsqrt(edge * edge + DELTA_SQ)
        nz = n_z[i + 1]
        upper = jnp.where(lane == 255, -edge, roll(nz, -1, 1))
        lower = jnp.where(lane == 0, edge, roll(nz, 1, 1))
        nn = n_y[i + 1]
        bending = -0.5 * (
            (n_x[i + 2] - n_x[i]) + (roll(nn, -1, 0) - roll(nn, 1, 0)) + (upper - lower)
        )
        keep = mask_y * plane_factor(x0 + i - 1, nx)
        bending = bending * keep
        fx, fy, fz = bending * gx, bending * gy, bending * gz
        k = jnp.clip(i - 1, 0, 15)
        vx = jnp.where(i == 0, xl[3], jnp.where(i == 17, xh[3], velocity[0, k]))
        s_x[i] = fx[8:24, :] + vx
        pad[7:8, :] = vyl[k, 3:4, :]
        pad[8:24, :] = velocity[1, k]
        pad[24:25, :] = vyh[k, 3:4, :]
        sy = fy + pad[...]
        dy = roll(sy, -1, 0) - roll(sy, 1, 0)
        sz = fz[8:24, :] + velocity[2, k]
        below, above = z_shifted(sz)
        part[i] = dy[8:24, :] + (above - below)
        return carry

    pad[...] = jnp.zeros_like(pad)
    lax.fori_loop(0, 18, stars, 0, unroll=True)

    def finish(i, carry):
        source[i] = -0.5 * (part[i + 1] + (s_x[i + 2] - s_x[i]))
        return carry

    lax.fori_loop(0, 16, finish, 0, unroll=True)
    send(source, wider, low, high, HALO)


def force(nx, ny, at, mid, yl, yh, velocity, xl, xh, vyl, vyh):
    n = (20, 32, 256)
    scratch = [(22, 32, 256), n, n, n, (18, 16, 256), (18, 16, 256), (32, 256), (16, 16, 256)]
    args = [at, mid, yl, yh, velocity, xl, xh, vyl, vyh]
    return call(functools.partial(force_body, nx, ny), send_shapes(HALO), scratch, args, 10000000)


def assemble(ext, mid, yl, yh, planes):
    def fill(i, carry):
        ext[i, 0:12, :] = yl[i, 4:16, :]
        ext[i, 12:28, :] = mid[i]
        ext[i, 28:40, :] = yh[i, 0:12, :]
        return carry

    lax.fori_loop(0, planes, fill, 0, unroll=True)


def descend(nx, ny, at, b, v, v_out, b1_out, u_out, b2_out, wide_rows, t, s1, t1):
    x1, y1 = at[0] * 8, at[1] * 8

    def keep_v(i, carry):
        v_out[i] = v[i + 7]
        return carry

    lax.fori_loop(0, 20, keep_v, 0, unroll=True)

    def residual(i):
        c, around = beside(v, i)
        return b[i + 1] - (6.0 * c - around)

    def pairs(i, carry):
        total = residual(2 * i + 1) + residual(2 * i + 2)
        for half in range(2):
            wide_rows[half] = total[:, 128 * half : 128 * half + 128]
            even = wide_rows[half, pl.ds(0, 20, stride=2), :]
            odd = wide_rows[half, pl.ds(1, 20, stride=2), :]
            t[i, 0:20, 128 * half : 128 * half + 128] = even + odd
        return carry

    lax.fori_loop(0, 16, pairs, 0, unroll=True)
    full = dot(t[...].reshape(16 * 24, 256), pair_matrix(256, 128, 0.125)).reshape(16, 24, 128)
    rows = iota((24, 128), 0)
    good = jnp.logical_and(inside(rows + (y1 - 6), ny // 2), rows < 20)
    for i in range(16):
        ok = jnp.logical_and(good, inside(x1 + i - 4, nx // 2))
        b1_out[i] = jnp.where(ok, full[i], 0.0)
    mask = jnp.where(good, 1.0, 0.0).astype(F32)
    weight = 4.0 * SIDE

    def smooth(i, carry):
        c, around = beside(b1_out, i + 1)
        u_out[i] = (weight * plane_factor(x1 + i - 3, nx // 2)) * mask * (1.2 * c + SIDE * around)
        return carry

    lax.fori_loop(0, 14, smooth, 0, unroll=True)
    t1[...] = jnp.zeros_like(t1)
    for k in range(4):
        total = 0.0
        for j in (2 * k, 2 * k + 1):
            c, around = beside(u_out, j + 3)
            total = total + (b1_out[j + 4] - 0.25 * (6.0 * c - around))
        s1[k] = total
        t1[k, 0:4, :] = s1[k, pl.ds(6, 4, stride=2), :] + s1[k, pl.ds(7, 4, stride=2), :]
    small = dot(t1[...].reshape(32, 128), pair_matrix(128, 128, 0.125)).reshape(4, 8, 128)
    tile = jnp.concatenate([small[0, 0:4], small[1, 0:4]], axis=0) + roll(
        jnp.concatenate([small[2, 0:4], small[3, 0:4]], axis=0), 64, 1
    )
    for k in range(b2_out.shape[0]):
        b2_out[k] = tile


def down_outs(ny):
    return [(20, 40, 256), (16, 24, 128), (14, 24, 128), (GROUP * ny // 16, 8, 128)]


DOWN_SCRATCH = [(34, 40, 256), (2, 40, 128), (16, 24, 256), (4, 24, 128), (4, 8, 128)]


def first_down_body(nx, ny, at, mid, yl, yh, b, v_out, b1_out, u_out, b2_out, v, *scratch):
    assemble(b, mid, yl, yh, 36)
    mask = row_mask((40, 256), at[1] * 16 - ROWS, ny)

    def smooth(i, carry):
        c, around = beside(b, i + 1)
        keep = mask * plane_factor(at[0] * 16 + i - 9, nx)
        v[i] = SIDE * keep * (1.2 * c + SIDE * around)
        return carry

    lax.fori_loop(0, 34, smooth, 0, unroll=True)
    descend(nx, ny, at, b, v, v_out, b1_out, u_out, b2_out, *scratch)


def first_down(nx, ny, at, mid, yl, yh):
    return call(
        functools.partial(first_down_body, nx, ny),
        [(36, 40, 256)] + down_outs(ny),
        DOWN_SCRATCH,
        [at, mid, yl, yh],
        20000000,
    )


def next_down_body(nx, ny, at, mid, yl, yh, b, v_out, b1_out, u_out, b2_out, v, wide_rows, t, s1, t1, start, once):
    assemble(start, mid, yl, yh, 38)
    mask = row_mask((40, 256), at[1] * 16 - ROWS, ny)

    def sweep(src, dst, first, shift):
        def plane(i, carry):
            c, around = beside(src, i + 1)
            keep = mask * plane_factor(at[0] * 16 + i + first, nx)
            dst[i] = keep * (0.2 * c + SIDE * (around + b[i + shift]))
            return carry

        return plane

    lax.fori_loop(0, 36, sweep(start, once, -10, 0), 0, unroll=True)
    lax.fori_loop(0, 34, sweep(once, v, -9, 1), 0, unroll=True)
    descend(nx, ny, at, b, v, v_out, b1_out, u_out, b2_out, wide_rows, t, s1, t1)


def next_down(nx, ny, at, mid, yl, yh, b):
    return call(
        functools.partial(next_down_body, nx, ny),
        down_outs(ny),
        DOWN_SCRATCH + [(38, 40, 256), (36, 40, 256)],
        [at, mid, yl, yh, b],
        30000000,
    )


def up_body(nx, ny, last, at, b2_all, before, after, b1, u, b, v_down, *refs):
    if last:
        out, *refs = refs
    else:
        wider, low, high, *refs = refs
        out = refs.pop()
    s2, v2, w2, t3, b3, c3, d3, dup, row2, m1, n1, m0, n0 = refs
    wide, narrow = at[0], at[1]
    spot = wide % GROUP
    rows2 = s2.shape[1]
    rows3 = rows2 // 2
    count = rows2 // 4
    lower = iota((8, 128), 1) < 64
    for j in range(7):
        block = spot + 1 + j
        layer, place = block // GROUP, block % GROUP
        for n in range(count):
            k = place * count + n
            tile = jnp.where(layer == 0, before[k], jnp.where(layer == 1, b2_all[k], after[k]))
            first = jnp.where(lower, tile, 0.0)
            second = jnp.where(lower, roll(tile, 64, 1), 0.0)
            for p in range(4):
                part = (first, second)[p // 2]
                s2[4 * j + p, 4 * n : 4 * n + 4, :] = part[4 * (p % 2) : 4 * (p % 2) + 4, :]

    def walled(c, rows, lanes):
        row, lane = iota(c.shape, 0), iota(c.shape, 1)
        lower = jnp.where(row == 0, 0.0, roll(c, 1, 0))
        upper = jnp.where(row == rows - 1, 0.0, roll(c, -1, 0))
        return (lower + upper) + (roll(c, 1, 1) + roll(c, -1, 1))

    def around(ref, i, rows, lanes):
        c = ref[i]
        return c, (ref[i - 1] + ref[i + 1]) + walled(c, rows, lanes)

    def lanes_below(rows, lanes):
        return jnp.where(iota((rows, 128), 1) < lanes, 1.0, 0.0).astype(F32)

    x2 = wide * 4
    mask2 = lanes_below(rows2, 64)
    weight2 = 16.0 * SIDE

    def smooth2(i, carry):
        c, near = around(s2, i, rows2, 64)
        v2[i] = (weight2 * plane_factor(x2 + i - 12, nx // 4)) * mask2 * (1.2 * c + SIDE * near)
        return carry

    lax.fori_loop(1, 27, smooth2, 0, unroll=True)

    def residual2(i):
        c, near = around(v2, i, rows2, 64)
        return s2[i] - (1.0 / 16.0) * (6.0 * c - near)

    def pairs2(i, carry):
        row2[...] = residual2(2 * i + 2) + residual2(2 * i + 3)
        t3[i] = row2[pl.ds(0, rows3, stride=2), :] + row2[pl.ds(1, rows3, stride=2), :]
        return carry

    lax.fori_loop(0, 12, pairs2, 0, unroll=True)
    full = dot(t3[...].reshape(12 * rows3, 128), pair_matrix(128, 128, 0.125)).reshape(12, rows3, 128)
    x3 = wide * 2
    mask3 = lanes_below(rows3, 32)
    weight3 = 64.0 * SIDE
    for i in range(12):
        value = full[i] * mask3 * (weight3 * plane_factor(x3 + i - 5, nx // 8))
        b3[i] = value
        c3[i] = value

    def sweep3(src, dst):
        def plane(i, carry):
            c, near = around(src, i, rows3, 32)
            dst[i] = mask3 * plane_factor(x3 + i - 5, nx // 8) * (0.2 * c + SIDE * near) + b3[i]
            return carry

        return plane

    lax.fori_loop(1, 11, sweep3(c3, d3), 0, unroll=True)
    lax.fori_loop(2, 10, sweep3(d3, c3), 0, unroll=True)
    lax.fori_loop(3, 9, sweep3(c3, d3), 0, unroll=True)
    spread = dot(d3[3:9].reshape(6 * rows3, 128), copy_matrix(128, 128)).reshape(6, rows3, 128)
    for i in range(6):
        dup[pl.ds(0, rows3, stride=2), :] = spread[i]
        dup[pl.ds(1, rows3, stride=2), :] = spread[i]
        for k in (8 + 2 * i, 9 + 2 * i):
            v2[k] = v2[k] + dup[0:rows2, :] * mask2 * plane_factor(x2 + k - 12, nx // 4)

    def sweep2(src, dst):
        def plane(i, carry):
            c, near = around(src, i, rows2, 64)
            keep = mask2 * plane_factor(x2 + i - 12, nx // 4)
            dst[i] = keep * (0.2 * c + SIDE * (near + 16.0 * s2[i]))
            return carry

        return plane

    lax.fori_loop(9, 19, sweep2(v2, w2), 0, unroll=True)
    lax.fori_loop(10, 18, sweep2(w2, v2), 0, unroll=True)
    turn = lax.rem(rows2 + 3 - 4 * narrow + rows2, rows2)
    picked = [pltpu.roll(v2[10 + i], turn, 0)[0:16, :] for i in range(8)]
    spread = dot(jnp.concatenate(picked, axis=0), copy_matrix(128, 128)).reshape(8, 16, 128)
    x1, y1 = wide * 8, narrow * 8
    mask1 = row_mask((24, 128), y1 - 6, ny // 2)
    for i in range(8):
        dup[pl.ds(0, 12, stride=2), :] = spread[i, 0:12, :]
        dup[pl.ds(1, 12, stride=2), :] = spread[i, 0:12, :]
        for k in (2 * i - 1, 2 * i):
            if 0 <= k < 14:
                m1[k] = (u[k] + dup[0:24, :]) * mask1 * plane_factor(x1 + k - 3, nx // 2)

    def sweep1(src, dst):
        def plane(i, carry):
            c, near = beside(src, i)
            keep = mask1 * plane_factor(x1 + i - 3, nx // 2)
            dst[i] = keep * (0.2 * c + SIDE * (near + 4.0 * b1[i + 1]))
            return carry

        return plane

    lax.fori_loop(1, 13, sweep1(m1, n1), 0, unroll=True)
    lax.fori_loop(2, 12, sweep1(n1, m1), 0, unroll=True)
    spread = dot(m1[2:12].reshape(10 * 24, 128), copy_matrix(128, 256)).reshape(10, 24, 256)
    x0, y0 = wide * 16, narrow * 16
    mask0 = row_mask((40, 256), y0 - ROWS, ny)
    for i in range(10):
        for half in range(2):
            value = spread[i, 0:20, 128 * half : 128 * half + 128]
            dup[pl.ds(0, 20, stride=2), :] = value
            dup[pl.ds(1, 20, stride=2), :] = value
            for k in (2 * i, 2 * i + 1):
                n0[k, :, 128 * half : 128 * half + 128] = dup[0:40, :]

    def add0(i, carry):
        m0[i] = (v_down[i] + n0[i]) * mask0 * plane_factor(x0 + i - 2, nx)
        return carry

    lax.fori_loop(0, 20, add0, 0, unroll=True)

    def sweep0(i, carry):
        c, near = beside(m0, i)
        keep = mask0 * plane_factor(x0 + i - 2, nx)
        n0[i] = keep * (0.2 * c + SIDE * (near + b[i + 8]))
        return carry

    lax.fori_loop(1, 19, sweep0, 0, unroll=True)

    def last0(i, carry):
        c, near = beside(n0, i + 2)
        value = 0.2 * c + SIDE * (near + b[i + 10])
        out[i] = value[12:28, :]
        return carry

    lax.fori_loop(0, 16, last0, 0, unroll=True)
    if not last:
        send(out, wider, low, high, HALO + 1)


def up(nx, ny, last, at, coarse, b1, u, b, v_down):
    rows2 = ny // 4
    rows3 = rows2 // 2
    wide_part = (28, rows2, 128)
    small = (12, rows3, 128)
    block = (16, 16, 256)
    scratch = [
        wide_part, wide_part, wide_part, small, small, small, small,
        (48, 128), (rows2, 128), (14, 24, 128), (14, 24, 128), (20, 40, 256), (20, 40, 256),
    ]
    return call(
        functools.partial(up_body, nx, ny, last),
        [block] if last else send_shapes(HALO + 1),
        scratch if last else scratch + [block],
        [at, *coarse, b1, u, b, v_down],
        20000000,
    )


def shifted(array, axis, step):
    count = lax.axis_size(axis)
    return lax.ppermute(
        array, axis, [(i, i + step) for i in range(count) if 0 <= i + step < count]
    )


def widen(wider, low, high):
    planes = low.shape[0]
    wider = lax.dynamic_update_slice(wider, shifted(high, "wide", 1), (0, 0, 0))
    return lax.dynamic_update_slice(wider, shifted(low, "wide", -1), (16 + planes, 0, 0))


def surround(wider, low, high):
    mid = widen(wider, low, high)
    return mid, shifted(mid, "narrow", 1), shifted(mid, "narrow", -1)


def spread_coarse(b2):
    wide, size = lax.axis_size("wide"), b2.shape[0]
    groups = [[g * size + k for k in range(size)] for g in range(wide // GROUP)]
    here = lax.all_to_all(b2, ("wide", "narrow"), 0, 0, axis_index_groups=groups)
    return here, shifted(here, "wide", GROUP), shifted(here, "wide", -GROUP)


def on_device(phase, distance, velocity):
    nx, ny = 16 * lax.axis_size("wide"), 16 * lax.axis_size("narrow")
    at = jnp.stack([lax.axis_index("wide"), lax.axis_index("narrow")]).astype(jnp.int32)
    psi, x_low, x_high, y_low, y_high = prepare(phase, distance, velocity)
    xl = shifted(x_high, "wide", 1)
    xh = shifted(x_low, "wide", -1)
    yl = shifted(y_high, "narrow", 1)
    yh = shifted(y_low, "narrow", -1)
    moved, *sends = transport(psi, velocity, xl, xh, yl, yh)
    mid = widen(*sends)
    m_low = shifted(mid[:, 13:, :], "narrow", 1)
    m_high = shifted(mid[:, :3, :], "narrow", -1)
    sends = force(nx, ny, at, mid, m_low, m_high, velocity, xl, xh, yl, yh)
    b, v, b1, u, b2 = first_down(nx, ny, at, *surround(*sends))
    sends = up(nx, ny, False, at, spread_coarse(b2), b1, u, b, v)
    v, b1, u, b2 = next_down(nx, ny, at, *surround(*sends), b)
    (pressure,) = up(nx, ny, True, at, spread_coarse(b2), b1, u, b, v)
    return (moved, pressure)


def solution(mesh):
    blocks = P("wide", "narrow", None)
    return jax.shard_map(
        on_device,
        mesh=mesh,
        in_specs=(blocks, blocks, P(None, "wide", "narrow", None)),
        out_specs=(blocks, blocks),
        check_vma=False,
    )
```

```python
import functools

import jax
import jax.numpy as jnp
from jax import lax
from jax.experimental import pallas as pl
from jax.experimental.pallas import tpu as pltpu
from jax.sharding import PartitionSpec as P

DELTA_SQ = 0.0025
WENO_EPS = 0.01
SIDE = 0.8 / 6.0
F32 = jnp.float32
HIGHEST = lax.Precision.HIGHEST

HALO = 14
KEEP = 4
NEAR = 4
GROUP = 4


def iota(shape, dim):
    return lax.broadcasted_iota(jnp.int32, shape, dim)


def roll(v, shift, axis):
    return pltpu.roll(v, shift % v.shape[axis], axis)


def z_shifted(v):
    lane = iota(v.shape, 1)
    last = v.shape[1] - 1
    lower = jnp.where(lane == 0, 0.0, roll(v, 1, 1))
    upper = jnp.where(lane == last, 0.0, roll(v, -1, 1))
    return lower, upper


def z_pair(v):
    lower, upper = z_shifted(v)
    return lower + upper


def y_pair(v):
    return roll(v, 1, 0) + roll(v, -1, 0)


def beside(ref, i):
    c = ref[i]
    return c, (ref[i - 1] + ref[i + 1]) + y_pair(c) + z_pair(c)


def inside(first, count):
    return jnp.logical_and(first >= 0, first < count)


def row_mask(shape, first, count):
    rows = iota(shape, 0) + first
    return jnp.where(inside(rows, count), 1.0, 0.0).astype(F32)


def plane_factor(index, count):
    return jnp.where(inside(index, count), 1.0, 0.0).astype(F32)


def dot(a, b):
    return lax.dot_general(
        a, b, (((1,), (0,)), ((), ())), precision=HIGHEST, preferred_element_type=F32
    )


def pair_matrix(rows, cols, value):
    return jnp.where((iota((rows, cols), 0) >> 1) == iota((rows, cols), 1), value, 0.0).astype(F32)


def copy_matrix(rows, cols):
    return jnp.where(iota((rows, cols), 0) == (iota((rows, cols), 1) >> 1), 1.0, 0.0).astype(F32)


def words(shape):
    *lead, rows, lanes = (1,) * (3 - len(shape)) + tuple(shape)
    size = -(-rows // 8) * 8 * (-(-lanes // 128) * 128)
    for n in lead:
        size *= n
    return size


def call(body, outs, scratch, args, flops):
    vmem = pl.BlockSpec(memory_space=pltpu.VMEM)
    smem = pl.BlockSpec(memory_space=pltpu.SMEM)
    total = sum(words(a.shape) for a in args) + sum(map(words, outs)) + sum(map(words, scratch))
    return pl.pallas_call(
        body,
        out_shape=[jax.ShapeDtypeStruct(s, F32) for s in outs],
        in_specs=[smem if a.dtype == jnp.int32 and a.ndim == 1 else vmem for a in args],
        out_specs=[vmem] * len(outs),
        scratch_shapes=[pltpu.VMEM(s, F32) for s in scratch],
        compiler_params=pltpu.CompilerParams(vmem_limit_bytes=4 * total + (6 << 20)),
        cost_estimate=pl.CostEstimate(flops=flops, bytes_accessed=4000000, transcendentals=0),
    )(*args)


def pick_sides(at, chip, link):
    odd = lax.rem(at[1], 2) == 1
    lower = lambda *k: jnp.where(odd, chip[k], link[k])
    upper = lambda *k: jnp.where(odd, link[k], chip[k])
    return lower, upper


def send_shapes(planes):
    return [(16 + 2 * planes, 16, 256), (planes, 16, 256), (planes, 16, 256)]


def send(block, wider, low, high, planes):
    for i in range(16):
        wider[planes + i] = block[i]
    for i in range(planes):
        low[i] = block[i]
        high[i] = block[16 - planes + i]


def prepare_body(at, phase, distance, velocity, psi, x_low, x_high, chip, link):
    odd = lax.rem(at[1], 2) == 1

    def plane(i, carry):
        orient = 2.0 * phase[i].astype(F32) - 1.0
        psi[i] = 1.0 / (1.0 + jnp.exp(-orient * distance[i]))
        first = jnp.concatenate([psi[i, 0:3, :], velocity[1, i, 0:1, :]], axis=0)
        final = jnp.concatenate([psi[i, 13:16, :], velocity[1, i, 15:16, :]], axis=0)
        chip[i] = jnp.where(odd, first, final)
        link[i] = jnp.where(odd, final, first)
        return carry

    lax.fori_loop(0, 16, plane, 0, unroll=True)
    for k in range(3):
        x_low[k] = psi[k]
        x_high[k] = psi[13 + k]
    x_low[3] = velocity[0, 0]
    x_high[3] = velocity[0, 15]


def prepare(at, phase, distance, velocity):
    outs = [(16, 16, 256), (4, 16, 256), (4, 16, 256), (16, 4, 256), (16, 4, 256)]
    return call(prepare_body, outs, [], [at, phase, distance, velocity], 1000000)


def indicators(a, b, c):
    d = a - c
    curve = (a + c) - 2.0 * b
    twice = 2.0 * curve
    base = (13.0 / 12.0) * (curve * curve) + WENO_EPS
    up, down = twice - d, twice + d
    p = base + 0.25 * (up * up)
    q = base + 0.25 * (d * d)
    r = base + 0.25 * (down * down)
    return p * p, q * q, r * r


def upwind_flux(s, l, p_left, q_left, r_left, p_right, q_right, r_right):
    ahead = s > 0.0
    pick = lambda x, y: jnp.where(ahead, x, y)
    a, b, c, e, f = pick(l[0], l[5]), pick(l[1], l[4]), pick(l[2], l[3]), pick(l[3], l[2]), pick(l[4], l[1])
    p, q, r = pick(p_left, r_right), pick(q_left, q_right), pick(r_left, p_right)
    w0, w1, w2 = 0.1 * (q * r), 0.6 * (p * r), 0.3 * (p * q)
    g0 = 2.0 * a - 7.0 * b + 11.0 * c
    g1 = 5.0 * c + 2.0 * e - b
    g2 = 2.0 * c + 5.0 * e - f
    top = w0 * g0 + w1 * g1 + w2 * g2
    return (s * top) / (6.0 * (w0 + w1 + w2))


def transport_body(at, psi, velocity, xl, xh, chip, link, moved, wider, low, high, ext, p_x, q_x, r_x, rows, speed):
    lower, upper = pick_sides(at, chip, link)
    for k in range(3):
        ext[k] = xl[k]
        ext[19 + k] = xh[k]

    def fill(i, carry):
        ext[3 + i] = psi[i]
        return carry

    lax.fori_loop(0, 16, fill, 0, unroll=True)

    def marks(i, carry):
        p, q, r = indicators(ext[i], ext[i + 1], ext[i + 2])
        p_x[i], q_x[i], r_x[i] = p, q, r
        return carry

    lax.fori_loop(0, 20, marks, 0, unroll=True)

    def x_flux(j, v_low, v_high):
        s = 0.5 * (v_low + v_high)
        l = [ext[j + k] for k in range(6)]
        return upwind_flux(
            s, l, p_x[j], q_x[j + 1], r_x[j + 2], p_x[j + 1], q_x[j + 2], r_x[j + 3]
        )

    def plane(i, below):
        here = velocity[0, i]
        following = jnp.where(i == 15, xh[3], velocity[0, jnp.minimum(i + 1, 15)])
        above = x_flux(i + 1, here, following)
        change = above - below
        y_low, y_high = lower(i), upper(i)
        rows[1:4, :] = y_low[0:3, :]
        rows[4:20, :] = psi[i]
        rows[20:23, :] = y_high[0:3, :]
        speed[3:4, :] = y_low[3:4, :]
        speed[4:20, :] = velocity[1, i]
        speed[20:21, :] = y_high[3:4, :]
        v = rows[...]
        u = speed[...]
        s = 0.5 * (u + roll(u, -1, 0))
        l = [roll(v, 2 - k, 0) for k in range(6)]
        p, q, r = indicators(l[1], l[2], l[3])
        q_next, r_next = roll(q, -1, 0), roll(r, -1, 0)
        flux = upwind_flux(s, l, roll(p, 1, 0), q, r_next, p, q_next, roll(r, -2, 0))
        rows_change = flux - roll(flux, 1, 0)
        change = change + rows_change[4:20, :]
        v = psi[i]
        w = velocity[2, i]
        lane = iota(v.shape, 1)

        def ahead(x, k):
            return jnp.where(lane > 255 - k, 0.0, roll(x, -k, 1))

        def behind(x, k):
            return jnp.where(lane < k, 0.0, roll(x, k, 1))

        l = [behind(v, 2), behind(v, 1), v, ahead(v, 1), ahead(v, 2), ahead(v, 3)]
        s = 0.5 * (w + ahead(w, 1))
        p, q, r = indicators(l[1], l[2], l[3])
        p1, q1, r1 = indicators(l[2], l[3], l[4])
        _, _, r2 = indicators(l[3], l[4], l[5])
        p0, _, _ = indicators(l[0], l[1], l[2])
        flux = upwind_flux(s, l, p0, q, r1, p, q1, r2)
        low = v[:, 0:128]
        none = jnp.zeros_like(low)
        l = [none, none, none, low, roll(low, -1, 1), roll(low, -2, 1)]
        p, q, r = indicators(l[1], l[2], l[3])
        p1, q1, r1 = indicators(l[2], l[3], l[4])
        _, _, r2 = indicators(l[3], l[4], l[5])
        p0, _, _ = indicators(none, none, none)
        wall = upwind_flux(0.5 * w[:, 0:128], l, p0, q, r1, p, q1, r2)
        wall = jnp.concatenate([wall, wall], axis=1)
        change = change + (flux - jnp.where(lane == 0, wall, roll(flux, 1, 1)))
        moved[i] = v - 0.25 * change
        return above

    rows[...] = jnp.zeros_like(rows)
    speed[...] = jnp.zeros_like(speed)
    lax.fori_loop(0, 16, plane, x_flux(0, xl[3], velocity[0, 0]), unroll=True)
    send(moved, wider, low, high, 3)


def transport(at, psi, velocity, xl, xh, chip, link):
    planes = (20, 16, 256)
    scratch = [(22, 16, 256), planes, planes, planes, (24, 256), (24, 256)]
    outs = [(16, 16, 256)] + send_shapes(3)
    return call(transport_body, outs, scratch, [at, psi, velocity, xl, xh, chip, link], 10000000)


def force_body(nx, ny, at, mid, chip, link, velocity, xl, xh, v_chip, v_link, wider, low, high, m, n_x, n_y, n_z, s_x, part, pad, source):
    lower, upper = pick_sides(at, chip, link)
    v_lower, v_upper = pick_sides(at, v_chip, v_link)
    x0, y0 = at[0] * 16, at[1] * 16
    shape = (32, 256)
    lane = iota(shape, 1)

    def fill(i, carry):
        m[i] = jnp.zeros(shape, F32)
        m[i, 5:8, :] = lower(i)
        m[i, 8:24, :] = mid[i]
        m[i, 24:27, :] = upper(i)
        return carry

    lax.fori_loop(0, 22, fill, 0, unroll=True)

    def gradient(i):
        c = m[i]
        below, above = z_shifted(c)
        gx = 0.5 * (m[i + 1] - m[i - 1])
        gy = 0.5 * (roll(c, -1, 0) - roll(c, 1, 0))
        return gx, gy, 0.5 * (above - below)

    def normals(i, carry):
        gx, gy, gz = gradient(i + 1)
        inverse = lax.rsqrt(gx * gx + gy * gy + gz * gz + DELTA_SQ)
        n_x[i], n_y[i], n_z[i] = gx * inverse, gy * inverse, gz * inverse
        return carry

    lax.fori_loop(0, 20, normals, 0, unroll=True)
    mask_y = row_mask(shape, y0 - 8, ny)

    def stars(i, carry):
        gx, gy, gz = gradient(i + 2)
        c = m[i + 2]
        edge = 0.5 * c
        edge = edge * lax.rsqrt(edge * edge + DELTA_SQ)
        nz = n_z[i + 1]
        above = jnp.where(lane == 255, -edge, roll(nz, -1, 1))
        below = jnp.where(lane == 0, edge, roll(nz, 1, 1))
        nn = n_y[i + 1]
        bending = -0.5 * (
            (n_x[i + 2] - n_x[i]) + (roll(nn, -1, 0) - roll(nn, 1, 0)) + (above - below)
        )
        keep = mask_y * plane_factor(x0 + i - 1, nx)
        bending = bending * keep
        fx, fy, fz = bending * gx, bending * gy, bending * gz
        k = jnp.clip(i - 1, 0, 15)
        vx = jnp.where(i == 0, xl[3], jnp.where(i == 17, xh[3], velocity[0, k]))
        s_x[i] = fx[8:24, :] + vx
        pad[7:8, :] = v_lower(k)[3:4, :]
        pad[8:24, :] = velocity[1, k]
        pad[24:25, :] = v_upper(k)[3:4, :]
        sy = fy + pad[...]
        dy = roll(sy, -1, 0) - roll(sy, 1, 0)
        sz = fz[8:24, :] + velocity[2, k]
        below, above = z_shifted(sz)
        part[i] = dy[8:24, :] + (above - below)
        return carry

    pad[...] = jnp.zeros_like(pad)
    lax.fori_loop(0, 18, stars, 0, unroll=True)

    def finish(i, carry):
        source[i] = -0.5 * (part[i + 1] + (s_x[i + 2] - s_x[i]))
        return carry

    lax.fori_loop(0, 16, finish, 0, unroll=True)
    send(source, wider, low, high, HALO)


def force(nx, ny, at, mid, chip, link, velocity, xl, xh, v_chip, v_link):
    n = (20, 32, 256)
    scratch = [(22, 32, 256), n, n, n, (18, 16, 256), (18, 16, 256), (32, 256), (16, 16, 256)]
    args = [at, mid, chip, link, velocity, xl, xh, v_chip, v_link]
    return call(functools.partial(force_body, nx, ny), send_shapes(HALO), scratch, args, 10000000)


class Field:
    def __init__(self, ref, lead):
        self.ref, self.lead = ref, lead

    def __getitem__(self, p):
        return self.ref[p + self.lead]

    def __setitem__(self, p, value):
        self.ref[p + self.lead] = value

    def beside(self, p):
        return beside(self.ref, p + self.lead)


def wall(at, nx, level, p, value):
    own = 16 >> level
    if 0 <= p < own:
        return value
    return value * plane_factor(at[0] * own + p, nx >> level)


def first_smooth(b, v, planes, weight, mask, at, nx, level):
    for p in planes:
        c, around = b.beside(p)
        v[p] = wall(at, nx, level, p, (weight * mask) * (1.2 * c + SIDE * around))


def sweep(src, dst, b, planes, factor, mask, at, nx, level):
    keep = SIDE * mask
    for p in planes:
        c, around = src.beside(p)
        near = around + (b[p] if factor == 1 else factor * b[p])
        dst[p] = 0.2 * c + wall(at, nx, level, p, keep) * near


def coarsen_level0(at, nx, ny, b, v, b1, planes, pair, t):
    first = planes[0]

    def residual(p):
        c, around = v.beside(p)
        return b[p] - (6.0 * c - around)

    for p in planes:
        total = residual(2 * p) + residual(2 * p + 1)
        for half in range(2):
            lanes = slice(128 * half, 128 * half + 128)
            pair[p - first, half] = total[:, lanes]
            even = pair[p - first, half, pl.ds(0, 24, stride=2), :]
            odd = pair[p - first, half, pl.ds(1, 24, stride=2), :]
            t[p - first, :, lanes] = even + odd
    count = len(planes)
    full = dot(t[...].reshape(count * 24, 256), pair_matrix(256, 128, 0.125))
    full = full.reshape(count, 24, 128)
    mask = row_mask((24, 128), at[1] * 8 - 8, ny // 2)
    for p in planes:
        b1[p] = wall(at, nx, 1, p, full[p - first] * mask)


def coarsen_level1(at, nx, ny, b1, u, planes, b2_out, s1, t1):
    mask = row_mask((24, 128), at[1] * 8 - 8, ny // 2)
    first_smooth(b1, u, planes, 4.0 * SIDE, mask, at, nx, 1)
    t1[...] = jnp.zeros_like(t1)
    for k in range(4):
        total = 0.0
        for p in (2 * k, 2 * k + 1):
            c, around = u.beside(p)
            total = total + (b1[p] - 0.25 * (6.0 * c - around))
        s1[k] = total
        t1[k, 0:4, :] = s1[k, pl.ds(8, 4, stride=2), :] + s1[k, pl.ds(9, 4, stride=2), :]
    small = dot(t1[...].reshape(32, 128), pair_matrix(128, 128, 0.125)).reshape(4, 8, 128)
    tile = jnp.concatenate([small[0, 0:4], small[1, 0:4]], axis=0) + roll(
        jnp.concatenate([small[2, 0:4], small[3, 0:4]], axis=0), 64, 1
    )
    for k in range(b2_out.shape[0]):
        b2_out[k] = tile


def reach(extra):
    e0 = extra + 2
    r1 = -(-e0 // 2)
    e1 = r1 + 2
    r2 = -(-e1 // 2)
    e2 = r2 + 2
    r3 = -(-e2 // 2)
    return e0, r1, e1, r2, e2, r3


E0, R1, E1, R2, E2, R3 = reach(KEEP)


def first_down_body(nx, ny, at, mid, chip, link, b_out, v_out, b1_out, u_out, b2_out, b, v, pair, t, s1, t1):
    lower, upper = pick_sides(at, chip, link)
    for i in range(16 + 2 * HALO):
        b[i, 0:16, :] = lower(i)
        b[i, 16:32, :] = mid[i]
        b[i, 32:48, :] = upper(i)
    b, v = Field(b, HALO), Field(v, HALO - 1)
    mask = row_mask((48, 256), at[1] * 16 - 16, ny)
    first_smooth(b, v, range(1 - HALO, 15 + HALO), SIDE, mask, at, nx, 0)
    v_out, b_out = Field(v_out, E0), Field(b_out, E0 - 1)
    for p in range(-E0, 16 + E0):
        v_out[p] = v[p]
    for p in range(1 - E0, 15 + E0):
        b_out[p] = b[p]
    b1, u = Field(b1_out, E1 + 1), Field(u_out, E1)
    coarsen_level0(at, nx, ny, b, v, b1, range(-E1 - 1, 9 + E1), pair, t)
    coarsen_level1(at, nx, ny, b1, u, range(-E1, 8 + E1), b2_out, s1, t1)


def tiles(ny):
    return (GROUP * ny // 16, 8, 128)


def around_block(size, extra, rows, lanes):
    return (size + 2 * extra, rows, lanes)


def first_down(nx, ny, at, mid, chip, link):
    level1 = around_block(8, E1 + 1, 24, 128)
    outs = [
        around_block(16, E0 - 1, 48, 256),
        around_block(16, E0, 48, 256),
        level1,
        around_block(8, E1, 24, 128),
        tiles(ny),
    ]
    scratch = [
        around_block(16, HALO, 48, 256),
        around_block(16, HALO - 1, 48, 256),
        (level1[0], 2, 48, 128),
        (level1[0], 24, 256),
        (4, 24, 128),
        (4, 8, 128),
    ]
    args = [at, mid, chip, link]
    return call(functools.partial(first_down_body, nx, ny), outs, scratch, args, 20000000)


def second_down_body(nx, ny, at, mid, chip, link, b1_out, u_out, b2_out, s1, t1):
    lower, upper = pick_sides(at, chip, link)
    for i in range(8 + 2 * NEAR):
        b1_out[i, 0:8, :] = lower(i)
        b1_out[i, 8:16, :] = mid[i]
        b1_out[i, 16:24, :] = upper(i)
    b1, u = Field(b1_out, NEAR), Field(u_out, NEAR - 1)
    coarsen_level1(at, nx, ny, b1, u, range(1 - NEAR, 7 + NEAR), b2_out, s1, t1)


def second_down(nx, ny, at, mid, chip, link):
    outs = [around_block(8, NEAR, 24, 128), around_block(8, NEAR - 1, 24, 128), tiles(ny)]
    scratch = [(4, 24, 128), (4, 8, 128)]
    args = [at, mid, chip, link]
    return call(functools.partial(second_down_body, nx, ny), outs, scratch, args, 2000000)


def solve_coarse(nx, ny, extra, at, coarse, s2, v2, w2, t3, b3, c3, d3, dup, row2):
    here, before, after = coarse
    _, _, _, r2, e2, r3 = reach(extra)
    spot = at[0] % GROUP
    rows2 = ny // 4
    rows3 = rows2 // 2
    count = rows2 // 4
    lead = 2 * (r3 + 3) + 2
    blocks = -(-lead // 4)
    s2, v2, w2 = Field(s2, 4 * blocks), Field(v2, lead - 1), Field(w2, e2)
    lane8 = iota((8, 128), 1) < 64
    for j in range(-blocks, blocks + 1):
        block = spot + GROUP + j
        layer, place = block // GROUP, block % GROUP
        for n in range(count):
            k = place * count + n
            tile = jnp.where(layer == 0, before[k], jnp.where(layer == 1, here[k], after[k]))
            halves = (jnp.where(lane8, tile, 0.0), jnp.where(lane8, roll(tile, 64, 1), 0.0))
            for p in range(4):
                part = halves[p // 2][4 * (p % 2) : 4 * (p % 2) + 4, :]
                s2.ref[4 * (j + blocks) + p, 4 * n : 4 * n + 4, :] = part

    def around(f, p):
        c = f[p]
        row = iota(c.shape, 0)
        lower = jnp.where(row == 0, 0.0, roll(c, 1, 0))
        upper = jnp.where(row == c.shape[0] - 1, 0.0, roll(c, -1, 0))
        beside = (lower + upper) + (roll(c, 1, 1) + roll(c, -1, 1))
        return c, (f[p - 1] + f[p + 1]) + beside

    def lanes_below(rows, lanes):
        return jnp.where(iota((rows, 128), 1) < lanes, 1.0, 0.0).astype(F32)

    mask2 = lanes_below(rows2, 64)
    for p in range(1 - lead, 3 + lead):
        c, near = around(s2, p)
        v2[p] = wall(at, nx, 2, p, (16.0 * SIDE) * mask2 * (1.2 * c + SIDE * near))

    def residual2(p):
        c, near = around(v2, p)
        return s2[p] - (1.0 / 16.0) * (6.0 * c - near)

    planes3 = range(-r3 - 3, 2 + r3 + 3)
    for i, p in enumerate(planes3):
        row2[i] = residual2(2 * p) + residual2(2 * p + 1)
        t3[i] = row2[i, pl.ds(0, rows3, stride=2), :] + row2[i, pl.ds(1, rows3, stride=2), :]
    total3 = len(planes3)
    full = dot(t3[...].reshape(total3 * rows3, 128), pair_matrix(128, 128, 0.125))
    full = full.reshape(total3, rows3, 128)
    mask3 = lanes_below(rows3, 32)
    b3, c3, d3 = Field(b3, r3 + 3), Field(c3, r3 + 3), Field(d3, r3 + 3)
    for i, p in enumerate(planes3):
        value = wall(at, nx, 3, p, full[i] * ((64.0 * SIDE) * mask3))
        b3[p] = value
    src, dst = b3, c3
    for step in (2, 1, 0):
        for p in range(-r3 - step, 2 + r3 + step):
            c, near = around(src, p)
            dst[p] = wall(at, nx, 3, p, mask3 * (0.2 * c + SIDE * near)) + b3[p]
        src, dst = dst, (d3 if dst is c3 else c3)
    final = src
    planes = range(-r3, 2 + r3)
    flat = jnp.concatenate([final[p] for p in planes], axis=0)
    spread = dot(flat, copy_matrix(128, 128)).reshape(len(planes), rows3, 128)
    for i, p in enumerate(planes):
        dup[i, pl.ds(0, rows3, stride=2), :] = spread[i]
        dup[i, pl.ds(1, rows3, stride=2), :] = spread[i]
        for q in (2 * p, 2 * p + 1):
            if -e2 <= q < 4 + e2:
                v2[q] = v2[q] + wall(at, nx, 2, q, dup[i, 0:rows2, :] * mask2)
    keep = SIDE * mask2
    for src, dst, step in ((v2, w2, 1), (w2, v2, 0)):
        for p in range(-r2 - step, 4 + r2 + step):
            c, near = around(src, p)
            dst[p] = 0.2 * c + wall(at, nx, 2, p, keep) * (near + 16.0 * s2[p])
    return v2


def coarse_scratch(ny, extra):
    _, _, _, _, e2, r3 = reach(extra)
    rows2 = ny // 4
    rows3 = rows2 // 2
    lead = 2 * (r3 + 3) + 2
    small = around_block(2, r3 + 3, rows3, 128)
    return [
        around_block(4, -(-lead // 4) * 4, rows2, 128),
        around_block(4, lead - 1, rows2, 128),
        around_block(4, e2, rows2, 128),
        small, small, small, small,
        (8, 48, 128),
        around_block(2, r3 + 3, rows2, 128),
    ]


def climb(nx, ny, extra, at, v2, b1, u, b, v_down, m1, n1, m0, n0, dup):
    e0, r1, e1, r2, _, _ = reach(extra)
    rows2 = ny // 4
    turn = lax.rem(rows2 + 4 - 4 * at[1] + rows2, rows2)
    planes = range(-r2, 4 + r2)
    picked = jnp.concatenate([pltpu.roll(v2[p], turn, 0)[0:16, :] for p in planes], axis=0)
    spread = dot(picked, copy_matrix(128, 128)).reshape(len(planes), 16, 128)
    mask1 = row_mask((24, 128), at[1] * 8 - 8, ny // 2)
    m1, n1 = Field(m1, e1), Field(n1, e1)
    for i, p in enumerate(planes):
        dup[i, 0, pl.ds(0, 12, stride=2), :] = spread[i, 0:12, :]
        dup[i, 0, pl.ds(1, 12, stride=2), :] = spread[i, 0:12, :]
        for q in (2 * p, 2 * p + 1):
            if -e1 <= q < 8 + e1:
                m1[q] = u[q] + wall(at, nx, 1, q, dup[i, 0, 0:24, :] * mask1)
    sweep(m1, n1, b1, range(1 - e1, 7 + e1), 4.0, mask1, at, nx, 1)
    sweep(n1, m1, b1, range(2 - e1, 6 + e1), 4.0, mask1, at, nx, 1)
    planes = range(-r1, 8 + r1)
    flat = jnp.concatenate([m1[p] for p in planes], axis=0)
    spread = dot(flat, copy_matrix(128, 256)).reshape(len(planes), 24, 256)
    mask0 = row_mask((48, 256), at[1] * 16 - 16, ny)
    m0, n0 = Field(m0, e0), Field(n0, e0)
    for i, p in enumerate(planes):
        for half in range(2):
            value = spread[i, :, 128 * half : 128 * half + 128]
            dup[i, half, pl.ds(0, 24, stride=2), :] = value
            dup[i, half, pl.ds(1, 24, stride=2), :] = value
        value = jnp.concatenate([dup[i, 0], dup[i, 1]], axis=1) * mask0
        for q in (2 * p, 2 * p + 1):
            if -e0 <= q < 16 + e0:
                m0[q] = v_down[q] + wall(at, nx, 0, q, value)
    sweep(m0, n0, b, range(1 - e0, 15 + e0), 1, mask0, at, nx, 0)
    if extra:
        sweep(n0, m0, b, range(2 - e0, 14 + e0), 1, mask0, at, nx, 0)
        return m0
    return n0


def climb_scratch(extra):
    e0, r1, e1, r2, _, _ = reach(extra)
    level1 = around_block(8, e1, 24, 128)
    level0 = around_block(16, e0, 48, 256)
    return [level1, level1, level0, level0, (max(8 + 2 * r1, 4 + 2 * r2), 2, 48, 128)]


def turn_body(nx, ny, at, here, before, after, b1, u, b, v_down, v_out, wider, low, high, own, pair, t, *scratch):
    v2 = solve_coarse(nx, ny, KEEP, at, (here, before, after), *scratch[:9])
    b = Field(b, E0 - 1)
    v = climb(nx, ny, KEEP, at, v2, Field(b1, E1 + 1), Field(u, E1), b, Field(v_down, E0), *scratch[9:])
    mask = row_mask((48, 256), at[1] * 16 - 16, ny)
    once, twice = Field(scratch[12], E0), Field(v_out, KEEP - 2)
    sweep(v, once, b, range(1 - KEEP, 15 + KEEP), 1, mask, at, nx, 0)
    sweep(once, twice, b, range(2 - KEEP, 14 + KEEP), 1, mask, at, nx, 0)
    coarsen_level0(at, nx, ny, b, twice, Field(own, 0), range(8), pair, t)
    for i in range(8):
        wider[NEAR + i] = own[i, 8:16, :]
    for i in range(NEAR):
        low[i] = own[i, 8:16, :]
        high[i] = own[8 - NEAR + i, 8:16, :]


def turn(nx, ny, at, coarse, b1, u, b, v_down):
    outs = [
        around_block(16, KEEP - 2, 48, 256),
        around_block(8, NEAR, 8, 128),
        (NEAR, 8, 128),
        (NEAR, 8, 128),
    ]
    scratch = [(8, 24, 128), (8, 2, 48, 128), (8, 24, 256)]
    scratch += coarse_scratch(ny, KEEP) + climb_scratch(KEEP)
    args = [at, *coarse, b1, u, b, v_down]
    return call(functools.partial(turn_body, nx, ny), outs, scratch, args, 30000000)


def finish_body(nx, ny, at, here, before, after, b1, u, b, v_down, out, *scratch):
    v2 = solve_coarse(nx, ny, 0, at, (here, before, after), *scratch[:9])
    b, v_down = Field(b, E0 - 1), Field(v_down, KEEP - 2)
    v = climb(nx, ny, 0, at, v2, Field(b1, NEAR), Field(u, NEAR - 1), b, v_down, *scratch[9:])
    for p in range(16):
        c, around = v.beside(p)
        out[p] = (0.2 * c + SIDE * (around + b[p]))[16:32, :]


def finish(nx, ny, at, coarse, b1, u, b, v_down):
    scratch = coarse_scratch(ny, 0) + climb_scratch(0)
    args = [at, *coarse, b1, u, b, v_down]
    return call(functools.partial(finish_body, nx, ny), [(16, 16, 256)], scratch, args, 20000000)[0]


def shifted(array, axis, step):
    count = lax.axis_size(axis)
    return lax.ppermute(
        array, axis, [(i, i + step) for i in range(count) if 0 <= i + step < count]
    )


def swapped(array, first):
    count = lax.axis_size("narrow")
    pairs = [(i, i + 1) for i in range(first, count - 1, 2)]
    return lax.ppermute(array, "narrow", pairs + [(j, i) for i, j in pairs])


def widen(wider, low, high):
    planes = low.shape[0]
    wider = lax.dynamic_update_slice(wider, shifted(high, "wide", 1), (0, 0, 0))
    upper = wider.shape[0] - planes
    return lax.dynamic_update_slice(wider, shifted(low, "wide", -1), (upper, 0, 0))


def surround(wider, low, high):
    mid = widen(wider, low, high)
    link = swapped(mid, 1)
    return mid, swapped(mid, 0), link


def spread_coarse(b2):
    wide, size = lax.axis_size("wide"), b2.shape[0]
    groups = [[g * size + k for k in range(size)] for g in range(wide // GROUP)]
    here = lax.all_to_all(b2, ("wide", "narrow"), 0, 0, axis_index_groups=groups)
    return here, shifted(here, "wide", GROUP), shifted(here, "wide", -GROUP)


def on_device(phase, distance, velocity):
    nx, ny = 16 * lax.axis_size("wide"), 16 * lax.axis_size("narrow")
    narrow = lax.axis_index("narrow")
    at = jnp.stack([lax.axis_index("wide"), narrow]).astype(jnp.int32)
    psi, x_low, x_high, chip, link = prepare(at, phase, distance, velocity)
    xl = shifted(x_high, "wide", 1)
    xh = shifted(x_low, "wide", -1)
    v_link = swapped(link, 1)
    v_chip = swapped(chip, 0)
    moved, *sends = transport(at, psi, velocity, xl, xh, v_chip, v_link)
    mid = widen(*sends)
    odd = lax.rem(narrow, 2) == 1
    first, final = mid[:, :3, :], mid[:, 13:, :]
    link = swapped(jnp.where(odd, final, first), 1)
    chip = swapped(jnp.where(odd, first, final), 0)
    sends = force(nx, ny, at, mid, chip, link, velocity, xl, xh, v_chip, v_link)
    b, v, b1, u, b2 = first_down(nx, ny, at, *surround(*sends))
    v, *sends = turn(nx, ny, at, spread_coarse(b2), b1, u, b, v)
    b1, u, b2 = second_down(nx, ny, at, *surround(*sends))
    pressure = finish(nx, ny, at, spread_coarse(b2), b1, u, b, v)
    return (moved, pressure)


def solution(mesh):
    blocks = P("wide", "narrow", None)
    return jax.shard_map(
        on_device,
        mesh=mesh,
        in_specs=(blocks, blocks, P(None, "wide", "narrow", None)),
        out_specs=(blocks, blocks),
        check_vma=False,
    )
```

```python
import functools

import jax
import jax.numpy as jnp
from jax import lax
from jax.experimental import pallas as pl
from jax.experimental.pallas import tpu as pltpu
from jax.sharding import PartitionSpec as P

DELTA_SQ = 0.0025
WENO_EPS = 0.01
SIDE = 0.8 / 6.0
F32 = jnp.float32
HIGHEST = lax.Precision.HIGHEST

HALO = 14
KEEP = 4
NEAR = 4
GROUP = 4


def iota(shape, dim):
    return lax.broadcasted_iota(jnp.int32, shape, dim)


def roll(v, shift, axis):
    return pltpu.roll(v, shift % v.shape[axis], axis)


def z_shifted(v):
    lane = iota(v.shape, 1)
    last = v.shape[1] - 1
    lower = jnp.where(lane == 0, 0.0, roll(v, 1, 1))
    upper = jnp.where(lane == last, 0.0, roll(v, -1, 1))
    return lower, upper


def z_pair(v):
    lower, upper = z_shifted(v)
    return lower + upper


def y_pair(v):
    return roll(v, 1, 0) + roll(v, -1, 0)


def beside(ref, i):
    c = ref[i]
    return c, (ref[i - 1] + ref[i + 1]) + y_pair(c) + z_pair(c)


def inside(first, count):
    return jnp.logical_and(first >= 0, first < count)


def row_mask(shape, first, count):
    rows = iota(shape, 0) + first
    return jnp.where(inside(rows, count), 1.0, 0.0).astype(F32)


def plane_factor(index, count):
    return jnp.where(inside(index, count), 1.0, 0.0).astype(F32)


def dot(a, b):
    return lax.dot_general(
        a, b, (((1,), (0,)), ((), ())), precision=HIGHEST, preferred_element_type=F32
    )


def pair_matrix(rows, cols, value):
    return jnp.where((iota((rows, cols), 0) >> 1) == iota((rows, cols), 1), value, 0.0).astype(F32)


def copy_matrix(rows, cols):
    return jnp.where(iota((rows, cols), 0) == (iota((rows, cols), 1) >> 1), 1.0, 0.0).astype(F32)


def words(shape):
    *lead, rows, lanes = (1,) * (3 - len(shape)) + tuple(shape)
    size = -(-rows // 8) * 8 * (-(-lanes // 128) * 128)
    for n in lead:
        size *= n
    return size


def call(body, outs, scratch, args, flops):
    vmem = pl.BlockSpec(memory_space=pltpu.VMEM)
    smem = pl.BlockSpec(memory_space=pltpu.SMEM)
    total = sum(words(a.shape) for a in args) + sum(map(words, outs)) + sum(map(words, scratch))
    return pl.pallas_call(
        body,
        out_shape=[jax.ShapeDtypeStruct(s, F32) for s in outs],
        in_specs=[smem if a.dtype == jnp.int32 and a.ndim == 1 else vmem for a in args],
        out_specs=[vmem] * len(outs),
        scratch_shapes=[pltpu.VMEM(s, F32) for s in scratch],
        compiler_params=pltpu.CompilerParams(vmem_limit_bytes=4 * total + (6 << 20)),
        cost_estimate=pl.CostEstimate(flops=flops, bytes_accessed=4000000, transcendentals=0),
    )(*args)


def pick_sides(at, chip, link):
    odd = lax.rem(at[1], 2) == 1
    lower = lambda *k: jnp.where(odd, chip[k], link[k])
    upper = lambda *k: jnp.where(odd, link[k], chip[k])
    return lower, upper


def send_shapes(planes):
    return [(16 + 2 * planes, 16, 256), (planes, 16, 256), (planes, 16, 256)]


def send(block, wider, low, high, planes):
    for i in range(16):
        wider[planes + i] = block[i]
    for i in range(planes):
        low[i] = block[i]
        high[i] = block[16 - planes + i]


PARTS = 4


def prepare_body(at, phase, distance, velocity, psi, x_low, x_high, chip, link, kind, away, x_face, y_face, sems):
    odd = lax.rem(at[1], 2) == 1
    step = 16 // PARTS
    copies = []

    def copy(src, dst):
        started = pltpu.make_async_copy(src, dst, sems.at[len(copies)])
        started.start()
        copies.append(started)

    for k in range(PARTS):
        planes = pl.ds(step * k, step)
        copy(phase.at[planes], kind.at[planes])
        copy(distance.at[planes], away.at[planes])
    copy(velocity.at[0, 0], x_face.at[0])
    copy(velocity.at[0, 15], x_face.at[1])
    copy(velocity.at[1, :, pl.ds(0, 8), :], y_face.at[0])
    copy(velocity.at[1, :, pl.ds(8, 8), :], y_face.at[1])
    for k in range(PARTS):
        copies[2 * k].wait()
        copies[2 * k + 1].wait()
        for i in range(step * k, step * k + step):
            orient = 2.0 * kind[i].astype(F32) - 1.0
            psi[i] = 1.0 / (1.0 + jnp.exp(-orient * away[i]))
    for started in copies[2 * PARTS :]:
        started.wait()
    for i in range(16):
        first = jnp.concatenate([psi[i, 0:3, :], y_face[0, i, 0:1, :]], axis=0)
        final = jnp.concatenate([psi[i, 13:16, :], y_face[1, i, 7:8, :]], axis=0)
        chip[i] = jnp.where(odd, first, final)
        link[i] = jnp.where(odd, final, first)
    for k in range(3):
        x_low[k] = psi[k]
        x_high[k] = psi[13 + k]
    x_low[3] = x_face[0]
    x_high[3] = x_face[1]


def prepare(at, phase, distance, velocity):
    vmem = pl.BlockSpec(memory_space=pltpu.VMEM)
    smem = pl.BlockSpec(memory_space=pltpu.SMEM)
    hbm = pl.BlockSpec(memory_space=pltpu.HBM)
    outs = [(16, 16, 256), (4, 16, 256), (4, 16, 256), (16, 4, 256), (16, 4, 256)]
    return pl.pallas_call(
        prepare_body,
        out_shape=[jax.ShapeDtypeStruct(s, F32) for s in outs],
        in_specs=[smem, hbm, hbm, hbm],
        out_specs=[vmem] * len(outs),
        scratch_shapes=[
            pltpu.VMEM((16, 16, 256), jnp.int32),
            pltpu.VMEM((16, 16, 256), F32),
            pltpu.VMEM((2, 16, 256), F32),
            pltpu.VMEM((2, 16, 8, 256), F32),
            pltpu.SemaphoreType.DMA((2 * PARTS + 4,)),
        ],
        compiler_params=pltpu.CompilerParams(vmem_limit_bytes=8 << 20),
        cost_estimate=pl.CostEstimate(flops=1000000, bytes_accessed=1000000, transcendentals=0),
    )(at, *(pltpu.with_memory_space_constraint(a, pltpu.HBM) for a in (phase, distance, velocity)))


def indicators(a, b, c):
    d = a - c
    curve = (a + c) - 2.0 * b
    twice = 2.0 * curve
    base = (13.0 / 12.0) * (curve * curve) + WENO_EPS
    up, down = twice - d, twice + d
    p = base + 0.25 * (up * up)
    q = base + 0.25 * (d * d)
    r = base + 0.25 * (down * down)
    return p * p, q * q, r * r


def upwind_flux(s, l, p_left, q_left, r_left, p_right, q_right, r_right):
    ahead = s > 0.0
    pick = lambda x, y: jnp.where(ahead, x, y)
    a, b, c, e, f = pick(l[0], l[5]), pick(l[1], l[4]), pick(l[2], l[3]), pick(l[3], l[2]), pick(l[4], l[1])
    p, q, r = pick(p_left, r_right), pick(q_left, q_right), pick(r_left, p_right)
    w0, w1, w2 = 0.1 * (q * r), 0.6 * (p * r), 0.3 * (p * q)
    g0 = 2.0 * a - 7.0 * b + 11.0 * c
    g1 = 5.0 * c + 2.0 * e - b
    g2 = 2.0 * c + 5.0 * e - f
    top = w0 * g0 + w1 * g1 + w2 * g2
    return (s * top) / (6.0 * (w0 + w1 + w2))


def transport_body(at, psi, velocity, xl, xh, chip, link, moved, wider, low, high, ext, p_x, q_x, r_x, rows, speed):
    lower, upper = pick_sides(at, chip, link)
    for k in range(3):
        ext[k] = xl[k]
        ext[19 + k] = xh[k]

    def fill(i, carry):
        ext[3 + i] = psi[i]
        return carry

    lax.fori_loop(0, 16, fill, 0, unroll=True)

    def marks(i, carry):
        p, q, r = indicators(ext[i], ext[i + 1], ext[i + 2])
        p_x[i], q_x[i], r_x[i] = p, q, r
        return carry

    lax.fori_loop(0, 20, marks, 0, unroll=True)

    def x_flux(j, v_low, v_high):
        s = 0.5 * (v_low + v_high)
        l = [ext[j + k] for k in range(6)]
        return upwind_flux(
            s, l, p_x[j], q_x[j + 1], r_x[j + 2], p_x[j + 1], q_x[j + 2], r_x[j + 3]
        )

    def plane(i, below):
        here = velocity[0, i]
        following = jnp.where(i == 15, xh[3], velocity[0, jnp.minimum(i + 1, 15)])
        above = x_flux(i + 1, here, following)
        change = above - below
        y_low, y_high = lower(i), upper(i)
        rows[1:4, :] = y_low[0:3, :]
        rows[4:20, :] = psi[i]
        rows[20:23, :] = y_high[0:3, :]
        speed[3:4, :] = y_low[3:4, :]
        speed[4:20, :] = velocity[1, i]
        speed[20:21, :] = y_high[3:4, :]
        v = rows[...]
        u = speed[...]
        s = 0.5 * (u + roll(u, -1, 0))
        l = [roll(v, 2 - k, 0) for k in range(6)]
        p, q, r = indicators(l[1], l[2], l[3])
        q_next, r_next = roll(q, -1, 0), roll(r, -1, 0)
        flux = upwind_flux(s, l, roll(p, 1, 0), q, r_next, p, q_next, roll(r, -2, 0))
        rows_change = flux - roll(flux, 1, 0)
        change = change + rows_change[4:20, :]
        v = psi[i]
        w = velocity[2, i]
        lane = iota(v.shape, 1)

        def ahead(x, k):
            return jnp.where(lane > 255 - k, 0.0, roll(x, -k, 1))

        def behind(x, k):
            return jnp.where(lane < k, 0.0, roll(x, k, 1))

        l = [behind(v, 2), behind(v, 1), v, ahead(v, 1), ahead(v, 2), ahead(v, 3)]
        s = 0.5 * (w + ahead(w, 1))
        p, q, r = indicators(l[1], l[2], l[3])
        square = v * v
        edge = WENO_EPS + (13.0 / 12.0 + 9.0 / 4.0) * square
        edge = edge * edge
        level = WENO_EPS + (13.0 / 12.0 + 1.0 / 4.0) * square
        level = level * level
        p_below = jnp.where(lane == 0, edge, roll(p, 1, 1))
        q_above = jnp.where(lane == 255, level, roll(q, -1, 1))
        r_above = jnp.where(lane == 255, edge, roll(r, -1, 1))
        r_far = jnp.where(lane == 255, WENO_EPS * WENO_EPS, roll(r_above, -1, 1))
        flux = upwind_flux(s, l, p_below, q, r_above, p, q_above, r_far)
        low = slice(0, 128)
        none = jnp.zeros((v.shape[0], 128), F32)
        l = [none, none, none, v[:, low], l[3][:, low], l[4][:, low]]
        wall = upwind_flux(
            0.5 * w[:, low], l, none + WENO_EPS * WENO_EPS, level[:, low], r[:, low],
            edge[:, low], q[:, low], r_above[:, low],
        )
        wall = jnp.concatenate([wall, wall], axis=1)
        change = change + (flux - jnp.where(lane == 0, wall, roll(flux, 1, 1)))
        moved[i] = v - 0.25 * change
        return above

    rows[...] = jnp.zeros_like(rows)
    speed[...] = jnp.zeros_like(speed)
    lax.fori_loop(0, 16, plane, x_flux(0, xl[3], velocity[0, 0]), unroll=True)
    send(moved, wider, low, high, 3)


def transport(at, psi, velocity, xl, xh, chip, link):
    planes = (20, 16, 256)
    scratch = [(22, 16, 256), planes, planes, planes, (24, 256), (24, 256)]
    outs = [(16, 16, 256)] + send_shapes(3)
    return call(transport_body, outs, scratch, [at, psi, velocity, xl, xh, chip, link], 10000000)


def force_body(nx, ny, at, mid, chip, link, velocity, xl, xh, v_chip, v_link, wider, low, high, m, n_x, n_y, n_z, s_x, part, pad, source):
    lower, upper = pick_sides(at, chip, link)
    v_lower, v_upper = pick_sides(at, v_chip, v_link)
    x0, y0 = at[0] * 16, at[1] * 16
    shape = (32, 256)
    lane = iota(shape, 1)

    def fill(i, carry):
        m[i] = jnp.zeros(shape, F32)
        m[i, 5:8, :] = lower(i)
        m[i, 8:24, :] = mid[i]
        m[i, 24:27, :] = upper(i)
        return carry

    lax.fori_loop(0, 22, fill, 0, unroll=True)

    def gradient(i):
        c = m[i]
        below, above = z_shifted(c)
        gx = 0.5 * (m[i + 1] - m[i - 1])
        gy = 0.5 * (roll(c, -1, 0) - roll(c, 1, 0))
        return gx, gy, 0.5 * (above - below)

    def normals(i, carry):
        gx, gy, gz = gradient(i + 1)
        inverse = lax.rsqrt(gx * gx + gy * gy + gz * gz + DELTA_SQ)
        n_x[i], n_y[i], n_z[i] = gx * inverse, gy * inverse, gz * inverse
        return carry

    lax.fori_loop(0, 20, normals, 0, unroll=True)
    mask_y = row_mask(shape, y0 - 8, ny)

    def stars(i, carry):
        gx, gy, gz = gradient(i + 2)
        c = m[i + 2]
        edge = 0.5 * c
        edge = edge * lax.rsqrt(edge * edge + DELTA_SQ)
        nz = n_z[i + 1]
        above = jnp.where(lane == 255, -edge, roll(nz, -1, 1))
        below = jnp.where(lane == 0, edge, roll(nz, 1, 1))
        nn = n_y[i + 1]
        bending = -0.5 * (
            (n_x[i + 2] - n_x[i]) + (roll(nn, -1, 0) - roll(nn, 1, 0)) + (above - below)
        )
        keep = mask_y * plane_factor(x0 + i - 1, nx)
        bending = bending * keep
        fx, fy, fz = bending * gx, bending * gy, bending * gz
        k = jnp.clip(i - 1, 0, 15)
        vx = jnp.where(i == 0, xl[3], jnp.where(i == 17, xh[3], velocity[0, k]))
        s_x[i] = fx[8:24, :] + vx
        pad[7:8, :] = v_lower(k)[3:4, :]
        pad[8:24, :] = velocity[1, k]
        pad[24:25, :] = v_upper(k)[3:4, :]
        sy = fy + pad[...]
        dy = roll(sy, -1, 0) - roll(sy, 1, 0)
        sz = fz[8:24, :] + velocity[2, k]
        below, above = z_shifted(sz)
        part[i] = dy[8:24, :] + (above - below)
        return carry

    pad[...] = jnp.zeros_like(pad)
    lax.fori_loop(0, 18, stars, 0, unroll=True)

    def finish(i, carry):
        source[i] = -0.5 * (part[i + 1] + (s_x[i + 2] - s_x[i]))
        return carry

    lax.fori_loop(0, 16, finish, 0, unroll=True)
    send(source, wider, low, high, HALO)


def force(nx, ny, at, mid, chip, link, velocity, xl, xh, v_chip, v_link):
    n = (20, 32, 256)
    scratch = [(22, 32, 256), n, n, n, (18, 16, 256), (18, 16, 256), (32, 256), (16, 16, 256)]
    args = [at, mid, chip, link, velocity, xl, xh, v_chip, v_link]
    return call(functools.partial(force_body, nx, ny), send_shapes(HALO), scratch, args, 10000000)


class Field:
    def __init__(self, ref, lead):
        self.ref, self.lead = ref, lead

    def __getitem__(self, p):
        return self.ref[p + self.lead]

    def __setitem__(self, p, value):
        self.ref[p + self.lead] = value

    def beside(self, p):
        return beside(self.ref, p + self.lead)


def wall(at, nx, level, p, value):
    own = 16 >> level
    if 0 <= p < own:
        return value
    return value * plane_factor(at[0] * own + p, nx >> level)


def first_smooth(b, v, planes, weight, mask, at, nx, level):
    for p in planes:
        c, around = b.beside(p)
        v[p] = wall(at, nx, level, p, (weight * mask) * (1.2 * c + SIDE * around))


def sweep(src, dst, b, planes, factor, mask, at, nx, level):
    keep = SIDE * mask
    for p in planes:
        c, around = src.beside(p)
        near = around + (b[p] if factor == 1 else factor * b[p])
        dst[p] = 0.2 * c + wall(at, nx, level, p, keep) * near


def coarsen_level0(at, nx, ny, b, v, b1, planes, pair, t):
    first = planes[0]
    rows = t.shape[1]

    def residual(p):
        c, around = v.beside(p)
        return b[p] - (6.0 * c - around)

    for p in planes:
        total = residual(2 * p) + residual(2 * p + 1)
        for half in range(2):
            lanes = slice(128 * half, 128 * half + 128)
            pair[p - first, half] = total[:, lanes]
            even = pair[p - first, half, pl.ds(0, rows, stride=2), :]
            odd = pair[p - first, half, pl.ds(1, rows, stride=2), :]
            t[p - first, :, lanes] = even + odd
    count = len(planes)
    full = dot(t[...].reshape(count * rows, 256), pair_matrix(256, 128, 0.125))
    full = full.reshape(count, rows, 128)
    mask = row_mask((rows, 128), at[1] * 8 + 4 - rows // 2, ny // 2)
    for p in planes:
        b1[p] = wall(at, nx, 1, p, full[p - first] * mask)


def smooth_level1(at, nx, ny, b1, u, planes):
    rows = b1.ref.shape[1]
    mask = row_mask((rows, 128), at[1] * 8 + 4 - rows // 2, ny // 2)
    first_smooth(b1, u, planes, 4.0 * SIDE, mask, at, nx, 1)


def coarsen_level1(b1, u, b2_out, s1, t1):
    start = b1.ref.shape[1] // 2 - 4
    t1[...] = jnp.zeros_like(t1)
    for k in range(4):
        total = 0.0
        for p in (2 * k, 2 * k + 1):
            c, around = u.beside(p)
            total = total + (b1[p] - 0.25 * (6.0 * c - around))
        s1[k] = total
        t1[k, 0:4, :] = s1[k, pl.ds(start, 4, stride=2), :] + s1[k, pl.ds(start + 1, 4, stride=2), :]
    small = dot(t1[...].reshape(32, 128), pair_matrix(128, 128, 0.125)).reshape(4, 8, 128)
    tile = jnp.concatenate([small[0, 0:4], small[1, 0:4]], axis=0) + roll(
        jnp.concatenate([small[2, 0:4], small[3, 0:4]], axis=0), 64, 1
    )
    for k in range(b2_out.shape[0]):
        b2_out[k] = tile


def reach(extra):
    e0 = extra + 2
    r1 = -(-e0 // 2)
    e1 = r1 + 2
    r2 = -(-e1 // 2)
    e2 = r2 + 2
    r3 = -(-e2 // 2)
    return e0, r1, e1, r2, e2, r3


E0, R1, E1, R2, E2, R3 = reach(KEEP)
SHORT = 6


def first_source_body(nx, ny, at, mid, chip, link, b2_out, b, v, b1, u, pair, t, s1, t1):
    lower, upper = pick_sides(at, chip, link)
    b, v = Field(b, SHORT), Field(v, SHORT - 1)
    for p in range(-SHORT, 16 + SHORT):
        b.ref[p + SHORT, 0:8, :] = lower(p + HALO, slice(8, 16))
        b.ref[p + SHORT, 8:24, :] = mid[p + HALO]
        b.ref[p + SHORT, 24:32, :] = upper(p + HALO, slice(0, 8))
    mask = row_mask((32, 256), at[1] * 16 - 8, ny)
    first_smooth(b, v, range(1 - SHORT, 15 + SHORT), SIDE, mask, at, nx, 0)
    b1, u = Field(b1, 2), Field(u, 1)
    coarsen_level0(at, nx, ny, b, v, b1, range(-2, 10), pair, t)
    smooth_level1(at, nx, ny, b1, u, range(-1, 9))
    coarsen_level1(b1, u, b2_out, s1, t1)


def first_source(nx, ny, at, mid, chip, link):
    scratch = [
        around_block(16, SHORT, 32, 256),
        around_block(16, SHORT - 1, 32, 256),
        (12, 16, 128),
        (10, 16, 128),
        (12, 2, 32, 128),
        (12, 16, 256),
        (4, 16, 128),
        (4, 8, 128),
    ]
    args = [at, mid, chip, link]
    return call(functools.partial(first_source_body, nx, ny), [tiles(ny)], scratch, args, 6000000)[0]


def first_down_body(nx, ny, at, mid, chip, link, b_out, v_out, b1_out, u_out, b, v, pair, t):
    lower, upper = pick_sides(at, chip, link)
    for i in range(16 + 2 * HALO):
        b[i, 0:16, :] = lower(i)
        b[i, 16:32, :] = mid[i]
        b[i, 32:48, :] = upper(i)
    b, v = Field(b, HALO), Field(v, HALO - 1)
    mask = row_mask((48, 256), at[1] * 16 - 16, ny)
    first_smooth(b, v, range(1 - HALO, 15 + HALO), SIDE, mask, at, nx, 0)
    v_out, b_out = Field(v_out, E0), Field(b_out, E0 - 1)
    for p in range(-E0, 16 + E0):
        v_out[p] = v[p][8:40, :]
    for p in range(1 - E0, 15 + E0):
        b_out[p] = b[p][8:40, :]
    b1, u = Field(b1_out, E1 + 1), Field(u_out, E1)
    coarsen_level0(at, nx, ny, b, v, b1, range(-E1 - 1, 9 + E1), pair, t)
    smooth_level1(at, nx, ny, b1, u, range(-E1, 8 + E1))


def tiles(ny):
    return (GROUP * ny // 16, 8, 128)


def around_block(size, extra, rows, lanes):
    return (size + 2 * extra, rows, lanes)


def first_down(nx, ny, at, mid, chip, link):
    level1 = around_block(8, E1 + 1, 24, 128)
    outs = [
        around_block(16, E0 - 1, 32, 256),
        around_block(16, E0, 32, 256),
        level1,
        around_block(8, E1, 24, 128),
    ]
    scratch = [
        around_block(16, HALO, 48, 256),
        around_block(16, HALO - 1, 48, 256),
        (level1[0], 2, 48, 128),
        (level1[0], 24, 256),
    ]
    args = [at, mid, chip, link]
    return call(functools.partial(first_down_body, nx, ny), outs, scratch, args, 20000000)


def second_down_body(nx, ny, at, mid, chip, link, b1_out, u_out, b2_out, s1, t1):
    lower, upper = pick_sides(at, chip, link)
    for i in range(8 + 2 * NEAR):
        b1_out[i, 0:8, :] = lower(i)
        b1_out[i, 8:16, :] = mid[i]
        b1_out[i, 16:24, :] = upper(i)
    b1, u = Field(b1_out, NEAR), Field(u_out, NEAR - 1)
    smooth_level1(at, nx, ny, b1, u, range(1 - NEAR, 7 + NEAR))
    coarsen_level1(b1, u, b2_out, s1, t1)


def second_down(nx, ny, at, mid, chip, link):
    outs = [around_block(8, NEAR, 24, 128), around_block(8, NEAR - 1, 24, 128), tiles(ny)]
    scratch = [(4, 24, 128), (4, 8, 128)]
    args = [at, mid, chip, link]
    return call(functools.partial(second_down_body, nx, ny), outs, scratch, args, 2000000)


def solve_coarse(nx, ny, extra, at, coarse, s2, v2, w2, t3, b3, c3, d3, dup, row2):
    here, before, after = coarse
    _, _, _, r2, e2, r3 = reach(extra)
    spot = at[0] % GROUP
    rows2 = ny // 4
    rows3 = rows2 // 2
    count = rows2 // 4
    lead = 2 * (r3 + 3) + 2
    blocks = -(-lead // 4)
    s2, v2, w2 = Field(s2, 4 * blocks), Field(v2, lead - 1), Field(w2, e2)
    lane8 = iota((8, 128), 1) < 64
    for j in range(-blocks, blocks + 1):
        block = spot + GROUP + j
        layer, place = block // GROUP, block % GROUP
        for n in range(count):
            k = place * count + n
            tile = jnp.where(layer == 0, before[k], jnp.where(layer == 1, here[k], after[k]))
            halves = (jnp.where(lane8, tile, 0.0), jnp.where(lane8, roll(tile, 64, 1), 0.0))
            for p in range(4):
                part = halves[p // 2][4 * (p % 2) : 4 * (p % 2) + 4, :]
                s2.ref[4 * (j + blocks) + p, 4 * n : 4 * n + 4, :] = part

    def around(f, p):
        c = f[p]
        row = iota(c.shape, 0)
        lower = jnp.where(row == 0, 0.0, roll(c, 1, 0))
        upper = jnp.where(row == c.shape[0] - 1, 0.0, roll(c, -1, 0))
        beside = (lower + upper) + (roll(c, 1, 1) + roll(c, -1, 1))
        return c, (f[p - 1] + f[p + 1]) + beside

    def lanes_below(rows, lanes):
        return jnp.where(iota((rows, 128), 1) < lanes, 1.0, 0.0).astype(F32)

    mask2 = lanes_below(rows2, 64)
    for p in range(1 - lead, 3 + lead):
        c, near = around(s2, p)
        v2[p] = wall(at, nx, 2, p, (16.0 * SIDE) * mask2 * (1.2 * c + SIDE * near))

    def residual2(p):
        c, near = around(v2, p)
        return s2[p] - (1.0 / 16.0) * (6.0 * c - near)

    planes3 = range(-r3 - 3, 2 + r3 + 3)
    for i, p in enumerate(planes3):
        row2[i] = residual2(2 * p) + residual2(2 * p + 1)
        t3[i] = row2[i, pl.ds(0, rows3, stride=2), :] + row2[i, pl.ds(1, rows3, stride=2), :]
    total3 = len(planes3)
    full = dot(t3[...].reshape(total3 * rows3, 128), pair_matrix(128, 128, 0.125))
    full = full.reshape(total3, rows3, 128)
    mask3 = lanes_below(rows3, 32)
    b3, c3, d3 = Field(b3, r3 + 3), Field(c3, r3 + 3), Field(d3, r3 + 3)
    for i, p in enumerate(planes3):
        value = wall(at, nx, 3, p, full[i] * ((64.0 * SIDE) * mask3))
        b3[p] = value
    src, dst = b3, c3
    for step in (2, 1, 0):
        for p in range(-r3 - step, 2 + r3 + step):
            c, near = around(src, p)
            dst[p] = wall(at, nx, 3, p, mask3 * (0.2 * c + SIDE * near)) + b3[p]
        src, dst = dst, (d3 if dst is c3 else c3)
    final = src
    planes = range(-r3, 2 + r3)
    flat = jnp.concatenate([final[p] for p in planes], axis=0)
    spread = dot(flat, copy_matrix(128, 128)).reshape(len(planes), rows3, 128)
    for i, p in enumerate(planes):
        dup[i, pl.ds(0, rows3, stride=2), :] = spread[i]
        dup[i, pl.ds(1, rows3, stride=2), :] = spread[i]
        for q in (2 * p, 2 * p + 1):
            if -e2 <= q < 4 + e2:
                v2[q] = v2[q] + wall(at, nx, 2, q, dup[i, 0:rows2, :] * mask2)
    keep = SIDE * mask2
    for src, dst, step in ((v2, w2, 1), (w2, v2, 0)):
        for p in range(-r2 - step, 4 + r2 + step):
            c, near = around(src, p)
            dst[p] = 0.2 * c + wall(at, nx, 2, p, keep) * (near + 16.0 * s2[p])
    return v2


def coarse_scratch(ny, extra):
    _, _, _, _, e2, r3 = reach(extra)
    rows2 = ny // 4
    rows3 = rows2 // 2
    lead = 2 * (r3 + 3) + 2
    small = around_block(2, r3 + 3, rows3, 128)
    return [
        around_block(4, -(-lead // 4) * 4, rows2, 128),
        around_block(4, lead - 1, rows2, 128),
        around_block(4, e2, rows2, 128),
        small, small, small, small,
        (8, 48, 128),
        around_block(2, r3 + 3, rows2, 128),
    ]


def climb(nx, ny, extra, at, v2, b1, u, b, v_down, m1, n1, m0, n0, dup):
    e0, r1, e1, r2, _, _ = reach(extra)
    rows2 = ny // 4
    turn = lax.rem(rows2 + 4 - 4 * at[1] + rows2, rows2)
    planes = range(-r2, 4 + r2)
    picked = jnp.concatenate([pltpu.roll(v2[p], turn, 0)[0:16, :] for p in planes], axis=0)
    spread = dot(picked, copy_matrix(128, 128)).reshape(len(planes), 16, 128)
    mask1 = row_mask((24, 128), at[1] * 8 - 8, ny // 2)
    m1, n1 = Field(m1, e1), Field(n1, e1)
    for i, p in enumerate(planes):
        dup[i, 0, pl.ds(0, 12, stride=2), :] = spread[i, 0:12, :]
        dup[i, 0, pl.ds(1, 12, stride=2), :] = spread[i, 0:12, :]
        for q in (2 * p, 2 * p + 1):
            if -e1 <= q < 8 + e1:
                m1[q] = u[q] + wall(at, nx, 1, q, dup[i, 0, 0:24, :] * mask1)
    sweep(m1, n1, b1, range(1 - e1, 7 + e1), 4.0, mask1, at, nx, 1)
    sweep(n1, m1, b1, range(2 - e1, 6 + e1), 4.0, mask1, at, nx, 1)
    planes = range(-r1, 8 + r1)
    flat = jnp.concatenate([m1[p][4:20, :] for p in planes], axis=0)
    spread = dot(flat, copy_matrix(128, 256)).reshape(len(planes), 16, 256)
    mask0 = row_mask((32, 256), at[1] * 16 - 8, ny)
    m0, n0 = Field(m0, e0), Field(n0, e0)
    for i, p in enumerate(planes):
        for half in range(2):
            value = spread[i, :, 128 * half : 128 * half + 128]
            dup[i, half, pl.ds(0, 16, stride=2), :] = value
            dup[i, half, pl.ds(1, 16, stride=2), :] = value
        value = jnp.concatenate([dup[i, 0], dup[i, 1]], axis=1) * mask0
        for q in (2 * p, 2 * p + 1):
            if -e0 <= q < 16 + e0:
                m0[q] = v_down[q] + wall(at, nx, 0, q, value)
    sweep(m0, n0, b, range(1 - e0, 15 + e0), 1, mask0, at, nx, 0)
    if extra:
        sweep(n0, m0, b, range(2 - e0, 14 + e0), 1, mask0, at, nx, 0)
        return m0
    return n0


def climb_scratch(extra):
    e0, r1, e1, r2, _, _ = reach(extra)
    level1 = around_block(8, e1, 24, 128)
    level0 = around_block(16, e0, 32, 256)
    return [level1, level1, level0, level0, (max(8 + 2 * r1, 4 + 2 * r2), 2, 32, 128)]


def turn_body(nx, ny, at, here, before, after, b1, u, b, v_down, v_out, wider, low, high, own, pair, t, *scratch):
    v2 = solve_coarse(nx, ny, KEEP, at, (here, before, after), *scratch[:9])
    b = Field(b, E0 - 1)
    v = climb(nx, ny, KEEP, at, v2, Field(b1, E1 + 1), Field(u, E1), b, Field(v_down, E0), *scratch[9:])
    mask = row_mask((32, 256), at[1] * 16 - 8, ny)
    once, twice = Field(scratch[12], E0), Field(v_out, KEEP - 2)
    sweep(v, once, b, range(1 - KEEP, 15 + KEEP), 1, mask, at, nx, 0)
    sweep(once, twice, b, range(2 - KEEP, 14 + KEEP), 1, mask, at, nx, 0)
    coarsen_level0(at, nx, ny, b, twice, Field(own, 0), range(8), pair, t)
    for i in range(8):
        wider[NEAR + i] = own[i, 4:12, :]
    for i in range(NEAR):
        low[i] = own[i, 4:12, :]
        high[i] = own[8 - NEAR + i, 4:12, :]


def turn(nx, ny, at, coarse, b1, u, b, v_down):
    outs = [
        around_block(16, KEEP - 2, 32, 256),
        around_block(8, NEAR, 8, 128),
        (NEAR, 8, 128),
        (NEAR, 8, 128),
    ]
    scratch = [(8, 16, 128), (8, 2, 32, 128), (8, 16, 256)]
    scratch += coarse_scratch(ny, KEEP) + climb_scratch(KEEP)
    args = [at, *coarse, b1, u, b, v_down]
    return call(functools.partial(turn_body, nx, ny), outs, scratch, args, 30000000)


def finish_body(nx, ny, at, here, before, after, b1, u, b, v_down, out, *scratch):
    v2 = solve_coarse(nx, ny, 0, at, (here, before, after), *scratch[:9])
    b, v_down = Field(b, E0 - 1), Field(v_down, KEEP - 2)
    v = climb(nx, ny, 0, at, v2, Field(b1, NEAR), Field(u, NEAR - 1), b, v_down, *scratch[9:])
    for p in range(16):
        c, around = v.beside(p)
        out[p] = (0.2 * c + SIDE * (around + b[p]))[8:24, :]


def finish(nx, ny, at, coarse, b1, u, b, v_down):
    scratch = coarse_scratch(ny, 0) + climb_scratch(0)
    args = [at, *coarse, b1, u, b, v_down]
    return call(functools.partial(finish_body, nx, ny), [(16, 16, 256)], scratch, args, 20000000)[0]


def shifted(array, axis, step):
    count = lax.axis_size(axis)
    return lax.ppermute(
        array, axis, [(i, i + step) for i in range(count) if 0 <= i + step < count]
    )


def swapped(array, first):
    count = lax.axis_size("narrow")
    pairs = [(i, i + 1) for i in range(first, count - 1, 2)]
    return lax.ppermute(array, "narrow", pairs + [(j, i) for i, j in pairs])


def widen(wider, low, high):
    planes = low.shape[0]
    wider = lax.dynamic_update_slice(wider, shifted(high, "wide", 1), (0, 0, 0))
    upper = wider.shape[0] - planes
    return lax.dynamic_update_slice(wider, shifted(low, "wide", -1), (upper, 0, 0))


def surround(wider, low, high):
    mid = widen(wider, low, high)
    link = swapped(mid, 1)
    return mid, swapped(mid, 0), link


def spread_coarse(b2):
    wide, size = lax.axis_size("wide"), b2.shape[0]
    groups = [[g * size + k for k in range(size)] for g in range(wide // GROUP)]
    here = lax.all_to_all(b2, ("wide", "narrow"), 0, 0, axis_index_groups=groups)
    return here, shifted(here, "wide", GROUP), shifted(here, "wide", -GROUP)


def on_device(phase, distance, velocity):
    nx, ny = 16 * lax.axis_size("wide"), 16 * lax.axis_size("narrow")
    narrow = lax.axis_index("narrow")
    at = jnp.stack([lax.axis_index("wide"), narrow]).astype(jnp.int32)
    psi, x_low, x_high, chip, link = prepare(at, phase, distance, velocity)
    xl = shifted(x_high, "wide", 1)
    xh = shifted(x_low, "wide", -1)
    v_link = swapped(link, 1)
    v_chip = swapped(chip, 0)
    moved, *sends = transport(at, psi, velocity, xl, xh, v_chip, v_link)
    mid = widen(*sends)
    odd = lax.rem(narrow, 2) == 1
    first, final = mid[:, :3, :], mid[:, 13:, :]
    link = swapped(jnp.where(odd, final, first), 1)
    chip = swapped(jnp.where(odd, first, final), 0)
    sends = force(nx, ny, at, mid, chip, link, velocity, xl, xh, v_chip, v_link)
    parts = surround(*sends)
    coarse = spread_coarse(first_source(nx, ny, at, *parts))
    b, v, b1, u = first_down(nx, ny, at, *parts)
    v, *sends = turn(nx, ny, at, coarse, b1, u, b, v)
    b1, u, b2 = second_down(nx, ny, at, *surround(*sends))
    pressure = finish(nx, ny, at, spread_coarse(b2), b1, u, b, v)
    return (moved, pressure)


def solution(mesh):
    blocks = P("wide", "narrow", None)
    return jax.shard_map(
        on_device,
        mesh=mesh,
        in_specs=(blocks, blocks, P(None, "wide", "narrow", None)),
        out_specs=(blocks, blocks),
        check_vma=False,
    )
```

```python
import functools

import jax
import jax.numpy as jnp
from jax import lax
from jax.experimental import pallas as pl
from jax.experimental.pallas import tpu as pltpu
from jax.sharding import PartitionSpec as P

DELTA_SQ = 0.0025
WENO_EPS = 0.01
SIDE = 0.8 / 6.0
F32 = jnp.float32

HALO = 14
KEEP = 4
NEAR = 4
GROUP = 4


def iota(shape, dim):
    return lax.broadcasted_iota(jnp.int32, shape, dim)


def roll(v, shift, axis):
    return pltpu.roll(v, shift % v.shape[axis], axis)


def z_shifted(v):
    lane = iota(v.shape, 1)
    last = v.shape[1] - 1
    lower = jnp.where(lane == 0, 0.0, roll(v, 1, 1))
    upper = jnp.where(lane == last, 0.0, roll(v, -1, 1))
    return lower, upper


def z_pair(v):
    lower, upper = z_shifted(v)
    return lower + upper


def y_pair(v):
    return roll(v, 1, 0) + roll(v, -1, 0)


def beside(ref, i):
    c = ref[i]
    return c, (ref[i - 1] + ref[i + 1]) + y_pair(c) + z_pair(c)


def inside(first, count):
    return jnp.logical_and(first >= 0, first < count)


def row_mask(shape, first, count):
    rows = iota(shape, 0) + first
    return jnp.where(inside(rows, count), 1.0, 0.0).astype(F32)


def plane_factor(index, count):
    return jnp.where(inside(index, count), 1.0, 0.0).astype(F32)


def dot(a, b):
    b = b.astype(jnp.bfloat16)
    high = a.astype(jnp.bfloat16)
    low = (a - high.astype(F32)).astype(jnp.bfloat16)
    return jnp.dot(high, b, preferred_element_type=F32) + jnp.dot(low, b, preferred_element_type=F32)


def pair_matrix(rows, cols, value):
    return jnp.where((iota((rows, cols), 0) >> 1) == iota((rows, cols), 1), value, 0.0).astype(F32)


def copy_matrix(rows, cols):
    return jnp.where(iota((rows, cols), 0) == (iota((rows, cols), 1) >> 1), 1.0, 0.0).astype(F32)


def words(shape):
    *lead, rows, lanes = (1,) * (3 - len(shape)) + tuple(shape)
    size = -(-rows // 8) * 8 * (-(-lanes // 128) * 128)
    for n in lead:
        size *= n
    return size


def call(body, outs, scratch, args, flops):
    vmem = pl.BlockSpec(memory_space=pltpu.VMEM)
    smem = pl.BlockSpec(memory_space=pltpu.SMEM)
    total = sum(words(a.shape) for a in args) + sum(map(words, outs)) + sum(map(words, scratch))
    return pl.pallas_call(
        body,
        out_shape=[jax.ShapeDtypeStruct(s, F32) for s in outs],
        in_specs=[smem if a.dtype == jnp.int32 and a.ndim == 1 else vmem for a in args],
        out_specs=[vmem] * len(outs),
        scratch_shapes=[pltpu.VMEM(s, F32) for s in scratch],
        compiler_params=pltpu.CompilerParams(vmem_limit_bytes=4 * total + (6 << 20)),
        cost_estimate=pl.CostEstimate(flops=flops, bytes_accessed=4000000, transcendentals=0),
    )(*args)


def pick_sides(at, chip, link):
    odd = lax.rem(at[1], 2) == 1
    lower = lambda *k: jnp.where(odd, chip[k], link[k])
    upper = lambda *k: jnp.where(odd, link[k], chip[k])
    return lower, upper


def send_shapes(planes):
    return [(16 + 2 * planes, 16, 256), (planes, 16, 256), (planes, 16, 256)]


def send(block, wider, low, high, planes):
    for i in range(16):
        wider[planes + i] = block[i]
    for i in range(planes):
        low[i] = block[i]
        high[i] = block[16 - planes + i]


PARTS = 4


def prepare_body(at, phase, distance, velocity, psi, x_low, x_high, chip, link, kind, away, x_face, y_face, sems):
    odd = lax.rem(at[1], 2) == 1
    step = 16 // PARTS
    copies = []

    def copy(src, dst):
        started = pltpu.make_async_copy(src, dst, sems.at[len(copies)])
        started.start()
        copies.append(started)

    for k in range(PARTS):
        planes = pl.ds(step * k, step)
        copy(phase.at[planes], kind.at[planes])
        copy(distance.at[planes], away.at[planes])
    copy(velocity.at[0, 0], x_face.at[0])
    copy(velocity.at[0, 15], x_face.at[1])
    copy(velocity.at[1, :, pl.ds(0, 8), :], y_face.at[0])
    copy(velocity.at[1, :, pl.ds(8, 8), :], y_face.at[1])
    for k in range(PARTS):
        copies[2 * k].wait()
        copies[2 * k + 1].wait()
        for i in range(step * k, step * k + step):
            orient = 2.0 * kind[i].astype(F32) - 1.0
            psi[i] = 1.0 / (1.0 + jnp.exp(-orient * away[i]))
    for started in copies[2 * PARTS :]:
        started.wait()
    for i in range(16):
        first = jnp.concatenate([psi[i, 0:3, :], y_face[0, i, 0:1, :]], axis=0)
        final = jnp.concatenate([psi[i, 13:16, :], y_face[1, i, 7:8, :]], axis=0)
        chip[i] = jnp.where(odd, first, final)
        link[i] = jnp.where(odd, final, first)
    for k in range(3):
        x_low[k] = psi[k]
        x_high[k] = psi[13 + k]
    x_low[3] = x_face[0]
    x_high[3] = x_face[1]


def prepare(at, phase, distance, velocity):
    vmem = pl.BlockSpec(memory_space=pltpu.VMEM)
    smem = pl.BlockSpec(memory_space=pltpu.SMEM)
    hbm = pl.BlockSpec(memory_space=pltpu.HBM)
    outs = [(16, 16, 256), (4, 16, 256), (4, 16, 256), (16, 4, 256), (16, 4, 256)]
    return pl.pallas_call(
        prepare_body,
        out_shape=[jax.ShapeDtypeStruct(s, F32) for s in outs],
        in_specs=[smem, hbm, hbm, hbm],
        out_specs=[vmem] * len(outs),
        scratch_shapes=[
            pltpu.VMEM((16, 16, 256), jnp.int32),
            pltpu.VMEM((16, 16, 256), F32),
            pltpu.VMEM((2, 16, 256), F32),
            pltpu.VMEM((2, 16, 8, 256), F32),
            pltpu.SemaphoreType.DMA((2 * PARTS + 4,)),
        ],
        compiler_params=pltpu.CompilerParams(vmem_limit_bytes=8 << 20),
        cost_estimate=pl.CostEstimate(flops=1000000, bytes_accessed=1000000, transcendentals=0),
    )(at, *(pltpu.with_memory_space_constraint(a, pltpu.HBM) for a in (phase, distance, velocity)))


def indicators(a, b, c):
    d = a - c
    curve = (a + c) - 2.0 * b
    twice = 2.0 * curve
    base = (13.0 / 12.0) * (curve * curve) + WENO_EPS
    up, down = twice - d, twice + d
    p = base + 0.25 * (up * up)
    q = base + 0.25 * (d * d)
    r = base + 0.25 * (down * down)
    return p * p, q * q, r * r


def upwind_flux(s, l, p_left, q_left, r_left, p_right, q_right, r_right):
    ahead = s > 0.0
    pick = lambda x, y: jnp.where(ahead, x, y)
    a, b, c, e, f = pick(l[0], l[5]), pick(l[1], l[4]), pick(l[2], l[3]), pick(l[3], l[2]), pick(l[4], l[1])
    p, q, r = pick(p_left, r_right), pick(q_left, q_right), pick(r_left, p_right)
    w0, w1, w2 = 0.1 * (q * r), 0.6 * (p * r), 0.3 * (p * q)
    g0 = 2.0 * a - 7.0 * b + 11.0 * c
    g1 = 5.0 * c + 2.0 * e - b
    g2 = 2.0 * c + 5.0 * e - f
    top = w0 * g0 + w1 * g1 + w2 * g2
    return (s * top) / (6.0 * (w0 + w1 + w2))


def transport_body(at, psi, velocity, xl, xh, chip, link, moved, wider, low, high, ext, p_x, q_x, r_x, rows, speed):
    lower, upper = pick_sides(at, chip, link)
    for k in range(3):
        ext[k] = xl[k]
        ext[19 + k] = xh[k]

    def fill(i, carry):
        ext[3 + i] = psi[i]
        return carry

    lax.fori_loop(0, 16, fill, 0, unroll=True)

    def marks(i, carry):
        p, q, r = indicators(ext[i], ext[i + 1], ext[i + 2])
        p_x[i], q_x[i], r_x[i] = p, q, r
        return carry

    lax.fori_loop(0, 20, marks, 0, unroll=True)

    def x_flux(j, v_low, v_high):
        s = 0.5 * (v_low + v_high)
        l = [ext[j + k] for k in range(6)]
        return upwind_flux(
            s, l, p_x[j], q_x[j + 1], r_x[j + 2], p_x[j + 1], q_x[j + 2], r_x[j + 3]
        )

    def plane(i, below):
        here = velocity[0, i]
        following = jnp.where(i == 15, xh[3], velocity[0, jnp.minimum(i + 1, 15)])
        above = x_flux(i + 1, here, following)
        change = above - below
        y_low, y_high = lower(i), upper(i)
        rows[1:4, :] = y_low[0:3, :]
        rows[4:20, :] = psi[i]
        rows[20:23, :] = y_high[0:3, :]
        speed[3:4, :] = y_low[3:4, :]
        speed[4:20, :] = velocity[1, i]
        speed[20:21, :] = y_high[3:4, :]
        v = rows[...]
        u = speed[...]
        s = 0.5 * (u + roll(u, -1, 0))
        l = [roll(v, 2 - k, 0) for k in range(6)]
        p, q, r = indicators(l[1], l[2], l[3])
        q_next, r_next = roll(q, -1, 0), roll(r, -1, 0)
        flux = upwind_flux(s, l, roll(p, 1, 0), q, r_next, p, q_next, roll(r, -2, 0))
        rows_change = flux - roll(flux, 1, 0)
        change = change + rows_change[4:20, :]
        v = psi[i]
        w = velocity[2, i]
        lane = iota(v.shape, 1)

        def ahead(x, k):
            return jnp.where(lane > 255 - k, 0.0, roll(x, -k, 1))

        def behind(x, k):
            return jnp.where(lane < k, 0.0, roll(x, k, 1))

        l = [behind(v, 2), behind(v, 1), v, ahead(v, 1), ahead(v, 2), ahead(v, 3)]
        s = 0.5 * (w + ahead(w, 1))
        p, q, r = indicators(l[1], l[2], l[3])
        _, q1, r1 = indicators(l[2], l[3], l[4])
        _, _, r2 = indicators(l[3], l[4], l[5])
        p0, _, _ = indicators(l[0], l[1], l[2])
        flux = upwind_flux(s, l, p0, q, r1, p, q1, r2)
        low = slice(0, 128)
        c = v[:, low]
        none = jnp.zeros_like(c)
        square = c * c
        edge = WENO_EPS + (13.0 / 12.0 + 9.0 / 4.0) * square
        level = WENO_EPS + (13.0 / 12.0 + 1.0 / 4.0) * square
        wall = upwind_flux(
            0.5 * w[:, low],
            [none, none, none, c, l[3][:, low], l[4][:, low]],
            none + WENO_EPS * WENO_EPS, level * level, r[:, low],
            edge * edge, q[:, low], r1[:, low],
        )
        wall = jnp.concatenate([wall, wall], axis=1)
        change = change + (flux - jnp.where(lane == 0, wall, roll(flux, 1, 1)))
        moved[i] = v - 0.25 * change
        return above

    rows[...] = jnp.zeros_like(rows)
    speed[...] = jnp.zeros_like(speed)
    lax.fori_loop(0, 16, plane, x_flux(0, xl[3], velocity[0, 0]), unroll=True)
    send(moved, wider, low, high, 3)


def transport(at, psi, velocity, xl, xh, chip, link):
    planes = (20, 16, 256)
    scratch = [(22, 16, 256), planes, planes, planes, (24, 256), (24, 256)]
    outs = [(16, 16, 256)] + send_shapes(3)
    return call(transport_body, outs, scratch, [at, psi, velocity, xl, xh, chip, link], 10000000)


def force_body(nx, ny, at, mid, chip, link, velocity, xl, xh, v_chip, v_link, wider, low, high, m, n_x, n_y, n_z, s_x, part, pad, source):
    lower, upper = pick_sides(at, chip, link)
    v_lower, v_upper = pick_sides(at, v_chip, v_link)
    x0, y0 = at[0] * 16, at[1] * 16
    shape = (32, 256)
    lane = iota(shape, 1)

    def fill(i, carry):
        m[i] = jnp.zeros(shape, F32)
        m[i, 5:8, :] = lower(i)
        m[i, 8:24, :] = mid[i]
        m[i, 24:27, :] = upper(i)
        return carry

    lax.fori_loop(0, 22, fill, 0, unroll=True)

    def gradient(i):
        c = m[i]
        below, above = z_shifted(c)
        gx = 0.5 * (m[i + 1] - m[i - 1])
        gy = 0.5 * (roll(c, -1, 0) - roll(c, 1, 0))
        return gx, gy, 0.5 * (above - below)

    def normals(i, carry):
        gx, gy, gz = gradient(i + 1)
        inverse = lax.rsqrt(gx * gx + gy * gy + gz * gz + DELTA_SQ)
        n_x[i], n_y[i], n_z[i] = gx * inverse, gy * inverse, gz * inverse
        return carry

    lax.fori_loop(0, 20, normals, 0, unroll=True)
    mask_y = row_mask(shape, y0 - 8, ny)

    def stars(i, carry):
        gx, gy, gz = gradient(i + 2)
        c = m[i + 2]
        edge = 0.5 * c
        edge = edge * lax.rsqrt(edge * edge + DELTA_SQ)
        nz = n_z[i + 1]
        above = jnp.where(lane == 255, -edge, roll(nz, -1, 1))
        below = jnp.where(lane == 0, edge, roll(nz, 1, 1))
        nn = n_y[i + 1]
        bending = -0.5 * (
            (n_x[i + 2] - n_x[i]) + (roll(nn, -1, 0) - roll(nn, 1, 0)) + (above - below)
        )
        keep = mask_y * plane_factor(x0 + i - 1, nx)
        bending = bending * keep
        fx, fy, fz = bending * gx, bending * gy, bending * gz
        k = jnp.clip(i - 1, 0, 15)
        vx = jnp.where(i == 0, xl[3], jnp.where(i == 17, xh[3], velocity[0, k]))
        s_x[i] = fx[8:24, :] + vx
        pad[7:8, :] = v_lower(k)[3:4, :]
        pad[8:24, :] = velocity[1, k]
        pad[24:25, :] = v_upper(k)[3:4, :]
        sy = fy + pad[...]
        dy = roll(sy, -1, 0) - roll(sy, 1, 0)
        sz = fz[8:24, :] + velocity[2, k]
        below, above = z_shifted(sz)
        part[i] = dy[8:24, :] + (above - below)
        return carry

    pad[...] = jnp.zeros_like(pad)
    lax.fori_loop(0, 18, stars, 0, unroll=True)

    def finish(i, carry):
        source[i] = -0.5 * (part[i + 1] + (s_x[i + 2] - s_x[i]))
        return carry

    lax.fori_loop(0, 16, finish, 0, unroll=True)
    send(source, wider, low, high, HALO)


def force(nx, ny, at, mid, chip, link, velocity, xl, xh, v_chip, v_link):
    n = (20, 32, 256)
    scratch = [(22, 32, 256), n, n, n, (18, 16, 256), (18, 16, 256), (32, 256), (16, 16, 256)]
    args = [at, mid, chip, link, velocity, xl, xh, v_chip, v_link]
    return call(functools.partial(force_body, nx, ny), send_shapes(HALO), scratch, args, 10000000)


class Field:
    def __init__(self, ref, lead):
        self.ref, self.lead = ref, lead

    def __getitem__(self, p):
        return self.ref[p + self.lead]

    def __setitem__(self, p, value):
        self.ref[p + self.lead] = value

    def beside(self, p):
        return beside(self.ref, p + self.lead)


def wall(at, nx, level, p, value):
    own = 16 >> level
    if 0 <= p < own:
        return value
    return value * plane_factor(at[0] * own + p, nx >> level)


def first_smooth(b, v, planes, weight, mask, at, nx, level):
    for p in planes:
        c, around = b.beside(p)
        v[p] = wall(at, nx, level, p, (weight * mask) * (1.2 * c + SIDE * around))


def sweep(src, dst, b, planes, factor, mask, at, nx, level):
    keep = SIDE * mask
    for p in planes:
        c, around = src.beside(p)
        near = around + (b[p] if factor == 1 else factor * b[p])
        dst[p] = 0.2 * c + wall(at, nx, level, p, keep) * near


def coarsen_level0(at, nx, ny, b, v, b1, planes, pair, t):
    first = planes[0]
    rows = t.shape[1]

    def residual(p):
        c, around = v.beside(p)
        return b[p] - (6.0 * c - around)

    for p in planes:
        total = residual(2 * p) + residual(2 * p + 1)
        for half in range(2):
            lanes = slice(128 * half, 128 * half + 128)
            pair[p - first, half] = total[:, lanes]
            even = pair[p - first, half, pl.ds(0, rows, stride=2), :]
            odd = pair[p - first, half, pl.ds(1, rows, stride=2), :]
            t[p - first, :, lanes] = even + odd
    count = len(planes)
    full = dot(t[...].reshape(count * rows, 256), pair_matrix(256, 128, 0.125))
    full = full.reshape(count, rows, 128)
    mask = row_mask((rows, 128), at[1] * 8 + 4 - rows // 2, ny // 2)
    for p in planes:
        b1[p] = wall(at, nx, 1, p, full[p - first] * mask)


def smooth_level1(at, nx, ny, b1, u, planes):
    rows = b1.ref.shape[1]
    mask = row_mask((rows, 128), at[1] * 8 + 4 - rows // 2, ny // 2)
    first_smooth(b1, u, planes, 4.0 * SIDE, mask, at, nx, 1)


def coarsen_level1(b1, u, b2_out, s1, t1):
    start = b1.ref.shape[1] // 2 - 4
    t1[...] = jnp.zeros_like(t1)
    for k in range(4):
        total = 0.0
        for p in (2 * k, 2 * k + 1):
            c, around = u.beside(p)
            total = total + (b1[p] - 0.25 * (6.0 * c - around))
        s1[k] = total
        t1[k, 0:4, :] = s1[k, pl.ds(start, 4, stride=2), :] + s1[k, pl.ds(start + 1, 4, stride=2), :]
    small = dot(t1[...].reshape(32, 128), pair_matrix(128, 128, 0.125)).reshape(4, 8, 128)
    tile = jnp.concatenate([small[0, 0:4], small[1, 0:4]], axis=0) + roll(
        jnp.concatenate([small[2, 0:4], small[3, 0:4]], axis=0), 64, 1
    )
    for k in range(b2_out.shape[0]):
        b2_out[k] = tile


def reach(extra):
    e0 = extra + 2
    r1 = -(-e0 // 2)
    e1 = r1 + 2
    r2 = -(-e1 // 2)
    e2 = r2 + 2
    r3 = -(-e2 // 2)
    return e0, r1, e1, r2, e2, r3


E0, R1, E1, R2, E2, R3 = reach(KEEP)
SHORT = 6


def first_source_body(nx, ny, at, mid, chip, link, b2_out, b, v, b1, u, pair, t, s1, t1):
    lower, upper = pick_sides(at, chip, link)
    b, v = Field(b, SHORT), Field(v, SHORT - 1)
    for p in range(-SHORT, 16 + SHORT):
        b.ref[p + SHORT, 0:8, :] = lower(p + HALO, slice(8, 16))
        b.ref[p + SHORT, 8:24, :] = mid[p + HALO]
        b.ref[p + SHORT, 24:32, :] = upper(p + HALO, slice(0, 8))
    mask = row_mask((32, 256), at[1] * 16 - 8, ny)
    first_smooth(b, v, range(1 - SHORT, 15 + SHORT), SIDE, mask, at, nx, 0)
    b1, u = Field(b1, 2), Field(u, 1)
    coarsen_level0(at, nx, ny, b, v, b1, range(-2, 10), pair, t)
    smooth_level1(at, nx, ny, b1, u, range(-1, 9))
    coarsen_level1(b1, u, b2_out, s1, t1)


def first_source(nx, ny, at, mid, chip, link):
    scratch = [
        around_block(16, SHORT, 32, 256),
        around_block(16, SHORT - 1, 32, 256),
        (12, 16, 128),
        (10, 16, 128),
        (12, 2, 32, 128),
        (12, 16, 256),
        (4, 16, 128),
        (4, 8, 128),
    ]
    args = [at, mid, chip, link]
    return call(functools.partial(first_source_body, nx, ny), [tiles(ny)], scratch, args, 6000000)[0]


def first_down_body(nx, ny, at, mid, chip, link, b_out, v_out, b1_out, u_out, b, v, pair, t):
    lower, upper = pick_sides(at, chip, link)
    for i in range(16 + 2 * HALO):
        b[i, 0:16, :] = lower(i)
        b[i, 16:32, :] = mid[i]
        b[i, 32:48, :] = upper(i)
    b, v = Field(b, HALO), Field(v, HALO - 1)
    mask = row_mask((48, 256), at[1] * 16 - 16, ny)
    first_smooth(b, v, range(1 - HALO, 15 + HALO), SIDE, mask, at, nx, 0)
    v_out, b_out = Field(v_out, E0), Field(b_out, E0 - 1)
    for p in range(-E0, 16 + E0):
        v_out[p] = v[p][8:40, :]
    for p in range(1 - E0, 15 + E0):
        b_out[p] = b[p][8:40, :]
    b1, u = Field(b1_out, E1 + 1), Field(u_out, E1)
    coarsen_level0(at, nx, ny, b, v, b1, range(-E1 - 1, 9 + E1), pair, t)
    smooth_level1(at, nx, ny, b1, u, range(-E1, 8 + E1))


def tiles(ny):
    return (GROUP * ny // 16, 8, 128)


def around_block(size, extra, rows, lanes):
    return (size + 2 * extra, rows, lanes)


def first_down(nx, ny, at, mid, chip, link):
    level1 = around_block(8, E1 + 1, 24, 128)
    outs = [
        around_block(16, E0 - 1, 32, 256),
        around_block(16, E0, 32, 256),
        level1,
        around_block(8, E1, 24, 128),
    ]
    scratch = [
        around_block(16, HALO, 48, 256),
        around_block(16, HALO - 1, 48, 256),
        (level1[0], 2, 48, 128),
        (level1[0], 24, 256),
    ]
    args = [at, mid, chip, link]
    return call(functools.partial(first_down_body, nx, ny), outs, scratch, args, 20000000)


def second_down_body(nx, ny, at, mid, chip, link, b1_out, u_out, b2_out, s1, t1):
    lower, upper = pick_sides(at, chip, link)
    for i in range(8 + 2 * NEAR):
        b1_out[i, 0:8, :] = lower(i)
        b1_out[i, 8:16, :] = mid[i]
        b1_out[i, 16:24, :] = upper(i)
    b1, u = Field(b1_out, NEAR), Field(u_out, NEAR - 1)
    smooth_level1(at, nx, ny, b1, u, range(1 - NEAR, 7 + NEAR))
    coarsen_level1(b1, u, b2_out, s1, t1)


def second_down(nx, ny, at, mid, chip, link):
    outs = [around_block(8, NEAR, 24, 128), around_block(8, NEAR - 1, 24, 128), tiles(ny)]
    scratch = [(4, 24, 128), (4, 8, 128)]
    args = [at, mid, chip, link]
    return call(functools.partial(second_down_body, nx, ny), outs, scratch, args, 2000000)


def solve_coarse(nx, ny, extra, at, coarse, s2, v2, w2, t3, b3, c3, d3, dup, row2):
    here, fetched, other = coarse
    odd = lax.rem(at[1], 2) == 1
    _, _, _, r2, e2, r3 = reach(extra)
    spot = at[0] % GROUP
    rows2 = ny // 4
    rows3 = rows2 // 2
    count = rows2 // 4
    lead = 2 * (r3 + 3) + 2
    blocks = -(-lead // 4)
    s2, v2, w2 = Field(s2, 4 * blocks), Field(v2, lead - 1), Field(w2, e2)
    lane8 = iota((8, 128), 1) < 64
    for j in range(-blocks, blocks + 1):
        block = spot + GROUP + j
        layer, place = block // GROUP, block % GROUP
        for n in range(count):
            k = place * count + n
            tile = jnp.where(
                layer == 1, here[k], jnp.where((layer == 2) == odd, fetched[k], other[k])
            )
            halves = (jnp.where(lane8, tile, 0.0), jnp.where(lane8, roll(tile, 64, 1), 0.0))
            for p in range(4):
                part = halves[p // 2][4 * (p % 2) : 4 * (p % 2) + 4, :]
                s2.ref[4 * (j + blocks) + p, 4 * n : 4 * n + 4, :] = part

    def around(f, p):
        c = f[p]
        row = iota(c.shape, 0)
        lower = jnp.where(row == 0, 0.0, roll(c, 1, 0))
        upper = jnp.where(row == c.shape[0] - 1, 0.0, roll(c, -1, 0))
        beside = (lower + upper) + (roll(c, 1, 1) + roll(c, -1, 1))
        return c, (f[p - 1] + f[p + 1]) + beside

    def lanes_below(rows, lanes):
        return jnp.where(iota((rows, 128), 1) < lanes, 1.0, 0.0).astype(F32)

    mask2 = lanes_below(rows2, 64)
    for p in range(1 - lead, 3 + lead):
        c, near = around(s2, p)
        v2[p] = wall(at, nx, 2, p, (16.0 * SIDE) * mask2 * (1.2 * c + SIDE * near))

    def residual2(p):
        c, near = around(v2, p)
        return s2[p] - (1.0 / 16.0) * (6.0 * c - near)

    planes3 = range(-r3 - 3, 2 + r3 + 3)
    for i, p in enumerate(planes3):
        row2[i] = residual2(2 * p) + residual2(2 * p + 1)
        t3[i] = row2[i, pl.ds(0, rows3, stride=2), :] + row2[i, pl.ds(1, rows3, stride=2), :]
    total3 = len(planes3)
    full = dot(t3[...].reshape(total3 * rows3, 128), pair_matrix(128, 128, 0.125))
    full = full.reshape(total3, rows3, 128)
    mask3 = lanes_below(rows3, 32)
    b3, c3, d3 = Field(b3, r3 + 3), Field(c3, r3 + 3), Field(d3, r3 + 3)
    for i, p in enumerate(planes3):
        value = wall(at, nx, 3, p, full[i] * ((64.0 * SIDE) * mask3))
        b3[p] = value
    src, dst = b3, c3
    for step in (2, 1, 0):
        for p in range(-r3 - step, 2 + r3 + step):
            c, near = around(src, p)
            dst[p] = wall(at, nx, 3, p, mask3 * (0.2 * c + SIDE * near)) + b3[p]
        src, dst = dst, (d3 if dst is c3 else c3)
    final = src
    planes = range(-r3, 2 + r3)
    flat = jnp.concatenate([final[p] for p in planes], axis=0)
    spread = dot(flat, copy_matrix(128, 128)).reshape(len(planes), rows3, 128)
    for i, p in enumerate(planes):
        dup[i, pl.ds(0, rows3, stride=2), :] = spread[i]
        dup[i, pl.ds(1, rows3, stride=2), :] = spread[i]
        for q in (2 * p, 2 * p + 1):
            if -e2 <= q < 4 + e2:
                v2[q] = v2[q] + wall(at, nx, 2, q, dup[i, 0:rows2, :] * mask2)
    keep = SIDE * mask2
    for src, dst, step in ((v2, w2, 1), (w2, v2, 0)):
        for p in range(-r2 - step, 4 + r2 + step):
            c, near = around(src, p)
            dst[p] = 0.2 * c + wall(at, nx, 2, p, keep) * (near + 16.0 * s2[p])
    return v2


def coarse_scratch(ny, extra):
    _, _, _, _, e2, r3 = reach(extra)
    rows2 = ny // 4
    rows3 = rows2 // 2
    lead = 2 * (r3 + 3) + 2
    small = around_block(2, r3 + 3, rows3, 128)
    return [
        around_block(4, -(-lead // 4) * 4, rows2, 128),
        around_block(4, lead - 1, rows2, 128),
        around_block(4, e2, rows2, 128),
        small, small, small, small,
        (8, 48, 128),
        around_block(2, r3 + 3, rows2, 128),
    ]


def climb(nx, ny, extra, at, v2, b1, u, b, v_down, m1, n1, m0, n0, dup):
    e0, r1, e1, r2, _, _ = reach(extra)
    rows2 = ny // 4
    turn = lax.rem(rows2 + 4 - 4 * at[1] + rows2, rows2)
    planes = range(-r2, 4 + r2)
    picked = jnp.concatenate([pltpu.roll(v2[p], turn, 0)[0:16, :] for p in planes], axis=0)
    spread = dot(picked, copy_matrix(128, 128)).reshape(len(planes), 16, 128)
    mask1 = row_mask((24, 128), at[1] * 8 - 8, ny // 2)
    m1, n1 = Field(m1, e1), Field(n1, e1)
    for i, p in enumerate(planes):
        dup[i, 0, pl.ds(0, 12, stride=2), :] = spread[i, 0:12, :]
        dup[i, 0, pl.ds(1, 12, stride=2), :] = spread[i, 0:12, :]
        for q in (2 * p, 2 * p + 1):
            if -e1 <= q < 8 + e1:
                m1[q] = u[q] + wall(at, nx, 1, q, dup[i, 0, 0:24, :] * mask1)
    sweep(m1, n1, b1, range(1 - e1, 7 + e1), 4.0, mask1, at, nx, 1)
    sweep(n1, m1, b1, range(2 - e1, 6 + e1), 4.0, mask1, at, nx, 1)
    planes = range(-r1, 8 + r1)
    flat = jnp.concatenate([m1[p][4:20, :] for p in planes], axis=0)
    spread = dot(flat, copy_matrix(128, 256)).reshape(len(planes), 16, 256)
    mask0 = row_mask((32, 256), at[1] * 16 - 8, ny)
    m0, n0 = Field(m0, e0), Field(n0, e0)
    for i, p in enumerate(planes):
        for half in range(2):
            value = spread[i, :, 128 * half : 128 * half + 128]
            dup[i, half, pl.ds(0, 16, stride=2), :] = value
            dup[i, half, pl.ds(1, 16, stride=2), :] = value
        value = jnp.concatenate([dup[i, 0], dup[i, 1]], axis=1) * mask0
        for q in (2 * p, 2 * p + 1):
            if -e0 <= q < 16 + e0:
                m0[q] = v_down[q] + wall(at, nx, 0, q, value)
    sweep(m0, n0, b, range(1 - e0, 15 + e0), 1, mask0, at, nx, 0)
    if extra:
        sweep(n0, m0, b, range(2 - e0, 14 + e0), 1, mask0, at, nx, 0)
        return m0
    return n0


def climb_scratch(extra):
    e0, r1, e1, r2, _, _ = reach(extra)
    level1 = around_block(8, e1, 24, 128)
    level0 = around_block(16, e0, 32, 256)
    return [level1, level1, level0, level0, (max(8 + 2 * r1, 4 + 2 * r2), 2, 32, 128)]


def turn_body(nx, ny, at, here, fetched, other, b1, u, b, v_down, v_out, wider, low, high, own, pair, t, *scratch):
    v2 = solve_coarse(nx, ny, KEEP, at, (here, fetched, other), *scratch[:9])
    b = Field(b, E0 - 1)
    v = climb(nx, ny, KEEP, at, v2, Field(b1, E1 + 1), Field(u, E1), b, Field(v_down, E0), *scratch[9:])
    mask = row_mask((32, 256), at[1] * 16 - 8, ny)
    once, twice = Field(scratch[12], E0), Field(v_out, KEEP - 2)
    sweep(v, once, b, range(1 - KEEP, 15 + KEEP), 1, mask, at, nx, 0)
    sweep(once, twice, b, range(2 - KEEP, 14 + KEEP), 1, mask, at, nx, 0)
    coarsen_level0(at, nx, ny, b, twice, Field(own, 0), range(8), pair, t)
    for i in range(8):
        wider[NEAR + i] = own[i, 4:12, :]
    for i in range(NEAR):
        low[i] = own[i, 4:12, :]
        high[i] = own[8 - NEAR + i, 4:12, :]


def turn(nx, ny, at, coarse, b1, u, b, v_down):
    outs = [
        around_block(16, KEEP - 2, 32, 256),
        around_block(8, NEAR, 8, 128),
        (NEAR, 8, 128),
        (NEAR, 8, 128),
    ]
    scratch = [(8, 16, 128), (8, 2, 32, 128), (8, 16, 256)]
    scratch += coarse_scratch(ny, KEEP) + climb_scratch(KEEP)
    args = [at, *coarse, b1, u, b, v_down]
    return call(functools.partial(turn_body, nx, ny), outs, scratch, args, 30000000)


def finish_body(nx, ny, at, here, fetched, other, b1, u, b, v_down, out, *scratch):
    v2 = solve_coarse(nx, ny, 0, at, (here, fetched, other), *scratch[:9])
    b, v_down = Field(b, E0 - 1), Field(v_down, KEEP - 2)
    v = climb(nx, ny, 0, at, v2, Field(b1, NEAR), Field(u, NEAR - 1), b, v_down, *scratch[9:])
    for p in range(16):
        c, around = v.beside(p)
        out[p] = (0.2 * c + SIDE * (around + b[p]))[8:24, :]


def finish(nx, ny, at, coarse, b1, u, b, v_down):
    scratch = coarse_scratch(ny, 0) + climb_scratch(0)
    args = [at, *coarse, b1, u, b, v_down]
    return call(functools.partial(finish_body, nx, ny), [(16, 16, 256)], scratch, args, 20000000)[0]


def shifted(array, axis, step):
    count = lax.axis_size(axis)
    return lax.ppermute(
        array, axis, [(i, i + step) for i in range(count) if 0 <= i + step < count]
    )


def swapped(array, first):
    count = lax.axis_size("narrow")
    pairs = [(i, i + 1) for i in range(first, count - 1, 2)]
    return lax.ppermute(array, "narrow", pairs + [(j, i) for i, j in pairs])


def widen(wider, low, high):
    planes = low.shape[0]
    wider = lax.dynamic_update_slice(wider, shifted(high, "wide", 1), (0, 0, 0))
    upper = wider.shape[0] - planes
    return lax.dynamic_update_slice(wider, shifted(low, "wide", -1), (upper, 0, 0))


def surround(wider, low, high):
    mid = widen(wider, low, high)
    link = swapped(mid, 1)
    return mid, swapped(mid, 0), link


def spread_coarse(b2):
    wide, size = lax.axis_size("wide"), b2.shape[0]
    groups = [[g * size + k for k in range(size)] for g in range(wide // GROUP)]
    here = lax.all_to_all(b2, ("wide", "narrow"), 0, 0, axis_index_groups=groups)
    cores, pairs = lax.axis_size("narrow"), []
    for i in range(wide):
        for j in range(cores):
            k = i + (GROUP if j % 2 == 0 else -GROUP)
            if 0 <= k < wide:
                pairs.append((i * cores + j, k * cores + j))
    fetched = lax.ppermute(here, ("wide", "narrow"), pairs)
    return here, fetched, swapped(fetched, 0)


def on_device(phase, distance, velocity):
    nx, ny = 16 * lax.axis_size("wide"), 16 * lax.axis_size("narrow")
    narrow = lax.axis_index("narrow")
    at = jnp.stack([lax.axis_index("wide"), narrow]).astype(jnp.int32)
    psi, x_low, x_high, chip, link = prepare(at, phase, distance, velocity)
    xl = shifted(x_high, "wide", 1)
    xh = shifted(x_low, "wide", -1)
    v_link = swapped(link, 1)
    v_chip = swapped(chip, 0)
    moved, *sends = transport(at, psi, velocity, xl, xh, v_chip, v_link)
    mid = widen(*sends)
    odd = lax.rem(narrow, 2) == 1
    first, final = mid[:, :3, :], mid[:, 13:, :]
    link = swapped(jnp.where(odd, final, first), 1)
    chip = swapped(jnp.where(odd, first, final), 0)
    sends = force(nx, ny, at, mid, chip, link, velocity, xl, xh, v_chip, v_link)
    parts = surround(*sends)
    coarse = spread_coarse(first_source(nx, ny, at, *parts))
    b, v, b1, u = first_down(nx, ny, at, *parts)
    v, *sends = turn(nx, ny, at, coarse, b1, u, b, v)
    b1, u, b2 = second_down(nx, ny, at, *surround(*sends))
    pressure = finish(nx, ny, at, spread_coarse(b2), b1, u, b, v)
    return (moved, pressure)


def solution(mesh):
    blocks = P("wide", "narrow", None)
    return jax.shard_map(
        on_device,
        mesh=mesh,
        in_specs=(blocks, blocks, P(None, "wide", "narrow", None)),
        out_specs=(blocks, blocks),
        check_vma=False,
    )
```

```python
import functools

import jax
import jax.numpy as jnp
from jax import lax
from jax.experimental import pallas as pl
from jax.experimental.pallas import tpu as pltpu
from jax.sharding import PartitionSpec as P

DELTA_SQ = 0.0025
WENO_EPS = 0.01
SIDE = 0.8 / 6.0
F32 = jnp.float32

HALO = 14
KEEP = 4
NEAR = 4
GROUP = 4


def iota(shape, dim):
    return lax.broadcasted_iota(jnp.int32, shape, dim)


def roll(v, shift, axis):
    return pltpu.roll(v, shift % v.shape[axis], axis)


def z_shifted(v):
    lane = iota(v.shape, 1)
    last = v.shape[1] - 1
    lower = jnp.where(lane == 0, 0.0, roll(v, 1, 1))
    upper = jnp.where(lane == last, 0.0, roll(v, -1, 1))
    return lower, upper


def z_pair(v):
    lower, upper = z_shifted(v)
    return lower + upper


def y_pair(v):
    return roll(v, 1, 0) + roll(v, -1, 0)


def beside(ref, i):
    c = ref[i]
    return c, (ref[i - 1] + ref[i + 1]) + y_pair(c) + z_pair(c)


def inside(first, count):
    return jnp.logical_and(first >= 0, first < count)


def row_mask(shape, first, count):
    rows = iota(shape, 0) + first
    return jnp.where(inside(rows, count), 1.0, 0.0).astype(F32)


def plane_factor(index, count):
    return jnp.where(inside(index, count), 1.0, 0.0).astype(F32)


def dot(a, b):
    b = b.astype(jnp.bfloat16)
    high = a.astype(jnp.bfloat16)
    low = (a - high.astype(F32)).astype(jnp.bfloat16)
    return jnp.dot(high, b, preferred_element_type=F32) + jnp.dot(low, b, preferred_element_type=F32)


def pair_matrix(rows, cols, value):
    return jnp.where((iota((rows, cols), 0) >> 1) == iota((rows, cols), 1), value, 0.0).astype(F32)


def copy_matrix(rows, cols):
    return jnp.where(iota((rows, cols), 0) == (iota((rows, cols), 1) >> 1), 1.0, 0.0).astype(F32)


def words(shape):
    *lead, rows, lanes = (1,) * (3 - len(shape)) + tuple(shape)
    size = -(-rows // 8) * 8 * (-(-lanes // 128) * 128)
    for n in lead:
        size *= n
    return size


def call(body, outs, scratch, args, flops):
    vmem = pl.BlockSpec(memory_space=pltpu.VMEM)
    smem = pl.BlockSpec(memory_space=pltpu.SMEM)
    total = sum(words(a.shape) for a in args) + sum(map(words, outs)) + sum(map(words, scratch))
    return pl.pallas_call(
        body,
        out_shape=[jax.ShapeDtypeStruct(s, F32) for s in outs],
        in_specs=[smem if a.dtype == jnp.int32 and a.ndim == 1 else vmem for a in args],
        out_specs=[vmem] * len(outs),
        scratch_shapes=[pltpu.VMEM(s, F32) for s in scratch],
        compiler_params=pltpu.CompilerParams(vmem_limit_bytes=4 * total + (6 << 20)),
        cost_estimate=pl.CostEstimate(flops=flops, bytes_accessed=4000000, transcendentals=0),
    )(*args)


def pick_sides(at, chip, link):
    odd = lax.rem(at[1], 2) == 1
    lower = lambda *k: jnp.where(odd, chip[k], link[k])
    upper = lambda *k: jnp.where(odd, link[k], chip[k])
    return lower, upper


def send_shapes(planes):
    return [(16 + 2 * planes, 16, 256), (planes, 16, 256), (planes, 16, 256)]


def send(block, wider, low, high, planes):
    for i in range(16):
        wider[planes + i] = block[i]
    for i in range(planes):
        low[i] = block[i]
        high[i] = block[16 - planes + i]


PARTS = 4


def prepare_body(at, phase, distance, velocity, psi, x_low, x_high, chip, link, kind, away, x_face, y_face, sems):
    odd = lax.rem(at[1], 2) == 1
    step = 16 // PARTS
    copies = []

    def copy(src, dst):
        started = pltpu.make_async_copy(src, dst, sems.at[len(copies)])
        started.start()
        copies.append(started)

    for k in range(PARTS):
        planes = pl.ds(step * k, step)
        copy(phase.at[planes], kind.at[planes])
        copy(distance.at[planes], away.at[planes])
    copy(velocity.at[0, 0], x_face.at[0])
    copy(velocity.at[0, 15], x_face.at[1])
    copy(velocity.at[1, :, pl.ds(0, 8), :], y_face.at[0])
    copy(velocity.at[1, :, pl.ds(8, 8), :], y_face.at[1])
    for k in range(PARTS):
        copies[2 * k].wait()
        copies[2 * k + 1].wait()
        for i in range(step * k, step * k + step):
            orient = 2.0 * kind[i].astype(F32) - 1.0
            psi[i] = 1.0 / (1.0 + jnp.exp(-orient * away[i]))
    for started in copies[2 * PARTS :]:
        started.wait()
    for i in range(16):
        first = jnp.concatenate([psi[i, 0:3, :], y_face[0, i, 0:1, :]], axis=0)
        final = jnp.concatenate([psi[i, 13:16, :], y_face[1, i, 7:8, :]], axis=0)
        chip[i] = jnp.where(odd, first, final)
        link[i] = jnp.where(odd, final, first)
    for k in range(3):
        x_low[k] = psi[k]
        x_high[k] = psi[13 + k]
    x_low[3] = x_face[0]
    x_high[3] = x_face[1]


def prepare(at, phase, distance, velocity):
    vmem = pl.BlockSpec(memory_space=pltpu.VMEM)
    smem = pl.BlockSpec(memory_space=pltpu.SMEM)
    hbm = pl.BlockSpec(memory_space=pltpu.HBM)
    outs = [(16, 16, 256), (4, 16, 256), (4, 16, 256), (16, 4, 256), (16, 4, 256)]
    return pl.pallas_call(
        prepare_body,
        out_shape=[jax.ShapeDtypeStruct(s, F32) for s in outs],
        in_specs=[smem, hbm, hbm, hbm],
        out_specs=[vmem] * len(outs),
        scratch_shapes=[
            pltpu.VMEM((16, 16, 256), jnp.int32),
            pltpu.VMEM((16, 16, 256), F32),
            pltpu.VMEM((2, 16, 256), F32),
            pltpu.VMEM((2, 16, 8, 256), F32),
            pltpu.SemaphoreType.DMA((2 * PARTS + 4,)),
        ],
        compiler_params=pltpu.CompilerParams(vmem_limit_bytes=8 << 20),
        cost_estimate=pl.CostEstimate(flops=1000000, bytes_accessed=1000000, transcendentals=0),
    )(at, *(pltpu.with_memory_space_constraint(a, pltpu.HBM) for a in (phase, distance, velocity)))


def indicators(a, b, c):
    d = a - c
    curve = (a + c) - 2.0 * b
    twice = 2.0 * curve
    base = (13.0 / 12.0) * (curve * curve) + WENO_EPS
    up, down = twice - d, twice + d
    p = base + 0.25 * (up * up)
    q = base + 0.25 * (d * d)
    r = base + 0.25 * (down * down)
    return p * p, q * q, r * r


def upwind_flux(s, l, p_left, q_left, r_left, p_right, q_right, r_right):
    ahead = s > 0.0
    pick = lambda x, y: jnp.where(ahead, x, y)
    a, b, c, e, f = pick(l[0], l[5]), pick(l[1], l[4]), pick(l[2], l[3]), pick(l[3], l[2]), pick(l[4], l[1])
    p, q, r = pick(p_left, r_right), pick(q_left, q_right), pick(r_left, p_right)
    w0, w1, w2 = 0.1 * (q * r), 0.6 * (p * r), 0.3 * (p * q)
    g0 = 2.0 * a - 7.0 * b + 11.0 * c
    g1 = 5.0 * c + 2.0 * e - b
    g2 = 2.0 * c + 5.0 * e - f
    top = w0 * g0 + w1 * g1 + w2 * g2
    return (s * top) / (6.0 * (w0 + w1 + w2))


def transport_body(at, psi, velocity, xl, xh, chip, link, moved, wider, low, high, ext, p_x, q_x, r_x, rows, speed):
    lower, upper = pick_sides(at, chip, link)
    for k in range(3):
        ext[k] = xl[k]
        ext[19 + k] = xh[k]

    def fill(i, carry):
        ext[3 + i] = psi[i]
        return carry

    lax.fori_loop(0, 16, fill, 0, unroll=True)

    def marks(i, carry):
        p, q, r = indicators(ext[i], ext[i + 1], ext[i + 2])
        p_x[i], q_x[i], r_x[i] = p, q, r
        return carry

    lax.fori_loop(0, 20, marks, 0, unroll=True)

    def x_flux(j, v_low, v_high):
        s = 0.5 * (v_low + v_high)
        l = [ext[j + k] for k in range(6)]
        return upwind_flux(
            s, l, p_x[j], q_x[j + 1], r_x[j + 2], p_x[j + 1], q_x[j + 2], r_x[j + 3]
        )

    def plane(i, below):
        here = velocity[0, i]
        following = jnp.where(i == 15, xh[3], velocity[0, jnp.minimum(i + 1, 15)])
        above = x_flux(i + 1, here, following)
        change = above - below
        y_low, y_high = lower(i), upper(i)
        rows[1:4, :] = y_low[0:3, :]
        rows[4:20, :] = psi[i]
        rows[20:23, :] = y_high[0:3, :]
        speed[3:4, :] = y_low[3:4, :]
        speed[4:20, :] = velocity[1, i]
        speed[20:21, :] = y_high[3:4, :]
        v = rows[...]
        u = speed[...]
        s = 0.5 * (u + roll(u, -1, 0))
        l = [roll(v, 2 - k, 0) for k in range(6)]
        p, q, r = indicators(l[1], l[2], l[3])
        q_next, r_next = roll(q, -1, 0), roll(r, -1, 0)
        flux = upwind_flux(s, l, roll(p, 1, 0), q, r_next, p, q_next, roll(r, -2, 0))
        rows_change = flux - roll(flux, 1, 0)
        change = change + rows_change[4:20, :]
        v = psi[i]
        w = velocity[2, i]
        lane = iota(v.shape, 1)

        def ahead(x, k):
            return jnp.where(lane > 255 - k, 0.0, roll(x, -k, 1))

        def behind(x, k):
            return jnp.where(lane < k, 0.0, roll(x, k, 1))

        l = [behind(v, 2), behind(v, 1), v, ahead(v, 1), ahead(v, 2), ahead(v, 3)]
        s = 0.5 * (w + ahead(w, 1))
        p, q, r = indicators(l[1], l[2], l[3])
        _, q1, r1 = indicators(l[2], l[3], l[4])
        _, _, r2 = indicators(l[3], l[4], l[5])
        p0, _, _ = indicators(l[0], l[1], l[2])
        flux = upwind_flux(s, l, p0, q, r1, p, q1, r2)
        low = slice(0, 128)
        c = v[:, low]
        none = jnp.zeros_like(c)
        square = c * c
        edge = WENO_EPS + (13.0 / 12.0 + 9.0 / 4.0) * square
        level = WENO_EPS + (13.0 / 12.0 + 1.0 / 4.0) * square
        wall = upwind_flux(
            0.5 * w[:, low],
            [none, none, none, c, l[3][:, low], l[4][:, low]],
            none + WENO_EPS * WENO_EPS, level * level, r[:, low],
            edge * edge, q[:, low], r1[:, low],
        )
        wall = jnp.concatenate([wall, wall], axis=1)
        change = change + (flux - jnp.where(lane == 0, wall, roll(flux, 1, 1)))
        moved[i] = v - 0.25 * change
        return above

    rows[...] = jnp.zeros_like(rows)
    speed[...] = jnp.zeros_like(speed)
    lax.fori_loop(0, 16, plane, x_flux(0, xl[3], velocity[0, 0]), unroll=True)
    send(moved, wider, low, high, 3)


def transport(at, psi, velocity, xl, xh, chip, link):
    planes = (20, 16, 256)
    scratch = [(22, 16, 256), planes, planes, planes, (24, 256), (24, 256)]
    outs = [(16, 16, 256)] + send_shapes(3)
    return call(transport_body, outs, scratch, [at, psi, velocity, xl, xh, chip, link], 10000000)


def force_body(nx, ny, at, mid, chip, link, velocity, xl, xh, v_chip, v_link, wider, low, high, m, n_x, n_y, n_z, s_x, part, pad, source):
    lower, upper = pick_sides(at, chip, link)
    v_lower, v_upper = pick_sides(at, v_chip, v_link)
    x0, y0 = at[0] * 16, at[1] * 16
    shape = (32, 256)
    lane = iota(shape, 1)

    def fill(i, carry):
        m[i] = jnp.zeros(shape, F32)
        m[i, 5:8, :] = lower(i)
        m[i, 8:24, :] = mid[i]
        m[i, 24:27, :] = upper(i)
        return carry

    lax.fori_loop(0, 22, fill, 0, unroll=True)

    def gradient(i):
        c = m[i]
        below, above = z_shifted(c)
        gx = 0.5 * (m[i + 1] - m[i - 1])
        gy = 0.5 * (roll(c, -1, 0) - roll(c, 1, 0))
        return gx, gy, 0.5 * (above - below)

    def normals(i, carry):
        gx, gy, gz = gradient(i + 1)
        inverse = lax.rsqrt(gx * gx + gy * gy + gz * gz + DELTA_SQ)
        n_x[i], n_y[i], n_z[i] = gx * inverse, gy * inverse, gz * inverse
        return carry

    lax.fori_loop(0, 20, normals, 0, unroll=True)
    mask_y = row_mask(shape, y0 - 8, ny)

    def stars(i, carry):
        gx, gy, gz = gradient(i + 2)
        c = m[i + 2]
        edge = 0.5 * c
        edge = edge * lax.rsqrt(edge * edge + DELTA_SQ)
        nz = n_z[i + 1]
        above = jnp.where(lane == 255, -edge, roll(nz, -1, 1))
        below = jnp.where(lane == 0, edge, roll(nz, 1, 1))
        nn = n_y[i + 1]
        bending = -0.5 * (
            (n_x[i + 2] - n_x[i]) + (roll(nn, -1, 0) - roll(nn, 1, 0)) + (above - below)
        )
        keep = mask_y * plane_factor(x0 + i - 1, nx)
        bending = bending * keep
        fx, fy, fz = bending * gx, bending * gy, bending * gz
        k = jnp.clip(i - 1, 0, 15)
        vx = jnp.where(i == 0, xl[3], jnp.where(i == 17, xh[3], velocity[0, k]))
        s_x[i] = fx[8:24, :] + vx
        pad[7:8, :] = v_lower(k)[3:4, :]
        pad[8:24, :] = velocity[1, k]
        pad[24:25, :] = v_upper(k)[3:4, :]
        sy = fy + pad[...]
        dy = roll(sy, -1, 0) - roll(sy, 1, 0)
        sz = fz[8:24, :] + velocity[2, k]
        below, above = z_shifted(sz)
        part[i] = dy[8:24, :] + (above - below)
        return carry

    pad[...] = jnp.zeros_like(pad)
    lax.fori_loop(0, 18, stars, 0, unroll=True)

    def finish(i, carry):
        source[i] = -0.5 * (part[i + 1] + (s_x[i + 2] - s_x[i]))
        return carry

    lax.fori_loop(0, 16, finish, 0, unroll=True)
    send(source, wider, low, high, HALO)


def force(nx, ny, at, mid, chip, link, velocity, xl, xh, v_chip, v_link):
    n = (20, 32, 256)
    scratch = [(22, 32, 256), n, n, n, (18, 16, 256), (18, 16, 256), (32, 256), (16, 16, 256)]
    args = [at, mid, chip, link, velocity, xl, xh, v_chip, v_link]
    return call(functools.partial(force_body, nx, ny), send_shapes(HALO), scratch, args, 10000000)


class Field:
    def __init__(self, ref, lead):
        self.ref, self.lead = ref, lead

    def __getitem__(self, p):
        return self.ref[p + self.lead]

    def __setitem__(self, p, value):
        self.ref[p + self.lead] = value

    def beside(self, p):
        return beside(self.ref, p + self.lead)


def wall(at, nx, level, p, value):
    own = 16 >> level
    if 0 <= p < own:
        return value
    return value * plane_factor(at[0] * own + p, nx >> level)


def first_smooth(b, v, planes, weight, mask, at, nx, level):
    for p in planes:
        c, around = b.beside(p)
        v[p] = wall(at, nx, level, p, (weight * mask) * (1.2 * c + SIDE * around))


def sweep(src, dst, b, planes, factor, mask, at, nx, level):
    keep = SIDE * mask
    for p in planes:
        c, around = src.beside(p)
        near = around + (b[p] if factor == 1 else factor * b[p])
        dst[p] = 0.2 * c + wall(at, nx, level, p, keep) * near


def coarsen_level0(at, nx, ny, b, v, b1, planes, pair, t):
    first = planes[0]
    rows = t.shape[1]

    def residual(p):
        c, around = v.beside(p)
        return b[p] - (6.0 * c - around)

    for p in planes:
        total = residual(2 * p) + residual(2 * p + 1)
        for half in range(2):
            lanes = slice(128 * half, 128 * half + 128)
            pair[p - first, half] = total[:, lanes]
            even = pair[p - first, half, pl.ds(0, rows, stride=2), :]
            odd = pair[p - first, half, pl.ds(1, rows, stride=2), :]
            t[p - first, :, lanes] = even + odd
    count = len(planes)
    full = dot(t[...].reshape(count * rows, 256), pair_matrix(256, 128, 0.125))
    full = full.reshape(count, rows, 128)
    mask = row_mask((rows, 128), at[1] * 8 + 4 - rows // 2, ny // 2)
    for p in planes:
        b1[p] = wall(at, nx, 1, p, full[p - first] * mask)


def smooth_level1(at, nx, ny, b1, u, planes):
    rows = b1.ref.shape[1]
    mask = row_mask((rows, 128), at[1] * 8 + 4 - rows // 2, ny // 2)
    first_smooth(b1, u, planes, 4.0 * SIDE, mask, at, nx, 1)


def coarsen_level1(b1, u, b2_out, s1, t1):
    start = b1.ref.shape[1] // 2 - 4
    t1[...] = jnp.zeros_like(t1)
    for k in range(4):
        total = 0.0
        for p in (2 * k, 2 * k + 1):
            c, around = u.beside(p)
            total = total + (b1[p] - 0.25 * (6.0 * c - around))
        s1[k] = total
        t1[k, 0:4, :] = s1[k, pl.ds(start, 4, stride=2), :] + s1[k, pl.ds(start + 1, 4, stride=2), :]
    small = dot(t1[...].reshape(32, 128), pair_matrix(128, 128, 0.125)).reshape(4, 8, 128)
    tile = jnp.concatenate([small[0, 0:4], small[1, 0:4]], axis=0) + roll(
        jnp.concatenate([small[2, 0:4], small[3, 0:4]], axis=0), 64, 1
    )
    b2_out[...] = tile


def reach(extra):
    e0 = extra + 2
    r1 = -(-e0 // 2)
    e1 = r1 + 2
    r2 = -(-e1 // 2)
    e2 = r2 + 2
    r3 = -(-e2 // 2)
    return e0, r1, e1, r2, e2, r3


E0, R1, E1, R2, E2, R3 = reach(KEEP)


def first_down_body(nx, ny, at, mid, chip, link, b_out, v_out, b1_out, u_out, b2_out, b, v, pair, t, s1, t1):
    lower, upper = pick_sides(at, chip, link)
    for i in range(16 + 2 * HALO):
        b[i, 0:16, :] = lower(i)
        b[i, 16:32, :] = mid[i]
        b[i, 32:48, :] = upper(i)
    b, v = Field(b, HALO), Field(v, HALO - 1)
    mask = row_mask((48, 256), at[1] * 16 - 16, ny)
    first_smooth(b, v, range(1 - HALO, 15 + HALO), SIDE, mask, at, nx, 0)
    v_out, b_out = Field(v_out, E0), Field(b_out, E0 - 1)
    for p in range(-E0, 16 + E0):
        v_out[p] = v[p][8:40, :]
    for p in range(1 - E0, 15 + E0):
        b_out[p] = b[p][8:40, :]
    b1, u = Field(b1_out, E1 + 1), Field(u_out, E1)
    coarsen_level0(at, nx, ny, b, v, b1, range(-E1 - 1, 9 + E1), pair, t)
    smooth_level1(at, nx, ny, b1, u, range(-E1, 8 + E1))
    coarsen_level1(b1, u, b2_out, s1, t1)


def around_block(size, extra, rows, lanes):
    return (size + 2 * extra, rows, lanes)


def first_down(nx, ny, at, mid, chip, link):
    level1 = around_block(8, E1 + 1, 24, 128)
    outs = [
        around_block(16, E0 - 1, 32, 256),
        around_block(16, E0, 32, 256),
        level1,
        around_block(8, E1, 24, 128),
        (8, 128),
    ]
    scratch = [
        around_block(16, HALO, 48, 256),
        around_block(16, HALO - 1, 48, 256),
        (level1[0], 2, 48, 128),
        (level1[0], 24, 256),
        (4, 24, 128),
        (4, 8, 128),
    ]
    args = [at, mid, chip, link]
    return call(functools.partial(first_down_body, nx, ny), outs, scratch, args, 20000000)


def second_down_body(nx, ny, at, mid, chip, link, b1_out, u_out, b2_out, s1, t1):
    lower, upper = pick_sides(at, chip, link)
    for i in range(8 + 2 * NEAR):
        b1_out[i, 0:8, :] = lower(i)
        b1_out[i, 8:16, :] = mid[i]
        b1_out[i, 16:24, :] = upper(i)
    b1, u = Field(b1_out, NEAR), Field(u_out, NEAR - 1)
    smooth_level1(at, nx, ny, b1, u, range(1 - NEAR, 7 + NEAR))
    coarsen_level1(b1, u, b2_out, s1, t1)


def second_down(nx, ny, at, mid, chip, link):
    outs = [around_block(8, NEAR, 24, 128), around_block(8, NEAR - 1, 24, 128), (8, 128)]
    scratch = [(4, 24, 128), (4, 8, 128)]
    args = [at, mid, chip, link]
    return call(functools.partial(second_down_body, nx, ny), outs, scratch, args, 2000000)


def solve_coarse(nx, ny, extra, at, coarse, s2, v2, w2, t3, b3, c3, d3, dup, row2):
    fetched, other = coarse
    odd = lax.rem(at[1], 2) == 1
    odd_layer = lax.rem(at[0] // GROUP, 2)
    _, _, _, r2, e2, r3 = reach(extra)
    spot = at[0] % GROUP
    rows2 = ny // 4
    rows3 = rows2 // 2
    count = rows2 // 4
    lead = 2 * (r3 + 3) + 2
    blocks = -(-lead // 4)
    s2, v2, w2 = Field(s2, 4 * blocks), Field(v2, lead - 1), Field(w2, e2)
    lane8 = iota((8, 128), 1) < 64
    for j in range(-blocks, blocks + 1):
        block = spot + GROUP + j
        layer, place = block // GROUP, block % GROUP
        first_cores = jnp.where(odd_layer == 1, layer <= 1, layer >= 1)
        mine = first_cores != odd
        inner = inside(at[0] + j, nx // 16)
        start = ((layer + odd_layer) // 2) * (GROUP * count // 2) + place * (count // 2)
        for n in range(count):
            rows = slice(8 * (n % 2), 8 * (n % 2) + 8)
            k = start + n // 2
            tile = jnp.where(mine, fetched[k, rows, :], other[k, rows, :])
            tile = jnp.where(inner, tile, 0.0)
            halves = (jnp.where(lane8, tile, 0.0), jnp.where(lane8, roll(tile, 64, 1), 0.0))
            for p in range(4):
                part = halves[p // 2][4 * (p % 2) : 4 * (p % 2) + 4, :]
                s2.ref[4 * (j + blocks) + p, 4 * n : 4 * n + 4, :] = part

    def around(f, p):
        c = f[p]
        row = iota(c.shape, 0)
        lower = jnp.where(row == 0, 0.0, roll(c, 1, 0))
        upper = jnp.where(row == c.shape[0] - 1, 0.0, roll(c, -1, 0))
        beside = (lower + upper) + (roll(c, 1, 1) + roll(c, -1, 1))
        return c, (f[p - 1] + f[p + 1]) + beside

    def lanes_below(rows, lanes):
        return jnp.where(iota((rows, 128), 1) < lanes, 1.0, 0.0).astype(F32)

    mask2 = lanes_below(rows2, 64)
    for p in range(1 - lead, 3 + lead):
        c, near = around(s2, p)
        v2[p] = wall(at, nx, 2, p, (16.0 * SIDE) * mask2 * (1.2 * c + SIDE * near))

    def residual2(p):
        c, near = around(v2, p)
        return s2[p] - (1.0 / 16.0) * (6.0 * c - near)

    planes3 = range(-r3 - 3, 2 + r3 + 3)
    for i, p in enumerate(planes3):
        row2[i] = residual2(2 * p) + residual2(2 * p + 1)
        t3[i] = row2[i, pl.ds(0, rows3, stride=2), :] + row2[i, pl.ds(1, rows3, stride=2), :]
    total3 = len(planes3)
    full = dot(t3[...].reshape(total3 * rows3, 128), pair_matrix(128, 128, 0.125))
    full = full.reshape(total3, rows3, 128)
    mask3 = lanes_below(rows3, 32)
    b3, c3, d3 = Field(b3, r3 + 3), Field(c3, r3 + 3), Field(d3, r3 + 3)
    for i, p in enumerate(planes3):
        value = wall(at, nx, 3, p, full[i] * ((64.0 * SIDE) * mask3))
        b3[p] = value
    src, dst = b3, c3
    for step in (2, 1, 0):
        for p in range(-r3 - step, 2 + r3 + step):
            c, near = around(src, p)
            dst[p] = wall(at, nx, 3, p, mask3 * (0.2 * c + SIDE * near)) + b3[p]
        src, dst = dst, (d3 if dst is c3 else c3)
    final = src
    planes = range(-r3, 2 + r3)
    flat = jnp.concatenate([final[p] for p in planes], axis=0)
    spread = dot(flat, copy_matrix(128, 128)).reshape(len(planes), rows3, 128)
    for i, p in enumerate(planes):
        dup[i, pl.ds(0, rows3, stride=2), :] = spread[i]
        dup[i, pl.ds(1, rows3, stride=2), :] = spread[i]
        for q in (2 * p, 2 * p + 1):
            if -e2 <= q < 4 + e2:
                v2[q] = v2[q] + wall(at, nx, 2, q, dup[i, 0:rows2, :] * mask2)
    keep = SIDE * mask2
    for src, dst, step in ((v2, w2, 1), (w2, v2, 0)):
        for p in range(-r2 - step, 4 + r2 + step):
            c, near = around(src, p)
            dst[p] = 0.2 * c + wall(at, nx, 2, p, keep) * (near + 16.0 * s2[p])
    return v2


def coarse_scratch(ny, extra):
    _, _, _, _, e2, r3 = reach(extra)
    rows2 = ny // 4
    rows3 = rows2 // 2
    lead = 2 * (r3 + 3) + 2
    small = around_block(2, r3 + 3, rows3, 128)
    return [
        around_block(4, -(-lead // 4) * 4, rows2, 128),
        around_block(4, lead - 1, rows2, 128),
        around_block(4, e2, rows2, 128),
        small, small, small, small,
        (8, 48, 128),
        around_block(2, r3 + 3, rows2, 128),
    ]


def climb(nx, ny, extra, at, v2, b1, u, b, v_down, m1, n1, m0, n0, dup):
    e0, r1, e1, r2, _, _ = reach(extra)
    rows2 = ny // 4
    turn = lax.rem(rows2 + 4 - 4 * at[1] + rows2, rows2)
    planes = range(-r2, 4 + r2)
    picked = jnp.concatenate([pltpu.roll(v2[p], turn, 0)[0:16, :] for p in planes], axis=0)
    spread = dot(picked, copy_matrix(128, 128)).reshape(len(planes), 16, 128)
    mask1 = row_mask((24, 128), at[1] * 8 - 8, ny // 2)
    m1, n1 = Field(m1, e1), Field(n1, e1)
    for i, p in enumerate(planes):
        dup[i, 0, pl.ds(0, 12, stride=2), :] = spread[i, 0:12, :]
        dup[i, 0, pl.ds(1, 12, stride=2), :] = spread[i, 0:12, :]
        for q in (2 * p, 2 * p + 1):
            if -e1 <= q < 8 + e1:
                m1[q] = u[q] + wall(at, nx, 1, q, dup[i, 0, 0:24, :] * mask1)
    sweep(m1, n1, b1, range(1 - e1, 7 + e1), 4.0, mask1, at, nx, 1)
    sweep(n1, m1, b1, range(2 - e1, 6 + e1), 4.0, mask1, at, nx, 1)
    planes = range(-r1, 8 + r1)
    flat = jnp.concatenate([m1[p][4:20, :] for p in planes], axis=0)
    spread = dot(flat, copy_matrix(128, 256)).reshape(len(planes), 16, 256)
    mask0 = row_mask((32, 256), at[1] * 16 - 8, ny)
    m0, n0 = Field(m0, e0), Field(n0, e0)
    for i, p in enumerate(planes):
        for half in range(2):
            value = spread[i, :, 128 * half : 128 * half + 128]
            dup[i, half, pl.ds(0, 16, stride=2), :] = value
            dup[i, half, pl.ds(1, 16, stride=2), :] = value
        value = jnp.concatenate([dup[i, 0], dup[i, 1]], axis=1) * mask0
        for q in (2 * p, 2 * p + 1):
            if -e0 <= q < 16 + e0:
                m0[q] = v_down[q] + wall(at, nx, 0, q, value)
    sweep(m0, n0, b, range(1 - e0, 15 + e0), 1, mask0, at, nx, 0)
    if extra:
        sweep(n0, m0, b, range(2 - e0, 14 + e0), 1, mask0, at, nx, 0)
        return m0
    return n0


def climb_scratch(extra):
    e0, r1, e1, r2, _, _ = reach(extra)
    level1 = around_block(8, e1, 24, 128)
    level0 = around_block(16, e0, 32, 256)
    return [level1, level1, level0, level0, (max(8 + 2 * r1, 4 + 2 * r2), 2, 32, 128)]


def turn_body(nx, ny, at, fetched, other, b1, u, b, v_down, v_out, wider, low, high, own, pair, t, *scratch):
    v2 = solve_coarse(nx, ny, KEEP, at, (fetched, other), *scratch[:9])
    b = Field(b, E0 - 1)
    v = climb(nx, ny, KEEP, at, v2, Field(b1, E1 + 1), Field(u, E1), b, Field(v_down, E0), *scratch[9:])
    mask = row_mask((32, 256), at[1] * 16 - 8, ny)
    once, twice = Field(scratch[12], E0), Field(v_out, KEEP - 2)
    sweep(v, once, b, range(1 - KEEP, 15 + KEEP), 1, mask, at, nx, 0)
    sweep(once, twice, b, range(2 - KEEP, 14 + KEEP), 1, mask, at, nx, 0)
    coarsen_level0(at, nx, ny, b, twice, Field(own, 0), range(8), pair, t)
    for i in range(8):
        wider[NEAR + i] = own[i, 4:12, :]
    for i in range(NEAR):
        low[i] = own[i, 4:12, :]
        high[i] = own[8 - NEAR + i, 4:12, :]


def turn(nx, ny, at, coarse, b1, u, b, v_down):
    outs = [
        around_block(16, KEEP - 2, 32, 256),
        around_block(8, NEAR, 8, 128),
        (NEAR, 8, 128),
        (NEAR, 8, 128),
    ]
    scratch = [(8, 16, 128), (8, 2, 32, 128), (8, 16, 256)]
    scratch += coarse_scratch(ny, KEEP) + climb_scratch(KEEP)
    args = [at, *coarse, b1, u, b, v_down]
    return call(functools.partial(turn_body, nx, ny), outs, scratch, args, 30000000)


def finish_body(nx, ny, at, fetched, other, b1, u, b, v_down, out, *scratch):
    v2 = solve_coarse(nx, ny, 0, at, (fetched, other), *scratch[:9])
    b, v_down = Field(b, E0 - 1), Field(v_down, KEEP - 2)
    v = climb(nx, ny, 0, at, v2, Field(b1, NEAR), Field(u, NEAR - 1), b, v_down, *scratch[9:])
    for p in range(16):
        c, around = v.beside(p)
        out[p] = (0.2 * c + SIDE * (around + b[p]))[8:24, :]


def finish(nx, ny, at, coarse, b1, u, b, v_down):
    scratch = coarse_scratch(ny, 0) + climb_scratch(0)
    args = [at, *coarse, b1, u, b, v_down]
    return call(functools.partial(finish_body, nx, ny), [(16, 16, 256)], scratch, args, 20000000)[0]


def shifted(array, axis, step):
    count = lax.axis_size(axis)
    return lax.ppermute(
        array, axis, [(i, i + step) for i in range(count) if 0 <= i + step < count]
    )


def swapped(array, first):
    count = lax.axis_size("narrow")
    pairs = [(i, i + 1) for i in range(first, count - 1, 2)]
    return lax.ppermute(array, "narrow", pairs + [(j, i) for i, j in pairs])


def widen(wider, low, high):
    planes = low.shape[0]
    wider = lax.dynamic_update_slice(wider, shifted(high, "wide", 1), (0, 0, 0))
    upper = wider.shape[0] - planes
    return lax.dynamic_update_slice(wider, shifted(low, "wide", -1), (upper, 0, 0))


def surround(wider, low, high):
    mid = widen(wider, low, high)
    link = swapped(mid, 1)
    return mid, swapped(mid, 0), link


def spread_coarse(b2):
    wide, cores = lax.axis_size("wide"), lax.axis_size("narrow")
    layers = wide // GROUP
    odd = lax.rem(lax.axis_index("narrow"), 2) == 1
    other = swapped(b2, 0)
    pair = jnp.concatenate([jnp.where(odd, other, b2), jnp.where(odd, b2, other)], axis=0)
    groups = [
        [
            (((2 * k + core + i) % layers) * GROUP + x) * cores + y
            for i in range(2)
            for x in range(GROUP)
            for y in range(core, cores, 2)
        ]
        for core in range(2)
        for k in range(layers // 2)
    ]
    pieces = jnp.broadcast_to(pair[None], (len(groups[0]),) + pair.shape)
    fetched = lax.all_to_all(pieces, ("wide", "narrow"), 0, 0, axis_index_groups=groups)
    return fetched, swapped(fetched, 0)


def on_device(phase, distance, velocity):
    nx, ny = 16 * lax.axis_size("wide"), 16 * lax.axis_size("narrow")
    narrow = lax.axis_index("narrow")
    at = jnp.stack([lax.axis_index("wide"), narrow]).astype(jnp.int32)
    psi, x_low, x_high, chip, link = prepare(at, phase, distance, velocity)
    xl = shifted(x_high, "wide", 1)
    xh = shifted(x_low, "wide", -1)
    v_link = swapped(link, 1)
    v_chip = swapped(chip, 0)
    moved, *sends = transport(at, psi, velocity, xl, xh, v_chip, v_link)
    mid = widen(*sends)
    odd = lax.rem(narrow, 2) == 1
    first, final = mid[:, :3, :], mid[:, 13:, :]
    link = swapped(jnp.where(odd, final, first), 1)
    chip = swapped(jnp.where(odd, first, final), 0)
    sends = force(nx, ny, at, mid, chip, link, velocity, xl, xh, v_chip, v_link)
    b, v, b1, u, b2 = first_down(nx, ny, at, *surround(*sends))
    v, *sends = turn(nx, ny, at, spread_coarse(b2), b1, u, b, v)
    b1, u, b2 = second_down(nx, ny, at, *surround(*sends))
    pressure = finish(nx, ny, at, spread_coarse(b2), b1, u, b, v)
    return (moved, pressure)


def solution(mesh):
    blocks = P("wide", "narrow", None)
    return jax.shard_map(
        on_device,
        mesh=mesh,
        in_specs=(blocks, blocks, P(None, "wide", "narrow", None)),
        out_specs=(blocks, blocks),
        check_vma=False,
    )
```

```python
import functools

import jax
import jax.numpy as jnp
from jax import lax
from jax.experimental import pallas as pl
from jax.experimental.pallas import tpu as pltpu
from jax.sharding import PartitionSpec as P

DELTA_SQ = 0.0025
WENO_EPS = 0.01
SIDE = 0.8 / 6.0
F32 = jnp.float32

HALO = 14
KEEP = 4
NEAR = 4
GROUP = 4


def iota(shape, dim):
    return lax.broadcasted_iota(jnp.int32, shape, dim)


def roll(v, shift, axis):
    return pltpu.roll(v, shift % v.shape[axis], axis)


def z_shifted(v):
    lane = iota(v.shape, 1)
    last = v.shape[1] - 1
    lower = jnp.where(lane == 0, 0.0, roll(v, 1, 1))
    upper = jnp.where(lane == last, 0.0, roll(v, -1, 1))
    return lower, upper


def z_pair(v):
    lower, upper = z_shifted(v)
    return lower + upper


def y_pair(v):
    return roll(v, 1, 0) + roll(v, -1, 0)


def beside(ref, i):
    c = ref[i]
    return c, (ref[i - 1] + ref[i + 1]) + y_pair(c) + z_pair(c)


def inside(first, count):
    return jnp.logical_and(first >= 0, first < count)


def row_mask(shape, first, count):
    rows = iota(shape, 0) + first
    return jnp.where(inside(rows, count), 1.0, 0.0).astype(F32)


def plane_factor(index, count):
    return jnp.where(inside(index, count), 1.0, 0.0).astype(F32)


def dot(a, b):
    b = b.astype(jnp.bfloat16)
    high = a.astype(jnp.bfloat16)
    low = (a - high.astype(F32)).astype(jnp.bfloat16)
    return jnp.dot(high, b, preferred_element_type=F32) + jnp.dot(low, b, preferred_element_type=F32)


def pair_matrix(rows, cols, value):
    return jnp.where((iota((rows, cols), 0) >> 1) == iota((rows, cols), 1), value, 0.0).astype(F32)


def copy_matrix(rows, cols):
    return jnp.where(iota((rows, cols), 0) == (iota((rows, cols), 1) >> 1), 1.0, 0.0).astype(F32)


def words(shape):
    *lead, rows, lanes = (1,) * (3 - len(shape)) + tuple(shape)
    size = -(-rows // 8) * 8 * (-(-lanes // 128) * 128)
    for n in lead:
        size *= n
    return size


def call(body, outs, scratch, args, flops):
    vmem = pl.BlockSpec(memory_space=pltpu.VMEM)
    smem = pl.BlockSpec(memory_space=pltpu.SMEM)
    total = sum(words(a.shape) for a in args) + sum(map(words, outs)) + sum(map(words, scratch))
    return pl.pallas_call(
        body,
        out_shape=[jax.ShapeDtypeStruct(s, F32) for s in outs],
        in_specs=[smem if a.dtype == jnp.int32 and a.ndim == 1 else vmem for a in args],
        out_specs=[vmem] * len(outs),
        scratch_shapes=[pltpu.VMEM(s, F32) for s in scratch],
        compiler_params=pltpu.CompilerParams(vmem_limit_bytes=4 * total + (6 << 20)),
        cost_estimate=pl.CostEstimate(flops=flops, bytes_accessed=4000000, transcendentals=0),
    )(*args)


def pick_sides(at, chip, link):
    odd = lax.rem(at[1], 2) == 1
    lower = lambda *k: jnp.where(odd, chip[k], link[k])
    upper = lambda *k: jnp.where(odd, link[k], chip[k])
    return lower, upper


def send_shapes(planes):
    return [(16 + 2 * planes, 16, 256), (planes, 16, 256), (planes, 16, 256)]


def send(block, wider, low, high, planes):
    for i in range(16):
        wider[planes + i] = block[i]
    for i in range(planes):
        low[i] = block[i]
        high[i] = block[16 - planes + i]


PARTS = 4
FAR, ALONG, ACROSS = 6, 4, 3
SENT = FAR + ALONG + 2 * ACROSS


def layer_cuts(dim):
    cuts, offset = [], FAR
    for component in range(3):
        layers = ALONG if component == dim else ACROSS
        cuts.append((component, layers, offset))
        offset += layers
    return cuts


def prepare_body(phase, distance, velocity, psi, x_low, x_high, kind, away, sems):
    step = 16 // PARTS
    copies = []

    def copy(src, dst):
        started = pltpu.make_async_copy(src, dst, sems.at[len(copies)])
        started.start()
        copies.append(started)

    for k in range(PARTS):
        planes = pl.ds(step * k, step)
        copy(phase.at[planes], kind.at[planes])
        copy(distance.at[planes], away.at[planes])
    for component, layers, offset in layer_cuts(0):
        copy(velocity.at[component, pl.ds(0, layers)], x_low.at[pl.ds(offset, layers)])
        copy(velocity.at[component, pl.ds(16 - layers, layers)], x_high.at[pl.ds(offset, layers)])
    for k in range(PARTS):
        copies[2 * k].wait()
        copies[2 * k + 1].wait()
        for i in range(step * k, step * k + step):
            orient = 2.0 * kind[i].astype(F32) - 1.0
            psi[i] = 1.0 / (1.0 + jnp.exp(-orient * away[i]))
    for k in range(FAR):
        x_low[k] = psi[k]
        x_high[k] = psi[16 - FAR + k]
    for started in copies[2 * PARTS :]:
        started.wait()


def prepare(phase, distance, velocity):
    vmem = pl.BlockSpec(memory_space=pltpu.VMEM)
    hbm = pl.BlockSpec(memory_space=pltpu.HBM)
    outs = [(16, 16, 256), (SENT, 16, 256), (SENT, 16, 256)]
    return pl.pallas_call(
        prepare_body,
        out_shape=[jax.ShapeDtypeStruct(s, F32) for s in outs],
        in_specs=[hbm, hbm, hbm],
        out_specs=[vmem] * len(outs),
        scratch_shapes=[
            pltpu.VMEM((16, 16, 256), jnp.int32),
            pltpu.VMEM((16, 16, 256), F32),
            pltpu.SemaphoreType.DMA((2 * PARTS + 6,)),
        ],
        compiler_params=pltpu.CompilerParams(vmem_limit_bytes=8 << 20),
        cost_estimate=pl.CostEstimate(flops=1000000, bytes_accessed=1000000, transcendentals=0),
    )(*(pltpu.with_memory_space_constraint(a, pltpu.HBM) for a in (phase, distance, velocity)))


def plane_of(own, low, high, p, offset, layers):
    if p < 0:
        return low[offset + layers + p]
    return own(p) if p < 16 else high[offset + p - 16]


def wide_planes(psi, velocity, low, high):
    def level(p):
        return plane_of(lambda k: psi[k], low, high, p, 0, FAR)

    def speed(component):
        _, layers, offset = layer_cuts(0)[component]

        def at_plane(p):
            if not -layers <= p < 16 + layers:
                return None
            return plane_of(lambda k: velocity[component, k], low, high, p, offset, layers)

        return at_plane

    return level, [speed(c) for c in range(3)]


def pack_body(at, psi, velocity, low, high, chip, link):
    odd = lax.rem(at[1], 2) == 1
    level, speeds = wide_planes(psi, velocity, low, high)
    for k in range(16 + 2 * FAR):
        v = level(k - FAR)
        first, final = [v[0:FAR]], [v[16 - FAR : 16]]
        for component, layers, _ in layer_cuts(1):
            w = speeds[component](k - FAR)
            if w is None:
                w = jnp.zeros((16, 256), F32)
            first.append(w[0:layers])
            final.append(w[16 - layers : 16])
        first = jnp.concatenate(first, axis=0)
        final = jnp.concatenate(final, axis=0)
        chip[k] = jnp.where(odd, first, final)
        link[k] = jnp.where(odd, final, first)


def pack(at, psi, velocity, low, high):
    outs = [(16 + 2 * FAR, SENT, 256)] * 2
    return call(pack_body, outs, [], [at, psi, velocity, low, high], 1000000)


FACE = 0.25 / 12.0


def indicators(a, b, c):
    d = a - c
    curve = (a + c) - 2.0 * b
    twice = 2.0 * curve
    base = (13.0 / 12.0) * (curve * curve) + WENO_EPS
    up, down = twice - d, twice + d
    p = base + 0.25 * (up * up)
    q = base + 0.25 * (d * d)
    r = base + 0.25 * (down * down)
    return p * p, q * q, r * r


def upwind_flux(s, l, p_left, q_left, r_left, p_right, q_right, r_right):
    ahead = s > 0.0
    pick = lambda x, y: jnp.where(ahead, x, y)
    a, b, c, e, f = pick(l[0], l[5]), pick(l[1], l[4]), pick(l[2], l[3]), pick(l[3], l[2]), pick(l[4], l[1])
    p, q, r = pick(p_left, r_right), pick(q_left, q_right), pick(r_left, p_right)
    w0, w1, w2 = q * r, 6.0 * (p * r), 3.0 * (p * q)
    g0 = 2.0 * a - 7.0 * b + 11.0 * c
    g1 = 5.0 * c + 2.0 * e - b
    g2 = 2.0 * c + 5.0 * e - f
    top = w0 * g0 + w1 * g1 + w2 * g2
    total = w0 + w1 + w2
    return (s * top) / total


def z_change(v, w):
    lane = iota(v.shape, 1)

    def ahead(x, k):
        return jnp.where(lane > 255 - k, 0.0, roll(x, -k, 1))

    def behind(x, k):
        return jnp.where(lane < k, 0.0, roll(x, k, 1))

    l = [behind(v, 2), behind(v, 1), v, ahead(v, 1), ahead(v, 2), ahead(v, 3)]
    s = FACE * (w + ahead(w, 1))
    p, q, r = indicators(l[1], l[2], l[3])
    _, q1, r1 = indicators(l[2], l[3], l[4])
    _, _, r2 = indicators(l[3], l[4], l[5])
    p0, _, _ = indicators(l[0], l[1], l[2])
    flux = upwind_flux(s, l, p0, q, r1, p, q1, r2)
    low = slice(0, 128)
    c = v[:, low]
    none = jnp.zeros_like(c)
    square = c * c
    edge = WENO_EPS + (13.0 / 12.0 + 9.0 / 4.0) * square
    level = WENO_EPS + (13.0 / 12.0 + 1.0 / 4.0) * square
    wall_flux = upwind_flux(
        FACE * w[:, low],
        [none, none, none, c, l[3][:, low], l[4][:, low]],
        none + WENO_EPS * WENO_EPS, level * level, r[:, low],
        edge * edge, q[:, low], r1[:, low],
    )
    wall_flux = jnp.concatenate([wall_flux, wall_flux], axis=1)
    return flux - jnp.where(lane == 0, wall_flux, roll(flux, 1, 1))


def y_change(v, w):
    s = FACE * (w + roll(w, -1, 0))
    l = [roll(v, 2 - k, 0) for k in range(6)]
    p, q, r = indicators(l[1], l[2], l[3])
    q_next, r_next = roll(q, -1, 0), roll(r, -1, 0)
    flux = upwind_flux(s, l, roll(p, 1, 0), q, r_next, p, q_next, roll(r, -2, 0))
    return flux - roll(flux, 1, 0)


SKIN = 3


def advance_body(
    nx, ny, at, psi, velocity, low, high, chip, link, moved, wider, first, final,
    v24, v32, u24, u32, w24, p_x, q_x, r_x, m, n_x, n_y, n_z, s_x, part, source,
):
    lower, upper = pick_sides(at, chip, link)
    level, speeds = wide_planes(psi, velocity, low, high)
    cuts = layer_cuts(1)

    def place(ref, i, start, rows, layers, below, above):
        total = ref.shape[1]
        ref[i, start - layers : start, :] = below
        ref[i, start : start + 16, :] = rows
        ref[i, start + 16 : start + 16 + layers, :] = above
        if start - layers:
            ref[i, 0 : start - layers, :] = jnp.zeros((start - layers, 256), F32)
        rest = total - start - 16 - layers
        if rest:
            ref[i, total - rest : total, :] = jnp.zeros((rest, 256), F32)

    for i in range(16 + 2 * FAR):
        p = i - FAR
        below, above = lower(i), upper(i)
        rows = level(p)
        place(v24, i, 4, rows, 4, below[FAR - 4 : FAR], above[0:4])
        if -SKIN <= p < 16 + SKIN:
            place(v32, p + SKIN, 8, rows, FAR, below[0:FAR], above[0:FAR])
        for component, ref, start in ((0, u24, 4), (1, u32, 8), (2, w24, 4)):
            rows = speeds[component](p)
            if rows is not None:
                _, count, offset = cuts[component]
                _, layers, _ = layer_cuts(0)[component]
                cut = slice(offset, offset + count)
                place(ref, p + layers, start, rows, count, below[cut], above[cut])

    for i in range(26):
        p_x[i], q_x[i], r_x[i] = indicators(v24[i], v24[i + 1], v24[i + 2])

    def x_flux(f):
        s = FACE * (u24[f - 1 + ALONG] + u24[f + ALONG])
        l = [v24[f - 3 + k + FAR] for k in range(6)]
        return upwind_flux(
            s, l, p_x[f + 3], q_x[f + 4], r_x[f + 5], p_x[f + 4], q_x[f + 5], r_x[f + 6]
        )

    shape = (24, 256)
    mask = row_mask(shape, at[1] * 16 - 4, ny)
    below = x_flux(-SKIN)
    for p in range(-SKIN, 16 + SKIN):
        above = x_flux(p + 1)
        v = v24[p + FAR]
        change = above - below
        change = change + y_change(v32[p + SKIN], u32[p + ACROSS])[4:28, :]
        change = change + z_change(v, w24[p + ACROSS])
        below = above
        value = wall(at, nx, 0, p, (v - change) * mask)
        m[p + SKIN] = value
        if 0 <= p < 16:
            moved[p] = value[4:20, :]

    lane = iota(shape, 1)

    def gradient(p):
        c = m[p + SKIN]
        down, ahead = z_shifted(c)
        gx = 0.5 * (m[p + SKIN + 1] - m[p + SKIN - 1])
        gy = 0.5 * (roll(c, -1, 0) - roll(c, 1, 0))
        return gx, gy, 0.5 * (ahead - down)

    for p in range(-2, 18):
        gx, gy, gz = gradient(p)
        inverse = lax.rsqrt(gx * gx + gy * gy + gz * gz + DELTA_SQ)
        n_x[p + 2], n_y[p + 2], n_z[p + 2] = gx * inverse, gy * inverse, gz * inverse
    for p in range(-1, 17):
        gx, gy, gz = gradient(p)
        edge = 0.5 * m[p + SKIN]
        edge = edge * lax.rsqrt(edge * edge + DELTA_SQ)
        nz, ny_here = n_z[p + 2], n_y[p + 2]
        ahead = jnp.where(lane == 255, -edge, roll(nz, -1, 1))
        behind = jnp.where(lane == 0, edge, roll(nz, 1, 1))
        bending = -0.5 * (
            (n_x[p + 3] - n_x[p + 1])
            + (roll(ny_here, -1, 0) - roll(ny_here, 1, 0))
            + (ahead - behind)
        )
        bending = wall(at, nx, 0, p, bending * mask)
        s_x[p + 1] = (bending * gx)[4:20, :] + u24[p + ALONG, 4:20, :]
        if 0 <= p < 16:
            sy = bending * gy + u32[p + ACROSS, 4:28, :]
            dy = roll(sy, -1, 0) - roll(sy, 1, 0)
            sz = (bending * gz)[4:20, :] + velocity[2, p]
            behind, ahead = z_shifted(sz)
            part[p] = dy[4:20, :] + (ahead - behind)
    for p in range(16):
        source[p] = -0.5 * (part[p] + (s_x[p + 2] - s_x[p]))
    send(source, wider, first, final, HALO)


def advance(nx, ny, at, psi, velocity, low, high, chip, link):
    marks, normals, block = (26, 24, 256), (20, 24, 256), (16, 16, 256)
    scratch = [
        (16 + 2 * FAR, 24, 256), (16 + 2 * SKIN, 32, 256), (16 + 2 * ALONG, 24, 256),
        (16 + 2 * ACROSS, 32, 256), (16 + 2 * ACROSS, 24, 256), marks, marks, marks,
        (16 + 2 * SKIN, 24, 256), normals, normals, normals, (18, 16, 256), block, block,
    ]
    args = [at, psi, velocity, low, high, chip, link]
    outs = [block] + send_shapes(HALO)
    return call(functools.partial(advance_body, nx, ny), outs, scratch, args, 30000000)


class Field:
    def __init__(self, ref, lead):
        self.ref, self.lead = ref, lead

    def __getitem__(self, p):
        return self.ref[p + self.lead]

    def __setitem__(self, p, value):
        self.ref[p + self.lead] = value

    def beside(self, p):
        return beside(self.ref, p + self.lead)


def wall(at, nx, level, p, value):
    own = 16 >> level
    if 0 <= p < own:
        return value
    return value * plane_factor(at[0] * own + p, nx >> level)


def first_smooth(b, v, planes, weight, mask, at, nx, level):
    for p in planes:
        c, around = b.beside(p)
        v[p] = wall(at, nx, level, p, (weight * mask) * (1.2 * c + SIDE * around))


def sweep(src, dst, b, planes, factor, mask, at, nx, level):
    keep = SIDE * mask
    for p in planes:
        c, around = src.beside(p)
        near = around + (b[p] if factor == 1 else factor * b[p])
        dst[p] = 0.2 * c + wall(at, nx, level, p, keep) * near


def coarsen_level0(at, nx, ny, b, v, b1, planes, pair, t):
    first = planes[0]
    rows = t.shape[1]

    def residual(p):
        c, around = v.beside(p)
        return b[p] - (6.0 * c - around)

    for p in planes:
        total = residual(2 * p) + residual(2 * p + 1)
        for half in range(2):
            lanes = slice(128 * half, 128 * half + 128)
            pair[p - first, half] = total[:, lanes]
            even = pair[p - first, half, pl.ds(0, rows, stride=2), :]
            odd = pair[p - first, half, pl.ds(1, rows, stride=2), :]
            t[p - first, :, lanes] = even + odd
    count = len(planes)
    full = dot(t[...].reshape(count * rows, 256), pair_matrix(256, 128, 0.125))
    full = full.reshape(count, rows, 128)
    mask = row_mask((rows, 128), at[1] * 8 + 4 - rows // 2, ny // 2)
    for p in planes:
        b1[p] = wall(at, nx, 1, p, full[p - first] * mask)


def smooth_level1(at, nx, ny, b1, u, planes):
    rows = b1.ref.shape[1]
    mask = row_mask((rows, 128), at[1] * 8 + 4 - rows // 2, ny // 2)
    first_smooth(b1, u, planes, 4.0 * SIDE, mask, at, nx, 1)


def coarsen_level1(b1, u, b2_out, s1, t1):
    start = b1.ref.shape[1] // 2 - 4
    t1[...] = jnp.zeros_like(t1)
    for k in range(4):
        total = 0.0
        for p in (2 * k, 2 * k + 1):
            c, around = u.beside(p)
            total = total + (b1[p] - 0.25 * (6.0 * c - around))
        s1[k] = total
        t1[k, 0:4, :] = s1[k, pl.ds(start, 4, stride=2), :] + s1[k, pl.ds(start + 1, 4, stride=2), :]
    small = dot(t1[...].reshape(32, 128), pair_matrix(128, 128, 0.125)).reshape(4, 8, 128)
    tile = jnp.concatenate([small[0, 0:4], small[1, 0:4]], axis=0) + roll(
        jnp.concatenate([small[2, 0:4], small[3, 0:4]], axis=0), 64, 1
    )
    b2_out[...] = tile


def reach(extra):
    e0 = extra + 2
    r1 = -(-e0 // 2)
    e1 = r1 + 2
    r2 = -(-e1 // 2)
    e2 = r2 + 2
    r3 = -(-e2 // 2)
    return e0, r1, e1, r2, e2, r3


E0, R1, E1, R2, E2, R3 = reach(KEEP)


def first_down_body(nx, ny, at, mid, chip, link, b_out, v_out, b1_out, u_out, b2_out, b, v, pair, t, s1, t1):
    lower, upper = pick_sides(at, chip, link)
    for i in range(16 + 2 * HALO):
        b[i, 0:16, :] = lower(i)
        b[i, 16:32, :] = mid[i]
        b[i, 32:48, :] = upper(i)
    b, v = Field(b, HALO), Field(v, HALO - 1)
    mask = row_mask((48, 256), at[1] * 16 - 16, ny)
    first_smooth(b, v, range(1 - HALO, 15 + HALO), SIDE, mask, at, nx, 0)
    v_out, b_out = Field(v_out, E0), Field(b_out, E0 - 1)
    for p in range(-E0, 16 + E0):
        v_out[p] = v[p][8:40, :]
    for p in range(1 - E0, 15 + E0):
        b_out[p] = b[p][8:40, :]
    b1, u = Field(b1_out, E1 + 1), Field(u_out, E1)
    coarsen_level0(at, nx, ny, b, v, b1, range(-E1 - 1, 9 + E1), pair, t)
    smooth_level1(at, nx, ny, b1, u, range(-E1, 8 + E1))
    coarsen_level1(b1, u, b2_out, s1, t1)


def around_block(size, extra, rows, lanes):
    return (size + 2 * extra, rows, lanes)


def first_down(nx, ny, at, mid, chip, link):
    level1 = around_block(8, E1 + 1, 24, 128)
    outs = [
        around_block(16, E0 - 1, 32, 256),
        around_block(16, E0, 32, 256),
        level1,
        around_block(8, E1, 24, 128),
        (8, 128),
    ]
    scratch = [
        around_block(16, HALO, 48, 256),
        around_block(16, HALO - 1, 48, 256),
        (level1[0], 2, 48, 128),
        (level1[0], 24, 256),
        (4, 24, 128),
        (4, 8, 128),
    ]
    args = [at, mid, chip, link]
    return call(functools.partial(first_down_body, nx, ny), outs, scratch, args, 20000000)


def second_down_body(nx, ny, at, mid, chip, link, b1_out, u_out, b2_out, s1, t1):
    lower, upper = pick_sides(at, chip, link)
    for i in range(8 + 2 * NEAR):
        b1_out[i, 0:8, :] = lower(i)
        b1_out[i, 8:16, :] = mid[i]
        b1_out[i, 16:24, :] = upper(i)
    b1, u = Field(b1_out, NEAR), Field(u_out, NEAR - 1)
    smooth_level1(at, nx, ny, b1, u, range(1 - NEAR, 7 + NEAR))
    coarsen_level1(b1, u, b2_out, s1, t1)


def second_down(nx, ny, at, mid, chip, link):
    outs = [around_block(8, NEAR, 24, 128), around_block(8, NEAR - 1, 24, 128), (8, 128)]
    scratch = [(4, 24, 128), (4, 8, 128)]
    args = [at, mid, chip, link]
    return call(functools.partial(second_down_body, nx, ny), outs, scratch, args, 2000000)


def solve_coarse(nx, ny, extra, at, coarse, s2, v2, w2, t3, b3, c3, d3, dup, row2):
    fetched, other = coarse
    odd = lax.rem(at[1], 2) == 1
    odd_layer = lax.rem(at[0] // GROUP, 2)
    _, _, _, r2, e2, r3 = reach(extra)
    spot = at[0] % GROUP
    rows2 = ny // 4
    rows3 = rows2 // 2
    count = rows2 // 4
    lead = 2 * (r3 + 3) + 2
    blocks = -(-lead // 4)
    s2, v2, w2 = Field(s2, 4 * blocks), Field(v2, lead - 1), Field(w2, e2)
    lane8 = iota((8, 128), 1) < 64
    for j in range(-blocks, blocks + 1):
        block = spot + GROUP + j
        layer, place = block // GROUP, block % GROUP
        first_cores = jnp.where(odd_layer == 1, layer <= 1, layer >= 1)
        mine = first_cores != odd
        inner = inside(at[0] + j, nx // 16)
        start = ((layer + odd_layer) // 2) * (GROUP * count // 2) + place * (count // 2)
        for n in range(count):
            rows = slice(8 * (n % 2), 8 * (n % 2) + 8)
            k = start + n // 2
            tile = jnp.where(mine, fetched[k, rows, :], other[k, rows, :])
            tile = jnp.where(inner, tile, 0.0)
            halves = (jnp.where(lane8, tile, 0.0), jnp.where(lane8, roll(tile, 64, 1), 0.0))
            for p in range(4):
                part = halves[p // 2][4 * (p % 2) : 4 * (p % 2) + 4, :]
                s2.ref[4 * (j + blocks) + p, 4 * n : 4 * n + 4, :] = part

    def around(f, p):
        c = f[p]
        row = iota(c.shape, 0)
        lower = jnp.where(row == 0, 0.0, roll(c, 1, 0))
        upper = jnp.where(row == c.shape[0] - 1, 0.0, roll(c, -1, 0))
        beside = (lower + upper) + (roll(c, 1, 1) + roll(c, -1, 1))
        return c, (f[p - 1] + f[p + 1]) + beside

    def lanes_below(rows, lanes):
        return jnp.where(iota((rows, 128), 1) < lanes, 1.0, 0.0).astype(F32)

    mask2 = lanes_below(rows2, 64)
    for p in range(1 - lead, 3 + lead):
        c, near = around(s2, p)
        v2[p] = wall(at, nx, 2, p, (16.0 * SIDE) * mask2 * (1.2 * c + SIDE * near))

    def residual2(p):
        c, near = around(v2, p)
        return s2[p] - (1.0 / 16.0) * (6.0 * c - near)

    planes3 = range(-r3 - 3, 2 + r3 + 3)
    for i, p in enumerate(planes3):
        row2[i] = residual2(2 * p) + residual2(2 * p + 1)
        t3[i] = row2[i, pl.ds(0, rows3, stride=2), :] + row2[i, pl.ds(1, rows3, stride=2), :]
    total3 = len(planes3)
    full = dot(t3[...].reshape(total3 * rows3, 128), pair_matrix(128, 128, 0.125))
    full = full.reshape(total3, rows3, 128)
    mask3 = lanes_below(rows3, 32)
    b3, c3, d3 = Field(b3, r3 + 3), Field(c3, r3 + 3), Field(d3, r3 + 3)
    for i, p in enumerate(planes3):
        value = wall(at, nx, 3, p, full[i] * ((64.0 * SIDE) * mask3))
        b3[p] = value
    src, dst = b3, c3
    for step in (2, 1, 0):
        for p in range(-r3 - step, 2 + r3 + step):
            c, near = around(src, p)
            dst[p] = wall(at, nx, 3, p, mask3 * (0.2 * c + SIDE * near)) + b3[p]
        src, dst = dst, (d3 if dst is c3 else c3)
    final = src
    planes = range(-r3, 2 + r3)
    flat = jnp.concatenate([final[p] for p in planes], axis=0)
    spread = dot(flat, copy_matrix(128, 128)).reshape(len(planes), rows3, 128)
    for i, p in enumerate(planes):
        dup[i, pl.ds(0, rows3, stride=2), :] = spread[i]
        dup[i, pl.ds(1, rows3, stride=2), :] = spread[i]
        for q in (2 * p, 2 * p + 1):
            if -e2 <= q < 4 + e2:
                v2[q] = v2[q] + wall(at, nx, 2, q, dup[i, 0:rows2, :] * mask2)
    keep = SIDE * mask2
    for src, dst, step in ((v2, w2, 1), (w2, v2, 0)):
        for p in range(-r2 - step, 4 + r2 + step):
            c, near = around(src, p)
            dst[p] = 0.2 * c + wall(at, nx, 2, p, keep) * (near + 16.0 * s2[p])
    return v2


def coarse_scratch(ny, extra):
    _, _, _, _, e2, r3 = reach(extra)
    rows2 = ny // 4
    rows3 = rows2 // 2
    lead = 2 * (r3 + 3) + 2
    small = around_block(2, r3 + 3, rows3, 128)
    return [
        around_block(4, -(-lead // 4) * 4, rows2, 128),
        around_block(4, lead - 1, rows2, 128),
        around_block(4, e2, rows2, 128),
        small, small, small, small,
        (8, 48, 128),
        around_block(2, r3 + 3, rows2, 128),
    ]


def climb(nx, ny, extra, at, v2, b1, u, b, v_down, m1, n1, m0, n0, dup):
    e0, r1, e1, r2, _, _ = reach(extra)
    rows2 = ny // 4
    turn = lax.rem(rows2 + 4 - 4 * at[1] + rows2, rows2)
    planes = range(-r2, 4 + r2)
    picked = jnp.concatenate([pltpu.roll(v2[p], turn, 0)[0:16, :] for p in planes], axis=0)
    spread = dot(picked, copy_matrix(128, 128)).reshape(len(planes), 16, 128)
    mask1 = row_mask((24, 128), at[1] * 8 - 8, ny // 2)
    m1, n1 = Field(m1, e1), Field(n1, e1)
    for i, p in enumerate(planes):
        dup[i, 0, pl.ds(0, 12, stride=2), :] = spread[i, 0:12, :]
        dup[i, 0, pl.ds(1, 12, stride=2), :] = spread[i, 0:12, :]
        for q in (2 * p, 2 * p + 1):
            if -e1 <= q < 8 + e1:
                m1[q] = u[q] + wall(at, nx, 1, q, dup[i, 0, 0:24, :] * mask1)
    sweep(m1, n1, b1, range(1 - e1, 7 + e1), 4.0, mask1, at, nx, 1)
    sweep(n1, m1, b1, range(2 - e1, 6 + e1), 4.0, mask1, at, nx, 1)
    planes = range(-r1, 8 + r1)
    flat = jnp.concatenate([m1[p][4:20, :] for p in planes], axis=0)
    spread = dot(flat, copy_matrix(128, 256)).reshape(len(planes), 16, 256)
    mask0 = row_mask((32, 256), at[1] * 16 - 8, ny)
    m0, n0 = Field(m0, e0), Field(n0, e0)
    for i, p in enumerate(planes):
        for half in range(2):
            value = spread[i, :, 128 * half : 128 * half + 128]
            dup[i, half, pl.ds(0, 16, stride=2), :] = value
            dup[i, half, pl.ds(1, 16, stride=2), :] = value
        value = jnp.concatenate([dup[i, 0], dup[i, 1]], axis=1) * mask0
        for q in (2 * p, 2 * p + 1):
            if -e0 <= q < 16 + e0:
                m0[q] = v_down[q] + wall(at, nx, 0, q, value)
    sweep(m0, n0, b, range(1 - e0, 15 + e0), 1, mask0, at, nx, 0)
    if extra:
        sweep(n0, m0, b, range(2 - e0, 14 + e0), 1, mask0, at, nx, 0)
        return m0
    return n0


def climb_scratch(extra):
    e0, r1, e1, r2, _, _ = reach(extra)
    level1 = around_block(8, e1, 24, 128)
    level0 = around_block(16, e0, 32, 256)
    return [level1, level1, level0, level0, (max(8 + 2 * r1, 4 + 2 * r2), 2, 32, 128)]


def turn_body(nx, ny, at, fetched, other, b1, u, b, v_down, v_out, wider, low, high, own, pair, t, *scratch):
    v2 = solve_coarse(nx, ny, KEEP, at, (fetched, other), *scratch[:9])
    b = Field(b, E0 - 1)
    v = climb(nx, ny, KEEP, at, v2, Field(b1, E1 + 1), Field(u, E1), b, Field(v_down, E0), *scratch[9:])
    mask = row_mask((32, 256), at[1] * 16 - 8, ny)
    once, twice = Field(scratch[12], E0), Field(v_out, KEEP - 2)
    sweep(v, once, b, range(1 - KEEP, 15 + KEEP), 1, mask, at, nx, 0)
    sweep(once, twice, b, range(2 - KEEP, 14 + KEEP), 1, mask, at, nx, 0)
    coarsen_level0(at, nx, ny, b, twice, Field(own, 0), range(8), pair, t)
    for i in range(8):
        wider[NEAR + i] = own[i, 4:12, :]
    for i in range(NEAR):
        low[i] = own[i, 4:12, :]
        high[i] = own[8 - NEAR + i, 4:12, :]


def turn(nx, ny, at, coarse, b1, u, b, v_down):
    outs = [
        around_block(16, KEEP - 2, 32, 256),
        around_block(8, NEAR, 8, 128),
        (NEAR, 8, 128),
        (NEAR, 8, 128),
    ]
    scratch = [(8, 16, 128), (8, 2, 32, 128), (8, 16, 256)]
    scratch += coarse_scratch(ny, KEEP) + climb_scratch(KEEP)
    args = [at, *coarse, b1, u, b, v_down]
    return call(functools.partial(turn_body, nx, ny), outs, scratch, args, 30000000)


def finish_body(nx, ny, at, fetched, other, b1, u, b, v_down, out, *scratch):
    v2 = solve_coarse(nx, ny, 0, at, (fetched, other), *scratch[:9])
    b, v_down = Field(b, E0 - 1), Field(v_down, KEEP - 2)
    v = climb(nx, ny, 0, at, v2, Field(b1, NEAR), Field(u, NEAR - 1), b, v_down, *scratch[9:])
    for p in range(16):
        c, around = v.beside(p)
        out[p] = (0.2 * c + SIDE * (around + b[p]))[8:24, :]


def finish(nx, ny, at, coarse, b1, u, b, v_down):
    scratch = coarse_scratch(ny, 0) + climb_scratch(0)
    args = [at, *coarse, b1, u, b, v_down]
    return call(functools.partial(finish_body, nx, ny), [(16, 16, 256)], scratch, args, 20000000)[0]


def shifted(array, axis, step):
    count = lax.axis_size(axis)
    return lax.ppermute(
        array, axis, [(i, i + step) for i in range(count) if 0 <= i + step < count]
    )


def swapped(array, first):
    count = lax.axis_size("narrow")
    pairs = [(i, i + 1) for i in range(first, count - 1, 2)]
    return lax.ppermute(array, "narrow", pairs + [(j, i) for i, j in pairs])


def widen(wider, low, high):
    planes = low.shape[0]
    wider = lax.dynamic_update_slice(wider, shifted(high, "wide", 1), (0, 0, 0))
    upper = wider.shape[0] - planes
    return lax.dynamic_update_slice(wider, shifted(low, "wide", -1), (upper, 0, 0))


def surround(wider, low, high):
    mid = widen(wider, low, high)
    link = swapped(mid, 1)
    return mid, swapped(mid, 0), link


def spread_coarse(b2):
    wide, cores = lax.axis_size("wide"), lax.axis_size("narrow")
    layers = wide // GROUP
    odd = lax.rem(lax.axis_index("narrow"), 2) == 1
    other = swapped(b2, 0)
    pair = jnp.concatenate([jnp.where(odd, other, b2), jnp.where(odd, b2, other)], axis=0)
    groups = [
        [
            (((2 * k + core + i) % layers) * GROUP + x) * cores + y
            for i in range(2)
            for x in range(GROUP)
            for y in range(core, cores, 2)
        ]
        for core in range(2)
        for k in range(layers // 2)
    ]
    pieces = jnp.broadcast_to(pair[None], (len(groups[0]),) + pair.shape)
    fetched = lax.all_to_all(pieces, ("wide", "narrow"), 0, 0, axis_index_groups=groups)
    return fetched, swapped(fetched, 0)


def on_device(phase, distance, velocity):
    nx, ny = 16 * lax.axis_size("wide"), 16 * lax.axis_size("narrow")
    at = jnp.stack([lax.axis_index("wide"), lax.axis_index("narrow")]).astype(jnp.int32)
    psi, x_low, x_high = prepare(phase, distance, velocity)
    low, high = shifted(x_high, "wide", 1), shifted(x_low, "wide", -1)
    chip, link = pack(at, psi, velocity, low, high)
    v_link = swapped(link, 1)
    v_chip = swapped(chip, 0)
    moved, *sends = advance(nx, ny, at, psi, velocity, low, high, v_chip, v_link)
    b, v, b1, u, b2 = first_down(nx, ny, at, *surround(*sends))
    v, *sends = turn(nx, ny, at, spread_coarse(b2), b1, u, b, v)
    b1, u, b2 = second_down(nx, ny, at, *surround(*sends))
    pressure = finish(nx, ny, at, spread_coarse(b2), b1, u, b, v)
    return (moved, pressure)


def solution(mesh):
    blocks = P("wide", "narrow", None)
    return jax.shard_map(
        on_device,
        mesh=mesh,
        in_specs=(blocks, blocks, P(None, "wide", "narrow", None)),
        out_specs=(blocks, blocks),
        check_vma=False,
    )
```

```python
import functools

import jax
import jax.numpy as jnp
from jax import lax
from jax.experimental import pallas as pl
from jax.experimental.pallas import tpu as pltpu
from jax.sharding import PartitionSpec as P

DELTA_SQ = 0.0025
WENO_EPS = 0.01
SIDE = 0.8 / 6.0
F32 = jnp.float32

HALO = 14
KEEP = 4
NEAR = 4
GROUP = 4


def iota(shape, dim):
    return lax.broadcasted_iota(jnp.int32, shape, dim)


def roll(v, shift, axis):
    return pltpu.roll(v, shift % v.shape[axis], axis)


def z_shifted(v):
    lane = iota(v.shape, 1)
    last = v.shape[1] - 1
    lower = jnp.where(lane == 0, 0.0, roll(v, 1, 1))
    upper = jnp.where(lane == last, 0.0, roll(v, -1, 1))
    return lower, upper


def z_pair(v):
    lower, upper = z_shifted(v)
    return lower + upper


def y_pair(v):
    return roll(v, 1, 0) + roll(v, -1, 0)


def beside(ref, i):
    c = ref[i]
    return c, (ref[i - 1] + ref[i + 1]) + y_pair(c) + z_pair(c)


def inside(first, count):
    return jnp.logical_and(first >= 0, first < count)


def row_mask(shape, first, count):
    rows = iota(shape, 0) + first
    return jnp.where(inside(rows, count), 1.0, 0.0).astype(F32)


def plane_factor(index, count):
    return jnp.where(inside(index, count), 1.0, 0.0).astype(F32)


def dot(a, b):
    b = b.astype(jnp.bfloat16)
    high = a.astype(jnp.bfloat16)
    low = (a - high.astype(F32)).astype(jnp.bfloat16)
    return jnp.dot(high, b, preferred_element_type=F32) + jnp.dot(low, b, preferred_element_type=F32)


def pair_matrix(rows, cols, value):
    return jnp.where((iota((rows, cols), 0) >> 1) == iota((rows, cols), 1), value, 0.0).astype(F32)


def copy_matrix(rows, cols):
    return jnp.where(iota((rows, cols), 0) == (iota((rows, cols), 1) >> 1), 1.0, 0.0).astype(F32)


def words(shape):
    *lead, rows, lanes = (1,) * (3 - len(shape)) + tuple(shape)
    size = -(-rows // 8) * 8 * (-(-lanes // 128) * 128)
    for n in lead:
        size *= n
    return size


def call(body, outs, scratch, args, flops):
    vmem = pl.BlockSpec(memory_space=pltpu.VMEM)
    smem = pl.BlockSpec(memory_space=pltpu.SMEM)
    total = sum(words(a.shape) for a in args) + sum(map(words, outs)) + sum(map(words, scratch))
    return pl.pallas_call(
        body,
        out_shape=[jax.ShapeDtypeStruct(s, F32) for s in outs],
        in_specs=[smem if a.dtype == jnp.int32 and a.ndim == 1 else vmem for a in args],
        out_specs=[vmem] * len(outs),
        scratch_shapes=[pltpu.VMEM(s, F32) for s in scratch],
        compiler_params=pltpu.CompilerParams(vmem_limit_bytes=4 * total + (6 << 20)),
        cost_estimate=pl.CostEstimate(flops=flops, bytes_accessed=4000000, transcendentals=0),
    )(*args)


def pick_sides(at, chip, link):
    odd = lax.rem(at[1], 2) == 1
    lower = lambda *k: jnp.where(odd, chip[k], link[k])
    upper = lambda *k: jnp.where(odd, link[k], chip[k])
    return lower, upper


PARTS = 4
FAR, ALONG, ACROSS = 6, 4, 3
SENT = FAR + ALONG + 2 * ACROSS


def layer_cuts(dim):
    cuts, offset = [], FAR
    for component in range(3):
        layers = ALONG if component == dim else ACROSS
        cuts.append((component, layers, offset))
        offset += layers
    return cuts


def prepare_body(phase, distance, velocity, psi, x_low, x_high, kind, away, sems):
    step = 16 // PARTS
    copies = []

    def copy(src, dst):
        started = pltpu.make_async_copy(src, dst, sems.at[len(copies)])
        started.start()
        copies.append(started)

    for k in range(PARTS):
        planes = pl.ds(step * k, step)
        copy(phase.at[planes], kind.at[planes])
        copy(distance.at[planes], away.at[planes])
    for component, layers, offset in layer_cuts(0):
        copy(velocity.at[component, pl.ds(0, layers)], x_low.at[pl.ds(offset, layers)])
        copy(velocity.at[component, pl.ds(16 - layers, layers)], x_high.at[pl.ds(offset, layers)])
    for k in range(PARTS):
        copies[2 * k].wait()
        copies[2 * k + 1].wait()
        for i in range(step * k, step * k + step):
            orient = 2.0 * kind[i].astype(F32) - 1.0
            psi[i] = 1.0 / (1.0 + jnp.exp(-orient * away[i]))
    for k in range(FAR):
        x_low[k] = psi[k]
        x_high[k] = psi[16 - FAR + k]
    for started in copies[2 * PARTS :]:
        started.wait()


def prepare(phase, distance, velocity):
    vmem = pl.BlockSpec(memory_space=pltpu.VMEM)
    hbm = pl.BlockSpec(memory_space=pltpu.HBM)
    outs = [(16, 16, 256), (SENT, 16, 256), (SENT, 16, 256)]
    return pl.pallas_call(
        prepare_body,
        out_shape=[jax.ShapeDtypeStruct(s, F32) for s in outs],
        in_specs=[hbm, hbm, hbm],
        out_specs=[vmem] * len(outs),
        scratch_shapes=[
            pltpu.VMEM((16, 16, 256), jnp.int32),
            pltpu.VMEM((16, 16, 256), F32),
            pltpu.SemaphoreType.DMA((2 * PARTS + 6,)),
        ],
        compiler_params=pltpu.CompilerParams(vmem_limit_bytes=8 << 20),
        cost_estimate=pl.CostEstimate(flops=1000000, bytes_accessed=1000000, transcendentals=0),
    )(*(pltpu.with_memory_space_constraint(a, pltpu.HBM) for a in (phase, distance, velocity)))


def plane_of(own, low, high, p, offset, layers):
    if p < 0:
        return low[offset + layers + p]
    return own(p) if p < 16 else high[offset + p - 16]


def wide_planes(psi, velocity, low, high):
    def level(p):
        return plane_of(lambda k: psi[k], low, high, p, 0, FAR)

    def speed(component):
        _, layers, offset = layer_cuts(0)[component]

        def at_plane(p):
            if not -layers <= p < 16 + layers:
                return None
            return plane_of(lambda k: velocity[component, k], low, high, p, offset, layers)

        return at_plane

    return level, [speed(c) for c in range(3)]


def narrow_segments():
    reached = (FAR, ALONG, ALONG, ACROSS)
    rows_own = (FAR, ACROSS, ALONG, ACROSS)
    found = {}
    for p in range(16):
        offset = 0
        for field, rows in enumerate(rows_own):
            found[field, p] = (p, offset, rows)
            offset += rows
    for side, edge in enumerate((0, 15)):
        for slot, layers in enumerate(((1, 4, 5), (2, 3))):
            offset = 0
            for d in layers:
                p = edge - d if side == 0 else edge + d
                for field, reach_of in enumerate(reached):
                    rows = min(reach_of - d, rows_own[field])
                    if rows > 0:
                        found[field, p] = (16 + 2 * side + slot, offset, rows)
                        offset += rows
    return found


SEGMENTS = narrow_segments()
SLOTS = 20


def pack_body(at, psi, velocity, low, high, chip, link):
    odd = lax.rem(at[1], 2) == 1
    level, speeds = wide_planes(psi, velocity, low, high)
    fields = [level] + speeds
    for k in range(SLOTS):
        inside_slot = [(offset, f, p, rows) for (f, p), (slot, offset, rows) in SEGMENTS.items() if slot == k]
        first, final, total = [], [], 0
        for offset, f, p, rows in sorted(inside_slot):
            v = fields[f](p)
            first.append(v[0:rows])
            final.append(v[16 - rows : 16])
            total += rows
        if total < SENT:
            first.append(jnp.zeros((SENT - total, 256), F32))
            final.append(first[-1])
        first = jnp.concatenate(first, axis=0)
        final = jnp.concatenate(final, axis=0)
        chip[k] = jnp.where(odd, first, final)
        link[k] = jnp.where(odd, final, first)


def pack(at, psi, velocity, low, high):
    outs = [(SLOTS, SENT, 256)] * 2
    return call(pack_body, outs, [], [at, psi, velocity, low, high], 1000000)


FACE = 0.25 / 12.0


def indicators(a, b, c):
    d = a - c
    curve = (a + c) - 2.0 * b
    twice = 2.0 * curve
    base = (13.0 / 12.0) * (curve * curve) + WENO_EPS
    up, down = twice - d, twice + d
    p = base + 0.25 * (up * up)
    q = base + 0.25 * (d * d)
    r = base + 0.25 * (down * down)
    return p * p, q * q, r * r


def upwind_flux(s, l, p_left, q_left, r_left, p_right, q_right, r_right):
    ahead = s > 0.0
    pick = lambda x, y: jnp.where(ahead, x, y)
    a, b, c, e, f = pick(l[0], l[5]), pick(l[1], l[4]), pick(l[2], l[3]), pick(l[3], l[2]), pick(l[4], l[1])
    p, q, r = pick(p_left, r_right), pick(q_left, q_right), pick(r_left, p_right)
    w0, w1, w2 = q * r, 6.0 * (p * r), 3.0 * (p * q)
    g0 = 2.0 * a - 7.0 * b + 11.0 * c
    g1 = 5.0 * c + 2.0 * e - b
    g2 = 2.0 * c + 5.0 * e - f
    top = w0 * g0 + w1 * g1 + w2 * g2
    total = w0 + w1 + w2
    return (s * top) / total


def z_change(v, w):
    lane = iota(v.shape, 1)

    def ahead(x, k):
        return jnp.where(lane > 255 - k, 0.0, roll(x, -k, 1))

    def behind(x, k):
        return jnp.where(lane < k, 0.0, roll(x, k, 1))

    l = [behind(v, 2), behind(v, 1), v, ahead(v, 1), ahead(v, 2), ahead(v, 3)]
    s = FACE * (w + ahead(w, 1))
    p, q, r = indicators(l[1], l[2], l[3])
    _, q1, r1 = indicators(l[2], l[3], l[4])
    _, _, r2 = indicators(l[3], l[4], l[5])
    p0, _, _ = indicators(l[0], l[1], l[2])
    flux = upwind_flux(s, l, p0, q, r1, p, q1, r2)
    low = slice(0, 128)
    c = v[:, low]
    none = jnp.zeros_like(c)
    square = c * c
    edge = WENO_EPS + (13.0 / 12.0 + 9.0 / 4.0) * square
    level = WENO_EPS + (13.0 / 12.0 + 1.0 / 4.0) * square
    wall_flux = upwind_flux(
        FACE * w[:, low],
        [none, none, none, c, l[3][:, low], l[4][:, low]],
        none + WENO_EPS * WENO_EPS, level * level, r[:, low],
        edge * edge, q[:, low], r1[:, low],
    )
    wall_flux = jnp.concatenate([wall_flux, wall_flux], axis=1)
    return flux - jnp.where(lane == 0, wall_flux, roll(flux, 1, 1))


def y_change(v, w):
    s = FACE * (w + roll(w, -1, 0))
    l = [roll(v, 2 - k, 0) for k in range(6)]
    p, q, r = indicators(l[1], l[2], l[3])
    q_next, r_next = roll(q, -1, 0), roll(r, -1, 0)
    flux = upwind_flux(s, l, roll(p, 1, 0), q, r_next, p, q_next, roll(r, -2, 0))
    return flux - roll(flux, 1, 0)


SKIN = 3


def x_marks(v, planes, marks):
    for i in range(planes):
        marks[0][i], marks[1][i], marks[2][i] = indicators(v(i - FAR), v(i - FAR + 1), v(i - FAR + 2))


def x_flux(f, v, w, marks):
    p_x, q_x, r_x = marks
    l = [v(f - 3 + k) for k in range(6)]
    return upwind_flux(
        FACE * (w(f - 1) + w(f)), l,
        p_x[f + 3], q_x[f + 4], r_x[f + 5], p_x[f + 4], q_x[f + 5], r_x[f + 6],
    )


def xz_change(v, u, w, marks, out):
    x_marks(v, 26, marks)
    below = x_flux(-SKIN, v, u, marks)
    for p in range(-SKIN, 16 + SKIN):
        above = x_flux(p + 1, v, u, marks)
        out[p + SKIN] = (above - below) + z_change(v(p), w(p))
        below = above


def inner_body(psi, velocity, low, high, out, *marks):
    level, speeds = wide_planes(psi, velocity, low, high)
    xz_change(level, speeds[0], speeds[2], marks, out)


def inner(psi, velocity, low, high):
    block = (16 + 2 * SKIN, 16, 256)
    scratch = [(26, 16, 256)] * 3
    return call(inner_body, [block], scratch, [psi, velocity, low, high], 8000000)[0]


def advance_body(
    nx, ny, at, psi, velocity, low, high, chip, link, change_in, moved, source, first, final,
    v8, u8, w8, v32, u32, c8, p_x, q_x, r_x, m, n_x, n_y, n_z, s_x, part,
):
    lower, upper = pick_sides(at, chip, link)
    level, speeds = wide_planes(psi, velocity, low, high)
    fields = [level] + speeds

    def halo(field, p, most):
        if (field, p) not in SEGMENTS:
            return 0, None, None
        slot, offset, rows = SEGMENTS[field, p]
        count = min(most, rows)
        below = lower(slot)[offset + rows - count : offset + rows]
        return count, below, upper(slot)[offset : offset + count]

    def beside_only(ref, i, field, p):
        ref[i] = jnp.zeros((8, 256), F32)
        count, below, above = halo(field, p, 4)
        if count:
            ref[i, 4 - count : 4, :] = below
            ref[i, 4 : 4 + count, :] = above

    def with_rows(ref, i, field, p, start):
        total = ref.shape[1]
        ref[i, 0:start, :] = jnp.zeros((start, 256), F32)
        ref[i, start + 16 : total, :] = jnp.zeros((total - start - 16, 256), F32)
        count, below, above = halo(field, p, start)
        ref[i, start : start + 16, :] = fields[field](p)
        if count:
            ref[i, start - count : start, :] = below
            ref[i, start + 16 : start + 16 + count, :] = above

    for p in range(-FAR, 16 + FAR):
        beside_only(v8, p + FAR, 0, p)
        if -ALONG <= p < 16 + ALONG:
            beside_only(u8, p + ALONG, 1, p)
        if -SKIN <= p < 16 + SKIN:
            beside_only(w8, p + SKIN, 3, p)
            with_rows(v32, p + SKIN, 0, p, 8)
            with_rows(u32, p + SKIN, 2, p, 8)

    xz_change(
        lambda p: v8[p + FAR], lambda p: u8[p + ALONG], lambda p: w8[p + SKIN], (p_x, q_x, r_x), c8
    )
    shape = (24, 256)
    mask = row_mask(shape, at[1] * 16 - 4, ny)
    for p in range(-SKIN, 16 + SKIN):
        i = p + SKIN
        sides = c8[i]
        change = jnp.concatenate([sides[0:4], change_in[i], sides[4:8]], axis=0)
        v = v32[i]
        change = change + y_change(v, u32[i])[4:28, :]
        value = wall(at, nx, 0, p, (v[4:28, :] - change) * mask)
        m[i] = value
        if 0 <= p < 16:
            moved[p] = value[4:20, :]

    lane = iota(shape, 1)

    def gradient(p):
        c = m[p + SKIN]
        down, ahead = z_shifted(c)
        gx = 0.5 * (m[p + SKIN + 1] - m[p + SKIN - 1])
        gy = 0.5 * (roll(c, -1, 0) - roll(c, 1, 0))
        return gx, gy, 0.5 * (ahead - down)

    for p in range(-2, 18):
        gx, gy, gz = gradient(p)
        inverse = lax.rsqrt(gx * gx + gy * gy + gz * gz + DELTA_SQ)
        n_x[p + 2], n_y[p + 2], n_z[p + 2] = gx * inverse, gy * inverse, gz * inverse
    for p in range(-1, 17):
        gx, gy, gz = gradient(p)
        edge = 0.5 * m[p + SKIN]
        edge = edge * lax.rsqrt(edge * edge + DELTA_SQ)
        nz, ny_here = n_z[p + 2], n_y[p + 2]
        ahead = jnp.where(lane == 255, -edge, roll(nz, -1, 1))
        behind = jnp.where(lane == 0, edge, roll(nz, 1, 1))
        bending = -0.5 * (
            (n_x[p + 3] - n_x[p + 1])
            + (roll(ny_here, -1, 0) - roll(ny_here, 1, 0))
            + (ahead - behind)
        )
        bending = wall(at, nx, 0, p, bending * mask)
        s_x[p + 1] = (bending * gx)[4:20, :] + speeds[0](p)
        if 0 <= p < 16:
            sy = bending * gy + u32[p + SKIN, 4:28, :]
            dy = roll(sy, -1, 0) - roll(sy, 1, 0)
            sz = (bending * gz)[4:20, :] + velocity[2, p]
            behind, ahead = z_shifted(sz)
            part[p] = dy[4:20, :] + (ahead - behind)
    for p in range(16):
        source[p] = -0.5 * (part[p] + (s_x[p + 2] - s_x[p]))
    for i in range(HALO):
        first[i] = source[i]
        final[i] = source[16 - HALO + i]


def advance(nx, ny, at, psi, velocity, low, high, chip, link, change):
    marks, normals, block = (26, 8, 256), (20, 24, 256), (16, 16, 256)
    skin = 16 + 2 * SKIN
    scratch = [
        (16 + 2 * FAR, 8, 256), (16 + 2 * ALONG, 8, 256), (skin, 8, 256), (skin, 32, 256),
        (skin, 32, 256), (skin, 8, 256), marks, marks, marks,
        (skin, 24, 256), normals, normals, normals, (18, 16, 256), block,
    ]
    args = [at, psi, velocity, low, high, chip, link, change]
    outs = [block, block, (HALO, 16, 256), (HALO, 16, 256)]
    return call(functools.partial(advance_body, nx, ny), outs, scratch, args, 30000000)


class Field:
    def __init__(self, ref, lead):
        self.ref, self.lead = ref, lead

    def __getitem__(self, p):
        return self.ref[p + self.lead]

    def __setitem__(self, p, value):
        self.ref[p + self.lead] = value

    def beside(self, p):
        return beside(self.ref, p + self.lead)


def wall(at, nx, level, p, value):
    own = 16 >> level
    if 0 <= p < own:
        return value
    return value * plane_factor(at[0] * own + p, nx >> level)


def first_smooth(b, v, planes, weight, mask, at, nx, level):
    for p in planes:
        c, around = b.beside(p)
        v[p] = wall(at, nx, level, p, (weight * mask) * (1.2 * c + SIDE * around))


def sweep(src, dst, b, planes, factor, mask, at, nx, level):
    keep = SIDE * mask
    for p in planes:
        c, around = src.beside(p)
        near = around + (b[p] if factor == 1 else factor * b[p])
        dst[p] = 0.2 * c + wall(at, nx, level, p, keep) * near


def coarsen_level0(at, nx, ny, b, v, b1, planes, pair, t):
    first = planes[0]
    rows = t.shape[1]

    def residual(p):
        c, around = v.beside(p)
        return b[p] - (6.0 * c - around)

    for p in planes:
        total = residual(2 * p) + residual(2 * p + 1)
        for half in range(2):
            lanes = slice(128 * half, 128 * half + 128)
            pair[p - first, half] = total[:, lanes]
            even = pair[p - first, half, pl.ds(0, rows, stride=2), :]
            odd = pair[p - first, half, pl.ds(1, rows, stride=2), :]
            t[p - first, :, lanes] = even + odd
    count = len(planes)
    full = dot(t[...].reshape(count * rows, 256), pair_matrix(256, 128, 0.125))
    full = full.reshape(count, rows, 128)
    mask = row_mask((rows, 128), at[1] * 8 + 4 - rows // 2, ny // 2)
    for p in planes:
        b1[p] = wall(at, nx, 1, p, full[p - first] * mask)


def smooth_level1(at, nx, ny, b1, u, planes):
    rows = b1.ref.shape[1]
    mask = row_mask((rows, 128), at[1] * 8 + 4 - rows // 2, ny // 2)
    first_smooth(b1, u, planes, 4.0 * SIDE, mask, at, nx, 1)


def coarsen_level1(b1, u, b2_out, s1, t1):
    start = b1.ref.shape[1] // 2 - 4
    t1[...] = jnp.zeros_like(t1)
    for k in range(4):
        total = 0.0
        for p in (2 * k, 2 * k + 1):
            c, around = u.beside(p)
            total = total + (b1[p] - 0.25 * (6.0 * c - around))
        s1[k] = total
        t1[k, 0:4, :] = s1[k, pl.ds(start, 4, stride=2), :] + s1[k, pl.ds(start + 1, 4, stride=2), :]
    small = dot(t1[...].reshape(32, 128), pair_matrix(128, 128, 0.125)).reshape(4, 8, 128)
    tile = jnp.concatenate([small[0, 0:4], small[1, 0:4]], axis=0) + roll(
        jnp.concatenate([small[2, 0:4], small[3, 0:4]], axis=0), 64, 1
    )
    b2_out[...] = tile


def reach(extra):
    e0 = extra + 2
    r1 = -(-e0 // 2)
    e1 = r1 + 2
    r2 = -(-e1 // 2)
    e2 = r2 + 2
    r3 = -(-e2 // 2)
    return e0, r1, e1, r2, e2, r3


E0, R1, E1, R2, E2, R3 = reach(KEEP)


def source_segments():
    whole, parts = [], []
    for p in range(-HALO, 16 + HALO):
        d = max(-p, p - 15, 0)
        rows = 16 - max(d, 2)
        if rows >= 8:
            whole.append((p, 0, 8))
        if rows % 8:
            parts.append((p, rows // 8 * 8, rows % 8))
    found = [(p, n, rows, tile, 0) for tile, (p, n, rows) in enumerate(whole)]
    room = []
    for p, n, rows in sorted(parts, key=lambda part: (-part[2], part[0])):
        for k, used in enumerate(room):
            if used + rows <= 8:
                break
        else:
            k = len(room)
            room.append(0)
        found.append((p, n, rows, len(whole) + k, room[k]))
        room[k] += rows
    return found, len(whole) + len(room)


SOURCE_SEGMENTS, SOURCE_TILES = source_segments()


def source_plane(own, low, high, p):
    return low[p + HALO] if p < 0 else own[p] if p < 16 else high[p - 16]


def weave_body(at, own, low, high, chip, link):
    odd = lax.rem(at[1], 2) == 1
    for k in range(SOURCE_TILES):
        first, final, total = [], [], 0
        for p, n, rows, tile, offset in sorted(SOURCE_SEGMENTS, key=lambda part: part[4]):
            if tile == k:
                v = source_plane(own, low, high, p)
                first.append(v[n : n + rows])
                final.append(v[16 - n - rows : 16 - n])
                total += rows
        if total < 8:
            first.append(jnp.zeros((8 - total, 256), F32))
            final.append(first[-1])
        if len(first) > 1:
            first = [jnp.concatenate(first, axis=0)]
            final = [jnp.concatenate(final, axis=0)]
        chip[k] = jnp.where(odd, first[0], final[0])
        link[k] = jnp.where(odd, final[0], first[0])


def weave(at, own, low, high):
    outs = [(SOURCE_TILES, 8, 256)] * 2
    return call(weave_body, outs, [], [at, own, low, high], 1000000)


def first_down_body(
    nx, ny, at, own, low, high, chip, link, b_out, v_out, b1_out, u_out, b2_out, b, v, pair, t, s1, t1
):
    lower, upper = pick_sides(at, chip, link)
    none = jnp.zeros((16, 256), F32)
    for p in range(-HALO, 16 + HALO):
        b[p + HALO, 0:16, :] = none
        b[p + HALO, 16:32, :] = source_plane(own, low, high, p)
        b[p + HALO, 32:48, :] = none
    for p, n, rows, tile, offset in SOURCE_SEGMENTS:
        cut = slice(offset, offset + rows)
        b[p + HALO, 16 - n - rows : 16 - n, :] = lower(tile)[cut]
        b[p + HALO, 32 + n : 32 + n + rows, :] = upper(tile)[cut]
    b, v = Field(b, HALO), Field(v, HALO - 1)
    mask = row_mask((48, 256), at[1] * 16 - 16, ny)
    first_smooth(b, v, range(1 - HALO, 15 + HALO), SIDE, mask, at, nx, 0)
    v_out, b_out = Field(v_out, E0), Field(b_out, E0 - 1)
    for p in range(-E0, 16 + E0):
        v_out[p] = v[p][8:40, :]
    for p in range(1 - E0, 15 + E0):
        b_out[p] = b[p][8:40, :]
    b1, u = Field(b1_out, E1 + 1), Field(u_out, E1)
    coarsen_level0(at, nx, ny, b, v, b1, range(-E1 - 1, 9 + E1), pair, t)
    smooth_level1(at, nx, ny, b1, u, range(-E1, 8 + E1))
    coarsen_level1(b1, u, b2_out, s1, t1)


def around_block(size, extra, rows, lanes):
    return (size + 2 * extra, rows, lanes)


def first_down(nx, ny, at, own, low, high, chip, link):
    level1 = around_block(8, E1 + 1, 24, 128)
    outs = [
        around_block(16, E0 - 1, 32, 256),
        around_block(16, E0, 32, 256),
        level1,
        around_block(8, E1, 24, 128),
        (8, 128),
    ]
    scratch = [
        around_block(16, HALO, 48, 256),
        around_block(16, HALO - 1, 48, 256),
        (level1[0], 2, 48, 128),
        (level1[0], 24, 256),
        (4, 24, 128),
        (4, 8, 128),
    ]
    args = [at, own, low, high, chip, link]
    return call(functools.partial(first_down_body, nx, ny), outs, scratch, args, 20000000)


def second_down_body(nx, ny, at, mid, chip, link, b1_out, u_out, b2_out, s1, t1):
    lower, upper = pick_sides(at, chip, link)
    for i in range(8 + 2 * NEAR):
        b1_out[i, 0:8, :] = lower(i)
        b1_out[i, 8:16, :] = mid[i]
        b1_out[i, 16:24, :] = upper(i)
    b1, u = Field(b1_out, NEAR), Field(u_out, NEAR - 1)
    smooth_level1(at, nx, ny, b1, u, range(1 - NEAR, 7 + NEAR))
    coarsen_level1(b1, u, b2_out, s1, t1)


def second_down(nx, ny, at, mid, chip, link):
    outs = [around_block(8, NEAR, 24, 128), around_block(8, NEAR - 1, 24, 128), (8, 128)]
    scratch = [(4, 24, 128), (4, 8, 128)]
    args = [at, mid, chip, link]
    return call(functools.partial(second_down_body, nx, ny), outs, scratch, args, 2000000)


def solve_coarse(nx, ny, extra, at, coarse, s2, v2, w2, t3, b3, c3, d3, dup, row2):
    fetched, other = coarse
    odd = lax.rem(at[1], 2) == 1
    odd_layer = lax.rem(at[0] // GROUP, 2)
    _, _, _, r2, e2, r3 = reach(extra)
    spot = at[0] % GROUP
    rows2 = ny // 4
    rows3 = rows2 // 2
    count = rows2 // 4
    lead = 2 * (r3 + 3) + 2
    blocks = -(-lead // 4)
    s2, v2, w2 = Field(s2, 4 * blocks), Field(v2, lead - 1), Field(w2, e2)
    lane8 = iota((8, 128), 1) < 64
    for j in range(-blocks, blocks + 1):
        block = spot + GROUP + j
        layer, place = block // GROUP, block % GROUP
        first_cores = jnp.where(odd_layer == 1, layer <= 1, layer >= 1)
        mine = first_cores != odd
        inner = inside(at[0] + j, nx // 16)
        start = ((layer + odd_layer) // 2) * (GROUP * count // 2) + place * (count // 2)
        for n in range(count):
            rows = slice(8 * (n % 2), 8 * (n % 2) + 8)
            k = start + n // 2
            tile = jnp.where(mine, fetched[k, rows, :], other[k, rows, :])
            tile = jnp.where(inner, tile, 0.0)
            halves = (jnp.where(lane8, tile, 0.0), jnp.where(lane8, roll(tile, 64, 1), 0.0))
            for p in range(4):
                part = halves[p // 2][4 * (p % 2) : 4 * (p % 2) + 4, :]
                s2.ref[4 * (j + blocks) + p, 4 * n : 4 * n + 4, :] = part

    def around(f, p):
        c = f[p]
        row = iota(c.shape, 0)
        lower = jnp.where(row == 0, 0.0, roll(c, 1, 0))
        upper = jnp.where(row == c.shape[0] - 1, 0.0, roll(c, -1, 0))
        beside = (lower + upper) + (roll(c, 1, 1) + roll(c, -1, 1))
        return c, (f[p - 1] + f[p + 1]) + beside

    def lanes_below(rows, lanes):
        return jnp.where(iota((rows, 128), 1) < lanes, 1.0, 0.0).astype(F32)

    mask2 = lanes_below(rows2, 64)
    for p in range(1 - lead, 3 + lead):
        c, near = around(s2, p)
        v2[p] = wall(at, nx, 2, p, (16.0 * SIDE) * mask2 * (1.2 * c + SIDE * near))

    def residual2(p):
        c, near = around(v2, p)
        return s2[p] - (1.0 / 16.0) * (6.0 * c - near)

    planes3 = range(-r3 - 3, 2 + r3 + 3)
    for i, p in enumerate(planes3):
        row2[i] = residual2(2 * p) + residual2(2 * p + 1)
        t3[i] = row2[i, pl.ds(0, rows3, stride=2), :] + row2[i, pl.ds(1, rows3, stride=2), :]
    total3 = len(planes3)
    full = dot(t3[...].reshape(total3 * rows3, 128), pair_matrix(128, 128, 0.125))
    full = full.reshape(total3, rows3, 128)
    mask3 = lanes_below(rows3, 32)
    b3, c3, d3 = Field(b3, r3 + 3), Field(c3, r3 + 3), Field(d3, r3 + 3)
    for i, p in enumerate(planes3):
        value = wall(at, nx, 3, p, full[i] * ((64.0 * SIDE) * mask3))
        b3[p] = value
    src, dst = b3, c3
    for step in (2, 1, 0):
        for p in range(-r3 - step, 2 + r3 + step):
            c, near = around(src, p)
            dst[p] = wall(at, nx, 3, p, mask3 * (0.2 * c + SIDE * near)) + b3[p]
        src, dst = dst, (d3 if dst is c3 else c3)
    final = src
    planes = range(-r3, 2 + r3)
    flat = jnp.concatenate([final[p] for p in planes], axis=0)
    spread = dot(flat, copy_matrix(128, 128)).reshape(len(planes), rows3, 128)
    for i, p in enumerate(planes):
        dup[i, pl.ds(0, rows3, stride=2), :] = spread[i]
        dup[i, pl.ds(1, rows3, stride=2), :] = spread[i]
        for q in (2 * p, 2 * p + 1):
            if -e2 <= q < 4 + e2:
                v2[q] = v2[q] + wall(at, nx, 2, q, dup[i, 0:rows2, :] * mask2)
    keep = SIDE * mask2
    for src, dst, step in ((v2, w2, 1), (w2, v2, 0)):
        for p in range(-r2 - step, 4 + r2 + step):
            c, near = around(src, p)
            dst[p] = 0.2 * c + wall(at, nx, 2, p, keep) * (near + 16.0 * s2[p])
    return v2


def coarse_scratch(ny, extra):
    _, _, _, _, e2, r3 = reach(extra)
    rows2 = ny // 4
    rows3 = rows2 // 2
    lead = 2 * (r3 + 3) + 2
    small = around_block(2, r3 + 3, rows3, 128)
    return [
        around_block(4, -(-lead // 4) * 4, rows2, 128),
        around_block(4, lead - 1, rows2, 128),
        around_block(4, e2, rows2, 128),
        small, small, small, small,
        (8, 48, 128),
        around_block(2, r3 + 3, rows2, 128),
    ]


def climb(nx, ny, extra, at, v2, b1, u, b, v_down, m1, n1, m0, n0, dup):
    e0, r1, e1, r2, _, _ = reach(extra)
    rows2 = ny // 4
    turn = lax.rem(rows2 + 4 - 4 * at[1] + rows2, rows2)
    planes = range(-r2, 4 + r2)
    picked = jnp.concatenate([pltpu.roll(v2[p], turn, 0)[0:16, :] for p in planes], axis=0)
    spread = dot(picked, copy_matrix(128, 128)).reshape(len(planes), 16, 128)
    mask1 = row_mask((24, 128), at[1] * 8 - 8, ny // 2)
    m1, n1 = Field(m1, e1), Field(n1, e1)
    for i, p in enumerate(planes):
        dup[i, 0, pl.ds(0, 12, stride=2), :] = spread[i, 0:12, :]
        dup[i, 0, pl.ds(1, 12, stride=2), :] = spread[i, 0:12, :]
        for q in (2 * p, 2 * p + 1):
            if -e1 <= q < 8 + e1:
                m1[q] = u[q] + wall(at, nx, 1, q, dup[i, 0, 0:24, :] * mask1)
    sweep(m1, n1, b1, range(1 - e1, 7 + e1), 4.0, mask1, at, nx, 1)
    sweep(n1, m1, b1, range(2 - e1, 6 + e1), 4.0, mask1, at, nx, 1)
    planes = range(-r1, 8 + r1)
    flat = jnp.concatenate([m1[p][4:20, :] for p in planes], axis=0)
    spread = dot(flat, copy_matrix(128, 256)).reshape(len(planes), 16, 256)
    mask0 = row_mask((32, 256), at[1] * 16 - 8, ny)
    m0, n0 = Field(m0, e0), Field(n0, e0)
    for i, p in enumerate(planes):
        for half in range(2):
            value = spread[i, :, 128 * half : 128 * half + 128]
            dup[i, half, pl.ds(0, 16, stride=2), :] = value
            dup[i, half, pl.ds(1, 16, stride=2), :] = value
        value = jnp.concatenate([dup[i, 0], dup[i, 1]], axis=1) * mask0
        for q in (2 * p, 2 * p + 1):
            if -e0 <= q < 16 + e0:
                m0[q] = v_down[q] + wall(at, nx, 0, q, value)
    sweep(m0, n0, b, range(1 - e0, 15 + e0), 1, mask0, at, nx, 0)
    if extra:
        sweep(n0, m0, b, range(2 - e0, 14 + e0), 1, mask0, at, nx, 0)
        return m0
    return n0


def climb_scratch(extra):
    e0, r1, e1, r2, _, _ = reach(extra)
    level1 = around_block(8, e1, 24, 128)
    level0 = around_block(16, e0, 32, 256)
    return [level1, level1, level0, level0, (max(8 + 2 * r1, 4 + 2 * r2), 2, 32, 128)]


def turn_body(nx, ny, at, fetched, other, b1, u, b, v_down, v_out, wider, low, high, own, pair, t, *scratch):
    v2 = solve_coarse(nx, ny, KEEP, at, (fetched, other), *scratch[:9])
    b = Field(b, E0 - 1)
    v = climb(nx, ny, KEEP, at, v2, Field(b1, E1 + 1), Field(u, E1), b, Field(v_down, E0), *scratch[9:])
    mask = row_mask((32, 256), at[1] * 16 - 8, ny)
    once, twice = Field(scratch[12], E0), Field(v_out, KEEP - 2)
    sweep(v, once, b, range(1 - KEEP, 15 + KEEP), 1, mask, at, nx, 0)
    sweep(once, twice, b, range(2 - KEEP, 14 + KEEP), 1, mask, at, nx, 0)
    coarsen_level0(at, nx, ny, b, twice, Field(own, 0), range(8), pair, t)
    for i in range(8):
        wider[NEAR + i] = own[i, 4:12, :]
    for i in range(NEAR):
        low[i] = own[i, 4:12, :]
        high[i] = own[8 - NEAR + i, 4:12, :]


def turn(nx, ny, at, coarse, b1, u, b, v_down):
    outs = [
        around_block(16, KEEP - 2, 32, 256),
        around_block(8, NEAR, 8, 128),
        (NEAR, 8, 128),
        (NEAR, 8, 128),
    ]
    scratch = [(8, 16, 128), (8, 2, 32, 128), (8, 16, 256)]
    scratch += coarse_scratch(ny, KEEP) + climb_scratch(KEEP)
    args = [at, *coarse, b1, u, b, v_down]
    return call(functools.partial(turn_body, nx, ny), outs, scratch, args, 30000000)


def finish_body(nx, ny, at, fetched, other, b1, u, b, v_down, out, *scratch):
    v2 = solve_coarse(nx, ny, 0, at, (fetched, other), *scratch[:9])
    b, v_down = Field(b, E0 - 1), Field(v_down, KEEP - 2)
    v = climb(nx, ny, 0, at, v2, Field(b1, NEAR), Field(u, NEAR - 1), b, v_down, *scratch[9:])
    for p in range(16):
        c, around = v.beside(p)
        out[p] = (0.2 * c + SIDE * (around + b[p]))[8:24, :]


def finish(nx, ny, at, coarse, b1, u, b, v_down):
    scratch = coarse_scratch(ny, 0) + climb_scratch(0)
    args = [at, *coarse, b1, u, b, v_down]
    return call(functools.partial(finish_body, nx, ny), [(16, 16, 256)], scratch, args, 20000000)[0]


def shifted(array, axis, step):
    count = lax.axis_size(axis)
    return lax.ppermute(
        array, axis, [(i, i + step) for i in range(count) if 0 <= i + step < count]
    )


def swapped(array, first):
    count = lax.axis_size("narrow")
    pairs = [(i, i + 1) for i in range(first, count - 1, 2)]
    return lax.ppermute(array, "narrow", pairs + [(j, i) for i, j in pairs])


def widen(wider, low, high):
    planes = low.shape[0]
    wider = lax.dynamic_update_slice(wider, shifted(high, "wide", 1), (0, 0, 0))
    upper = wider.shape[0] - planes
    return lax.dynamic_update_slice(wider, shifted(low, "wide", -1), (upper, 0, 0))


def surround(wider, low, high):
    mid = widen(wider, low, high)
    link = swapped(mid, 1)
    return mid, swapped(mid, 0), link


def spread_coarse(b2):
    wide, cores = lax.axis_size("wide"), lax.axis_size("narrow")
    layers = wide // GROUP
    odd = lax.rem(lax.axis_index("narrow"), 2) == 1
    other = swapped(b2, 0)
    pair = jnp.concatenate([jnp.where(odd, other, b2), jnp.where(odd, b2, other)], axis=0)
    groups = [
        [
            (((2 * k + core + i) % layers) * GROUP + x) * cores + y
            for i in range(2)
            for x in range(GROUP)
            for y in range(core, cores, 2)
        ]
        for core in range(2)
        for k in range(layers // 2)
    ]
    pieces = jnp.broadcast_to(pair[None], (len(groups[0]),) + pair.shape)
    fetched = lax.all_to_all(pieces, ("wide", "narrow"), 0, 0, axis_index_groups=groups)
    return fetched, swapped(fetched, 0)


def on_device(phase, distance, velocity):
    nx, ny = 16 * lax.axis_size("wide"), 16 * lax.axis_size("narrow")
    at = jnp.stack([lax.axis_index("wide"), lax.axis_index("narrow")]).astype(jnp.int32)
    psi, x_low, x_high = prepare(phase, distance, velocity)
    low, high = shifted(x_high, "wide", 1), shifted(x_low, "wide", -1)
    chip, link = pack(at, psi, velocity, low, high)
    v_link = swapped(link, 1)
    v_chip = swapped(chip, 0)
    change = inner(psi, velocity, low, high)
    moved, source, first, final = advance(
        nx, ny, at, psi, velocity, low, high, v_chip, v_link, change
    )
    low, high = shifted(final, "wide", 1), shifted(first, "wide", -1)
    chip, link = weave(at, source, low, high)
    b_link = swapped(link, 1)
    b_chip = swapped(chip, 0)
    b, v, b1, u, b2 = first_down(nx, ny, at, source, low, high, b_chip, b_link)
    v, *sends = turn(nx, ny, at, spread_coarse(b2), b1, u, b, v)
    b1, u, b2 = second_down(nx, ny, at, *surround(*sends))
    pressure = finish(nx, ny, at, spread_coarse(b2), b1, u, b, v)
    return (moved, pressure)


def solution(mesh):
    blocks = P("wide", "narrow", None)
    return jax.shard_map(
        on_device,
        mesh=mesh,
        in_specs=(blocks, blocks, P(None, "wide", "narrow", None)),
        out_specs=(blocks, blocks),
        check_vma=False,
    )
```

```python
import functools

import jax
import jax.numpy as jnp
from jax import lax
from jax.experimental import pallas as pl
from jax.experimental.pallas import tpu as pltpu
from jax.sharding import PartitionSpec as P

DELTA_SQ = 0.0025
WENO_EPS = 0.01
SIDE = 0.8 / 6.0
F32 = jnp.float32

HALO = 14
KEEP = 4
NEAR = 4
GROUP = 4


def iota(shape, dim):
    return lax.broadcasted_iota(jnp.int32, shape, dim)


def roll(v, shift, axis):
    return pltpu.roll(v, shift % v.shape[axis], axis)


def z_shifted(v):
    lane = iota(v.shape, 1)
    last = v.shape[1] - 1
    lower = jnp.where(lane == 0, 0.0, roll(v, 1, 1))
    upper = jnp.where(lane == last, 0.0, roll(v, -1, 1))
    return lower, upper


def z_pair(v):
    lower, upper = z_shifted(v)
    return lower + upper


def y_pair(v):
    return roll(v, 1, 0) + roll(v, -1, 0)


def beside(ref, i):
    c = ref[i]
    return c, (ref[i - 1] + ref[i + 1]) + y_pair(c) + z_pair(c)


def inside(first, count):
    return jnp.logical_and(first >= 0, first < count)


def row_mask(shape, first, count):
    rows = iota(shape, 0) + first
    return jnp.where(inside(rows, count), 1.0, 0.0).astype(F32)


def plane_factor(index, count):
    return jnp.where(inside(index, count), 1.0, 0.0).astype(F32)


def dot(a, b):
    b = b.astype(jnp.bfloat16)
    high = a.astype(jnp.bfloat16)
    low = (a - high.astype(F32)).astype(jnp.bfloat16)
    return jnp.dot(high, b, preferred_element_type=F32) + jnp.dot(low, b, preferred_element_type=F32)


def pair_matrix(rows, cols, value):
    return jnp.where((iota((rows, cols), 0) >> 1) == iota((rows, cols), 1), value, 0.0).astype(F32)


def copy_matrix(rows, cols):
    return jnp.where(iota((rows, cols), 0) == (iota((rows, cols), 1) >> 1), 1.0, 0.0).astype(F32)


def words(shape):
    *lead, rows, lanes = (1,) * (3 - len(shape)) + tuple(shape)
    size = -(-rows // 8) * 8 * (-(-lanes // 128) * 128)
    for n in lead:
        size *= n
    return size


def call(body, outs, scratch, args, flops):
    vmem = pl.BlockSpec(memory_space=pltpu.VMEM)
    smem = pl.BlockSpec(memory_space=pltpu.SMEM)
    total = sum(words(a.shape) for a in args) + sum(map(words, outs)) + sum(map(words, scratch))
    return pl.pallas_call(
        body,
        out_shape=[jax.ShapeDtypeStruct(s, F32) for s in outs],
        in_specs=[smem if a.dtype == jnp.int32 and a.ndim == 1 else vmem for a in args],
        out_specs=[vmem] * len(outs),
        scratch_shapes=[pltpu.VMEM(s, F32) for s in scratch],
        compiler_params=pltpu.CompilerParams(vmem_limit_bytes=4 * total + (6 << 20)),
        cost_estimate=pl.CostEstimate(flops=flops, bytes_accessed=4000000, transcendentals=0),
    )(*args)


def pick_sides(at, chip, link):
    odd = lax.rem(at[1], 2) == 1
    lower = lambda *k: jnp.where(odd, chip[k], link[k])
    upper = lambda *k: jnp.where(odd, link[k], chip[k])
    return lower, upper


PARTS = 4
FAR, ALONG, ACROSS = 6, 4, 3
SENT = FAR + ALONG + 2 * ACROSS


def layer_cuts(dim):
    cuts, offset = [], FAR
    for component in range(3):
        layers = ALONG if component == dim else ACROSS
        cuts.append((component, layers, offset))
        offset += layers
    return cuts


def prepare_body(phase, distance, velocity, psi, x_low, x_high, kind, away, sems):
    step = 16 // PARTS
    copies = []

    def copy(src, dst):
        started = pltpu.make_async_copy(src, dst, sems.at[len(copies)])
        started.start()
        copies.append(started)

    for k in range(PARTS):
        planes = pl.ds(step * k, step)
        copy(phase.at[planes], kind.at[planes])
        copy(distance.at[planes], away.at[planes])
    for component, layers, offset in layer_cuts(0):
        copy(velocity.at[component, pl.ds(0, layers)], x_low.at[pl.ds(offset, layers)])
        copy(velocity.at[component, pl.ds(16 - layers, layers)], x_high.at[pl.ds(offset, layers)])
    for k in range(PARTS):
        copies[2 * k].wait()
        copies[2 * k + 1].wait()
        for i in range(step * k, step * k + step):
            orient = 2.0 * kind[i].astype(F32) - 1.0
            psi[i] = 1.0 / (1.0 + jnp.exp(-orient * away[i]))
    for k in range(FAR):
        x_low[k] = psi[k]
        x_high[k] = psi[16 - FAR + k]
    for started in copies[2 * PARTS :]:
        started.wait()


def prepare(phase, distance, velocity):
    vmem = pl.BlockSpec(memory_space=pltpu.VMEM)
    hbm = pl.BlockSpec(memory_space=pltpu.HBM)
    outs = [(16, 16, 256), (SENT, 16, 256), (SENT, 16, 256)]
    return pl.pallas_call(
        prepare_body,
        out_shape=[jax.ShapeDtypeStruct(s, F32) for s in outs],
        in_specs=[hbm, hbm, hbm],
        out_specs=[vmem] * len(outs),
        scratch_shapes=[
            pltpu.VMEM((16, 16, 256), jnp.int32),
            pltpu.VMEM((16, 16, 256), F32),
            pltpu.SemaphoreType.DMA((2 * PARTS + 6,)),
        ],
        compiler_params=pltpu.CompilerParams(vmem_limit_bytes=8 << 20),
        cost_estimate=pl.CostEstimate(flops=1000000, bytes_accessed=1000000, transcendentals=0),
    )(*(pltpu.with_memory_space_constraint(a, pltpu.HBM) for a in (phase, distance, velocity)))


def plane_of(own, low, high, p, offset, layers):
    if p < 0:
        return low[offset + layers + p]
    return own(p) if p < 16 else high[offset + p - 16]


def wide_planes(psi, velocity, low, high):
    def level(p):
        return plane_of(lambda k: psi[k], low, high, p, 0, FAR)

    def speed(component):
        _, layers, offset = layer_cuts(0)[component]

        def at_plane(p):
            if not -layers <= p < 16 + layers:
                return None
            return plane_of(lambda k: velocity[component, k], low, high, p, offset, layers)

        return at_plane

    return level, [speed(c) for c in range(3)]


def narrow_segments():
    reached = (FAR, ALONG, ALONG, ACROSS)
    rows_own = (FAR, ACROSS, ALONG, ACROSS)
    found = {}
    for p in range(16):
        offset = 0
        for field, rows in enumerate(rows_own):
            found[field, p] = (p, offset, rows)
            offset += rows
    for side, edge in enumerate((0, 15)):
        for slot, layers in enumerate(((1, 4, 5), (2, 3))):
            offset = 0
            for d in layers:
                p = edge - d if side == 0 else edge + d
                for field, reach_of in enumerate(reached):
                    rows = min(reach_of - d, rows_own[field])
                    if rows > 0:
                        found[field, p] = (16 + 2 * side + slot, offset, rows)
                        offset += rows
    return found


SEGMENTS = narrow_segments()
SLOTS = 20


def pack_body(at, psi, velocity, low, high, link, chip):
    odd = lax.rem(at[1], 2) == 1
    level, speeds = wide_planes(psi, velocity, low, high)
    fields = [level] + speeds
    for k in range(SLOTS):
        inside_slot = [(offset, f, p, rows) for (f, p), (slot, offset, rows) in SEGMENTS.items() if slot == k]
        first, final, total = [], [], 0
        for offset, f, p, rows in sorted(inside_slot):
            v = fields[f](p)
            first.append(v[0:rows])
            final.append(v[16 - rows : 16])
            total += rows
        if total < SENT:
            first.append(jnp.zeros((SENT - total, 256), F32))
            final.append(first[-1])
        first = jnp.concatenate(first, axis=0)
        final = jnp.concatenate(final, axis=0)
        chip[k] = jnp.where(odd, first, final)
        link[k] = jnp.where(odd, final, first)


def pack(at, psi, velocity, low, high):
    outs = [(SLOTS, SENT, 256)] * 2
    return call(pack_body, outs, [], [at, psi, velocity, low, high], 1000000)


FACE = 0.25 / 12.0


def indicators(a, b, c):
    d = a - c
    curve = (a + c) - 2.0 * b
    twice = 2.0 * curve
    base = (13.0 / 12.0) * (curve * curve) + WENO_EPS
    up, down = twice - d, twice + d
    p = base + 0.25 * (up * up)
    q = base + 0.25 * (d * d)
    r = base + 0.25 * (down * down)
    return p * p, q * q, r * r


def upwind_flux(s, l, p_left, q_left, r_left, p_right, q_right, r_right):
    ahead = s > 0.0
    pick = lambda x, y: jnp.where(ahead, x, y)
    a, b, c, e, f = pick(l[0], l[5]), pick(l[1], l[4]), pick(l[2], l[3]), pick(l[3], l[2]), pick(l[4], l[1])
    p, q, r = pick(p_left, r_right), pick(q_left, q_right), pick(r_left, p_right)
    w0, w1, w2 = q * r, 6.0 * (p * r), 3.0 * (p * q)
    g0 = 2.0 * a - 7.0 * b + 11.0 * c
    g1 = 5.0 * c + 2.0 * e - b
    g2 = 2.0 * c + 5.0 * e - f
    top = w0 * g0 + w1 * g1 + w2 * g2
    total = w0 + w1 + w2
    return (s * top) / total


def z_change(v, w):
    lane = iota(v.shape, 1)

    def ahead(x, k):
        return jnp.where(lane > 255 - k, 0.0, roll(x, -k, 1))

    def behind(x, k):
        return jnp.where(lane < k, 0.0, roll(x, k, 1))

    l = [behind(v, 2), behind(v, 1), v, ahead(v, 1), ahead(v, 2), ahead(v, 3)]
    s = FACE * (w + ahead(w, 1))
    p, q, r = indicators(l[1], l[2], l[3])
    _, q1, r1 = indicators(l[2], l[3], l[4])
    _, _, r2 = indicators(l[3], l[4], l[5])
    p0, _, _ = indicators(l[0], l[1], l[2])
    flux = upwind_flux(s, l, p0, q, r1, p, q1, r2)
    low = slice(0, 128)
    c = v[:, low]
    none = jnp.zeros_like(c)
    square = c * c
    edge = WENO_EPS + (13.0 / 12.0 + 9.0 / 4.0) * square
    level = WENO_EPS + (13.0 / 12.0 + 1.0 / 4.0) * square
    wall_flux = upwind_flux(
        FACE * w[:, low],
        [none, none, none, c, l[3][:, low], l[4][:, low]],
        none + WENO_EPS * WENO_EPS, level * level, r[:, low],
        edge * edge, q[:, low], r1[:, low],
    )
    wall_flux = jnp.concatenate([wall_flux, wall_flux], axis=1)
    return flux - jnp.where(lane == 0, wall_flux, roll(flux, 1, 1))


def y_change(v, w):
    s = FACE * (w + roll(w, -1, 0))
    l = [roll(v, 2 - k, 0) for k in range(6)]
    p, q, r = indicators(l[1], l[2], l[3])
    q_next, r_next = roll(q, -1, 0), roll(r, -1, 0)
    flux = upwind_flux(s, l, roll(p, 1, 0), q, r_next, p, q_next, roll(r, -2, 0))
    return flux - roll(flux, 1, 0)


SKIN = 3


def x_marks(v, planes, marks):
    for i in range(planes):
        marks[0][i], marks[1][i], marks[2][i] = indicators(v(i - FAR), v(i - FAR + 1), v(i - FAR + 2))


def x_flux(f, v, w, marks):
    p_x, q_x, r_x = marks
    l = [v(f - 3 + k) for k in range(6)]
    return upwind_flux(
        FACE * (w(f - 1) + w(f)), l,
        p_x[f + 3], q_x[f + 4], r_x[f + 5], p_x[f + 4], q_x[f + 5], r_x[f + 6],
    )


def xz_change(v, u, w, marks, out):
    x_marks(v, 26, marks)
    below = x_flux(-SKIN, v, u, marks)
    for p in range(-SKIN, 16 + SKIN):
        above = x_flux(p + 1, v, u, marks)
        out[p + SKIN] = (above - below) + z_change(v(p), w(p))
        below = above


def inner_body(psi, velocity, low, high, out, *marks):
    level, speeds = wide_planes(psi, velocity, low, high)
    xz_change(level, speeds[0], speeds[2], marks, out)


def inner(psi, velocity, low, high):
    block = (16 + 2 * SKIN, 16, 256)
    scratch = [(26, 16, 256)] * 3
    return call(inner_body, [block], scratch, [psi, velocity, low, high], 8000000)[0]


def advance_body(
    nx, ny, at, psi, velocity, low, high, link, chip, change_in, moved, source, first, final,
    v8, u8, w8, v32, u32, c8, p_x, q_x, r_x, m, n_x, n_y, n_z, s_x, part,
):
    lower, upper = pick_sides(at, chip, link)
    level, speeds = wide_planes(psi, velocity, low, high)
    fields = [level] + speeds

    def halo(field, p, most):
        if (field, p) not in SEGMENTS:
            return 0, None, None
        slot, offset, rows = SEGMENTS[field, p]
        count = min(most, rows)
        below = lower(slot)[offset + rows - count : offset + rows]
        return count, below, upper(slot)[offset : offset + count]

    def beside_only(ref, i, field, p):
        ref[i] = jnp.zeros((8, 256), F32)
        count, below, above = halo(field, p, 4)
        if count:
            ref[i, 4 - count : 4, :] = below
            ref[i, 4 : 4 + count, :] = above

    def with_rows(ref, i, field, p, start):
        total = ref.shape[1]
        ref[i, 0:start, :] = jnp.zeros((start, 256), F32)
        ref[i, start + 16 : total, :] = jnp.zeros((total - start - 16, 256), F32)
        count, below, above = halo(field, p, start)
        ref[i, start : start + 16, :] = fields[field](p)
        if count:
            ref[i, start - count : start, :] = below
            ref[i, start + 16 : start + 16 + count, :] = above

    for p in range(-FAR, 16 + FAR):
        beside_only(v8, p + FAR, 0, p)
        if -ALONG <= p < 16 + ALONG:
            beside_only(u8, p + ALONG, 1, p)
        if -SKIN <= p < 16 + SKIN:
            beside_only(w8, p + SKIN, 3, p)
            with_rows(v32, p + SKIN, 0, p, 8)
            with_rows(u32, p + SKIN, 2, p, 8)

    xz_change(
        lambda p: v8[p + FAR], lambda p: u8[p + ALONG], lambda p: w8[p + SKIN], (p_x, q_x, r_x), c8
    )
    shape = (24, 256)
    mask = row_mask(shape, at[1] * 16 - 4, ny)
    for p in range(-SKIN, 16 + SKIN):
        i = p + SKIN
        sides = c8[i]
        change = jnp.concatenate([sides[0:4], change_in[i], sides[4:8]], axis=0)
        v = v32[i]
        change = change + y_change(v, u32[i])[4:28, :]
        value = wall(at, nx, 0, p, (v[4:28, :] - change) * mask)
        m[i] = value
        if 0 <= p < 16:
            moved[p] = value[4:20, :]

    lane = iota(shape, 1)

    def gradient(p):
        c = m[p + SKIN]
        down, ahead = z_shifted(c)
        gx = 0.5 * (m[p + SKIN + 1] - m[p + SKIN - 1])
        gy = 0.5 * (roll(c, -1, 0) - roll(c, 1, 0))
        return gx, gy, 0.5 * (ahead - down)

    for p in range(-2, 18):
        gx, gy, gz = gradient(p)
        inverse = lax.rsqrt(gx * gx + gy * gy + gz * gz + DELTA_SQ)
        n_x[p + 2], n_y[p + 2], n_z[p + 2] = gx * inverse, gy * inverse, gz * inverse
    for p in range(-1, 17):
        gx, gy, gz = gradient(p)
        edge = 0.5 * m[p + SKIN]
        edge = edge * lax.rsqrt(edge * edge + DELTA_SQ)
        nz, ny_here = n_z[p + 2], n_y[p + 2]
        ahead = jnp.where(lane == 255, -edge, roll(nz, -1, 1))
        behind = jnp.where(lane == 0, edge, roll(nz, 1, 1))
        bending = -0.5 * (
            (n_x[p + 3] - n_x[p + 1])
            + (roll(ny_here, -1, 0) - roll(ny_here, 1, 0))
            + (ahead - behind)
        )
        bending = wall(at, nx, 0, p, bending * mask)
        s_x[p + 1] = (bending * gx)[4:20, :] + speeds[0](p)
        if 0 <= p < 16:
            sy = bending * gy + u32[p + SKIN, 4:28, :]
            dy = roll(sy, -1, 0) - roll(sy, 1, 0)
            sz = (bending * gz)[4:20, :] + velocity[2, p]
            behind, ahead = z_shifted(sz)
            part[p] = dy[4:20, :] + (ahead - behind)
    for p in range(16):
        source[p] = -0.5 * (part[p] + (s_x[p + 2] - s_x[p]))
    for i in range(HALO):
        first[i] = source[i]
        final[i] = source[16 - HALO + i]


def advance(nx, ny, at, psi, velocity, low, high, chip, link, change):
    marks, normals, block = (26, 8, 256), (20, 24, 256), (16, 16, 256)
    skin = 16 + 2 * SKIN
    scratch = [
        (16 + 2 * FAR, 8, 256), (16 + 2 * ALONG, 8, 256), (skin, 8, 256), (skin, 32, 256),
        (skin, 32, 256), (skin, 8, 256), marks, marks, marks,
        (skin, 24, 256), normals, normals, normals, (18, 16, 256), block,
    ]
    args = [at, psi, velocity, low, high, link, chip, change]
    outs = [block, block, (HALO, 16, 256), (HALO, 16, 256)]
    return call(functools.partial(advance_body, nx, ny), outs, scratch, args, 30000000)


class Field:
    def __init__(self, ref, lead):
        self.ref, self.lead = ref, lead

    def __getitem__(self, p):
        return self.ref[p + self.lead]

    def __setitem__(self, p, value):
        self.ref[p + self.lead] = value

    def beside(self, p):
        return beside(self.ref, p + self.lead)


def wall(at, nx, level, p, value):
    own = 16 >> level
    if 0 <= p < own:
        return value
    return value * plane_factor(at[0] * own + p, nx >> level)


def first_smooth(b, v, planes, weight, mask, at, nx, level):
    for p in planes:
        c, around = b.beside(p)
        v[p] = wall(at, nx, level, p, (weight * mask) * (1.2 * c + SIDE * around))


def sweep(src, dst, b, planes, factor, mask, at, nx, level):
    keep = SIDE * mask
    for p in planes:
        c, around = src.beside(p)
        near = around + (b[p] if factor == 1 else factor * b[p])
        dst[p] = 0.2 * c + wall(at, nx, level, p, keep) * near


def coarsen_level0(at, nx, ny, b, v, b1, planes, pair, t):
    first = planes[0]
    rows = t.shape[1]

    def residual(p):
        c, around = v.beside(p)
        return b[p] - (6.0 * c - around)

    for p in planes:
        total = residual(2 * p) + residual(2 * p + 1)
        for half in range(2):
            lanes = slice(128 * half, 128 * half + 128)
            pair[p - first, half] = total[:, lanes]
            even = pair[p - first, half, pl.ds(0, rows, stride=2), :]
            odd = pair[p - first, half, pl.ds(1, rows, stride=2), :]
            t[p - first, :, lanes] = even + odd
    count = len(planes)
    full = dot(t[...].reshape(count * rows, 256), pair_matrix(256, 128, 0.125))
    full = full.reshape(count, rows, 128)
    mask = row_mask((rows, 128), at[1] * 8 + 4 - rows // 2, ny // 2)
    for p in planes:
        b1[p] = wall(at, nx, 1, p, full[p - first] * mask)


def smooth_level1(at, nx, ny, b1, u, planes):
    rows = b1.ref.shape[1]
    mask = row_mask((rows, 128), at[1] * 8 + 4 - rows // 2, ny // 2)
    first_smooth(b1, u, planes, 4.0 * SIDE, mask, at, nx, 1)


def coarsen_level1(b1, u, b2_out, s1, t1):
    start = b1.ref.shape[1] // 2 - 4
    t1[...] = jnp.zeros_like(t1)
    for k in range(4):
        total = 0.0
        for p in (2 * k, 2 * k + 1):
            c, around = u.beside(p)
            total = total + (b1[p] - 0.25 * (6.0 * c - around))
        s1[k] = total
        t1[k, 0:4, :] = s1[k, pl.ds(start, 4, stride=2), :] + s1[k, pl.ds(start + 1, 4, stride=2), :]
    small = dot(t1[...].reshape(32, 128), pair_matrix(128, 128, 0.125)).reshape(4, 8, 128)
    tile = jnp.concatenate([small[0, 0:4], small[1, 0:4]], axis=0) + roll(
        jnp.concatenate([small[2, 0:4], small[3, 0:4]], axis=0), 64, 1
    )
    b2_out[...] = tile


def reach(extra):
    e0 = extra + 2
    r1 = -(-e0 // 2)
    e1 = r1 + 2
    r2 = -(-e1 // 2)
    e2 = r2 + 2
    r3 = -(-e2 // 2)
    return e0, r1, e1, r2, e2, r3


E0, R1, E1, R2, E2, R3 = reach(KEEP)


def source_segments():
    whole, parts = [], []
    for p in range(-HALO, 16 + HALO):
        d = max(-p, p - 15, 0)
        rows = 16 - max(d, 2)
        if rows >= 8:
            whole.append((p, 0, 8))
        if rows % 8:
            parts.append((p, rows // 8 * 8, rows % 8))
    found = [(p, n, rows, tile, 0) for tile, (p, n, rows) in enumerate(whole)]
    room = []
    for p, n, rows in sorted(parts, key=lambda part: (-part[2], part[0])):
        for k, used in enumerate(room):
            if used + rows <= 8:
                break
        else:
            k = len(room)
            room.append(0)
        found.append((p, n, rows, len(whole) + k, room[k]))
        room[k] += rows
    return found, len(whole) + len(room)


SOURCE_SEGMENTS, SOURCE_TILES = source_segments()


def source_plane(own, low, high, p):
    return low[p + HALO] if p < 0 else own[p] if p < 16 else high[p - 16]


def weave_body(at, own, low, high, link, chip):
    odd = lax.rem(at[1], 2) == 1
    for k in range(SOURCE_TILES):
        first, final, total = [], [], 0
        for p, n, rows, tile, offset in sorted(SOURCE_SEGMENTS, key=lambda part: part[4]):
            if tile == k:
                v = source_plane(own, low, high, p)
                first.append(v[n : n + rows])
                final.append(v[16 - n - rows : 16 - n])
                total += rows
        if total < 8:
            first.append(jnp.zeros((8 - total, 256), F32))
            final.append(first[-1])
        if len(first) > 1:
            first = [jnp.concatenate(first, axis=0)]
            final = [jnp.concatenate(final, axis=0)]
        chip[k] = jnp.where(odd, first[0], final[0])
        link[k] = jnp.where(odd, final[0], first[0])


def weave(at, own, low, high):
    outs = [(SOURCE_TILES, 8, 256)] * 2
    return call(weave_body, outs, [], [at, own, low, high], 1000000)


def first_down_body(
    nx, ny, at, own, low, high, link, chip, b_out, v_out, b1_out, u_out, b2_out, b, v, pair, t, s1, t1
):
    lower, upper = pick_sides(at, chip, link)
    none = jnp.zeros((16, 256), F32)
    for p in range(-HALO, 16 + HALO):
        b[p + HALO, 0:16, :] = none
        b[p + HALO, 16:32, :] = source_plane(own, low, high, p)
        b[p + HALO, 32:48, :] = none
    for p, n, rows, tile, offset in SOURCE_SEGMENTS:
        cut = slice(offset, offset + rows)
        b[p + HALO, 16 - n - rows : 16 - n, :] = lower(tile)[cut]
        b[p + HALO, 32 + n : 32 + n + rows, :] = upper(tile)[cut]
    b, v = Field(b, HALO), Field(v, HALO - 1)
    mask = row_mask((48, 256), at[1] * 16 - 16, ny)
    first_smooth(b, v, range(1 - HALO, 15 + HALO), SIDE, mask, at, nx, 0)
    v_out, b_out = Field(v_out, E0), Field(b_out, E0 - 1)
    for p in range(-E0, 16 + E0):
        v_out[p] = v[p][8:40, :]
    for p in range(1 - E0, 15 + E0):
        b_out[p] = b[p][8:40, :]
    b1, u = Field(b1_out, E1 + 1), Field(u_out, E1)
    coarsen_level0(at, nx, ny, b, v, b1, range(-E1 - 1, 9 + E1), pair, t)
    smooth_level1(at, nx, ny, b1, u, range(-E1, 8 + E1))
    coarsen_level1(b1, u, b2_out, s1, t1)


def around_block(size, extra, rows, lanes):
    return (size + 2 * extra, rows, lanes)


def first_down(nx, ny, at, own, low, high, chip, link):
    level1 = around_block(8, E1 + 1, 24, 128)
    outs = [
        around_block(16, E0 - 1, 32, 256),
        around_block(16, E0, 32, 256),
        level1,
        around_block(8, E1, 24, 128),
        (8, 128),
    ]
    scratch = [
        around_block(16, HALO, 48, 256),
        around_block(16, HALO - 1, 48, 256),
        (level1[0], 2, 48, 128),
        (level1[0], 24, 256),
        (4, 24, 128),
        (4, 8, 128),
    ]
    args = [at, own, low, high, link, chip]
    return call(functools.partial(first_down_body, nx, ny), outs, scratch, args, 20000000)


def second_down_body(nx, ny, at, mid, chip, link, b1_out, u_out, b2_out, s1, t1):
    lower, upper = pick_sides(at, chip, link)
    for i in range(8 + 2 * NEAR):
        b1_out[i, 0:8, :] = lower(i)
        b1_out[i, 8:16, :] = mid[i]
        b1_out[i, 16:24, :] = upper(i)
    b1, u = Field(b1_out, NEAR), Field(u_out, NEAR - 1)
    smooth_level1(at, nx, ny, b1, u, range(1 - NEAR, 7 + NEAR))
    coarsen_level1(b1, u, b2_out, s1, t1)


def second_down(nx, ny, at, mid, chip, link):
    outs = [around_block(8, NEAR, 24, 128), around_block(8, NEAR - 1, 24, 128), (8, 128)]
    scratch = [(4, 24, 128), (4, 8, 128)]
    args = [at, mid, chip, link]
    return call(functools.partial(second_down_body, nx, ny), outs, scratch, args, 2000000)


def solve_coarse(nx, ny, extra, at, coarse, s2, v2, w2, t3, b3, c3, d3, dup, row2):
    fetched, other = coarse
    odd = lax.rem(at[1], 2) == 1
    odd_layer = lax.rem(at[0] // GROUP, 2)
    _, _, _, r2, e2, r3 = reach(extra)
    spot = at[0] % GROUP
    rows2 = ny // 4
    rows3 = rows2 // 2
    count = rows2 // 4
    lead = 2 * (r3 + 3) + 2
    blocks = -(-lead // 4)
    s2, v2, w2 = Field(s2, 4 * blocks), Field(v2, lead - 1), Field(w2, e2)
    lane8 = iota((8, 128), 1) < 64
    for j in range(-blocks, blocks + 1):
        block = spot + GROUP + j
        layer, place = block // GROUP, block % GROUP
        first_cores = jnp.where(odd_layer == 1, layer <= 1, layer >= 1)
        mine = first_cores != odd
        inner = inside(at[0] + j, nx // 16)
        start = ((layer + odd_layer) // 2) * (GROUP * count // 2) + place * (count // 2)
        for n in range(count):
            rows = slice(8 * (n % 2), 8 * (n % 2) + 8)
            k = start + n // 2
            tile = jnp.where(mine, fetched[k, rows, :], other[k, rows, :])
            tile = jnp.where(inner, tile, 0.0)
            halves = (jnp.where(lane8, tile, 0.0), jnp.where(lane8, roll(tile, 64, 1), 0.0))
            for p in range(4):
                part = halves[p // 2][4 * (p % 2) : 4 * (p % 2) + 4, :]
                s2.ref[4 * (j + blocks) + p, 4 * n : 4 * n + 4, :] = part

    def around(f, p):
        c = f[p]
        row = iota(c.shape, 0)
        lower = jnp.where(row == 0, 0.0, roll(c, 1, 0))
        upper = jnp.where(row == c.shape[0] - 1, 0.0, roll(c, -1, 0))
        beside = (lower + upper) + (roll(c, 1, 1) + roll(c, -1, 1))
        return c, (f[p - 1] + f[p + 1]) + beside

    def lanes_below(rows, lanes):
        return jnp.where(iota((rows, 128), 1) < lanes, 1.0, 0.0).astype(F32)

    mask2 = lanes_below(rows2, 64)
    for p in range(1 - lead, 3 + lead):
        c, near = around(s2, p)
        v2[p] = wall(at, nx, 2, p, (16.0 * SIDE) * mask2 * (1.2 * c + SIDE * near))

    def residual2(p):
        c, near = around(v2, p)
        return s2[p] - (1.0 / 16.0) * (6.0 * c - near)

    planes3 = range(-r3 - 3, 2 + r3 + 3)
    for i, p in enumerate(planes3):
        row2[i] = residual2(2 * p) + residual2(2 * p + 1)
        t3[i] = row2[i, pl.ds(0, rows3, stride=2), :] + row2[i, pl.ds(1, rows3, stride=2), :]
    total3 = len(planes3)
    full = dot(t3[...].reshape(total3 * rows3, 128), pair_matrix(128, 128, 0.125))
    full = full.reshape(total3, rows3, 128)
    mask3 = lanes_below(rows3, 32)
    b3, c3, d3 = Field(b3, r3 + 3), Field(c3, r3 + 3), Field(d3, r3 + 3)
    for i, p in enumerate(planes3):
        value = wall(at, nx, 3, p, full[i] * ((64.0 * SIDE) * mask3))
        b3[p] = value
    src, dst = b3, c3
    for step in (2, 1, 0):
        for p in range(-r3 - step, 2 + r3 + step):
            c, near = around(src, p)
            dst[p] = wall(at, nx, 3, p, mask3 * (0.2 * c + SIDE * near)) + b3[p]
        src, dst = dst, (d3 if dst is c3 else c3)
    final = src
    planes = range(-r3, 2 + r3)
    flat = jnp.concatenate([final[p] for p in planes], axis=0)
    spread = dot(flat, copy_matrix(128, 128)).reshape(len(planes), rows3, 128)
    for i, p in enumerate(planes):
        dup[i, pl.ds(0, rows3, stride=2), :] = spread[i]
        dup[i, pl.ds(1, rows3, stride=2), :] = spread[i]
        for q in (2 * p, 2 * p + 1):
            if -e2 <= q < 4 + e2:
                v2[q] = v2[q] + wall(at, nx, 2, q, dup[i, 0:rows2, :] * mask2)
    keep = SIDE * mask2
    for src, dst, step in ((v2, w2, 1), (w2, v2, 0)):
        for p in range(-r2 - step, 4 + r2 + step):
            c, near = around(src, p)
            dst[p] = 0.2 * c + wall(at, nx, 2, p, keep) * (near + 16.0 * s2[p])
    return v2


def coarse_scratch(ny, extra):
    _, _, _, _, e2, r3 = reach(extra)
    rows2 = ny // 4
    rows3 = rows2 // 2
    lead = 2 * (r3 + 3) + 2
    small = around_block(2, r3 + 3, rows3, 128)
    return [
        around_block(4, -(-lead // 4) * 4, rows2, 128),
        around_block(4, lead - 1, rows2, 128),
        around_block(4, e2, rows2, 128),
        small, small, small, small,
        (8, 48, 128),
        around_block(2, r3 + 3, rows2, 128),
    ]


def climb(nx, ny, extra, at, v2, b1, u, b, v_down, m1, n1, m0, n0, dup):
    e0, r1, e1, r2, _, _ = reach(extra)
    rows2 = ny // 4
    turn = lax.rem(rows2 + 4 - 4 * at[1] + rows2, rows2)
    planes = range(-r2, 4 + r2)
    picked = jnp.concatenate([pltpu.roll(v2[p], turn, 0)[0:16, :] for p in planes], axis=0)
    spread = dot(picked, copy_matrix(128, 128)).reshape(len(planes), 16, 128)
    mask1 = row_mask((24, 128), at[1] * 8 - 8, ny // 2)
    m1, n1 = Field(m1, e1), Field(n1, e1)
    for i, p in enumerate(planes):
        dup[i, 0, pl.ds(0, 12, stride=2), :] = spread[i, 0:12, :]
        dup[i, 0, pl.ds(1, 12, stride=2), :] = spread[i, 0:12, :]
        for q in (2 * p, 2 * p + 1):
            if -e1 <= q < 8 + e1:
                m1[q] = u[q] + wall(at, nx, 1, q, dup[i, 0, 0:24, :] * mask1)
    sweep(m1, n1, b1, range(1 - e1, 7 + e1), 4.0, mask1, at, nx, 1)
    sweep(n1, m1, b1, range(2 - e1, 6 + e1), 4.0, mask1, at, nx, 1)
    planes = range(-r1, 8 + r1)
    flat = jnp.concatenate([m1[p][4:20, :] for p in planes], axis=0)
    spread = dot(flat, copy_matrix(128, 256)).reshape(len(planes), 16, 256)
    mask0 = row_mask((32, 256), at[1] * 16 - 8, ny)
    m0, n0 = Field(m0, e0), Field(n0, e0)
    for i, p in enumerate(planes):
        for half in range(2):
            value = spread[i, :, 128 * half : 128 * half + 128]
            dup[i, half, pl.ds(0, 16, stride=2), :] = value
            dup[i, half, pl.ds(1, 16, stride=2), :] = value
        value = jnp.concatenate([dup[i, 0], dup[i, 1]], axis=1) * mask0
        for q in (2 * p, 2 * p + 1):
            if -e0 <= q < 16 + e0:
                m0[q] = v_down[q] + wall(at, nx, 0, q, value)
    sweep(m0, n0, b, range(1 - e0, 15 + e0), 1, mask0, at, nx, 0)
    if extra:
        sweep(n0, m0, b, range(2 - e0, 14 + e0), 1, mask0, at, nx, 0)
        return m0
    return n0


def climb_scratch(extra):
    e0, r1, e1, r2, _, _ = reach(extra)
    level1 = around_block(8, e1, 24, 128)
    level0 = around_block(16, e0, 32, 256)
    return [level1, level1, level0, level0, (max(8 + 2 * r1, 4 + 2 * r2), 2, 32, 128)]


def turn_body(nx, ny, at, fetched, other, b1, u, b, v_down, v_out, wider, low, high, own, pair, t, *scratch):
    v2 = solve_coarse(nx, ny, KEEP, at, (fetched, other), *scratch[:9])
    b = Field(b, E0 - 1)
    v = climb(nx, ny, KEEP, at, v2, Field(b1, E1 + 1), Field(u, E1), b, Field(v_down, E0), *scratch[9:])
    mask = row_mask((32, 256), at[1] * 16 - 8, ny)
    once, twice = Field(scratch[12], E0), Field(v_out, KEEP - 2)
    sweep(v, once, b, range(1 - KEEP, 15 + KEEP), 1, mask, at, nx, 0)
    sweep(once, twice, b, range(2 - KEEP, 14 + KEEP), 1, mask, at, nx, 0)
    coarsen_level0(at, nx, ny, b, twice, Field(own, 0), range(8), pair, t)
    for i in range(8):
        wider[NEAR + i] = own[i, 4:12, :]
    for i in range(NEAR):
        low[i] = own[i, 4:12, :]
        high[i] = own[8 - NEAR + i, 4:12, :]


def turn(nx, ny, at, coarse, b1, u, b, v_down):
    outs = [
        around_block(16, KEEP - 2, 32, 256),
        around_block(8, NEAR, 8, 128),
        (NEAR, 8, 128),
        (NEAR, 8, 128),
    ]
    scratch = [(8, 16, 128), (8, 2, 32, 128), (8, 16, 256)]
    scratch += coarse_scratch(ny, KEEP) + climb_scratch(KEEP)
    args = [at, *coarse, b1, u, b, v_down]
    return call(functools.partial(turn_body, nx, ny), outs, scratch, args, 30000000)


def finish_body(nx, ny, at, fetched, other, b1, u, b, v_down, out, *scratch):
    v2 = solve_coarse(nx, ny, 0, at, (fetched, other), *scratch[:9])
    b, v_down = Field(b, E0 - 1), Field(v_down, KEEP - 2)
    v = climb(nx, ny, 0, at, v2, Field(b1, NEAR), Field(u, NEAR - 1), b, v_down, *scratch[9:])
    for p in range(16):
        c, around = v.beside(p)
        out[p] = (0.2 * c + SIDE * (around + b[p]))[8:24, :]


def finish(nx, ny, at, coarse, b1, u, b, v_down):
    scratch = coarse_scratch(ny, 0) + climb_scratch(0)
    args = [at, *coarse, b1, u, b, v_down]
    return call(functools.partial(finish_body, nx, ny), [(16, 16, 256)], scratch, args, 20000000)[0]


def shifted(array, axis, step):
    count = lax.axis_size(axis)
    return lax.ppermute(
        array, axis, [(i, i + step) for i in range(count) if 0 <= i + step < count]
    )


def swapped(array, first):
    count = lax.axis_size("narrow")
    pairs = [(i, i + 1) for i in range(first, count - 1, 2)]
    return lax.ppermute(array, "narrow", pairs + [(j, i) for i, j in pairs])


def widen(wider, low, high):
    planes = low.shape[0]
    wider = lax.dynamic_update_slice(wider, shifted(high, "wide", 1), (0, 0, 0))
    upper = wider.shape[0] - planes
    return lax.dynamic_update_slice(wider, shifted(low, "wide", -1), (upper, 0, 0))


def surround(wider, low, high):
    mid = widen(wider, low, high)
    link = swapped(mid, 1)
    return mid, swapped(mid, 0), link


def spread_coarse(b2):
    wide, cores = lax.axis_size("wide"), lax.axis_size("narrow")
    layers = wide // GROUP
    odd = lax.rem(lax.axis_index("narrow"), 2) == 1
    other = swapped(b2, 0)
    pair = jnp.concatenate([jnp.where(odd, other, b2), jnp.where(odd, b2, other)], axis=0)
    groups = [
        [
            (((2 * k + core + i) % layers) * GROUP + x) * cores + y
            for i in range(2)
            for x in range(GROUP)
            for y in range(core, cores, 2)
        ]
        for core in range(2)
        for k in range(layers // 2)
    ]
    pieces = jnp.broadcast_to(pair[None], (len(groups[0]),) + pair.shape)
    fetched = lax.all_to_all(pieces, ("wide", "narrow"), 0, 0, axis_index_groups=groups)
    return fetched, swapped(fetched, 0)


def on_device(phase, distance, velocity):
    nx, ny = 16 * lax.axis_size("wide"), 16 * lax.axis_size("narrow")
    at = jnp.stack([lax.axis_index("wide"), lax.axis_index("narrow")]).astype(jnp.int32)
    psi, x_low, x_high = prepare(phase, distance, velocity)
    low, high = shifted(x_high, "wide", 1), shifted(x_low, "wide", -1)
    link, chip = pack(at, psi, velocity, low, high)
    v_link = swapped(link, 1)
    v_chip = swapped(chip, 0)
    change = inner(psi, velocity, low, high)
    moved, source, first, final = advance(
        nx, ny, at, psi, velocity, low, high, v_chip, v_link, change
    )
    low, high = shifted(final, "wide", 1), shifted(first, "wide", -1)
    link, chip = weave(at, source, low, high)
    b_link = swapped(link, 1)
    b_chip = swapped(chip, 0)
    b, v, b1, u, b2 = first_down(nx, ny, at, source, low, high, b_chip, b_link)
    v, *sends = turn(nx, ny, at, spread_coarse(b2), b1, u, b, v)
    b1, u, b2 = second_down(nx, ny, at, *surround(*sends))
    pressure = finish(nx, ny, at, spread_coarse(b2), b1, u, b, v)
    return (moved, pressure)


def solution(mesh):
    blocks = P("wide", "narrow", None)
    return jax.shard_map(
        on_device,
        mesh=mesh,
        in_specs=(blocks, blocks, P(None, "wide", "narrow", None)),
        out_specs=(blocks, blocks),
        check_vma=False,
    )
```

```python
import functools

import jax
import jax.numpy as jnp
from jax import lax
from jax.experimental import pallas as pl
from jax.experimental.pallas import tpu as pltpu
from jax.sharding import PartitionSpec as P

DELTA_SQ = 0.0025
WENO_EPS = 0.01
SIDE = 0.8 / 6.0
F32 = jnp.float32

HALO = 14
KEEP = 4
NEAR = 4
GROUP = 4


def iota(shape, dim):
    return lax.broadcasted_iota(jnp.int32, shape, dim)


def roll(v, shift, axis):
    return pltpu.roll(v, shift % v.shape[axis], axis)


def z_shifted(v):
    lane = iota(v.shape, 1)
    last = v.shape[1] - 1
    lower = jnp.where(lane == 0, 0.0, roll(v, 1, 1))
    upper = jnp.where(lane == last, 0.0, roll(v, -1, 1))
    return lower, upper


def z_pair(v):
    lower, upper = z_shifted(v)
    return lower + upper


def y_pair(v):
    return roll(v, 1, 0) + roll(v, -1, 0)


def beside(ref, i):
    c = ref[i]
    return c, (ref[i - 1] + ref[i + 1]) + y_pair(c) + z_pair(c)


def inside(first, count):
    return jnp.logical_and(first >= 0, first < count)


def row_mask(shape, first, count):
    rows = iota(shape, 0) + first
    return jnp.where(inside(rows, count), 1.0, 0.0).astype(F32)


def plane_factor(index, count):
    return jnp.where(inside(index, count), 1.0, 0.0).astype(F32)


def dot(a, b):
    b = b.astype(jnp.bfloat16)
    high = a.astype(jnp.bfloat16)
    low = (a - high.astype(F32)).astype(jnp.bfloat16)
    return jnp.dot(high, b, preferred_element_type=F32) + jnp.dot(low, b, preferred_element_type=F32)


def pair_matrix(rows, cols, value):
    return jnp.where((iota((rows, cols), 0) >> 1) == iota((rows, cols), 1), value, 0.0).astype(F32)


def copy_matrix(rows, cols):
    return jnp.where(iota((rows, cols), 0) == (iota((rows, cols), 1) >> 1), 1.0, 0.0).astype(F32)


def words(shape):
    *lead, rows, lanes = (1,) * (3 - len(shape)) + tuple(shape)
    size = -(-rows // 8) * 8 * (-(-lanes // 128) * 128)
    for n in lead:
        size *= n
    return size


def call(body, outs, scratch, args, flops):
    vmem = pl.BlockSpec(memory_space=pltpu.VMEM)
    smem = pl.BlockSpec(memory_space=pltpu.SMEM)
    total = sum(words(a.shape) for a in args) + sum(map(words, outs)) + sum(map(words, scratch))
    return pl.pallas_call(
        body,
        out_shape=[jax.ShapeDtypeStruct(s, F32) for s in outs],
        in_specs=[smem if a.dtype == jnp.int32 and a.ndim == 1 else vmem for a in args],
        out_specs=[vmem] * len(outs),
        scratch_shapes=[pltpu.VMEM(s, F32) for s in scratch],
        compiler_params=pltpu.CompilerParams(vmem_limit_bytes=4 * total + (6 << 20)),
        cost_estimate=pl.CostEstimate(flops=flops, bytes_accessed=4000000, transcendentals=0),
    )(*args)


def pick_sides(at, chip, link):
    odd = lax.rem(at[1], 2) == 1
    lower = lambda *k: jnp.where(odd, chip[k], link[k])
    upper = lambda *k: jnp.where(odd, link[k], chip[k])
    return lower, upper


PARTS = 4
FAR, ALONG, ACROSS = 6, 4, 3
SENT = FAR + ALONG + 2 * ACROSS


def layer_cuts(dim):
    cuts, offset = [], FAR
    for component in range(3):
        layers = ALONG if component == dim else ACROSS
        cuts.append((component, layers, offset))
        offset += layers
    return cuts


def prepare_body(phase, distance, velocity, psi, x_low, x_high, kind, away, sems):
    step = 16 // PARTS
    copies = []

    def copy(src, dst):
        started = pltpu.make_async_copy(src, dst, sems.at[len(copies)])
        started.start()
        copies.append(started)

    for k in range(PARTS):
        planes = pl.ds(step * k, step)
        copy(phase.at[planes], kind.at[planes])
        copy(distance.at[planes], away.at[planes])
    for component, layers, offset in layer_cuts(0):
        copy(velocity.at[component, pl.ds(0, layers)], x_low.at[pl.ds(offset, layers)])
        copy(velocity.at[component, pl.ds(16 - layers, layers)], x_high.at[pl.ds(offset, layers)])
    for k in range(PARTS):
        copies[2 * k].wait()
        copies[2 * k + 1].wait()
        for i in range(step * k, step * k + step):
            orient = 2.0 * kind[i].astype(F32) - 1.0
            psi[i] = 1.0 / (1.0 + jnp.exp(-orient * away[i]))
    for k in range(FAR):
        x_low[k] = psi[k]
        x_high[k] = psi[16 - FAR + k]
    for started in copies[2 * PARTS :]:
        started.wait()


def prepare(phase, distance, velocity):
    vmem = pl.BlockSpec(memory_space=pltpu.VMEM)
    hbm = pl.BlockSpec(memory_space=pltpu.HBM)
    outs = [(16, 16, 256), (SENT, 16, 256), (SENT, 16, 256)]
    return pl.pallas_call(
        prepare_body,
        out_shape=[jax.ShapeDtypeStruct(s, F32) for s in outs],
        in_specs=[hbm, hbm, hbm],
        out_specs=[vmem] * len(outs),
        scratch_shapes=[
            pltpu.VMEM((16, 16, 256), jnp.int32),
            pltpu.VMEM((16, 16, 256), F32),
            pltpu.SemaphoreType.DMA((2 * PARTS + 6,)),
        ],
        compiler_params=pltpu.CompilerParams(vmem_limit_bytes=8 << 20),
        cost_estimate=pl.CostEstimate(flops=1000000, bytes_accessed=1000000, transcendentals=0),
    )(*(pltpu.with_memory_space_constraint(a, pltpu.HBM) for a in (phase, distance, velocity)))


def plane_of(own, low, high, p, offset, layers):
    if p < 0:
        return low[offset + layers + p]
    return own(p) if p < 16 else high[offset + p - 16]


def wide_planes(psi, velocity, low, high):
    def level(p):
        return plane_of(lambda k: psi[k], low, high, p, 0, FAR)

    def speed(component):
        _, layers, offset = layer_cuts(0)[component]

        def at_plane(p):
            if not -layers <= p < 16 + layers:
                return None
            return plane_of(lambda k: velocity[component, k], low, high, p, offset, layers)

        return at_plane

    return level, [speed(c) for c in range(3)]


def narrow_segments():
    reached = (FAR, ALONG, ALONG, ACROSS)
    rows_own = (FAR, ACROSS, ALONG, ACROSS)
    found = {}
    for p in range(16):
        offset = 0
        for field, rows in enumerate(rows_own):
            found[field, p] = (p, offset, rows)
            offset += rows
    for side, edge in enumerate((0, 15)):
        for slot, layers in enumerate(((1, 4, 5), (2, 3))):
            offset = 0
            for d in layers:
                p = edge - d if side == 0 else edge + d
                for field, reach_of in enumerate(reached):
                    rows = min(reach_of - d, rows_own[field])
                    if rows > 0:
                        found[field, p] = (16 + 2 * side + slot, offset, rows)
                        offset += rows
    return found


SEGMENTS = narrow_segments()
SLOTS = 20


def pack_body(at, psi, velocity, low, high, link, chip):
    odd = lax.rem(at[1], 2) == 1
    level, speeds = wide_planes(psi, velocity, low, high)
    fields = [level] + speeds
    for k in range(SLOTS):
        inside_slot = [(offset, f, p, rows) for (f, p), (slot, offset, rows) in SEGMENTS.items() if slot == k]
        first, final, total = [], [], 0
        for offset, f, p, rows in sorted(inside_slot):
            v = fields[f](p)
            first.append(v[0:rows])
            final.append(v[16 - rows : 16])
            total += rows
        if total < SENT:
            first.append(jnp.zeros((SENT - total, 256), F32))
            final.append(first[-1])
        first = jnp.concatenate(first, axis=0)
        final = jnp.concatenate(final, axis=0)
        chip[k] = jnp.where(odd, first, final)
        link[k] = jnp.where(odd, final, first)


def pack(at, psi, velocity, low, high):
    outs = [(SLOTS, SENT, 256)] * 2
    return call(pack_body, outs, [], [at, psi, velocity, low, high], 1000000)


FACE = 0.25 / 12.0


def indicators(a, b, c):
    d = a - c
    curve = (a + c) - 2.0 * b
    twice = 2.0 * curve
    base = (13.0 / 12.0) * (curve * curve) + WENO_EPS
    up, down = twice - d, twice + d
    p = base + 0.25 * (up * up)
    q = base + 0.25 * (d * d)
    r = base + 0.25 * (down * down)
    return p * p, q * q, r * r


def upwind_flux(s, l, p_left, q_left, r_left, p_right, q_right, r_right):
    ahead = s > 0.0
    pick = lambda x, y: jnp.where(ahead, x, y)
    a, b, c, e, f = pick(l[0], l[5]), pick(l[1], l[4]), pick(l[2], l[3]), pick(l[3], l[2]), pick(l[4], l[1])
    p, q, r = pick(p_left, r_right), pick(q_left, q_right), pick(r_left, p_right)
    w0, w1, w2 = q * r, 6.0 * (p * r), 3.0 * (p * q)
    g0 = 2.0 * a - 7.0 * b + 11.0 * c
    g1 = 5.0 * c + 2.0 * e - b
    g2 = 2.0 * c + 5.0 * e - f
    top = w0 * g0 + w1 * g1 + w2 * g2
    total = w0 + w1 + w2
    return (s * top) / total


def z_change(v, w):
    lane = iota(v.shape, 1)

    def ahead(x, k):
        return jnp.where(lane > 255 - k, 0.0, roll(x, -k, 1))

    def behind(x, k):
        return jnp.where(lane < k, 0.0, roll(x, k, 1))

    l = [behind(v, 2), behind(v, 1), v, ahead(v, 1), ahead(v, 2), ahead(v, 3)]
    s = FACE * (w + ahead(w, 1))
    p, q, r = indicators(l[1], l[2], l[3])
    _, q1, r1 = indicators(l[2], l[3], l[4])
    _, _, r2 = indicators(l[3], l[4], l[5])
    p0, _, _ = indicators(l[0], l[1], l[2])
    flux = upwind_flux(s, l, p0, q, r1, p, q1, r2)
    low = slice(0, 128)
    c = v[:, low]
    none = jnp.zeros_like(c)
    square = c * c
    edge = WENO_EPS + (13.0 / 12.0 + 9.0 / 4.0) * square
    level = WENO_EPS + (13.0 / 12.0 + 1.0 / 4.0) * square
    wall_flux = upwind_flux(
        FACE * w[:, low],
        [none, none, none, c, l[3][:, low], l[4][:, low]],
        none + WENO_EPS * WENO_EPS, level * level, r[:, low],
        edge * edge, q[:, low], r1[:, low],
    )
    wall_flux = jnp.concatenate([wall_flux, wall_flux], axis=1)
    return flux - jnp.where(lane == 0, wall_flux, roll(flux, 1, 1))


def y_change(v, w):
    s = FACE * (w + roll(w, -1, 0))
    l = [roll(v, 2 - k, 0) for k in range(6)]
    p, q, r = indicators(l[1], l[2], l[3])
    q_next, r_next = roll(q, -1, 0), roll(r, -1, 0)
    flux = upwind_flux(s, l, roll(p, 1, 0), q, r_next, p, q_next, roll(r, -2, 0))
    return flux - roll(flux, 1, 0)


SKIN = 3


def x_marks(v, planes, marks):
    for i in range(planes):
        marks[0][i], marks[1][i], marks[2][i] = indicators(v(i - FAR), v(i - FAR + 1), v(i - FAR + 2))


def x_flux(f, v, w, marks):
    p_x, q_x, r_x = marks
    l = [v(f - 3 + k) for k in range(6)]
    return upwind_flux(
        FACE * (w(f - 1) + w(f)), l,
        p_x[f + 3], q_x[f + 4], r_x[f + 5], p_x[f + 4], q_x[f + 5], r_x[f + 6],
    )


def xz_change(v, u, w, marks, out, known=None):
    x_marks(v, 26, marks)
    below = x_flux(-SKIN, v, u, marks)
    for p in range(-SKIN, 16 + SKIN):
        above = x_flux(p + 1, v, u, marks)
        along_z = known[p] if known is not None and 0 <= p < 16 else z_change(v(p), w(p))
        out[p + SKIN] = (above - below) + along_z
        below = above


def inner_z_body(psi, velocity, out):
    for p in range(16):
        out[p] = z_change(psi[p], velocity[2, p])


def inner_z(psi, velocity):
    return call(inner_z_body, [(16, 16, 256)], [], [psi, velocity], 8000000)[0]


def inner_body(psi, velocity, low, high, known, out, *marks):
    level, speeds = wide_planes(psi, velocity, low, high)
    xz_change(level, speeds[0], speeds[2], marks, out, known)


def inner(psi, velocity, low, high, known):
    block = (16 + 2 * SKIN, 16, 256)
    scratch = [(26, 16, 256)] * 3
    return call(inner_body, [block], scratch, [psi, velocity, low, high, known], 8000000)[0]


def advance_body(
    nx, ny, at, psi, velocity, low, high, link, chip, change_in, moved, source, first, final,
    v8, u8, w8, v32, u32, c8, p_x, q_x, r_x, m, n_x, n_y, n_z, s_x, part,
):
    lower, upper = pick_sides(at, chip, link)
    level, speeds = wide_planes(psi, velocity, low, high)
    fields = [level] + speeds

    def halo(field, p, most):
        if (field, p) not in SEGMENTS:
            return 0, None, None
        slot, offset, rows = SEGMENTS[field, p]
        count = min(most, rows)
        below = lower(slot)[offset + rows - count : offset + rows]
        return count, below, upper(slot)[offset : offset + count]

    def beside_only(ref, i, field, p):
        ref[i] = jnp.zeros((8, 256), F32)
        count, below, above = halo(field, p, 4)
        if count:
            ref[i, 4 - count : 4, :] = below
            ref[i, 4 : 4 + count, :] = above

    def with_rows(ref, i, field, p, start):
        total = ref.shape[1]
        ref[i, 0:start, :] = jnp.zeros((start, 256), F32)
        ref[i, start + 16 : total, :] = jnp.zeros((total - start - 16, 256), F32)
        count, below, above = halo(field, p, start)
        ref[i, start : start + 16, :] = fields[field](p)
        if count:
            ref[i, start - count : start, :] = below
            ref[i, start + 16 : start + 16 + count, :] = above

    for p in range(-FAR, 16 + FAR):
        beside_only(v8, p + FAR, 0, p)
        if -ALONG <= p < 16 + ALONG:
            beside_only(u8, p + ALONG, 1, p)
        if -SKIN <= p < 16 + SKIN:
            beside_only(w8, p + SKIN, 3, p)
            with_rows(v32, p + SKIN, 0, p, 8)
            with_rows(u32, p + SKIN, 2, p, 8)

    xz_change(
        lambda p: v8[p + FAR], lambda p: u8[p + ALONG], lambda p: w8[p + SKIN], (p_x, q_x, r_x), c8
    )
    shape = (24, 256)
    mask = row_mask(shape, at[1] * 16 - 4, ny)
    for p in range(-SKIN, 16 + SKIN):
        i = p + SKIN
        sides = c8[i]
        change = jnp.concatenate([sides[0:4], change_in[i], sides[4:8]], axis=0)
        v = v32[i]
        change = change + y_change(v, u32[i])[4:28, :]
        value = wall(at, nx, 0, p, (v[4:28, :] - change) * mask)
        m[i] = value
        if 0 <= p < 16:
            moved[p] = value[4:20, :]

    lane = iota(shape, 1)

    def gradient(p):
        c = m[p + SKIN]
        down, ahead = z_shifted(c)
        gx = 0.5 * (m[p + SKIN + 1] - m[p + SKIN - 1])
        gy = 0.5 * (roll(c, -1, 0) - roll(c, 1, 0))
        return gx, gy, 0.5 * (ahead - down)

    for p in range(-2, 18):
        gx, gy, gz = gradient(p)
        inverse = lax.rsqrt(gx * gx + gy * gy + gz * gz + DELTA_SQ)
        n_x[p + 2], n_y[p + 2], n_z[p + 2] = gx * inverse, gy * inverse, gz * inverse
    for p in range(-1, 17):
        gx, gy, gz = gradient(p)
        edge = 0.5 * m[p + SKIN]
        edge = edge * lax.rsqrt(edge * edge + DELTA_SQ)
        nz, ny_here = n_z[p + 2], n_y[p + 2]
        ahead = jnp.where(lane == 255, -edge, roll(nz, -1, 1))
        behind = jnp.where(lane == 0, edge, roll(nz, 1, 1))
        bending = -0.5 * (
            (n_x[p + 3] - n_x[p + 1])
            + (roll(ny_here, -1, 0) - roll(ny_here, 1, 0))
            + (ahead - behind)
        )
        bending = wall(at, nx, 0, p, bending * mask)
        s_x[p + 1] = (bending * gx)[4:20, :] + speeds[0](p)
        if 0 <= p < 16:
            sy = bending * gy + u32[p + SKIN, 4:28, :]
            dy = roll(sy, -1, 0) - roll(sy, 1, 0)
            sz = (bending * gz)[4:20, :] + velocity[2, p]
            behind, ahead = z_shifted(sz)
            part[p] = dy[4:20, :] + (ahead - behind)
    for p in range(16):
        source[p] = -0.5 * (part[p] + (s_x[p + 2] - s_x[p]))
    for i in range(HALO):
        first[i] = source[i]
        final[i] = source[16 - HALO + i]


def advance(nx, ny, at, psi, velocity, low, high, chip, link, change):
    marks, normals, block = (26, 8, 256), (20, 24, 256), (16, 16, 256)
    skin = 16 + 2 * SKIN
    scratch = [
        (16 + 2 * FAR, 8, 256), (16 + 2 * ALONG, 8, 256), (skin, 8, 256), (skin, 32, 256),
        (skin, 32, 256), (skin, 8, 256), marks, marks, marks,
        (skin, 24, 256), normals, normals, normals, (18, 16, 256), block,
    ]
    args = [at, psi, velocity, low, high, link, chip, change]
    outs = [block, block, (HALO, 16, 256), (HALO, 16, 256)]
    return call(functools.partial(advance_body, nx, ny), outs, scratch, args, 30000000)


class Field:
    def __init__(self, ref, lead):
        self.ref, self.lead = ref, lead

    def __getitem__(self, p):
        return self.ref[p + self.lead]

    def __setitem__(self, p, value):
        self.ref[p + self.lead] = value

    def beside(self, p):
        return beside(self.ref, p + self.lead)


def wall(at, nx, level, p, value):
    own = 16 >> level
    if 0 <= p < own:
        return value
    return value * plane_factor(at[0] * own + p, nx >> level)


def first_smooth(b, v, planes, weight, mask, at, nx, level):
    for p in planes:
        c, around = b.beside(p)
        v[p] = wall(at, nx, level, p, (weight * mask) * (1.2 * c + SIDE * around))


def sweep(src, dst, b, planes, factor, mask, at, nx, level):
    keep = SIDE * mask
    for p in planes:
        c, around = src.beside(p)
        near = around + (b[p] if factor == 1 else factor * b[p])
        dst[p] = 0.2 * c + wall(at, nx, level, p, keep) * near


def coarsen_level0(at, nx, ny, b, v, b1, planes, pair, t):
    first = planes[0]
    rows = t.shape[1]

    def residual(p):
        c, around = v.beside(p)
        return b[p] - (6.0 * c - around)

    for p in planes:
        total = residual(2 * p) + residual(2 * p + 1)
        for half in range(2):
            lanes = slice(128 * half, 128 * half + 128)
            pair[p - first, half] = total[:, lanes]
            even = pair[p - first, half, pl.ds(0, rows, stride=2), :]
            odd = pair[p - first, half, pl.ds(1, rows, stride=2), :]
            t[p - first, :, lanes] = even + odd
    count = len(planes)
    full = dot(t[...].reshape(count * rows, 256), pair_matrix(256, 128, 0.125))
    full = full.reshape(count, rows, 128)
    mask = row_mask((rows, 128), at[1] * 8 + 4 - rows // 2, ny // 2)
    for p in planes:
        b1[p] = wall(at, nx, 1, p, full[p - first] * mask)


def smooth_level1(at, nx, ny, b1, u, planes):
    rows = b1.ref.shape[1]
    mask = row_mask((rows, 128), at[1] * 8 + 4 - rows // 2, ny // 2)
    first_smooth(b1, u, planes, 4.0 * SIDE, mask, at, nx, 1)


def coarsen_level1(b1, u, b2_out, s1, t1):
    start = b1.ref.shape[1] // 2 - 4
    t1[...] = jnp.zeros_like(t1)
    for k in range(4):
        total = 0.0
        for p in (2 * k, 2 * k + 1):
            c, around = u.beside(p)
            total = total + (b1[p] - 0.25 * (6.0 * c - around))
        s1[k] = total
        t1[k, 0:4, :] = s1[k, pl.ds(start, 4, stride=2), :] + s1[k, pl.ds(start + 1, 4, stride=2), :]
    small = dot(t1[...].reshape(32, 128), pair_matrix(128, 128, 0.125)).reshape(4, 8, 128)
    tile = jnp.concatenate([small[0, 0:4], small[1, 0:4]], axis=0) + roll(
        jnp.concatenate([small[2, 0:4], small[3, 0:4]], axis=0), 64, 1
    )
    b2_out[...] = tile


def reach(extra):
    e0 = extra + 2
    r1 = -(-e0 // 2)
    e1 = r1 + 2
    r2 = -(-e1 // 2)
    e2 = r2 + 2
    r3 = -(-e2 // 2)
    return e0, r1, e1, r2, e2, r3


E0, R1, E1, R2, E2, R3 = reach(KEEP)


def source_segments():
    whole, parts = [], []
    for p in range(-HALO, 16 + HALO):
        d = max(-p, p - 15, 0)
        rows = 16 - max(d, 2)
        if rows >= 8:
            whole.append((p, 0, 8))
        if rows % 8:
            parts.append((p, rows // 8 * 8, rows % 8))
    found = [(p, n, rows, tile, 0) for tile, (p, n, rows) in enumerate(whole)]
    room = []
    for p, n, rows in sorted(parts, key=lambda part: (-part[2], part[0])):
        for k, used in enumerate(room):
            if used + rows <= 8:
                break
        else:
            k = len(room)
            room.append(0)
        found.append((p, n, rows, len(whole) + k, room[k]))
        room[k] += rows
    return found, len(whole) + len(room)


SOURCE_SEGMENTS, SOURCE_TILES = source_segments()


def source_plane(own, low, high, p):
    return low[p + HALO] if p < 0 else own[p] if p < 16 else high[p - 16]


def weave_body(at, own, low, high, link, chip):
    odd = lax.rem(at[1], 2) == 1
    for k in range(SOURCE_TILES):
        first, final, total = [], [], 0
        for p, n, rows, tile, offset in sorted(SOURCE_SEGMENTS, key=lambda part: part[4]):
            if tile == k:
                v = source_plane(own, low, high, p)
                first.append(v[n : n + rows])
                final.append(v[16 - n - rows : 16 - n])
                total += rows
        if total < 8:
            first.append(jnp.zeros((8 - total, 256), F32))
            final.append(first[-1])
        if len(first) > 1:
            first = [jnp.concatenate(first, axis=0)]
            final = [jnp.concatenate(final, axis=0)]
        chip[k] = jnp.where(odd, first[0], final[0])
        link[k] = jnp.where(odd, final[0], first[0])


def weave(at, own, low, high):
    outs = [(SOURCE_TILES, 8, 256)] * 2
    return call(weave_body, outs, [], [at, own, low, high], 1000000)


def first_down_body(
    nx, ny, at, own, low, high, link, chip, b_out, v_out, b1_out, u_out, b2_out, b, v, pair, t, s1, t1
):
    lower, upper = pick_sides(at, chip, link)
    none = jnp.zeros((16, 256), F32)
    for p in range(-HALO, 16 + HALO):
        b[p + HALO, 0:16, :] = none
        b[p + HALO, 16:32, :] = source_plane(own, low, high, p)
        b[p + HALO, 32:48, :] = none
    for p, n, rows, tile, offset in SOURCE_SEGMENTS:
        cut = slice(offset, offset + rows)
        b[p + HALO, 16 - n - rows : 16 - n, :] = lower(tile)[cut]
        b[p + HALO, 32 + n : 32 + n + rows, :] = upper(tile)[cut]
    b, v = Field(b, HALO), Field(v, HALO - 1)
    mask = row_mask((48, 256), at[1] * 16 - 16, ny)
    first_smooth(b, v, range(1 - HALO, 15 + HALO), SIDE, mask, at, nx, 0)
    v_out, b_out = Field(v_out, E0), Field(b_out, E0 - 1)
    for p in range(-E0, 16 + E0):
        v_out[p] = v[p][8:40, :]
    for p in range(1 - E0, 15 + E0):
        b_out[p] = b[p][8:40, :]
    b1, u = Field(b1_out, E1 + 1), Field(u_out, E1)
    coarsen_level0(at, nx, ny, b, v, b1, range(-E1 - 1, 9 + E1), pair, t)
    smooth_level1(at, nx, ny, b1, u, range(-E1, 8 + E1))
    coarsen_level1(b1, u, b2_out, s1, t1)


def around_block(size, extra, rows, lanes):
    return (size + 2 * extra, rows, lanes)


def first_down(nx, ny, at, own, low, high, chip, link):
    level1 = around_block(8, E1 + 1, 24, 128)
    outs = [
        around_block(16, E0 - 1, 32, 256),
        around_block(16, E0, 32, 256),
        level1,
        around_block(8, E1, 24, 128),
        (8, 128),
    ]
    scratch = [
        around_block(16, HALO, 48, 256),
        around_block(16, HALO - 1, 48, 256),
        (level1[0], 2, 48, 128),
        (level1[0], 24, 256),
        (4, 24, 128),
        (4, 8, 128),
    ]
    args = [at, own, low, high, link, chip]
    return call(functools.partial(first_down_body, nx, ny), outs, scratch, args, 20000000)


def second_down_body(nx, ny, at, mid, chip, link, b1_out, u_out, b2_out, s1, t1):
    lower, upper = pick_sides(at, chip, link)
    for i in range(8 + 2 * NEAR):
        b1_out[i, 0:8, :] = lower(i)
        b1_out[i, 8:16, :] = mid[i]
        b1_out[i, 16:24, :] = upper(i)
    b1, u = Field(b1_out, NEAR), Field(u_out, NEAR - 1)
    smooth_level1(at, nx, ny, b1, u, range(1 - NEAR, 7 + NEAR))
    coarsen_level1(b1, u, b2_out, s1, t1)


def second_down(nx, ny, at, mid, chip, link):
    outs = [around_block(8, NEAR, 24, 128), around_block(8, NEAR - 1, 24, 128), (8, 128)]
    scratch = [(4, 24, 128), (4, 8, 128)]
    args = [at, mid, chip, link]
    return call(functools.partial(second_down_body, nx, ny), outs, scratch, args, 2000000)


def solve_coarse(nx, ny, extra, at, coarse, s2, v2, w2, t3, b3, c3, d3, dup, row2):
    fetched, other = coarse
    odd = lax.rem(at[1], 2) == 1
    odd_layer = lax.rem(at[0] // GROUP, 2)
    _, _, _, r2, e2, r3 = reach(extra)
    spot = at[0] % GROUP
    rows2 = ny // 4
    rows3 = rows2 // 2
    count = rows2 // 4
    lead = 2 * (r3 + 3) + 2
    blocks = -(-lead // 4)
    s2, v2, w2 = Field(s2, 4 * blocks), Field(v2, lead - 1), Field(w2, e2)
    lane8 = iota((8, 128), 1) < 64
    for j in range(-blocks, blocks + 1):
        block = spot + GROUP + j
        layer, place = block // GROUP, block % GROUP
        first_cores = jnp.where(odd_layer == 1, layer <= 1, layer >= 1)
        mine = first_cores != odd
        inner = inside(at[0] + j, nx // 16)
        start = ((layer + odd_layer) // 2) * (GROUP * count // 2) + place * (count // 2)
        for n in range(count):
            rows = slice(8 * (n % 2), 8 * (n % 2) + 8)
            k = start + n // 2
            tile = jnp.where(mine, fetched[k, rows, :], other[k, rows, :])
            tile = jnp.where(inner, tile, 0.0)
            halves = (jnp.where(lane8, tile, 0.0), jnp.where(lane8, roll(tile, 64, 1), 0.0))
            for p in range(4):
                part = halves[p // 2][4 * (p % 2) : 4 * (p % 2) + 4, :]
                s2.ref[4 * (j + blocks) + p, 4 * n : 4 * n + 4, :] = part

    def around(f, p):
        c = f[p]
        row = iota(c.shape, 0)
        lower = jnp.where(row == 0, 0.0, roll(c, 1, 0))
        upper = jnp.where(row == c.shape[0] - 1, 0.0, roll(c, -1, 0))
        beside = (lower + upper) + (roll(c, 1, 1) + roll(c, -1, 1))
        return c, (f[p - 1] + f[p + 1]) + beside

    def lanes_below(rows, lanes):
        return jnp.where(iota((rows, 128), 1) < lanes, 1.0, 0.0).astype(F32)

    mask2 = lanes_below(rows2, 64)
    for p in range(1 - lead, 3 + lead):
        c, near = around(s2, p)
        v2[p] = wall(at, nx, 2, p, (16.0 * SIDE) * mask2 * (1.2 * c + SIDE * near))

    def residual2(p):
        c, near = around(v2, p)
        return s2[p] - (1.0 / 16.0) * (6.0 * c - near)

    planes3 = range(-r3 - 3, 2 + r3 + 3)
    for i, p in enumerate(planes3):
        row2[i] = residual2(2 * p) + residual2(2 * p + 1)
        t3[i] = row2[i, pl.ds(0, rows3, stride=2), :] + row2[i, pl.ds(1, rows3, stride=2), :]
    total3 = len(planes3)
    full = dot(t3[...].reshape(total3 * rows3, 128), pair_matrix(128, 128, 0.125))
    full = full.reshape(total3, rows3, 128)
    mask3 = lanes_below(rows3, 32)
    b3, c3, d3 = Field(b3, r3 + 3), Field(c3, r3 + 3), Field(d3, r3 + 3)
    for i, p in enumerate(planes3):
        value = wall(at, nx, 3, p, full[i] * ((64.0 * SIDE) * mask3))
        b3[p] = value
    src, dst = b3, c3
    for step in (2, 1, 0):
        for p in range(-r3 - step, 2 + r3 + step):
            c, near = around(src, p)
            dst[p] = wall(at, nx, 3, p, mask3 * (0.2 * c + SIDE * near)) + b3[p]
        src, dst = dst, (d3 if dst is c3 else c3)
    final = src
    planes = range(-r3, 2 + r3)
    flat = jnp.concatenate([final[p] for p in planes], axis=0)
    spread = dot(flat, copy_matrix(128, 128)).reshape(len(planes), rows3, 128)
    for i, p in enumerate(planes):
        dup[i, pl.ds(0, rows3, stride=2), :] = spread[i]
        dup[i, pl.ds(1, rows3, stride=2), :] = spread[i]
        for q in (2 * p, 2 * p + 1):
            if -e2 <= q < 4 + e2:
                v2[q] = v2[q] + wall(at, nx, 2, q, dup[i, 0:rows2, :] * mask2)
    keep = SIDE * mask2
    for src, dst, step in ((v2, w2, 1), (w2, v2, 0)):
        for p in range(-r2 - step, 4 + r2 + step):
            c, near = around(src, p)
            dst[p] = 0.2 * c + wall(at, nx, 2, p, keep) * (near + 16.0 * s2[p])
    return v2


def coarse_scratch(ny, extra):
    _, _, _, _, e2, r3 = reach(extra)
    rows2 = ny // 4
    rows3 = rows2 // 2
    lead = 2 * (r3 + 3) + 2
    small = around_block(2, r3 + 3, rows3, 128)
    return [
        around_block(4, -(-lead // 4) * 4, rows2, 128),
        around_block(4, lead - 1, rows2, 128),
        around_block(4, e2, rows2, 128),
        small, small, small, small,
        (8, 48, 128),
        around_block(2, r3 + 3, rows2, 128),
    ]


def climb(nx, ny, extra, at, v2, b1, u, b, v_down, m1, n1, m0, n0, dup):
    e0, r1, e1, r2, _, _ = reach(extra)
    rows2 = ny // 4
    turn = lax.rem(rows2 + 4 - 4 * at[1] + rows2, rows2)
    planes = range(-r2, 4 + r2)
    picked = jnp.concatenate([pltpu.roll(v2[p], turn, 0)[0:16, :] for p in planes], axis=0)
    spread = dot(picked, copy_matrix(128, 128)).reshape(len(planes), 16, 128)
    mask1 = row_mask((24, 128), at[1] * 8 - 8, ny // 2)
    m1, n1 = Field(m1, e1), Field(n1, e1)
    for i, p in enumerate(planes):
        dup[i, 0, pl.ds(0, 12, stride=2), :] = spread[i, 0:12, :]
        dup[i, 0, pl.ds(1, 12, stride=2), :] = spread[i, 0:12, :]
        for q in (2 * p, 2 * p + 1):
            if -e1 <= q < 8 + e1:
                m1[q] = u[q] + wall(at, nx, 1, q, dup[i, 0, 0:24, :] * mask1)
    sweep(m1, n1, b1, range(1 - e1, 7 + e1), 4.0, mask1, at, nx, 1)
    sweep(n1, m1, b1, range(2 - e1, 6 + e1), 4.0, mask1, at, nx, 1)
    planes = range(-r1, 8 + r1)
    flat = jnp.concatenate([m1[p][4:20, :] for p in planes], axis=0)
    spread = dot(flat, copy_matrix(128, 256)).reshape(len(planes), 16, 256)
    mask0 = row_mask((32, 256), at[1] * 16 - 8, ny)
    m0, n0 = Field(m0, e0), Field(n0, e0)
    for i, p in enumerate(planes):
        for half in range(2):
            value = spread[i, :, 128 * half : 128 * half + 128]
            dup[i, half, pl.ds(0, 16, stride=2), :] = value
            dup[i, half, pl.ds(1, 16, stride=2), :] = value
        value = jnp.concatenate([dup[i, 0], dup[i, 1]], axis=1) * mask0
        for q in (2 * p, 2 * p + 1):
            if -e0 <= q < 16 + e0:
                m0[q] = v_down[q] + wall(at, nx, 0, q, value)
    sweep(m0, n0, b, range(1 - e0, 15 + e0), 1, mask0, at, nx, 0)
    if extra:
        sweep(n0, m0, b, range(2 - e0, 14 + e0), 1, mask0, at, nx, 0)
        return m0
    return n0


def climb_scratch(extra):
    e0, r1, e1, r2, _, _ = reach(extra)
    level1 = around_block(8, e1, 24, 128)
    level0 = around_block(16, e0, 32, 256)
    return [level1, level1, level0, level0, (max(8 + 2 * r1, 4 + 2 * r2), 2, 32, 128)]


def turn_body(nx, ny, at, fetched, other, b1, u, b, v_down, v_out, wider, low, high, own, pair, t, *scratch):
    v2 = solve_coarse(nx, ny, KEEP, at, (fetched, other), *scratch[:9])
    b = Field(b, E0 - 1)
    v = climb(nx, ny, KEEP, at, v2, Field(b1, E1 + 1), Field(u, E1), b, Field(v_down, E0), *scratch[9:])
    mask = row_mask((32, 256), at[1] * 16 - 8, ny)
    once, twice = Field(scratch[12], E0), Field(v_out, KEEP - 2)
    sweep(v, once, b, range(1 - KEEP, 15 + KEEP), 1, mask, at, nx, 0)
    sweep(once, twice, b, range(2 - KEEP, 14 + KEEP), 1, mask, at, nx, 0)
    coarsen_level0(at, nx, ny, b, twice, Field(own, 0), range(8), pair, t)
    for i in range(8):
        wider[NEAR + i] = own[i, 4:12, :]
    for i in range(NEAR):
        low[i] = own[i, 4:12, :]
        high[i] = own[8 - NEAR + i, 4:12, :]


def turn(nx, ny, at, coarse, b1, u, b, v_down):
    outs = [
        around_block(16, KEEP - 2, 32, 256),
        around_block(8, NEAR, 8, 128),
        (NEAR, 8, 128),
        (NEAR, 8, 128),
    ]
    scratch = [(8, 16, 128), (8, 2, 32, 128), (8, 16, 256)]
    scratch += coarse_scratch(ny, KEEP) + climb_scratch(KEEP)
    args = [at, *coarse, b1, u, b, v_down]
    return call(functools.partial(turn_body, nx, ny), outs, scratch, args, 30000000)


def finish_body(nx, ny, at, fetched, other, b1, u, b, v_down, out, *scratch):
    v2 = solve_coarse(nx, ny, 0, at, (fetched, other), *scratch[:9])
    b, v_down = Field(b, E0 - 1), Field(v_down, KEEP - 2)
    v = climb(nx, ny, 0, at, v2, Field(b1, NEAR), Field(u, NEAR - 1), b, v_down, *scratch[9:])
    for p in range(16):
        c, around = v.beside(p)
        out[p] = (0.2 * c + SIDE * (around + b[p]))[8:24, :]


def finish(nx, ny, at, coarse, b1, u, b, v_down):
    scratch = coarse_scratch(ny, 0) + climb_scratch(0)
    args = [at, *coarse, b1, u, b, v_down]
    return call(functools.partial(finish_body, nx, ny), [(16, 16, 256)], scratch, args, 20000000)[0]


def shifted(array, axis, step):
    count = lax.axis_size(axis)
    return lax.ppermute(
        array, axis, [(i, i + step) for i in range(count) if 0 <= i + step < count]
    )


def swapped(array, first):
    count = lax.axis_size("narrow")
    pairs = [(i, i + 1) for i in range(first, count - 1, 2)]
    return lax.ppermute(array, "narrow", pairs + [(j, i) for i, j in pairs])


def widen(wider, low, high):
    planes = low.shape[0]
    wider = lax.dynamic_update_slice(wider, shifted(high, "wide", 1), (0, 0, 0))
    upper = wider.shape[0] - planes
    return lax.dynamic_update_slice(wider, shifted(low, "wide", -1), (upper, 0, 0))


def surround(wider, low, high):
    mid = widen(wider, low, high)
    link = swapped(mid, 1)
    return mid, swapped(mid, 0), link


def spread_coarse(b2):
    wide, cores = lax.axis_size("wide"), lax.axis_size("narrow")
    layers = wide // GROUP
    odd = lax.rem(lax.axis_index("narrow"), 2) == 1
    other = swapped(b2, 0)
    pair = jnp.concatenate([jnp.where(odd, other, b2), jnp.where(odd, b2, other)], axis=0)
    groups = [
        [
            (((2 * k + core + i) % layers) * GROUP + x) * cores + y
            for i in range(2)
            for x in range(GROUP)
            for y in range(core, cores, 2)
        ]
        for core in range(2)
        for k in range(layers // 2)
    ]
    pieces = jnp.broadcast_to(pair[None], (len(groups[0]),) + pair.shape)
    fetched = lax.all_to_all(pieces, ("wide", "narrow"), 0, 0, axis_index_groups=groups)
    return fetched, swapped(fetched, 0)


def on_device(phase, distance, velocity):
    nx, ny = 16 * lax.axis_size("wide"), 16 * lax.axis_size("narrow")
    at = jnp.stack([lax.axis_index("wide"), lax.axis_index("narrow")]).astype(jnp.int32)
    psi, x_low, x_high = prepare(phase, distance, velocity)
    low, high = shifted(x_high, "wide", 1), shifted(x_low, "wide", -1)
    known = inner_z(psi, velocity)
    link, chip = pack(at, psi, velocity, low, high)
    v_link = swapped(link, 1)
    v_chip = swapped(chip, 0)
    change = inner(psi, velocity, low, high, known)
    moved, source, first, final = advance(
        nx, ny, at, psi, velocity, low, high, v_chip, v_link, change
    )
    low, high = shifted(final, "wide", 1), shifted(first, "wide", -1)
    link, chip = weave(at, source, low, high)
    b_link = swapped(link, 1)
    b_chip = swapped(chip, 0)
    b, v, b1, u, b2 = first_down(nx, ny, at, source, low, high, b_chip, b_link)
    v, *sends = turn(nx, ny, at, spread_coarse(b2), b1, u, b, v)
    b1, u, b2 = second_down(nx, ny, at, *surround(*sends))
    pressure = finish(nx, ny, at, spread_coarse(b2), b1, u, b, v)
    return (moved, pressure)


def solution(mesh):
    blocks = P("wide", "narrow", None)
    return jax.shard_map(
        on_device,
        mesh=mesh,
        in_specs=(blocks, blocks, P(None, "wide", "narrow", None)),
        out_specs=(blocks, blocks),
        check_vma=False,
    )
```

```python
import functools

import jax
import jax.numpy as jnp
from jax import lax
from jax.experimental import pallas as pl
from jax.experimental.pallas import tpu as pltpu
from jax.sharding import PartitionSpec as P

DELTA_SQ = 0.0025
WENO_EPS = 0.01
SIDE = 0.8 / 6.0
F32 = jnp.float32

HALO = 14
KEEP = 4
NEAR = 4
GROUP = 4


def iota(shape, dim):
    return lax.broadcasted_iota(jnp.int32, shape, dim)


def roll(v, shift, axis):
    return pltpu.roll(v, shift % v.shape[axis], axis)


def z_shifted(v):
    lane = iota(v.shape, 1)
    last = v.shape[1] - 1
    lower = jnp.where(lane == 0, 0.0, roll(v, 1, 1))
    upper = jnp.where(lane == last, 0.0, roll(v, -1, 1))
    return lower, upper


def z_pair(v):
    lower, upper = z_shifted(v)
    return lower + upper


def y_pair(v):
    return roll(v, 1, 0) + roll(v, -1, 0)


def beside(ref, i):
    c = ref[i]
    return c, (ref[i - 1] + ref[i + 1]) + y_pair(c) + z_pair(c)


def inside(first, count):
    return jnp.logical_and(first >= 0, first < count)


def row_mask(shape, first, count):
    rows = iota(shape, 0) + first
    return jnp.where(inside(rows, count), 1.0, 0.0).astype(F32)


def plane_factor(index, count):
    return jnp.where(inside(index, count), 1.0, 0.0).astype(F32)


def dot(a, b):
    b = b.astype(jnp.bfloat16)
    high = a.astype(jnp.bfloat16)
    low = (a - high.astype(F32)).astype(jnp.bfloat16)
    return jnp.dot(high, b, preferred_element_type=F32) + jnp.dot(low, b, preferred_element_type=F32)


def pair_matrix(rows, cols, value):
    return jnp.where((iota((rows, cols), 0) >> 1) == iota((rows, cols), 1), value, 0.0).astype(F32)


def copy_matrix(rows, cols):
    return jnp.where(iota((rows, cols), 0) == (iota((rows, cols), 1) >> 1), 1.0, 0.0).astype(F32)


def words(shape):
    *lead, rows, lanes = (1,) * (3 - len(shape)) + tuple(shape)
    size = -(-rows // 8) * 8 * (-(-lanes // 128) * 128)
    for n in lead:
        size *= n
    return size


def call(body, outs, scratch, args, flops):
    vmem = pl.BlockSpec(memory_space=pltpu.VMEM)
    smem = pl.BlockSpec(memory_space=pltpu.SMEM)
    total = sum(words(a.shape) for a in args) + sum(map(words, outs)) + sum(map(words, scratch))
    return pl.pallas_call(
        body,
        out_shape=[jax.ShapeDtypeStruct(s, F32) for s in outs],
        in_specs=[smem if a.dtype == jnp.int32 and a.ndim == 1 else vmem for a in args],
        out_specs=[vmem] * len(outs),
        scratch_shapes=[pltpu.VMEM(s, F32) for s in scratch],
        compiler_params=pltpu.CompilerParams(vmem_limit_bytes=4 * total + (6 << 20)),
        cost_estimate=pl.CostEstimate(flops=flops, bytes_accessed=4000000, transcendentals=0),
    )(*args)


def pick_sides(at, chip, link):
    odd = lax.rem(at[1], 2) == 1
    lower = lambda *k: jnp.where(odd, chip[k], link[k])
    upper = lambda *k: jnp.where(odd, link[k], chip[k])
    return lower, upper


PARTS = 4
FAR, ALONG, ACROSS = 6, 4, 3
SENT = FAR + ALONG + 2 * ACROSS


def layer_cuts(dim):
    cuts, offset = [], FAR
    for component in range(3):
        layers = ALONG if component == dim else ACROSS
        cuts.append((component, layers, offset))
        offset += layers
    return cuts


def prepare_body(phase, distance, velocity, psi, x_low, x_high, kind, away, sems):
    step = 16 // PARTS
    copies = []

    def copy(src, dst):
        started = pltpu.make_async_copy(src, dst, sems.at[len(copies)])
        started.start()
        copies.append(started)

    for k in range(PARTS):
        planes = pl.ds(step * k, step)
        copy(phase.at[planes], kind.at[planes])
        copy(distance.at[planes], away.at[planes])
    for component, layers, offset in layer_cuts(0):
        copy(velocity.at[component, pl.ds(0, layers)], x_low.at[pl.ds(offset, layers)])
        copy(velocity.at[component, pl.ds(16 - layers, layers)], x_high.at[pl.ds(offset, layers)])
    for k in range(PARTS):
        copies[2 * k].wait()
        copies[2 * k + 1].wait()
        for i in range(step * k, step * k + step):
            orient = 2.0 * kind[i].astype(F32) - 1.0
            psi[i] = 1.0 / (1.0 + jnp.exp(-orient * away[i]))
    for k in range(FAR):
        x_low[k] = psi[k]
        x_high[k] = psi[16 - FAR + k]
    for started in copies[2 * PARTS :]:
        started.wait()


def prepare(phase, distance, velocity):
    vmem = pl.BlockSpec(memory_space=pltpu.VMEM)
    hbm = pl.BlockSpec(memory_space=pltpu.HBM)
    outs = [(16, 16, 256), (SENT, 16, 256), (SENT, 16, 256)]
    return pl.pallas_call(
        prepare_body,
        out_shape=[jax.ShapeDtypeStruct(s, F32) for s in outs],
        in_specs=[hbm, hbm, hbm],
        out_specs=[vmem] * len(outs),
        scratch_shapes=[
            pltpu.VMEM((16, 16, 256), jnp.int32),
            pltpu.VMEM((16, 16, 256), F32),
            pltpu.SemaphoreType.DMA((2 * PARTS + 6,)),
        ],
        compiler_params=pltpu.CompilerParams(vmem_limit_bytes=8 << 20),
        cost_estimate=pl.CostEstimate(flops=1000000, bytes_accessed=1000000, transcendentals=0),
    )(*(pltpu.with_memory_space_constraint(a, pltpu.HBM) for a in (phase, distance, velocity)))


def plane_of(own, low, high, p, offset, layers):
    if p < 0:
        return low[offset + layers + p]
    return own(p) if p < 16 else high[offset + p - 16]


def wide_planes(psi, velocity, low, high):
    def level(p):
        return plane_of(lambda k: psi[k], low, high, p, 0, FAR)

    def speed(component):
        _, layers, offset = layer_cuts(0)[component]

        def at_plane(p):
            if not -layers <= p < 16 + layers:
                return None
            return plane_of(lambda k: velocity[component, k], low, high, p, offset, layers)

        return at_plane

    return level, [speed(c) for c in range(3)]


def narrow_segments():
    reached = (FAR, ALONG, ALONG, ACROSS)
    rows_own = (FAR, ACROSS, ALONG, ACROSS)
    found = {}
    for p in range(16):
        offset = 0
        for field, rows in enumerate(rows_own):
            found[field, p] = (p, offset, rows)
            offset += rows
    for side, edge in enumerate((0, 15)):
        for slot, layers in enumerate(((1, 4, 5), (2, 3))):
            offset = 0
            for d in layers:
                p = edge - d if side == 0 else edge + d
                for field, reach_of in enumerate(reached):
                    rows = min(reach_of - d, rows_own[field])
                    if rows > 0:
                        found[field, p] = (16 + 2 * side + slot, offset, rows)
                        offset += rows
    return found


SEGMENTS = narrow_segments()
SLOTS = 20


def pack_body(at, psi, velocity, low, high, known, link, chip):
    odd = lax.rem(at[1], 2) == 1
    level, speeds = wide_planes(psi, velocity, low, high)
    fields = [level] + speeds
    for k in range(SLOTS):
        inside_slot = [(offset, f, p, rows) for (f, p), (slot, offset, rows) in SEGMENTS.items() if slot == k]
        first, final, total = [], [], 0
        for offset, f, p, rows in sorted(inside_slot):
            v = fields[f](p)
            first.append(v[0:rows])
            final.append(v[16 - rows : 16])
            total += rows
        if total < SENT:
            first.append(jnp.zeros((SENT - total, 256), F32))
            final.append(first[-1])
        first = jnp.concatenate(first, axis=0)
        final = jnp.concatenate(final, axis=0)
        chip[k] = jnp.where(odd, first, final)
        link[k] = jnp.where(odd, final, first)


def pack(at, psi, velocity, low, high, known):
    outs = [(SLOTS, SENT, 256)] * 2
    return call(pack_body, outs, [], [at, psi, velocity, low, high, known], 1000000)


FACE = 0.25 / 12.0


def indicators(a, b, c):
    d = a - c
    curve = (a + c) - 2.0 * b
    twice = 2.0 * curve
    base = (13.0 / 12.0) * (curve * curve) + WENO_EPS
    up, down = twice - d, twice + d
    p = base + 0.25 * (up * up)
    q = base + 0.25 * (d * d)
    r = base + 0.25 * (down * down)
    return p * p, q * q, r * r


def upwind_flux(s, l, p_left, q_left, r_left, p_right, q_right, r_right):
    ahead = s > 0.0
    pick = lambda x, y: jnp.where(ahead, x, y)
    a, b, c, e, f = pick(l[0], l[5]), pick(l[1], l[4]), pick(l[2], l[3]), pick(l[3], l[2]), pick(l[4], l[1])
    p, q, r = pick(p_left, r_right), pick(q_left, q_right), pick(r_left, p_right)
    w0, w1, w2 = q * r, 6.0 * (p * r), 3.0 * (p * q)
    g0 = 2.0 * a - 7.0 * b + 11.0 * c
    g1 = 5.0 * c + 2.0 * e - b
    g2 = 2.0 * c + 5.0 * e - f
    top = w0 * g0 + w1 * g1 + w2 * g2
    total = w0 + w1 + w2
    return (s * top) / total


def z_change(v, w):
    lane = iota(v.shape, 1)

    def ahead(x, k):
        return jnp.where(lane > 255 - k, 0.0, roll(x, -k, 1))

    def behind(x, k):
        return jnp.where(lane < k, 0.0, roll(x, k, 1))

    l = [behind(v, 2), behind(v, 1), v, ahead(v, 1), ahead(v, 2), ahead(v, 3)]
    s = FACE * (w + ahead(w, 1))
    p, q, r = indicators(l[1], l[2], l[3])
    _, q1, r1 = indicators(l[2], l[3], l[4])
    _, _, r2 = indicators(l[3], l[4], l[5])
    p0, _, _ = indicators(l[0], l[1], l[2])
    flux = upwind_flux(s, l, p0, q, r1, p, q1, r2)
    low = slice(0, 128)
    c = v[:, low]
    none = jnp.zeros_like(c)
    square = c * c
    edge = WENO_EPS + (13.0 / 12.0 + 9.0 / 4.0) * square
    level = WENO_EPS + (13.0 / 12.0 + 1.0 / 4.0) * square
    wall_flux = upwind_flux(
        FACE * w[:, low],
        [none, none, none, c, l[3][:, low], l[4][:, low]],
        none + WENO_EPS * WENO_EPS, level * level, r[:, low],
        edge * edge, q[:, low], r1[:, low],
    )
    wall_flux = jnp.concatenate([wall_flux, wall_flux], axis=1)
    return flux - jnp.where(lane == 0, wall_flux, roll(flux, 1, 1))


def y_change(v, w):
    s = FACE * (w + roll(w, -1, 0))
    l = [roll(v, 2 - k, 0) for k in range(6)]
    p, q, r = indicators(l[1], l[2], l[3])
    q_next, r_next = roll(q, -1, 0), roll(r, -1, 0)
    flux = upwind_flux(s, l, roll(p, 1, 0), q, r_next, p, q_next, roll(r, -2, 0))
    return flux - roll(flux, 1, 0)


SKIN = 3


def x_marks(v, planes, marks):
    for i in range(planes):
        marks[0][i], marks[1][i], marks[2][i] = indicators(v(i - FAR), v(i - FAR + 1), v(i - FAR + 2))


def x_flux(f, v, w, marks):
    p_x, q_x, r_x = marks
    l = [v(f - 3 + k) for k in range(6)]
    return upwind_flux(
        FACE * (w(f - 1) + w(f)), l,
        p_x[f + 3], q_x[f + 4], r_x[f + 5], p_x[f + 4], q_x[f + 5], r_x[f + 6],
    )


def xz_change(v, u, w, marks, out, known=None):
    x_marks(v, 26, marks)
    below = x_flux(-SKIN, v, u, marks)
    for p in range(-SKIN, 16 + SKIN):
        above = x_flux(p + 1, v, u, marks)
        along_z = known[p] if known is not None and 0 <= p < 16 else z_change(v(p), w(p))
        out[p + SKIN] = (above - below) + along_z
        below = above


def inner_z_body(psi, velocity, out):
    for p in range(16):
        out[p] = z_change(psi[p], velocity[2, p])


def inner_z(psi, velocity):
    return call(inner_z_body, [(16, 16, 256)], [], [psi, velocity], 8000000)[0]


def inner_body(psi, velocity, low, high, known, out, *marks):
    level, speeds = wide_planes(psi, velocity, low, high)
    xz_change(level, speeds[0], speeds[2], marks, out, known)


def inner(psi, velocity, low, high, known):
    block = (16 + 2 * SKIN, 16, 256)
    scratch = [(26, 16, 256)] * 3
    return call(inner_body, [block], scratch, [psi, velocity, low, high, known], 8000000)[0]


def advance_body(
    nx, ny, at, psi, velocity, low, high, link, chip, change_in, moved, source, first, final,
    v8, u8, w8, v32, u32, c8, p_x, q_x, r_x, m, n_x, n_y, n_z, s_x, part,
):
    lower, upper = pick_sides(at, chip, link)
    level, speeds = wide_planes(psi, velocity, low, high)
    fields = [level] + speeds

    def halo(field, p, most):
        if (field, p) not in SEGMENTS:
            return 0, None, None
        slot, offset, rows = SEGMENTS[field, p]
        count = min(most, rows)
        below = lower(slot)[offset + rows - count : offset + rows]
        return count, below, upper(slot)[offset : offset + count]

    def beside_only(ref, i, field, p):
        ref[i] = jnp.zeros((8, 256), F32)
        count, below, above = halo(field, p, 4)
        if count:
            ref[i, 4 - count : 4, :] = below
            ref[i, 4 : 4 + count, :] = above

    def with_rows(ref, i, field, p, start):
        total = ref.shape[1]
        ref[i, 0:start, :] = jnp.zeros((start, 256), F32)
        ref[i, start + 16 : total, :] = jnp.zeros((total - start - 16, 256), F32)
        count, below, above = halo(field, p, start)
        ref[i, start : start + 16, :] = fields[field](p)
        if count:
            ref[i, start - count : start, :] = below
            ref[i, start + 16 : start + 16 + count, :] = above

    for p in range(-FAR, 16 + FAR):
        beside_only(v8, p + FAR, 0, p)
        if -ALONG <= p < 16 + ALONG:
            beside_only(u8, p + ALONG, 1, p)
        if -SKIN <= p < 16 + SKIN:
            beside_only(w8, p + SKIN, 3, p)
            with_rows(v32, p + SKIN, 0, p, 8)
            with_rows(u32, p + SKIN, 2, p, 8)

    xz_change(
        lambda p: v8[p + FAR], lambda p: u8[p + ALONG], lambda p: w8[p + SKIN], (p_x, q_x, r_x), c8
    )
    shape = (24, 256)
    mask = row_mask(shape, at[1] * 16 - 4, ny)
    for p in range(-SKIN, 16 + SKIN):
        i = p + SKIN
        sides = c8[i]
        change = jnp.concatenate([sides[0:4], change_in[i], sides[4:8]], axis=0)
        v = v32[i]
        change = change + y_change(v, u32[i])[4:28, :]
        value = wall(at, nx, 0, p, (v[4:28, :] - change) * mask)
        m[i] = value
        if 0 <= p < 16:
            moved[p] = value[4:20, :]

    lane = iota(shape, 1)

    def gradient(p):
        c = m[p + SKIN]
        down, ahead = z_shifted(c)
        gx = 0.5 * (m[p + SKIN + 1] - m[p + SKIN - 1])
        gy = 0.5 * (roll(c, -1, 0) - roll(c, 1, 0))
        return gx, gy, 0.5 * (ahead - down)

    for p in range(-2, 18):
        gx, gy, gz = gradient(p)
        inverse = lax.rsqrt(gx * gx + gy * gy + gz * gz + DELTA_SQ)
        n_x[p + 2], n_y[p + 2], n_z[p + 2] = gx * inverse, gy * inverse, gz * inverse
    for p in range(-1, 17):
        gx, gy, gz = gradient(p)
        edge = 0.5 * m[p + SKIN]
        edge = edge * lax.rsqrt(edge * edge + DELTA_SQ)
        nz, ny_here = n_z[p + 2], n_y[p + 2]
        ahead = jnp.where(lane == 255, -edge, roll(nz, -1, 1))
        behind = jnp.where(lane == 0, edge, roll(nz, 1, 1))
        bending = -0.5 * (
            (n_x[p + 3] - n_x[p + 1])
            + (roll(ny_here, -1, 0) - roll(ny_here, 1, 0))
            + (ahead - behind)
        )
        bending = wall(at, nx, 0, p, bending * mask)
        s_x[p + 1] = (bending * gx)[4:20, :] + speeds[0](p)
        if 0 <= p < 16:
            sy = bending * gy + u32[p + SKIN, 4:28, :]
            dy = roll(sy, -1, 0) - roll(sy, 1, 0)
            sz = (bending * gz)[4:20, :] + velocity[2, p]
            behind, ahead = z_shifted(sz)
            part[p] = dy[4:20, :] + (ahead - behind)
    for p in range(16):
        source[p] = -0.5 * (part[p] + (s_x[p + 2] - s_x[p]))
    for i in range(HALO):
        first[i] = source[i]
        final[i] = source[16 - HALO + i]


def advance(nx, ny, at, psi, velocity, low, high, chip, link, change):
    marks, normals, block = (26, 8, 256), (20, 24, 256), (16, 16, 256)
    skin = 16 + 2 * SKIN
    scratch = [
        (16 + 2 * FAR, 8, 256), (16 + 2 * ALONG, 8, 256), (skin, 8, 256), (skin, 32, 256),
        (skin, 32, 256), (skin, 8, 256), marks, marks, marks,
        (skin, 24, 256), normals, normals, normals, (18, 16, 256), block,
    ]
    args = [at, psi, velocity, low, high, link, chip, change]
    outs = [block, block, (HALO, 16, 256), (HALO, 16, 256)]
    return call(functools.partial(advance_body, nx, ny), outs, scratch, args, 30000000)


class Field:
    def __init__(self, ref, lead):
        self.ref, self.lead = ref, lead

    def __getitem__(self, p):
        return self.ref[p + self.lead]

    def __setitem__(self, p, value):
        self.ref[p + self.lead] = value

    def beside(self, p):
        return beside(self.ref, p + self.lead)


def wall(at, nx, level, p, value):
    own = 16 >> level
    if 0 <= p < own:
        return value
    return value * plane_factor(at[0] * own + p, nx >> level)


def first_smooth(b, v, planes, weight, mask, at, nx, level):
    for p in planes:
        c, around = b.beside(p)
        v[p] = wall(at, nx, level, p, (weight * mask) * (1.2 * c + SIDE * around))


def sweep(src, dst, b, planes, factor, mask, at, nx, level):
    keep = SIDE * mask
    for p in planes:
        c, around = src.beside(p)
        near = around + (b[p] if factor == 1 else factor * b[p])
        dst[p] = 0.2 * c + wall(at, nx, level, p, keep) * near


def coarsen_level0(at, nx, ny, b, v, b1, planes, pair, t):
    first = planes[0]
    rows = t.shape[1]

    def residual(p):
        c, around = v.beside(p)
        return b[p] - (6.0 * c - around)

    for p in planes:
        total = residual(2 * p) + residual(2 * p + 1)
        for half in range(2):
            lanes = slice(128 * half, 128 * half + 128)
            pair[p - first, half] = total[:, lanes]
            even = pair[p - first, half, pl.ds(0, rows, stride=2), :]
            odd = pair[p - first, half, pl.ds(1, rows, stride=2), :]
            t[p - first, :, lanes] = even + odd
    count = len(planes)
    full = dot(t[...].reshape(count * rows, 256), pair_matrix(256, 128, 0.125))
    full = full.reshape(count, rows, 128)
    mask = row_mask((rows, 128), at[1] * 8 + 4 - rows // 2, ny // 2)
    for p in planes:
        b1[p] = wall(at, nx, 1, p, full[p - first] * mask)


def smooth_level1(at, nx, ny, b1, u, planes):
    rows = b1.ref.shape[1]
    mask = row_mask((rows, 128), at[1] * 8 + 4 - rows // 2, ny // 2)
    first_smooth(b1, u, planes, 4.0 * SIDE, mask, at, nx, 1)


def coarsen_level1(b1, u, b2_out, s1, t1):
    start = b1.ref.shape[1] // 2 - 4
    t1[...] = jnp.zeros_like(t1)
    for k in range(4):
        total = 0.0
        for p in (2 * k, 2 * k + 1):
            c, around = u.beside(p)
            total = total + (b1[p] - 0.25 * (6.0 * c - around))
        s1[k] = total
        t1[k, 0:4, :] = s1[k, pl.ds(start, 4, stride=2), :] + s1[k, pl.ds(start + 1, 4, stride=2), :]
    small = dot(t1[...].reshape(32, 128), pair_matrix(128, 128, 0.125)).reshape(4, 8, 128)
    tile = jnp.concatenate([small[0, 0:4], small[1, 0:4]], axis=0) + roll(
        jnp.concatenate([small[2, 0:4], small[3, 0:4]], axis=0), 64, 1
    )
    b2_out[...] = tile


def reach(extra):
    e0 = extra + 2
    r1 = -(-e0 // 2)
    e1 = r1 + 2
    r2 = -(-e1 // 2)
    e2 = r2 + 2
    r3 = -(-e2 // 2)
    return e0, r1, e1, r2, e2, r3


E0, R1, E1, R2, E2, R3 = reach(KEEP)


def source_segments():
    whole, parts = [], []
    for p in range(-HALO, 16 + HALO):
        d = max(-p, p - 15, 0)
        rows = 16 - max(d, 2)
        if rows >= 8:
            whole.append((p, 0, 8))
        if rows % 8:
            parts.append((p, rows // 8 * 8, rows % 8))
    found = [(p, n, rows, tile, 0) for tile, (p, n, rows) in enumerate(whole)]
    room = []
    for p, n, rows in sorted(parts, key=lambda part: (-part[2], part[0])):
        for k, used in enumerate(room):
            if used + rows <= 8:
                break
        else:
            k = len(room)
            room.append(0)
        found.append((p, n, rows, len(whole) + k, room[k]))
        room[k] += rows
    return found, len(whole) + len(room)


SOURCE_SEGMENTS, SOURCE_TILES = source_segments()


def source_plane(own, low, high, p):
    return low[p + HALO] if p < 0 else own[p] if p < 16 else high[p - 16]


def weave_body(at, own, low, high, link, chip):
    odd = lax.rem(at[1], 2) == 1
    for k in range(SOURCE_TILES):
        first, final, total = [], [], 0
        for p, n, rows, tile, offset in sorted(SOURCE_SEGMENTS, key=lambda part: part[4]):
            if tile == k:
                v = source_plane(own, low, high, p)
                first.append(v[n : n + rows])
                final.append(v[16 - n - rows : 16 - n])
                total += rows
        if total < 8:
            first.append(jnp.zeros((8 - total, 256), F32))
            final.append(first[-1])
        if len(first) > 1:
            first = [jnp.concatenate(first, axis=0)]
            final = [jnp.concatenate(final, axis=0)]
        chip[k] = jnp.where(odd, first[0], final[0])
        link[k] = jnp.where(odd, final[0], first[0])


def weave(at, own, low, high):
    outs = [(SOURCE_TILES, 8, 256)] * 2
    return call(weave_body, outs, [], [at, own, low, high], 1000000)


def first_down_body(
    nx, ny, at, own, low, high, link, chip, b_out, v_out, b1_out, u_out, b2_out, b, v, pair, t, s1, t1
):
    lower, upper = pick_sides(at, chip, link)
    none = jnp.zeros((16, 256), F32)
    for p in range(-HALO, 16 + HALO):
        b[p + HALO, 0:16, :] = none
        b[p + HALO, 16:32, :] = source_plane(own, low, high, p)
        b[p + HALO, 32:48, :] = none
    for p, n, rows, tile, offset in SOURCE_SEGMENTS:
        cut = slice(offset, offset + rows)
        b[p + HALO, 16 - n - rows : 16 - n, :] = lower(tile)[cut]
        b[p + HALO, 32 + n : 32 + n + rows, :] = upper(tile)[cut]
    b, v = Field(b, HALO), Field(v, HALO - 1)
    mask = row_mask((48, 256), at[1] * 16 - 16, ny)
    first_smooth(b, v, range(1 - HALO, 15 + HALO), SIDE, mask, at, nx, 0)
    v_out, b_out = Field(v_out, E0), Field(b_out, E0 - 1)
    for p in range(-E0, 16 + E0):
        v_out[p] = v[p][8:40, :]
    for p in range(1 - E0, 15 + E0):
        b_out[p] = b[p][8:40, :]
    b1, u = Field(b1_out, E1 + 1), Field(u_out, E1)
    coarsen_level0(at, nx, ny, b, v, b1, range(-E1 - 1, 9 + E1), pair, t)
    smooth_level1(at, nx, ny, b1, u, range(-E1, 8 + E1))
    coarsen_level1(b1, u, b2_out, s1, t1)


def around_block(size, extra, rows, lanes):
    return (size + 2 * extra, rows, lanes)


def first_down(nx, ny, at, own, low, high, chip, link):
    level1 = around_block(8, E1 + 1, 24, 128)
    outs = [
        around_block(16, E0 - 1, 32, 256),
        around_block(16, E0, 32, 256),
        level1,
        around_block(8, E1, 24, 128),
        (8, 128),
    ]
    scratch = [
        around_block(16, HALO, 48, 256),
        around_block(16, HALO - 1, 48, 256),
        (level1[0], 2, 48, 128),
        (level1[0], 24, 256),
        (4, 24, 128),
        (4, 8, 128),
    ]
    args = [at, own, low, high, link, chip]
    return call(functools.partial(first_down_body, nx, ny), outs, scratch, args, 20000000)


def second_down_body(nx, ny, at, mid, chip, link, b1_out, u_out, b2_out, s1, t1):
    lower, upper = pick_sides(at, chip, link)
    for i in range(8 + 2 * NEAR):
        b1_out[i, 0:8, :] = lower(i)
        b1_out[i, 8:16, :] = mid[i]
        b1_out[i, 16:24, :] = upper(i)
    b1, u = Field(b1_out, NEAR), Field(u_out, NEAR - 1)
    smooth_level1(at, nx, ny, b1, u, range(1 - NEAR, 7 + NEAR))
    coarsen_level1(b1, u, b2_out, s1, t1)


def second_down(nx, ny, at, mid, chip, link):
    outs = [around_block(8, NEAR, 24, 128), around_block(8, NEAR - 1, 24, 128), (8, 128)]
    scratch = [(4, 24, 128), (4, 8, 128)]
    args = [at, mid, chip, link]
    return call(functools.partial(second_down_body, nx, ny), outs, scratch, args, 2000000)


def solve_coarse(nx, ny, extra, at, coarse, s2, v2, w2, t3, b3, c3, d3, dup, row2):
    fetched, other = coarse
    odd = lax.rem(at[1], 2) == 1
    odd_layer = lax.rem(at[0] // GROUP, 2)
    _, _, _, r2, e2, r3 = reach(extra)
    spot = at[0] % GROUP
    rows2 = ny // 4
    rows3 = rows2 // 2
    count = rows2 // 4
    lead = 2 * (r3 + 3) + 2
    blocks = -(-lead // 4)
    s2, v2, w2 = Field(s2, 4 * blocks), Field(v2, lead - 1), Field(w2, e2)
    lane8 = iota((8, 128), 1) < 64
    for j in range(-blocks, blocks + 1):
        block = spot + GROUP + j
        layer, place = block // GROUP, block % GROUP
        first_cores = jnp.where(odd_layer == 1, layer <= 1, layer >= 1)
        mine = first_cores != odd
        inner = inside(at[0] + j, nx // 16)
        start = ((layer + odd_layer) // 2) * (GROUP * count // 2) + place * (count // 2)
        for n in range(count):
            rows = slice(8 * (n % 2), 8 * (n % 2) + 8)
            k = start + n // 2
            tile = jnp.where(mine, fetched[k, rows, :], other[k, rows, :])
            tile = jnp.where(inner, tile, 0.0)
            halves = (jnp.where(lane8, tile, 0.0), jnp.where(lane8, roll(tile, 64, 1), 0.0))
            for p in range(4):
                part = halves[p // 2][4 * (p % 2) : 4 * (p % 2) + 4, :]
                s2.ref[4 * (j + blocks) + p, 4 * n : 4 * n + 4, :] = part

    def around(f, p):
        c = f[p]
        row = iota(c.shape, 0)
        lower = jnp.where(row == 0, 0.0, roll(c, 1, 0))
        upper = jnp.where(row == c.shape[0] - 1, 0.0, roll(c, -1, 0))
        beside = (lower + upper) + (roll(c, 1, 1) + roll(c, -1, 1))
        return c, (f[p - 1] + f[p + 1]) + beside

    def lanes_below(rows, lanes):
        return jnp.where(iota((rows, 128), 1) < lanes, 1.0, 0.0).astype(F32)

    mask2 = lanes_below(rows2, 64)
    for p in range(1 - lead, 3 + lead):
        c, near = around(s2, p)
        v2[p] = wall(at, nx, 2, p, (16.0 * SIDE) * mask2 * (1.2 * c + SIDE * near))

    def residual2(p):
        c, near = around(v2, p)
        return s2[p] - (1.0 / 16.0) * (6.0 * c - near)

    planes3 = range(-r3 - 3, 2 + r3 + 3)
    for i, p in enumerate(planes3):
        row2[i] = residual2(2 * p) + residual2(2 * p + 1)
        t3[i] = row2[i, pl.ds(0, rows3, stride=2), :] + row2[i, pl.ds(1, rows3, stride=2), :]
    total3 = len(planes3)
    full = dot(t3[...].reshape(total3 * rows3, 128), pair_matrix(128, 128, 0.125))
    full = full.reshape(total3, rows3, 128)
    mask3 = lanes_below(rows3, 32)
    b3, c3, d3 = Field(b3, r3 + 3), Field(c3, r3 + 3), Field(d3, r3 + 3)
    for i, p in enumerate(planes3):
        value = wall(at, nx, 3, p, full[i] * ((64.0 * SIDE) * mask3))
        b3[p] = value
    src, dst = b3, c3
    for step in (2, 1, 0):
        for p in range(-r3 - step, 2 + r3 + step):
            c, near = around(src, p)
            dst[p] = wall(at, nx, 3, p, mask3 * (0.2 * c + SIDE * near)) + b3[p]
        src, dst = dst, (d3 if dst is c3 else c3)
    final = src
    planes = range(-r3, 2 + r3)
    flat = jnp.concatenate([final[p] for p in planes], axis=0)
    spread = dot(flat, copy_matrix(128, 128)).reshape(len(planes), rows3, 128)
    for i, p in enumerate(planes):
        dup[i, pl.ds(0, rows3, stride=2), :] = spread[i]
        dup[i, pl.ds(1, rows3, stride=2), :] = spread[i]
        for q in (2 * p, 2 * p + 1):
            if -e2 <= q < 4 + e2:
                v2[q] = v2[q] + wall(at, nx, 2, q, dup[i, 0:rows2, :] * mask2)
    keep = SIDE * mask2
    for src, dst, step in ((v2, w2, 1), (w2, v2, 0)):
        for p in range(-r2 - step, 4 + r2 + step):
            c, near = around(src, p)
            dst[p] = 0.2 * c + wall(at, nx, 2, p, keep) * (near + 16.0 * s2[p])
    return v2


def coarse_scratch(ny, extra):
    _, _, _, _, e2, r3 = reach(extra)
    rows2 = ny // 4
    rows3 = rows2 // 2
    lead = 2 * (r3 + 3) + 2
    small = around_block(2, r3 + 3, rows3, 128)
    return [
        around_block(4, -(-lead // 4) * 4, rows2, 128),
        around_block(4, lead - 1, rows2, 128),
        around_block(4, e2, rows2, 128),
        small, small, small, small,
        (8, 48, 128),
        around_block(2, r3 + 3, rows2, 128),
    ]


def climb(nx, ny, extra, at, v2, b1, u, b, v_down, m1, n1, m0, n0, dup):
    e0, r1, e1, r2, _, _ = reach(extra)
    rows2 = ny // 4
    turn = lax.rem(rows2 + 4 - 4 * at[1] + rows2, rows2)
    planes = range(-r2, 4 + r2)
    picked = jnp.concatenate([pltpu.roll(v2[p], turn, 0)[0:16, :] for p in planes], axis=0)
    spread = dot(picked, copy_matrix(128, 128)).reshape(len(planes), 16, 128)
    mask1 = row_mask((24, 128), at[1] * 8 - 8, ny // 2)
    m1, n1 = Field(m1, e1), Field(n1, e1)
    for i, p in enumerate(planes):
        dup[i, 0, pl.ds(0, 12, stride=2), :] = spread[i, 0:12, :]
        dup[i, 0, pl.ds(1, 12, stride=2), :] = spread[i, 0:12, :]
        for q in (2 * p, 2 * p + 1):
            if -e1 <= q < 8 + e1:
                m1[q] = u[q] + wall(at, nx, 1, q, dup[i, 0, 0:24, :] * mask1)
    sweep(m1, n1, b1, range(1 - e1, 7 + e1), 4.0, mask1, at, nx, 1)
    sweep(n1, m1, b1, range(2 - e1, 6 + e1), 4.0, mask1, at, nx, 1)
    planes = range(-r1, 8 + r1)
    flat = jnp.concatenate([m1[p][4:20, :] for p in planes], axis=0)
    spread = dot(flat, copy_matrix(128, 256)).reshape(len(planes), 16, 256)
    mask0 = row_mask((32, 256), at[1] * 16 - 8, ny)
    m0, n0 = Field(m0, e0), Field(n0, e0)
    for i, p in enumerate(planes):
        for half in range(2):
            value = spread[i, :, 128 * half : 128 * half + 128]
            dup[i, half, pl.ds(0, 16, stride=2), :] = value
            dup[i, half, pl.ds(1, 16, stride=2), :] = value
        value = jnp.concatenate([dup[i, 0], dup[i, 1]], axis=1) * mask0
        for q in (2 * p, 2 * p + 1):
            if -e0 <= q < 16 + e0:
                m0[q] = v_down[q] + wall(at, nx, 0, q, value)
    sweep(m0, n0, b, range(1 - e0, 15 + e0), 1, mask0, at, nx, 0)
    if extra:
        sweep(n0, m0, b, range(2 - e0, 14 + e0), 1, mask0, at, nx, 0)
        return m0
    return n0


def climb_scratch(extra):
    e0, r1, e1, r2, _, _ = reach(extra)
    level1 = around_block(8, e1, 24, 128)
    level0 = around_block(16, e0, 32, 256)
    return [level1, level1, level0, level0, (max(8 + 2 * r1, 4 + 2 * r2), 2, 32, 128)]


def turn_body(nx, ny, at, fetched, other, b1, u, b, v_down, v_out, wider, low, high, own, pair, t, *scratch):
    v2 = solve_coarse(nx, ny, KEEP, at, (fetched, other), *scratch[:9])
    b = Field(b, E0 - 1)
    v = climb(nx, ny, KEEP, at, v2, Field(b1, E1 + 1), Field(u, E1), b, Field(v_down, E0), *scratch[9:])
    mask = row_mask((32, 256), at[1] * 16 - 8, ny)
    once, twice = Field(scratch[12], E0), Field(v_out, KEEP - 2)
    sweep(v, once, b, range(1 - KEEP, 15 + KEEP), 1, mask, at, nx, 0)
    sweep(once, twice, b, range(2 - KEEP, 14 + KEEP), 1, mask, at, nx, 0)
    coarsen_level0(at, nx, ny, b, twice, Field(own, 0), range(8), pair, t)
    for i in range(8):
        wider[NEAR + i] = own[i, 4:12, :]
    for i in range(NEAR):
        low[i] = own[i, 4:12, :]
        high[i] = own[8 - NEAR + i, 4:12, :]


def turn(nx, ny, at, coarse, b1, u, b, v_down):
    outs = [
        around_block(16, KEEP - 2, 32, 256),
        around_block(8, NEAR, 8, 128),
        (NEAR, 8, 128),
        (NEAR, 8, 128),
    ]
    scratch = [(8, 16, 128), (8, 2, 32, 128), (8, 16, 256)]
    scratch += coarse_scratch(ny, KEEP) + climb_scratch(KEEP)
    args = [at, *coarse, b1, u, b, v_down]
    return call(functools.partial(turn_body, nx, ny), outs, scratch, args, 30000000)


def finish_body(nx, ny, at, fetched, other, b1, u, b, v_down, out, *scratch):
    v2 = solve_coarse(nx, ny, 0, at, (fetched, other), *scratch[:9])
    b, v_down = Field(b, E0 - 1), Field(v_down, KEEP - 2)
    v = climb(nx, ny, 0, at, v2, Field(b1, NEAR), Field(u, NEAR - 1), b, v_down, *scratch[9:])
    for p in range(16):
        c, around = v.beside(p)
        out[p] = (0.2 * c + SIDE * (around + b[p]))[8:24, :]


def finish(nx, ny, at, coarse, b1, u, b, v_down):
    scratch = coarse_scratch(ny, 0) + climb_scratch(0)
    args = [at, *coarse, b1, u, b, v_down]
    return call(functools.partial(finish_body, nx, ny), [(16, 16, 256)], scratch, args, 20000000)[0]


def shifted(array, axis, step):
    count = lax.axis_size(axis)
    return lax.ppermute(
        array, axis, [(i, i + step) for i in range(count) if 0 <= i + step < count]
    )


def swapped(array, first):
    count = lax.axis_size("narrow")
    pairs = [(i, i + 1) for i in range(first, count - 1, 2)]
    return lax.ppermute(array, "narrow", pairs + [(j, i) for i, j in pairs])


def widen(wider, low, high):
    planes = low.shape[0]
    wider = lax.dynamic_update_slice(wider, shifted(high, "wide", 1), (0, 0, 0))
    upper = wider.shape[0] - planes
    return lax.dynamic_update_slice(wider, shifted(low, "wide", -1), (upper, 0, 0))


def surround(wider, low, high):
    mid = widen(wider, low, high)
    link = swapped(mid, 1)
    return mid, swapped(mid, 0), link


def spread_coarse(b2):
    wide, cores = lax.axis_size("wide"), lax.axis_size("narrow")
    layers = wide // GROUP
    odd = lax.rem(lax.axis_index("narrow"), 2) == 1
    other = swapped(b2, 0)
    pair = jnp.concatenate([jnp.where(odd, other, b2), jnp.where(odd, b2, other)], axis=0)
    groups = [
        [
            (((2 * k + core + i) % layers) * GROUP + x) * cores + y
            for i in range(2)
            for x in range(GROUP)
            for y in range(core, cores, 2)
        ]
        for core in range(2)
        for k in range(layers // 2)
    ]
    pieces = jnp.broadcast_to(pair[None], (len(groups[0]),) + pair.shape)
    fetched = lax.all_to_all(pieces, ("wide", "narrow"), 0, 0, axis_index_groups=groups)
    return fetched, swapped(fetched, 0)


def on_device(phase, distance, velocity):
    nx, ny = 16 * lax.axis_size("wide"), 16 * lax.axis_size("narrow")
    at = jnp.stack([lax.axis_index("wide"), lax.axis_index("narrow")]).astype(jnp.int32)
    psi, x_low, x_high = prepare(phase, distance, velocity)
    low, high = shifted(x_high, "wide", 1), shifted(x_low, "wide", -1)
    known = inner_z(psi, velocity)
    link, chip = pack(at, psi, velocity, low, high, known)
    v_link = swapped(link, 1)
    v_chip = swapped(chip, 0)
    change = inner(psi, velocity, low, high, known)
    moved, source, first, final = advance(
        nx, ny, at, psi, velocity, low, high, v_chip, v_link, change
    )
    low, high = shifted(final, "wide", 1), shifted(first, "wide", -1)
    link, chip = weave(at, source, low, high)
    b_link = swapped(link, 1)
    b_chip = swapped(chip, 0)
    b, v, b1, u, b2 = first_down(nx, ny, at, source, low, high, b_chip, b_link)
    v, *sends = turn(nx, ny, at, spread_coarse(b2), b1, u, b, v)
    b1, u, b2 = second_down(nx, ny, at, *surround(*sends))
    pressure = finish(nx, ny, at, spread_coarse(b2), b1, u, b, v)
    return (moved, pressure)


def solution(mesh):
    blocks = P("wide", "narrow", None)
    return jax.shard_map(
        on_device,
        mesh=mesh,
        in_specs=(blocks, blocks, P(None, "wide", "narrow", None)),
        out_specs=(blocks, blocks),
        check_vma=False,
    )
```

```python
import functools

import jax
import jax.numpy as jnp
from jax import lax
from jax.experimental import pallas as pl
from jax.experimental.pallas import tpu as pltpu
from jax.sharding import PartitionSpec as P

DELTA_SQ = 0.0025
WENO_EPS = 0.01
SIDE = 0.8 / 6.0
F32 = jnp.float32

HALO = 14
KEEP = 4
NEAR = 4
GROUP = 4


def iota(shape, dim):
    return lax.broadcasted_iota(jnp.int32, shape, dim)


def roll(v, shift, axis):
    return pltpu.roll(v, shift % v.shape[axis], axis)


def z_shifted(v):
    lane = iota(v.shape, 1)
    last = v.shape[1] - 1
    lower = jnp.where(lane == 0, 0.0, roll(v, 1, 1))
    upper = jnp.where(lane == last, 0.0, roll(v, -1, 1))
    return lower, upper


def z_pair(v):
    lower, upper = z_shifted(v)
    return lower + upper


def y_pair(v):
    return roll(v, 1, 0) + roll(v, -1, 0)


def beside(ref, i):
    c = ref[i]
    return c, (ref[i - 1] + ref[i + 1]) + y_pair(c) + z_pair(c)


def inside(first, count):
    return jnp.logical_and(first >= 0, first < count)


def row_mask(shape, first, count):
    rows = iota(shape, 0) + first
    return jnp.where(inside(rows, count), 1.0, 0.0).astype(F32)


def plane_factor(index, count):
    return jnp.where(inside(index, count), 1.0, 0.0).astype(F32)


def dot(a, b):
    b = b.astype(jnp.bfloat16)
    high = a.astype(jnp.bfloat16)
    low = (a - high.astype(F32)).astype(jnp.bfloat16)
    return jnp.dot(high, b, preferred_element_type=F32) + jnp.dot(low, b, preferred_element_type=F32)


def pair_matrix(rows, cols, value):
    return jnp.where((iota((rows, cols), 0) >> 1) == iota((rows, cols), 1), value, 0.0).astype(F32)


def copy_matrix(rows, cols):
    return jnp.where(iota((rows, cols), 0) == (iota((rows, cols), 1) >> 1), 1.0, 0.0).astype(F32)


def words(shape):
    *lead, rows, lanes = (1,) * (3 - len(shape)) + tuple(shape)
    size = -(-rows // 8) * 8 * (-(-lanes // 128) * 128)
    for n in lead:
        size *= n
    return size


def call(body, outs, scratch, args, flops):
    vmem = pl.BlockSpec(memory_space=pltpu.VMEM)
    smem = pl.BlockSpec(memory_space=pltpu.SMEM)
    total = sum(words(a.shape) for a in args) + sum(map(words, outs)) + sum(map(words, scratch))
    return pl.pallas_call(
        body,
        out_shape=[jax.ShapeDtypeStruct(s, F32) for s in outs],
        in_specs=[smem if a.dtype == jnp.int32 and a.ndim == 1 else vmem for a in args],
        out_specs=[vmem] * len(outs),
        scratch_shapes=[pltpu.VMEM(s, F32) for s in scratch],
        compiler_params=pltpu.CompilerParams(vmem_limit_bytes=4 * total + (6 << 20)),
        cost_estimate=pl.CostEstimate(flops=flops, bytes_accessed=4000000, transcendentals=0),
    )(*args)


def pick_sides(at, chip, link):
    odd = lax.rem(at[1], 2) == 1
    lower = lambda *k: jnp.where(odd, chip[k], link[k])
    upper = lambda *k: jnp.where(odd, link[k], chip[k])
    return lower, upper


PARTS = 4
FAR, ALONG, ACROSS = 6, 4, 3
SENT = FAR + ALONG + 2 * ACROSS


def layer_cuts(dim):
    cuts, offset = [], FAR
    for component in range(3):
        layers = ALONG if component == dim else ACROSS
        cuts.append((component, layers, offset))
        offset += layers
    return cuts


def prepare_body(phase, distance, velocity, psi, x_low, x_high, kind, away, sems):
    step = 16 // PARTS
    copies = []

    def copy(src, dst):
        started = pltpu.make_async_copy(src, dst, sems.at[len(copies)])
        started.start()
        copies.append(started)

    for k in range(PARTS):
        planes = pl.ds(step * k, step)
        copy(phase.at[planes], kind.at[planes])
        copy(distance.at[planes], away.at[planes])
    for component, layers, offset in layer_cuts(0):
        copy(velocity.at[component, pl.ds(0, layers)], x_low.at[pl.ds(offset, layers)])
        copy(velocity.at[component, pl.ds(16 - layers, layers)], x_high.at[pl.ds(offset, layers)])
    for k in range(PARTS):
        copies[2 * k].wait()
        copies[2 * k + 1].wait()
        for i in range(step * k, step * k + step):
            orient = 2.0 * kind[i].astype(F32) - 1.0
            psi[i] = 1.0 / (1.0 + jnp.exp(-orient * away[i]))
    for k in range(FAR):
        x_low[k] = psi[k]
        x_high[k] = psi[16 - FAR + k]
    for started in copies[2 * PARTS :]:
        started.wait()


def prepare(phase, distance, velocity):
    vmem = pl.BlockSpec(memory_space=pltpu.VMEM)
    hbm = pl.BlockSpec(memory_space=pltpu.HBM)
    outs = [(16, 16, 256), (SENT, 16, 256), (SENT, 16, 256)]
    return pl.pallas_call(
        prepare_body,
        out_shape=[jax.ShapeDtypeStruct(s, F32) for s in outs],
        in_specs=[hbm, hbm, hbm],
        out_specs=[vmem] * len(outs),
        scratch_shapes=[
            pltpu.VMEM((16, 16, 256), jnp.int32),
            pltpu.VMEM((16, 16, 256), F32),
            pltpu.SemaphoreType.DMA((2 * PARTS + 6,)),
        ],
        compiler_params=pltpu.CompilerParams(vmem_limit_bytes=8 << 20),
        cost_estimate=pl.CostEstimate(flops=1000000, bytes_accessed=1000000, transcendentals=0),
    )(*(pltpu.with_memory_space_constraint(a, pltpu.HBM) for a in (phase, distance, velocity)))


def plane_of(own, low, high, p, offset, layers):
    if p < 0:
        return low[offset + layers + p]
    return own(p) if p < 16 else high[offset + p - 16]


def wide_planes(psi, velocity, low, high):
    def level(p):
        return plane_of(lambda k: psi[k], low, high, p, 0, FAR)

    def speed(component):
        _, layers, offset = layer_cuts(0)[component]

        def at_plane(p):
            if not -layers <= p < 16 + layers:
                return None
            return plane_of(lambda k: velocity[component, k], low, high, p, offset, layers)

        return at_plane

    return level, [speed(c) for c in range(3)]


def narrow_segments():
    reached = (FAR, ALONG, ALONG, ACROSS)
    rows_own = (FAR, ACROSS, ALONG, ACROSS)
    found = {}
    for p in range(16):
        offset = 0
        for field, rows in enumerate(rows_own):
            found[field, p] = (p, offset, rows)
            offset += rows
    for side, edge in enumerate((0, 15)):
        for slot, layers in enumerate(((1, 4, 5), (2, 3))):
            offset = 0
            for d in layers:
                p = edge - d if side == 0 else edge + d
                for field, reach_of in enumerate(reached):
                    rows = min(reach_of - d, rows_own[field])
                    if rows > 0:
                        found[field, p] = (16 + 2 * side + slot, offset, rows)
                        offset += rows
    return found


SEGMENTS = narrow_segments()
SLOTS = 20


def pack_body(at, psi, velocity, low, high, known, link, chip):
    odd = lax.rem(at[1], 2) == 1
    level, speeds = wide_planes(psi, velocity, low, high)
    fields = [level] + speeds
    for k in range(SLOTS):
        inside_slot = [(offset, f, p, rows) for (f, p), (slot, offset, rows) in SEGMENTS.items() if slot == k]
        first, final, total = [], [], 0
        for offset, f, p, rows in sorted(inside_slot):
            v = fields[f](p)
            first.append(v[0:rows])
            final.append(v[16 - rows : 16])
            total += rows
        if total < SENT:
            first.append(jnp.zeros((SENT - total, 256), F32))
            final.append(first[-1])
        first = jnp.concatenate(first, axis=0)
        final = jnp.concatenate(final, axis=0)
        chip[k] = jnp.where(odd, first, final)
        link[k] = jnp.where(odd, final, first)


def pack(at, psi, velocity, low, high, known):
    outs = [(SLOTS, SENT, 256)] * 2
    return call(pack_body, outs, [], [at, psi, velocity, low, high, known], 1000000)


FACE = 0.25 / 12.0


def indicators(a, b, c):
    d = a - c
    curve = (a + c) - 2.0 * b
    twice = 2.0 * curve
    base = (13.0 / 12.0) * (curve * curve) + WENO_EPS
    up, down = twice - d, twice + d
    p = base + 0.25 * (up * up)
    q = base + 0.25 * (d * d)
    r = base + 0.25 * (down * down)
    return p * p, q * q, r * r


def upwind_flux(s, l, p_left, q_left, r_left, p_right, q_right, r_right):
    ahead = s > 0.0
    pick = lambda x, y: jnp.where(ahead, x, y)
    a, b, c, e, f = pick(l[0], l[5]), pick(l[1], l[4]), pick(l[2], l[3]), pick(l[3], l[2]), pick(l[4], l[1])
    p, q, r = pick(p_left, r_right), pick(q_left, q_right), pick(r_left, p_right)
    w0, w1, w2 = q * r, 6.0 * (p * r), 3.0 * (p * q)
    g0 = 2.0 * a - 7.0 * b + 11.0 * c
    g1 = 5.0 * c + 2.0 * e - b
    g2 = 2.0 * c + 5.0 * e - f
    top = w0 * g0 + w1 * g1 + w2 * g2
    total = w0 + w1 + w2
    return (s * top) / total


def z_change(v, w):
    lane = iota(v.shape, 1)

    def ahead(x, k):
        return jnp.where(lane > 255 - k, 0.0, roll(x, -k, 1))

    def behind(x, k):
        return jnp.where(lane < k, 0.0, roll(x, k, 1))

    l = [behind(v, 2), behind(v, 1), v, ahead(v, 1), ahead(v, 2), ahead(v, 3)]
    s = FACE * (w + ahead(w, 1))
    p, q, r = indicators(l[1], l[2], l[3])
    _, q1, r1 = indicators(l[2], l[3], l[4])
    _, _, r2 = indicators(l[3], l[4], l[5])
    p0, _, _ = indicators(l[0], l[1], l[2])
    flux = upwind_flux(s, l, p0, q, r1, p, q1, r2)
    low = slice(0, 128)
    c = v[:, low]
    none = jnp.zeros_like(c)
    square = c * c
    edge = WENO_EPS + (13.0 / 12.0 + 9.0 / 4.0) * square
    level = WENO_EPS + (13.0 / 12.0 + 1.0 / 4.0) * square
    wall_flux = upwind_flux(
        FACE * w[:, low],
        [none, none, none, c, l[3][:, low], l[4][:, low]],
        none + WENO_EPS * WENO_EPS, level * level, r[:, low],
        edge * edge, q[:, low], r1[:, low],
    )
    wall_flux = jnp.concatenate([wall_flux, wall_flux], axis=1)
    return flux - jnp.where(lane == 0, wall_flux, roll(flux, 1, 1))


def y_change(v, w):
    s = FACE * (w + roll(w, -1, 0))
    l = [roll(v, 2 - k, 0) for k in range(6)]
    p, q, r = indicators(l[1], l[2], l[3])
    q_next, r_next = roll(q, -1, 0), roll(r, -1, 0)
    flux = upwind_flux(s, l, roll(p, 1, 0), q, r_next, p, q_next, roll(r, -2, 0))
    return flux - roll(flux, 1, 0)


SKIN = 3


def x_marks(v, planes, marks):
    for i in range(planes):
        marks[0][i], marks[1][i], marks[2][i] = indicators(v(i - FAR), v(i - FAR + 1), v(i - FAR + 2))


def x_flux(f, v, w, marks):
    p_x, q_x, r_x = marks
    l = [v(f - 3 + k) for k in range(6)]
    return upwind_flux(
        FACE * (w(f - 1) + w(f)), l,
        p_x[f + 3], q_x[f + 4], r_x[f + 5], p_x[f + 4], q_x[f + 5], r_x[f + 6],
    )


def xz_change(v, u, w, marks, out, known=None):
    x_marks(v, 26, marks)
    below = x_flux(-SKIN, v, u, marks)
    for p in range(-SKIN, 16 + SKIN):
        above = x_flux(p + 1, v, u, marks)
        along_z = known[p] if known is not None and 0 <= p < 16 else z_change(v(p), w(p))
        out[p + SKIN] = (above - below) + along_z
        below = above


def inner_z_body(psi, velocity, out):
    for p in range(16):
        out[p] = z_change(psi[p], velocity[2, p])


def inner_z(psi, velocity):
    return call(inner_z_body, [(16, 16, 256)], [], [psi, velocity], 8000000)[0]


def inner_body(psi, velocity, low, high, known, out, *marks):
    level, speeds = wide_planes(psi, velocity, low, high)
    xz_change(level, speeds[0], speeds[2], marks, out, known)


def inner(psi, velocity, low, high, known):
    block = (16 + 2 * SKIN, 16, 256)
    scratch = [(26, 16, 256)] * 3
    return call(inner_body, [block], scratch, [psi, velocity, low, high, known], 8000000)[0]


def advance_body(
    nx, ny, at, psi, velocity, low, high, link, chip, change_in, moved, source, first, final,
    v8, u8, w8, v32, u32, c8, p_x, q_x, r_x, m, n_x, n_y, n_z, s_x, part,
):
    lower, upper = pick_sides(at, chip, link)
    level, speeds = wide_planes(psi, velocity, low, high)
    fields = [level] + speeds

    def halo(field, p, most):
        if (field, p) not in SEGMENTS:
            return 0, None, None
        slot, offset, rows = SEGMENTS[field, p]
        count = min(most, rows)
        below = lower(slot)[offset + rows - count : offset + rows]
        return count, below, upper(slot)[offset : offset + count]

    def beside_only(ref, i, field, p):
        ref[i] = jnp.zeros((8, 256), F32)
        count, below, above = halo(field, p, 4)
        if count:
            ref[i, 4 - count : 4, :] = below
            ref[i, 4 : 4 + count, :] = above

    def with_rows(ref, i, field, p, start):
        total = ref.shape[1]
        ref[i, 0:start, :] = jnp.zeros((start, 256), F32)
        ref[i, start + 16 : total, :] = jnp.zeros((total - start - 16, 256), F32)
        count, below, above = halo(field, p, start)
        ref[i, start : start + 16, :] = fields[field](p)
        if count:
            ref[i, start - count : start, :] = below
            ref[i, start + 16 : start + 16 + count, :] = above

    for p in range(-FAR, 16 + FAR):
        beside_only(v8, p + FAR, 0, p)
        if -ALONG <= p < 16 + ALONG:
            beside_only(u8, p + ALONG, 1, p)
        if -SKIN <= p < 16 + SKIN:
            beside_only(w8, p + SKIN, 3, p)
            with_rows(v32, p + SKIN, 0, p, 8)
            with_rows(u32, p + SKIN, 2, p, 8)

    xz_change(
        lambda p: v8[p + FAR], lambda p: u8[p + ALONG], lambda p: w8[p + SKIN], (p_x, q_x, r_x), c8
    )
    shape = (24, 256)
    mask = row_mask(shape, at[1] * 16 - 4, ny)
    for p in range(-SKIN, 16 + SKIN):
        i = p + SKIN
        sides = c8[i]
        change = jnp.concatenate([sides[0:4], change_in[i], sides[4:8]], axis=0)
        v = v32[i]
        change = change + y_change(v, u32[i])[4:28, :]
        value = wall(at, nx, 0, p, (v[4:28, :] - change) * mask)
        m[i] = value
        if 0 <= p < 16:
            moved[p] = value[4:20, :]

    lane = iota(shape, 1)

    def gradient(p):
        c = m[p + SKIN]
        down, ahead = z_shifted(c)
        gx = 0.5 * (m[p + SKIN + 1] - m[p + SKIN - 1])
        gy = 0.5 * (roll(c, -1, 0) - roll(c, 1, 0))
        return gx, gy, 0.5 * (ahead - down)

    for p in range(-2, 18):
        gx, gy, gz = gradient(p)
        inverse = lax.rsqrt(gx * gx + gy * gy + gz * gz + DELTA_SQ)
        n_x[p + 2], n_y[p + 2], n_z[p + 2] = gx * inverse, gy * inverse, gz * inverse
    for p in range(-1, 17):
        gx, gy, gz = gradient(p)
        edge = 0.5 * m[p + SKIN]
        edge = edge * lax.rsqrt(edge * edge + DELTA_SQ)
        nz, ny_here = n_z[p + 2], n_y[p + 2]
        ahead = jnp.where(lane == 255, -edge, roll(nz, -1, 1))
        behind = jnp.where(lane == 0, edge, roll(nz, 1, 1))
        bending = -0.5 * (
            (n_x[p + 3] - n_x[p + 1])
            + (roll(ny_here, -1, 0) - roll(ny_here, 1, 0))
            + (ahead - behind)
        )
        bending = wall(at, nx, 0, p, bending * mask)
        s_x[p + 1] = (bending * gx)[4:20, :] + speeds[0](p)
        if 0 <= p < 16:
            sy = bending * gy + u32[p + SKIN, 4:28, :]
            dy = roll(sy, -1, 0) - roll(sy, 1, 0)
            sz = (bending * gz)[4:20, :] + velocity[2, p]
            behind, ahead = z_shifted(sz)
            part[p] = dy[4:20, :] + (ahead - behind)
    for p in range(16):
        source[p] = -0.5 * (part[p] + (s_x[p + 2] - s_x[p]))
    for i in range(HALO):
        first[i] = source[i]
        final[i] = source[16 - HALO + i]


def advance(nx, ny, at, psi, velocity, low, high, chip, link, change):
    marks, normals, block = (26, 8, 256), (20, 24, 256), (16, 16, 256)
    skin = 16 + 2 * SKIN
    scratch = [
        (16 + 2 * FAR, 8, 256), (16 + 2 * ALONG, 8, 256), (skin, 8, 256), (skin, 32, 256),
        (skin, 32, 256), (skin, 8, 256), marks, marks, marks,
        (skin, 24, 256), normals, normals, normals, (18, 16, 256), block,
    ]
    args = [at, psi, velocity, low, high, link, chip, change]
    outs = [block, block, (HALO, 16, 256), (HALO, 16, 256)]
    return call(functools.partial(advance_body, nx, ny), outs, scratch, args, 30000000)


class Field:
    def __init__(self, ref, lead):
        self.ref, self.lead = ref, lead

    def __getitem__(self, p):
        return self.ref[p + self.lead]

    def __setitem__(self, p, value):
        self.ref[p + self.lead] = value

    def beside(self, p):
        return beside(self.ref, p + self.lead)


def wall(at, nx, level, p, value):
    own = 16 >> level
    if 0 <= p < own:
        return value
    return value * plane_factor(at[0] * own + p, nx >> level)


def first_smooth(b, v, planes, weight, mask, at, nx, level):
    for p in planes:
        c, around = b.beside(p)
        v[p] = wall(at, nx, level, p, (weight * mask) * (1.2 * c + SIDE * around))


def sweep(src, dst, b, planes, factor, mask, at, nx, level):
    keep = SIDE * mask
    for p in planes:
        c, around = src.beside(p)
        near = around + (b[p] if factor == 1 else factor * b[p])
        dst[p] = 0.2 * c + wall(at, nx, level, p, keep) * near


def coarsen_level0(at, nx, ny, b, v, b1, planes, pair, t):
    first = planes[0]
    rows = t.shape[1]

    def residual(p):
        c, around = v.beside(p)
        return b[p] - (6.0 * c - around)

    for p in planes:
        total = residual(2 * p) + residual(2 * p + 1)
        for half in range(2):
            lanes = slice(128 * half, 128 * half + 128)
            pair[p - first, half, 0 : 2 * rows, :] = total[:, lanes]
            even = pair[p - first, half, pl.ds(0, rows, stride=2), :]
            odd = pair[p - first, half, pl.ds(1, rows, stride=2), :]
            t[p - first, :, lanes] = even + odd
    count = len(planes)
    full = dot(t[...].reshape(count * rows, 256), pair_matrix(256, 128, 0.125))
    full = full.reshape(count, rows, 128)
    mask = row_mask((rows, 128), at[1] * 8 + 4 - rows // 2, ny // 2)
    for p in planes:
        b1[p] = wall(at, nx, 1, p, full[p - first] * mask)


def smooth_level1(at, nx, ny, b1, u, planes):
    rows = b1.ref.shape[1]
    mask = row_mask((rows, 128), at[1] * 8 + 4 - rows // 2, ny // 2)
    first_smooth(b1, u, planes, 4.0 * SIDE, mask, at, nx, 1)


def coarsen_level1(b1, u, b2_out, s1, t1):
    start = b1.ref.shape[1] // 2 - 4
    t1[...] = jnp.zeros_like(t1)
    for k in range(4):
        total = 0.0
        for p in (2 * k, 2 * k + 1):
            c, around = u.beside(p)
            total = total + (b1[p] - 0.25 * (6.0 * c - around))
        s1[k] = total
        t1[k, 0:4, :] = s1[k, pl.ds(start, 4, stride=2), :] + s1[k, pl.ds(start + 1, 4, stride=2), :]
    small = dot(t1[...].reshape(32, 128), pair_matrix(128, 128, 0.125)).reshape(4, 8, 128)
    tile = jnp.concatenate([small[0, 0:4], small[1, 0:4]], axis=0) + roll(
        jnp.concatenate([small[2, 0:4], small[3, 0:4]], axis=0), 64, 1
    )
    b2_out[...] = tile


def reach(extra):
    e0 = extra + 2
    r1 = -(-e0 // 2)
    e1 = r1 + 2
    r2 = -(-e1 // 2)
    e2 = r2 + 2
    r3 = -(-e2 // 2)
    return e0, r1, e1, r2, e2, r3


E0, R1, E1, R2, E2, R3 = reach(KEEP)


def source_segments():
    whole, parts = [], []
    for p in range(-HALO, 16 + HALO):
        d = max(-p, p - 15, 0)
        rows = 16 - max(d, 2)
        if rows >= 8:
            whole.append((p, 0, 8))
        if rows % 8:
            parts.append((p, rows // 8 * 8, rows % 8))
    found = [(p, n, rows, tile, 0) for tile, (p, n, rows) in enumerate(whole)]
    room = []
    for p, n, rows in sorted(parts, key=lambda part: (-part[2], part[0])):
        for k, used in enumerate(room):
            if used + rows <= 8:
                break
        else:
            k = len(room)
            room.append(0)
        found.append((p, n, rows, len(whole) + k, room[k]))
        room[k] += rows
    return found, len(whole) + len(room)


SOURCE_SEGMENTS, SOURCE_TILES = source_segments()


def source_plane(own, low, high, p):
    return low[p + HALO] if p < 0 else own[p] if p < 16 else high[p - 16]


def weave_body(at, own, low, high, link, chip):
    odd = lax.rem(at[1], 2) == 1
    for k in range(SOURCE_TILES):
        first, final, total = [], [], 0
        for p, n, rows, tile, offset in sorted(SOURCE_SEGMENTS, key=lambda part: part[4]):
            if tile == k:
                v = source_plane(own, low, high, p)
                first.append(v[n : n + rows])
                final.append(v[16 - n - rows : 16 - n])
                total += rows
        if total < 8:
            first.append(jnp.zeros((8 - total, 256), F32))
            final.append(first[-1])
        if len(first) > 1:
            first = [jnp.concatenate(first, axis=0)]
            final = [jnp.concatenate(final, axis=0)]
        chip[k] = jnp.where(odd, first[0], final[0])
        link[k] = jnp.where(odd, final[0], first[0])


def weave(at, own, low, high):
    outs = [(SOURCE_TILES, 8, 256)] * 2
    return call(weave_body, outs, [], [at, own, low, high], 1000000)


def first_down_body(
    nx, ny, at, own, low, high, link, chip, b_out, v_out, b1_out, u_out, b2_out, b, v, pair, t, s1, t1
):
    lower, upper = pick_sides(at, chip, link)
    none = jnp.zeros((16, 256), F32)
    for p in range(-HALO, 16 + HALO):
        b[p + HALO, 0:16, :] = none
        b[p + HALO, 16:32, :] = source_plane(own, low, high, p)
        b[p + HALO, 32:48, :] = none
    for p, n, rows, tile, offset in SOURCE_SEGMENTS:
        cut = slice(offset, offset + rows)
        b[p + HALO, 16 - n - rows : 16 - n, :] = lower(tile)[cut]
        b[p + HALO, 32 + n : 32 + n + rows, :] = upper(tile)[cut]
    b, v = Field(b, HALO), Field(v, HALO - 1)
    mask = row_mask((48, 256), at[1] * 16 - 16, ny)
    first_smooth(b, v, range(1 - HALO, 15 + HALO), SIDE, mask, at, nx, 0)
    v_out, b_out = Field(v_out, E0), Field(b_out, E0 - 1)
    for p in range(-E0, 16 + E0):
        v_out[p] = v[p][8:40, :]
    for p in range(1 - E0, 15 + E0):
        b_out[p] = b[p][8:40, :]
    b1, u = Field(b1_out, E1 + 1), Field(u_out, E1)
    coarsen_level0(at, nx, ny, b, v, b1, range(-E1 - 1, 9 + E1), pair, t)
    smooth_level1(at, nx, ny, b1, u, range(-E1, 8 + E1))
    coarsen_level1(b1, u, b2_out, s1, t1)


def around_block(size, extra, rows, lanes):
    return (size + 2 * extra, rows, lanes)


def first_down(nx, ny, at, own, low, high, chip, link):
    level1 = around_block(8, E1 + 1, 24, 128)
    outs = [
        around_block(16, E0 - 1, 32, 256),
        around_block(16, E0, 32, 256),
        level1,
        around_block(8, E1, 24, 128),
        (8, 128),
    ]
    scratch = [
        around_block(16, HALO, 48, 256),
        around_block(16, HALO - 1, 48, 256),
        (level1[0], 2, 56, 128),
        (level1[0], 24, 256),
        (4, 24, 128),
        (4, 8, 128),
    ]
    args = [at, own, low, high, link, chip]
    return call(functools.partial(first_down_body, nx, ny), outs, scratch, args, 20000000)


def second_down_body(nx, ny, at, mid, chip, link, b1_out, u_out, b2_out, s1, t1):
    lower, upper = pick_sides(at, chip, link)
    for i in range(8 + 2 * NEAR):
        b1_out[i, 0:8, :] = lower(i)
        b1_out[i, 8:16, :] = mid[i]
        b1_out[i, 16:24, :] = upper(i)
    b1, u = Field(b1_out, NEAR), Field(u_out, NEAR - 1)
    smooth_level1(at, nx, ny, b1, u, range(1 - NEAR, 7 + NEAR))
    coarsen_level1(b1, u, b2_out, s1, t1)


def second_down(nx, ny, at, mid, chip, link):
    outs = [around_block(8, NEAR, 24, 128), around_block(8, NEAR - 1, 24, 128), (8, 128)]
    scratch = [(4, 24, 128), (4, 8, 128)]
    args = [at, mid, chip, link]
    return call(functools.partial(second_down_body, nx, ny), outs, scratch, args, 2000000)


def solve_coarse(nx, ny, extra, at, coarse, s2, v2, w2, t3, b3, c3, d3, dup, row2):
    fetched, other = coarse
    odd = lax.rem(at[1], 2) == 1
    odd_layer = lax.rem(at[0] // GROUP, 2)
    _, _, _, r2, e2, r3 = reach(extra)
    spot = at[0] % GROUP
    rows2 = ny // 4
    rows3 = rows2 // 2
    count = rows2 // 4
    lead = 2 * (r3 + 3) + 2
    blocks = -(-lead // 4)
    s2, v2, w2 = Field(s2, 4 * blocks), Field(v2, lead - 1), Field(w2, e2)
    lane8 = iota((8, 128), 1) < 64
    for j in range(-blocks, blocks + 1):
        block = spot + GROUP + j
        layer, place = block // GROUP, block % GROUP
        first_cores = jnp.where(odd_layer == 1, layer <= 1, layer >= 1)
        mine = first_cores != odd
        inner = inside(at[0] + j, nx // 16)
        start = ((layer + odd_layer) // 2) * (GROUP * count // 2) + place * (count // 2)
        for n in range(count):
            rows = slice(8 * (n % 2), 8 * (n % 2) + 8)
            k = start + n // 2
            tile = jnp.where(mine, fetched[k, rows, :], other[k, rows, :])
            tile = jnp.where(inner, tile, 0.0)
            halves = (jnp.where(lane8, tile, 0.0), jnp.where(lane8, roll(tile, 64, 1), 0.0))
            for p in range(4):
                part = halves[p // 2][4 * (p % 2) : 4 * (p % 2) + 4, :]
                s2.ref[4 * (j + blocks) + p, 4 * n : 4 * n + 4, :] = part

    def around(f, p):
        c = f[p]
        row = iota(c.shape, 0)
        lower = jnp.where(row == 0, 0.0, roll(c, 1, 0))
        upper = jnp.where(row == c.shape[0] - 1, 0.0, roll(c, -1, 0))
        beside = (lower + upper) + (roll(c, 1, 1) + roll(c, -1, 1))
        return c, (f[p - 1] + f[p + 1]) + beside

    def lanes_below(rows, lanes):
        return jnp.where(iota((rows, 128), 1) < lanes, 1.0, 0.0).astype(F32)

    mask2 = lanes_below(rows2, 64)
    for p in range(1 - lead, 3 + lead):
        c, near = around(s2, p)
        v2[p] = wall(at, nx, 2, p, (16.0 * SIDE) * mask2 * (1.2 * c + SIDE * near))

    def residual2(p):
        c, near = around(v2, p)
        return s2[p] - (1.0 / 16.0) * (6.0 * c - near)

    planes3 = range(-r3 - 3, 2 + r3 + 3)
    for i, p in enumerate(planes3):
        row2[i, 0:rows2, :] = residual2(2 * p) + residual2(2 * p + 1)
        t3[i] = row2[i, pl.ds(0, rows3, stride=2), :] + row2[i, pl.ds(1, rows3, stride=2), :]
    total3 = len(planes3)
    full = dot(t3[...].reshape(total3 * rows3, 128), pair_matrix(128, 128, 0.125))
    full = full.reshape(total3, rows3, 128)
    mask3 = lanes_below(rows3, 32)
    b3, c3, d3 = Field(b3, r3 + 3), Field(c3, r3 + 3), Field(d3, r3 + 3)
    for i, p in enumerate(planes3):
        value = wall(at, nx, 3, p, full[i] * ((64.0 * SIDE) * mask3))
        b3[p] = value
    src, dst = b3, c3
    for step in (2, 1, 0):
        for p in range(-r3 - step, 2 + r3 + step):
            c, near = around(src, p)
            dst[p] = wall(at, nx, 3, p, mask3 * (0.2 * c + SIDE * near)) + b3[p]
        src, dst = dst, (d3 if dst is c3 else c3)
    final = src
    planes = range(-r3, 2 + r3)
    flat = jnp.concatenate([final[p] for p in planes], axis=0)
    spread = dot(flat, copy_matrix(128, 128)).reshape(len(planes), rows3, 128)
    for i, p in enumerate(planes):
        dup[i, pl.ds(0, rows3, stride=2), :] = spread[i]
        dup[i, pl.ds(1, rows3, stride=2), :] = spread[i]
        for q in (2 * p, 2 * p + 1):
            if -e2 <= q < 4 + e2:
                v2[q] = v2[q] + wall(at, nx, 2, q, dup[i, 0:rows2, :] * mask2)
    keep = SIDE * mask2
    for src, dst, step in ((v2, w2, 1), (w2, v2, 0)):
        for p in range(-r2 - step, 4 + r2 + step):
            c, near = around(src, p)
            dst[p] = 0.2 * c + wall(at, nx, 2, p, keep) * (near + 16.0 * s2[p])
    return v2


def coarse_scratch(ny, extra):
    _, _, _, _, e2, r3 = reach(extra)
    rows2 = ny // 4
    rows3 = rows2 // 2
    lead = 2 * (r3 + 3) + 2
    small = around_block(2, r3 + 3, rows3, 128)
    return [
        around_block(4, -(-lead // 4) * 4, rows2, 128),
        around_block(4, lead - 1, rows2, 128),
        around_block(4, e2, rows2, 128),
        small, small, small, small,
        (8, 48, 128),
        around_block(2, r3 + 3, rows2 + 8, 128),
    ]


def climb(nx, ny, extra, at, v2, b1, u, b, v_down, m1, n1, m0, n0, dup):
    e0, r1, e1, r2, _, _ = reach(extra)
    rows2 = ny // 4
    turn = lax.rem(rows2 + 4 - 4 * at[1] + rows2, rows2)
    planes = range(-r2, 4 + r2)
    picked = jnp.concatenate([pltpu.roll(v2[p], turn, 0)[0:16, :] for p in planes], axis=0)
    spread = dot(picked, copy_matrix(128, 128)).reshape(len(planes), 16, 128)
    mask1 = row_mask((24, 128), at[1] * 8 - 8, ny // 2)
    m1, n1 = Field(m1, e1), Field(n1, e1)
    for i, p in enumerate(planes):
        dup[i, 0, pl.ds(0, 12, stride=2), :] = spread[i, 0:12, :]
        dup[i, 0, pl.ds(1, 12, stride=2), :] = spread[i, 0:12, :]
        for q in (2 * p, 2 * p + 1):
            if -e1 <= q < 8 + e1:
                m1[q] = u[q] + wall(at, nx, 1, q, dup[i, 0, 0:24, :] * mask1)
    sweep(m1, n1, b1, range(1 - e1, 7 + e1), 4.0, mask1, at, nx, 1)
    sweep(n1, m1, b1, range(2 - e1, 6 + e1), 4.0, mask1, at, nx, 1)
    planes = range(-r1, 8 + r1)
    flat = jnp.concatenate([m1[p][4:20, :] for p in planes], axis=0)
    spread = dot(flat, copy_matrix(128, 256)).reshape(len(planes), 16, 256)
    mask0 = row_mask((32, 256), at[1] * 16 - 8, ny)
    m0, n0 = Field(m0, e0), Field(n0, e0)
    for i, p in enumerate(planes):
        for half in range(2):
            value = spread[i, :, 128 * half : 128 * half + 128]
            dup[i, half, pl.ds(0, 16, stride=2), :] = value
            dup[i, half, pl.ds(1, 16, stride=2), :] = value
        value = jnp.concatenate([dup[i, 0, 0:32, :], dup[i, 1, 0:32, :]], axis=1) * mask0
        for q in (2 * p, 2 * p + 1):
            if -e0 <= q < 16 + e0:
                m0[q] = v_down[q] + wall(at, nx, 0, q, value)
    sweep(m0, n0, b, range(1 - e0, 15 + e0), 1, mask0, at, nx, 0)
    if extra:
        sweep(n0, m0, b, range(2 - e0, 14 + e0), 1, mask0, at, nx, 0)
        return m0
    return n0


def climb_scratch(extra):
    e0, r1, e1, r2, _, _ = reach(extra)
    level1 = around_block(8, e1, 24, 128)
    level0 = around_block(16, e0, 32, 256)
    return [level1, level1, level0, level0, (max(8 + 2 * r1, 4 + 2 * r2), 2, 40, 128)]


def turn_body(nx, ny, at, fetched, other, b1, u, b, v_down, v_out, wider, low, high, own, pair, t, *scratch):
    v2 = solve_coarse(nx, ny, KEEP, at, (fetched, other), *scratch[:9])
    b = Field(b, E0 - 1)
    v = climb(nx, ny, KEEP, at, v2, Field(b1, E1 + 1), Field(u, E1), b, Field(v_down, E0), *scratch[9:])
    mask = row_mask((32, 256), at[1] * 16 - 8, ny)
    once, twice = Field(scratch[12], E0), Field(v_out, KEEP - 2)
    sweep(v, once, b, range(1 - KEEP, 15 + KEEP), 1, mask, at, nx, 0)
    sweep(once, twice, b, range(2 - KEEP, 14 + KEEP), 1, mask, at, nx, 0)
    coarsen_level0(at, nx, ny, b, twice, Field(own, 0), range(8), pair, t)
    for i in range(8):
        wider[NEAR + i] = own[i, 4:12, :]
    for i in range(NEAR):
        low[i] = own[i, 4:12, :]
        high[i] = own[8 - NEAR + i, 4:12, :]


def turn(nx, ny, at, coarse, b1, u, b, v_down):
    outs = [
        around_block(16, KEEP - 2, 32, 256),
        around_block(8, NEAR, 8, 128),
        (NEAR, 8, 128),
        (NEAR, 8, 128),
    ]
    scratch = [(8, 16, 128), (8, 2, 40, 128), (8, 16, 256)]
    scratch += coarse_scratch(ny, KEEP) + climb_scratch(KEEP)
    args = [at, *coarse, b1, u, b, v_down]
    return call(functools.partial(turn_body, nx, ny), outs, scratch, args, 30000000)


def finish_body(nx, ny, at, fetched, other, b1, u, b, v_down, out, *scratch):
    v2 = solve_coarse(nx, ny, 0, at, (fetched, other), *scratch[:9])
    b, v_down = Field(b, E0 - 1), Field(v_down, KEEP - 2)
    v = climb(nx, ny, 0, at, v2, Field(b1, NEAR), Field(u, NEAR - 1), b, v_down, *scratch[9:])
    for p in range(16):
        c, around = v.beside(p)
        out[p] = (0.2 * c + SIDE * (around + b[p]))[8:24, :]


def finish(nx, ny, at, coarse, b1, u, b, v_down):
    scratch = coarse_scratch(ny, 0) + climb_scratch(0)
    args = [at, *coarse, b1, u, b, v_down]
    return call(functools.partial(finish_body, nx, ny), [(16, 16, 256)], scratch, args, 20000000)[0]


def shifted(array, axis, step):
    count = lax.axis_size(axis)
    return lax.ppermute(
        array, axis, [(i, i + step) for i in range(count) if 0 <= i + step < count]
    )


def swapped(array, first):
    count = lax.axis_size("narrow")
    pairs = [(i, i + 1) for i in range(first, count - 1, 2)]
    return lax.ppermute(array, "narrow", pairs + [(j, i) for i, j in pairs])


def widen(wider, low, high):
    planes = low.shape[0]
    wider = lax.dynamic_update_slice(wider, shifted(high, "wide", 1), (0, 0, 0))
    upper = wider.shape[0] - planes
    return lax.dynamic_update_slice(wider, shifted(low, "wide", -1), (upper, 0, 0))


def surround(wider, low, high):
    mid = widen(wider, low, high)
    link = swapped(mid, 1)
    return mid, swapped(mid, 0), link


def spread_coarse(b2):
    wide, cores = lax.axis_size("wide"), lax.axis_size("narrow")
    layers = wide // GROUP
    odd = lax.rem(lax.axis_index("narrow"), 2) == 1
    other = swapped(b2, 0)
    pair = jnp.concatenate([jnp.where(odd, other, b2), jnp.where(odd, b2, other)], axis=0)
    groups = [
        [
            (((2 * k + core + i) % layers) * GROUP + x) * cores + y
            for i in range(2)
            for x in range(GROUP)
            for y in range(core, cores, 2)
        ]
        for core in range(2)
        for k in range(layers // 2)
    ]
    pieces = jnp.broadcast_to(pair[None], (len(groups[0]),) + pair.shape)
    fetched = lax.all_to_all(pieces, ("wide", "narrow"), 0, 0, axis_index_groups=groups)
    return fetched, swapped(fetched, 0)


def on_device(phase, distance, velocity):
    nx, ny = 16 * lax.axis_size("wide"), 16 * lax.axis_size("narrow")
    at = jnp.stack([lax.axis_index("wide"), lax.axis_index("narrow")]).astype(jnp.int32)
    psi, x_low, x_high = prepare(phase, distance, velocity)
    low, high = shifted(x_high, "wide", 1), shifted(x_low, "wide", -1)
    known = inner_z(psi, velocity)
    link, chip = pack(at, psi, velocity, low, high, known)
    v_link = swapped(link, 1)
    v_chip = swapped(chip, 0)
    change = inner(psi, velocity, low, high, known)
    moved, source, first, final = advance(
        nx, ny, at, psi, velocity, low, high, v_chip, v_link, change
    )
    low, high = shifted(final, "wide", 1), shifted(first, "wide", -1)
    link, chip = weave(at, source, low, high)
    b_link = swapped(link, 1)
    b_chip = swapped(chip, 0)
    b, v, b1, u, b2 = first_down(nx, ny, at, source, low, high, b_chip, b_link)
    v, *sends = turn(nx, ny, at, spread_coarse(b2), b1, u, b, v)
    b1, u, b2 = second_down(nx, ny, at, *surround(*sends))
    pressure = finish(nx, ny, at, spread_coarse(b2), b1, u, b, v)
    return (moved, pressure)


def solution(mesh):
    blocks = P("wide", "narrow", None)
    return jax.shard_map(
        on_device,
        mesh=mesh,
        in_specs=(blocks, blocks, P(None, "wide", "narrow", None)),
        out_specs=(blocks, blocks),
        check_vma=False,
    )
```
